128 devices in a mesh: dp: 8 (over x, z_hi), fsdp: 16 (over z_lo, y, core).
Axes of the slice: x: 4, y: 4, z: 4 (z_hi: 2, z_lo: 2; z = z_hi * 2 + z_lo), core: 2. Of those that a mesh axis runs over, the one named last changes fastest.
Arguments:
- hidden: bfloat16 [16, 1536, 1024], P('fsdp', 'dp'), may hold values from -6 to 6
- lengths: int32 [16, 3], P('fsdp'), may hold values from 1 to 1534, as said below
- w_query: bfloat16 [1024, 2048], P(('dp', 'fsdp')), may hold values from -0.1875 to 0.1875
- w_key: bfloat16 [1024, 1024], P(('dp', 'fsdp')), may hold values from -0.1875 to 0.1875
- w_value: bfloat16 [1024, 1024], P(('dp', 'fsdp')), may hold values from -0.1875 to 0.1875
- w_out: bfloat16 [2048, 1024], P(('dp', 'fsdp')), may hold values from -0.75 to 0.75
- w_gate: bfloat16 [1024, 3072], P(('dp', 'fsdp')), may hold values from -0.1875 to 0.1875
- w_up: bfloat16 [1024, 3072], P(('dp', 'fsdp')), may hold values from -0.1875 to 0.1875
- w_down: bfloat16 [3072, 1024], P(('dp', 'fsdp')), may hold values from -0.109375 to 0.109375
- gains: bfloat16 [2304], P(('dp', 'fsdp')), may hold values from 0.099609375 to 1.8984375
- cotangent: bfloat16 [16, 1536, 1024], P('fsdp', 'dp'), may hold values from -6 to 6
Outputs:
- activations: bfloat16 [16, 1536, 1024], P('fsdp', 'dp')
- input_grad: float32 [16, 1536, 1024], P('fsdp', 'dp')
- grad_query: float32 [1024, 2048], P(('dp', 'fsdp'))
- grad_key: float32 [1024, 1024], P(('dp', 'fsdp'))
- grad_value: float32 [1024, 1024], P(('dp', 'fsdp'))
- grad_out: float32 [2048, 1024], P(('dp', 'fsdp'))
- grad_gate: float32 [1024, 3072], P(('dp', 'fsdp'))
- grad_up: float32 [1024, 3072], P(('dp', 'fsdp'))
- grad_down: float32 [3072, 1024], P(('dp', 'fsdp'))
- grad_gains: float32 [2304], P(('dp', 'fsdp'))
The draws below stay inside these ranges and needn't reach their ends.
Inputs may be any that keep to these rules, and one draw needn't show every extreme that they name: `lengths`: in each pack the first and the last document hold 1 to 96 tokens each and the middle one the rest of the 1536 tokens.
All inputs are finite; a program needn't handle non-finite values.
Results may differ from the reference program's by a relative error of at most 0.017.
Values may be sent and summed in bfloat16 or wider, within the bound.
No kernel may reach another device: no remote copies, remote signals or barrier semaphores. Data moves between devices by JAX's collectives and lax.ppermute only.
A program may use at most 192 MiB of HBM per device.

```python
import jax
import jax.numpy as jnp
from jax import lax

D = 1024
FF = 3072
HEADS = 16
KV_HEADS = 8
HEAD = 128
TOK_DEV = 192
QW = 2048
KW = 1024
GROUP_TOK = 1536
PACKS = 16


def draw_lengths(key, part):
    key = jax.random.fold_in(key, 7)
    first_key, last_key, pick_key = jax.random.split(key, 3)
    first_len = jax.random.randint(first_key, (PACKS,), 1, TOK_DEV // 2 + 1, dtype=jnp.int32)
    last_len = jax.random.randint(last_key, (PACKS,), 1, TOK_DEV // 2 + 1, dtype=jnp.int32)
    chosen = jax.random.randint(pick_key, (), 0, PACKS, dtype=jnp.int32)
    picked = jnp.arange(PACKS, dtype=jnp.int32) == chosen
    first_len = jnp.where(picked, jnp.int32(1), first_len)
    last_len = jnp.where(picked, jnp.int32(1), last_len)
    middle_len = GROUP_TOK - first_len - last_len
    return jnp.stack([first_len, middle_len, last_len], axis=-1).astype(jnp.int32)


def level_of(rng, dims, cuts, low, high):
    def one(axis_at, blocks):
        heights = jax.random.uniform(jax.random.fold_in(jax.random.fold_in(rng, 6), axis_at), (blocks,), jnp.float32, low / len(cuts), high / len(cuts))
        return jnp.repeat(jnp.exp(heights), dims[axis_at] // blocks).reshape((-1,) + (1,) * (len(dims) - axis_at - 1))

    loudness = one(*cuts[0])
    for cut in cuts[1:]:
        loudness = loudness * one(*cut)
    return loudness


def noise(rng, dims, scale, most, shards=(), kind=jnp.bfloat16):
    factor_of = level_of(rng, dims, shards, -0.22, 0.18) if shards else 1.0
    array = jax.random.normal(rng, dims, jnp.float32) * scale * factor_of
    return jnp.minimum(jnp.maximum(array, -most), most).astype(kind)


def setup_inputs(seed: int = 0) -> dict:
    arg_keys = jax.random.split(jax.random.key(seed), 12)
    hidden = noise(arg_keys[0], (PACKS, GROUP_TOK, D), 1.0, 6.0, ((0, 16), (1, 8)))
    lengths = draw_lengths(jax.random.fold_in(arg_keys[11], 71), 0)
    w_query = noise(arg_keys[2], (D, QW), D ** -0.5, 0.1875, ((0, 128),))
    w_key = noise(arg_keys[3], (D, KW), D ** -0.5, 0.1875, ((0, 128),))
    w_value = noise(arg_keys[4], (D, KW), D ** -0.5, 0.1875, ((0, 128),))
    w_out = noise(arg_keys[5], (QW, D), (QW // 32) ** -0.5, 0.75, ((0, 128),))
    w_gate = noise(arg_keys[6], (D, FF), D ** -0.5, 0.1875, ((0, 128),))
    w_up = noise(arg_keys[7], (D, FF), D ** -0.5, 0.1875, ((0, 128),))
    w_down = noise(arg_keys[8], (FF, D), FF ** -0.5, 0.109375, ((0, 128),))
    gains = jnp.clip(1.0 + 0.18 * jax.random.normal(arg_keys[9], (2 * D + 2 * HEAD,), jnp.float32), 0.099609375, 1.8984375).astype(jnp.bfloat16)
    cotangent = noise(arg_keys[10], (PACKS, GROUP_TOK, D), 1.0, 6.0, ((0, 16), (1, 8)))
    return dict(hidden=hidden, lengths=lengths, w_query=w_query, w_key=w_key, w_value=w_value, w_out=w_out, w_gate=w_gate, w_up=w_up, w_down=w_down, gains=gains, cotangent=cotangent)


@jax.custom_vjp
def low(v):
    return lax.optimization_barrier(v.astype(jnp.bfloat16)).astype(jnp.float32)

@jax.custom_vjp
def low_back(v):
    return v

def low_keep(v):
    return (low(v), None)

def low_pass(kept, grad):
    return (grad,)

def back_keep(v):
    return (v, None)

def back_low(kept, grad):
    return (low(grad),)
low.defvjp(low_keep, low_pass)
low_back.defvjp(back_keep, back_low)
EPSILON = 1e-06
ROPE_BASE = 1000000.0
MASKED = -1e+30
HIGH = lax.Precision.HIGHEST

def scaled_norm(values, gain_vec):
    return values * lax.rsqrt(lax.optimization_barrier(jnp.mean(values * values, axis=-1, keepdims=True)) + EPSILON) * gain_vec

def rotate_half(values):
    half_width = values.shape[-1] // 2
    return jnp.concatenate([-values[..., half_width:], values[..., :half_width]], axis=-1)

def rope_tables(position, head_width):
    half_width = head_width // 2
    inverse = jnp.power(ROPE_BASE, -2.0 * jnp.arange(half_width, dtype=jnp.float32) / head_width)
    angles = position.astype(jnp.float32)[:, None] * inverse[None, :]
    angles = jnp.concatenate([angles, angles], axis=-1)
    return (jnp.cos(angles), jnp.sin(angles))

def head_rotary(values, gain_vec, cosine_table, sine_table):
    normal = scaled_norm(values, gain_vec)
    return normal * cosine_table[:, None, :] + rotate_half(normal) * sine_table[:, None, :]

def doc_layout(pack_lengths, positions):
    seq_ends = jnp.cumsum(pack_lengths, axis=-1).astype(jnp.int32)
    passed = (positions[..., None] >= seq_ends[..., None, :]).astype(jnp.int32)
    segment = lax.optimization_barrier(jnp.sum(passed, axis=-1)).astype(jnp.int32)
    seq_start = lax.optimization_barrier(jnp.sum(passed * pack_lengths[..., None, :], axis=-1)).astype(jnp.int32)
    return (segment, positions - seq_start)

def attend_pack(operands):
    queries, keys, values, segment = operands
    pack_rows = segment.shape[0]
    per_group = queries.shape[1] // keys.shape[1]
    keys_wide = jnp.repeat(keys, per_group, axis=1)
    values_wide = jnp.repeat(values, per_group, axis=1)
    raw_scores = jnp.einsum('qhd,khd->hqk', queries, keys_wide, precision=HIGH)
    score_scale = queries.shape[-1] ** (-0.5)
    scores = low_back(raw_scores) * score_scale
    positions = jnp.arange(pack_rows, dtype=jnp.int32)
    allowed = (segment[:, None] == segment[None, :]) & (positions[None, :] <= positions[:, None])
    scores = jnp.where(allowed[None], scores, MASKED)
    probabilities = jax.nn.softmax(scores, axis=-1)
    return jnp.einsum('hqk,khd->qhd', low(probabilities), values_wide, precision=HIGH)

def reference(hidden, lengths, w_query, w_key, w_value, w_out, w_gate, w_up, w_down, gains, cotangent):
    pack_count, pack_rows, feature_width = hidden.shape
    positions = jnp.broadcast_to(jnp.arange(pack_rows, dtype=jnp.int32)[None, :], (pack_count, pack_rows))
    segment, position = doc_layout(lengths, positions)
    cosine_table, sine_table = rope_tables(position.reshape(-1), HEAD)

    def forward(inputs, weight_query, weight_key, weight_value, weight_out, weight_gate, weight_up, weight_down, gain_all):
        gain_attn = gain_all[:feature_width]
        gain_mlp = gain_all[feature_width:2 * feature_width]
        gain_query = gain_all[2 * feature_width:2 * feature_width + HEAD]
        gain_key = gain_all[2 * feature_width + HEAD:]
        normed = low(scaled_norm(inputs, gain_attn))
        query_pre = low_back(jnp.dot(normed, weight_query, precision=HIGH))
        key_pre = low_back(jnp.dot(normed, weight_key, precision=HIGH))
        values = low(low_back(jnp.dot(normed, weight_value, precision=HIGH)))
        queries = low(head_rotary(query_pre.reshape(-1, HEADS, HEAD), gain_query, cosine_table, sine_table))
        keys = low(head_rotary(key_pre.reshape(-1, KV_HEADS, HEAD), gain_key, cosine_table, sine_table))
        attended = lax.map(jax.checkpoint(attend_pack), (queries.reshape(pack_count, pack_rows, HEADS, HEAD), keys.reshape(pack_count, pack_rows, KV_HEADS, HEAD), values.reshape(pack_count, pack_rows, KV_HEADS, HEAD), segment))
        attended = low(low_back(attended.reshape(-1, HEADS * HEAD)))
        middle = inputs + low_back(jnp.dot(attended, weight_out, precision=HIGH))
        mixed_in = low(scaled_norm(middle, gain_mlp))
        gate_pre = low_back(jnp.dot(mixed_in, weight_gate, precision=HIGH))
        up_pre = low_back(jnp.dot(mixed_in, weight_up, precision=HIGH))
        hidden_act = low(jax.nn.silu(gate_pre) * up_pre)
        return middle + low_back(jnp.dot(hidden_act, weight_down, precision=HIGH))
    casted = (hidden.reshape(-1, feature_width).astype(jnp.float32), w_query.astype(jnp.float32), w_key.astype(jnp.float32), w_value.astype(jnp.float32), w_out.astype(jnp.float32), w_gate.astype(jnp.float32), w_up.astype(jnp.float32), w_down.astype(jnp.float32), gains.astype(jnp.float32))
    result, pullback = jax.vjp(forward, *casted)
    gradients = pullback(cotangent.reshape(-1, feature_width).astype(jnp.float32))
    return (result.astype(jnp.bfloat16).reshape(hidden.shape), gradients[0].reshape(hidden.shape), gradients[1], gradients[2], gradients[3], gradients[4], gradients[5], gradients[6], gradients[7], gradients[8])
```

```python
import functools

import jax
import jax.numpy as jnp
import numpy as np
from jax import lax
from jax.experimental import pallas as pl
from jax.experimental.pallas import tpu as pltpu
from jax.sharding import PartitionSpec as P

HEADS = 16
KV_HEADS = 8
HEAD = 128
EPSILON = 1e-06
ROPE_BASE = 1000000.0
DEVICES = 128
WIDTH = 1024
FF = 3072
TOK = 192
PACK = 1536
BLOCK = 256
LOG2E = 1.4426950408889634
SCALE = HEAD ** (-0.5)
EVERY = ("dp", "fsdp")
VMEM_LIMIT = 48 * 1024 * 1024

XA, XB, ZH, ZA, ZB, YA, YB, CORE = 32, 96, 16, 8, 24, 2, 6, 1
PACK_ORDERS = ((XA, XB, ZH), (XB, ZH, XA), (ZH, XA, XB))


def both_cores(order):
    other = {XA: XB, XB: XA, YA: YB, YB: YA, ZA: ZB, ZB: ZA}
    return (tuple(order), tuple(other[m] for m in order))


CHIP_ORDERS = (
    both_cores((YA, YB, ZA, ZB, XA, XB)),
    both_cores((ZA, ZB, XA, XB, YA, YB)),
    both_cores((XA, XB, YA, YB, ZA, ZB)),
)


def swap(values, mask, other_mask=None):
    masks = (mask, mask if other_mask is None else other_mask)
    return lax.ppermute(values, EVERY, [(k, k ^ masks[k & 1]) for k in range(DEVICES)])


def low(values):
    return values.astype(jnp.bfloat16)


def wide(values):
    return values.astype(jnp.float32)


def dot(left, right):
    return jnp.dot(left, right, preferred_element_type=jnp.float32)


def contract_rows(left, right):
    return lax.dot_general(
        left, right, (((0,), (0,)), ((), ())), preferred_element_type=jnp.float32
    )


def contract_cols(left, right):
    return lax.dot_general(
        left, right, (((1,), (1,)), ((), ())), preferred_element_type=jnp.float32
    )


def norm_scale(values):
    return lax.rsqrt(jnp.mean(values * values, axis=-1, keepdims=True) + EPSILON)


def norm_back(values, gain, grad):
    scale = norm_scale(values)
    normal = values * scale
    inner = grad * gain
    return scale * (inner - normal * jnp.mean(inner * normal, axis=-1, keepdims=True))


def rope(values, cosine, sine):
    return values * cosine + pltpu.roll(values, 64, 1) * sine


def rope_back(grad, cosine, sine):
    return grad * cosine + pltpu.roll(grad * sine, 64, 1)


def qkv_kernel(
    pos_ref, part_a, part_b, part_c, w_ref, ga_ref, gq_ref, gk_ref, cos_ref, sin_ref,
    normed_ref, pre_ref, qkv_ref,
):
    rows = part_a.shape[1]
    for n, part in enumerate((part_a, part_b, part_c)):
        x = wide(part[0])
        normed_ref[n * rows : (n + 1) * rows, :] = low(x * norm_scale(x) * ga_ref[...])
    pre = dot(normed_ref[...], w_ref[...])
    pre_ref[...] = pre[:, : 3 * HEAD]
    cosine, sine = cos_ref[...], sin_ref[...]
    for h in range(3):
        u = pre[:, h * HEAD : (h + 1) * HEAD]
        gain = gk_ref[...] if h == 2 else gq_ref[...]
        normal = u * norm_scale(u) * gain
        qkv_ref[:, h * HEAD : (h + 1) * HEAD] = low(rope(normal, cosine, sine))
    qkv_ref[:, 3 * HEAD :] = low(pre[:, 3 * HEAD :])


def project(parts, pos, weights, gain_attn, gain_query, gain_key, cosine, sine):
    chunk = parts[0].shape[1]
    rows = 3 * chunk
    count = parts[0].shape[0]
    part_spec = [
        pl.BlockSpec((1, chunk, WIDTH), lambda d, pos, n=n: (pos[n, d], 0, 0))
        for n in range(3)
    ]
    whole = lambda shape: pl.BlockSpec(shape, lambda d, pos: (0, 0))
    by_row = lambda cols: pl.BlockSpec((rows, cols), lambda d, pos: (d, 0))
    return pl.pallas_call(
        qkv_kernel,
        grid_spec=pltpu.PrefetchScalarGridSpec(
            num_scalar_prefetch=1,
            grid=(count,),
            in_specs=part_spec
            + [whole((WIDTH, 512)), whole((1, WIDTH)), whole((1, HEAD)), whole((1, HEAD))]
            + [by_row(HEAD), by_row(HEAD)],
            out_specs=[by_row(WIDTH), by_row(3 * HEAD), by_row(512)],
        ),
        out_shape=[
            jax.ShapeDtypeStruct((PACK, WIDTH), jnp.bfloat16),
            jax.ShapeDtypeStruct((PACK, 3 * HEAD), jnp.float32),
            jax.ShapeDtypeStruct((PACK, 512), jnp.bfloat16),
        ],
        compiler_params=pltpu.CompilerParams(vmem_limit_bytes=VMEM_LIMIT),
        cost_estimate=pl.CostEstimate(flops=1610612736, bytes_accessed=12000000, transcendentals=0),
        name="project",
    )(pos, *parts, weights, gain_attn, gain_query, gain_key, cosine, sine)


def row_start(rows, ends):
    first, second = ends
    return jnp.where(rows >= second, second, jnp.where(rows >= first, first, 0))


def allowed_block(q_block, k_block, ends, transposed):
    q_axis, k_axis = (1, 0) if transposed else (0, 1)
    q_rows = q_block * BLOCK + lax.broadcasted_iota(jnp.int32, (BLOCK, BLOCK), q_axis)
    k_rows = k_block * BLOCK + lax.broadcasted_iota(jnp.int32, (BLOCK, BLOCK), k_axis)
    return (k_rows <= q_rows) & (k_rows >= row_start(q_rows, ends))


def over_blocks(q_block, step, carry):
    last = PACK // BLOCK - 1
    masked_from = jnp.where(q_block == last, 1, jnp.maximum(q_block, 1))
    carry = step(0, True, carry)
    carry = lax.fori_loop(1, masked_from, lambda k, c: step(k, False, c), carry)
    return lax.fori_loop(masked_from, q_block + 1, lambda k, c: step(k, True, c), carry)


def attend_kernel(ends_ref, q_ref, k_ref, v_ref, mix_ref, out_ref, mixed_ref, inverse_ref):
    q_block = pl.program_id(0)
    ends = (ends_ref[0], ends_ref[1])
    heads = [q_ref[:, :HEAD], q_ref[:, HEAD:]]

    def step(k_block, masked, carry):
        rows = pl.ds(pl.multiple_of(k_block * BLOCK, BLOCK), BLOCK)
        keys, values = k_ref[rows, :], v_ref[rows, :]
        allowed = allowed_block(q_block, k_block, ends, False) if masked else None
        new = []
        for h in range(2):
            total, part = carry[2 * h], carry[2 * h + 1]
            shifted = jnp.exp2(contract_cols(heads[h], keys) * (SCALE * LOG2E))
            if masked:
                shifted = jnp.where(allowed, shifted, 0.0)
            new.append(total + dot(low(shifted), values))
            new.append(part + shifted[:, :HEAD] + shifted[:, HEAD:])
        return tuple(new)

    zero = jnp.zeros((BLOCK, HEAD), jnp.float32)
    carry = over_blocks(q_block, step, (zero, zero, zero, zero))
    for h in range(2):
        total, part = carry[2 * h], carry[2 * h + 1]
        row_total = jnp.sum(part, axis=1, keepdims=True)
        out_ref[:, h * HEAD : (h + 1) * HEAD] = low(total / row_total)
        across = jnp.sum(jnp.swapaxes(part, 0, 1), axis=0, keepdims=True)
        inverse_ref[h : h + 1, :] = 1.0 / across
    mixed_ref[...] = low(dot(out_ref[...], mix_ref[...]))


def attend(ends, qkv, mix):
    blocks = PACK // BLOCK
    return pl.pallas_call(
        attend_kernel,
        grid_spec=pltpu.PrefetchScalarGridSpec(
            num_scalar_prefetch=1,
            grid=(blocks,),
            in_specs=[
                pl.BlockSpec((BLOCK, 2 * HEAD), lambda q, ends: (q, 0)),
                pl.BlockSpec((PACK, HEAD), lambda q, ends: (0, 2)),
                pl.BlockSpec((PACK, HEAD), lambda q, ends: (0, 3)),
                pl.BlockSpec((2 * HEAD, 2 * HEAD), lambda q, ends: (0, 0)),
            ],
            out_specs=[
                pl.BlockSpec((BLOCK, 2 * HEAD), lambda q, ends: (q, 0)),
                pl.BlockSpec((BLOCK, 2 * HEAD), lambda q, ends: (q, 0)),
                pl.BlockSpec((2, BLOCK), lambda q, ends: (0, q)),
            ],
        ),
        out_shape=[
            jax.ShapeDtypeStruct((PACK, 2 * HEAD), jnp.bfloat16),
            jax.ShapeDtypeStruct((PACK, 2 * HEAD), jnp.bfloat16),
            jax.ShapeDtypeStruct((2, PACK), jnp.float32),
        ],
        compiler_params=pltpu.CompilerParams(vmem_limit_bytes=VMEM_LIMIT),
        cost_estimate=pl.CostEstimate(flops=3000000000, bytes_accessed=4000000, transcendentals=3000000),
        name="attend",
    )(ends, qkv, qkv, qkv, mix)


def attend_back_kernel(
    ends_ref, q_ref, k_ref, v_ref, grad_ref, out_ref, inverse_ref, mix_ref,
    dq_ref, dk_ref, dv_ref,
):
    q_block = pl.program_id(0)
    ends = (ends_ref[0], ends_ref[1])

    @pl.when(q_block == 0)
    def _():
        dk_ref[...] = jnp.zeros_like(dk_ref)
        dv_ref[...] = jnp.zeros_like(dv_ref)

    grad = low(contract_cols(grad_ref[...], mix_ref[...]))
    heads = [q_ref[:, :HEAD], q_ref[:, HEAD:]]
    grads = [grad[:, :HEAD], grad[:, HEAD:]]
    inverse = [inverse_ref[h : h + 1, :] for h in range(2)]
    delta = []
    for h in range(2):
        product = wide(grads[h]) * wide(out_ref[:, h * HEAD : (h + 1) * HEAD])
        delta.append(jnp.sum(jnp.swapaxes(product, 0, 1), axis=0, keepdims=True))

    def step(k_block, masked, carry):
        rows = pl.ds(pl.multiple_of(k_block * BLOCK, BLOCK), BLOCK)
        keys, values = k_ref[rows, :], v_ref[rows, :]
        allowed = allowed_block(q_block, k_block, ends, True) if masked else None
        new = []
        d_keys, d_values = dk_ref[rows, :], dv_ref[rows, :]
        for h in range(2):
            prob = jnp.exp2(contract_cols(keys, heads[h]) * (SCALE * LOG2E)) * inverse[h]
            if masked:
                prob = jnp.where(allowed, prob, 0.0)
            d_prob = contract_cols(values, grads[h])
            d_score = low(prob * (d_prob - delta[h]) * SCALE)
            d_keys += dot(d_score, heads[h])
            d_values += dot(low(prob), grads[h])
            new.append(carry[h] + contract_rows(d_score, keys))
        dk_ref[rows, :] = d_keys
        dv_ref[rows, :] = d_values
        return tuple(new)

    zero = jnp.zeros((BLOCK, HEAD), jnp.float32)
    carry = over_blocks(q_block, step, (zero, zero))
    dq_ref[:, :HEAD] = carry[0]
    dq_ref[:, HEAD:] = carry[1]


def attend_back(ends, qkv, grad, out, inverse, mix):
    blocks = PACK // BLOCK
    by_block = pl.BlockSpec((BLOCK, 2 * HEAD), lambda q, ends: (q, 0))
    whole = pl.BlockSpec((PACK, HEAD), lambda q, ends: (0, 0))
    return pl.pallas_call(
        attend_back_kernel,
        grid_spec=pltpu.PrefetchScalarGridSpec(
            num_scalar_prefetch=1,
            grid=(blocks,),
            in_specs=[
                by_block,
                pl.BlockSpec((PACK, HEAD), lambda q, ends: (0, 2)),
                pl.BlockSpec((PACK, HEAD), lambda q, ends: (0, 3)),
                by_block,
                by_block,
                pl.BlockSpec((2, BLOCK), lambda q, ends: (0, q)),
                pl.BlockSpec((2 * HEAD, 2 * HEAD), lambda q, ends: (0, 0)),
            ],
            out_specs=[by_block, whole, whole],
        ),
        out_shape=[
            jax.ShapeDtypeStruct((PACK, 2 * HEAD), jnp.float32),
            jax.ShapeDtypeStruct((PACK, HEAD), jnp.float32),
            jax.ShapeDtypeStruct((PACK, HEAD), jnp.float32),
        ],
        compiler_params=pltpu.CompilerParams(vmem_limit_bytes=VMEM_LIMIT),
        cost_estimate=pl.CostEstimate(flops=8000000000, bytes_accessed=8000000, transcendentals=3000000),
        name="attend_back",
    )(ends, qkv, qkv, qkv, grad, out, inverse, mix)


def qkv_back_kernel(
    pos_ref, pre_ref, dq_ref, dk_ref, dv_ref, cos_ref, sin_ref, normed_ref, w_ref, gq_ref, gk_ref,
    d_pre_ref, part_a, part_b, part_c, d_attn_ref, d_head_ref,
):
    @pl.when(pl.program_id(0) == 0)
    def _():
        d_attn_ref[...] = jnp.zeros_like(d_attn_ref)
        d_head_ref[...] = jnp.zeros_like(d_head_ref)

    cosine, sine = cos_ref[...], sin_ref[...]
    for h in range(3):
        u = pre_ref[:, h * HEAD : (h + 1) * HEAD]
        gain = gk_ref[...] if h == 2 else gq_ref[...]
        grad = dk_ref[...] if h == 2 else dq_ref[:, h * HEAD : (h + 1) * HEAD]
        grad = rope_back(grad, cosine, sine)
        row = 1 if h == 2 else 0
        d_head_ref[row : row + 1, :] += jnp.sum(
            grad * u * norm_scale(u), axis=0, keepdims=True
        )
        d_pre_ref[:, h * HEAD : (h + 1) * HEAD] = low(norm_back(u, gain, grad))
    d_pre_ref[:, 3 * HEAD :] = low(dv_ref[...])
    d_normed = contract_cols(d_pre_ref[...], w_ref[...])
    d_attn_ref[...] += jnp.sum(wide(normed_ref[...]) * d_normed, axis=0, keepdims=True)
    rows = part_a.shape[1]
    for n, part in enumerate((part_a, part_b, part_c)):
        part[0] = low(d_normed[n * rows : (n + 1) * rows, :])


def project_back(pos, pre, d_query, d_key, d_value, cosine, sine, normed, weights, gain_query, gain_key):
    count, rows = pos.shape[1], PACK // pos.shape[1]
    chunk = rows // 3
    part_spec = [
        pl.BlockSpec((1, chunk, WIDTH), lambda d, pos, n=n: (pos[n, d], 0, 0))
        for n in range(3)
    ]
    whole = lambda shape: pl.BlockSpec(shape, lambda d, pos: (0, 0))
    by_row = lambda cols: pl.BlockSpec((rows, cols), lambda d, pos: (d, 0))
    part_shape = jax.ShapeDtypeStruct((count, chunk, WIDTH), jnp.bfloat16)
    return pl.pallas_call(
        qkv_back_kernel,
        grid_spec=pltpu.PrefetchScalarGridSpec(
            num_scalar_prefetch=1,
            grid=(count,),
            in_specs=[by_row(3 * HEAD), by_row(2 * HEAD), by_row(HEAD), by_row(HEAD)]
            + [by_row(HEAD), by_row(HEAD), by_row(WIDTH)]
            + [whole((WIDTH, 512)), whole((1, HEAD)), whole((1, HEAD))],
            out_specs=[by_row(512)] + part_spec + [whole((1, WIDTH)), whole((2, HEAD))],
        ),
        out_shape=[
            jax.ShapeDtypeStruct((PACK, 512), jnp.bfloat16),
            part_shape,
            part_shape,
            part_shape,
            jax.ShapeDtypeStruct((1, WIDTH), jnp.float32),
            jax.ShapeDtypeStruct((2, HEAD), jnp.float32),
        ],
        compiler_params=pltpu.CompilerParams(vmem_limit_bytes=VMEM_LIMIT),
        cost_estimate=pl.CostEstimate(flops=1610612736, bytes_accessed=15000000, transcendentals=0),
        name="project_back",
    )(pos, pre, d_query, d_key, d_value, cosine, sine, normed, weights, gain_query, gain_key)


def one_hot(rows, columns):
    hits = lax.broadcasted_iota(jnp.int32, (rows, columns.shape[0]), 0) == columns[None, :]
    return hits.astype(jnp.bfloat16)


def feature_mix(per_device, devices):
    slices = per_device // 8
    spot = np.arange(per_device * devices)
    k, dev, r = spot // (8 * devices), spot // 8 % devices, spot % 8
    return one_hot(per_device * devices, jnp.asarray(dev * per_device + 8 * k + r, jnp.int32)), slices


def hidden_units_apart(weights):
    mix, slices = feature_mix(24, 16)
    blocks = weights.reshape(-1, 384)
    moved = low(dot(blocks, mix))
    return moved.reshape(weights.shape[0], -1, slices, 128).transpose(0, 2, 1, 3).reshape(weights.shape)


def hidden_units_back(grads):
    mix, slices = feature_mix(24, 16)
    blocks = grads.reshape(grads.shape[0], slices, -1, 128).transpose(0, 2, 1, 3).reshape(-1, 384)
    moved = lax.dot_general(
        blocks, wide(mix), (((1,), (1,)), ((), ())), precision=lax.Precision.HIGHEST
    )
    return moved.reshape(grads.shape)


def chip_order(index, order):
    spots = []
    for masks in order:
        spot = np.zeros(64, np.int32)
        for step, mask in enumerate(masks):
            spot ^= np.where(np.arange(64) >> (5 - step) & 1, mask, 0).astype(np.int32)
        spots.append(spot)
    chosen = jnp.where(index & 1 == 1, jnp.asarray(spots[1]), jnp.asarray(spots[0]))
    owner = index ^ chosen
    return one_hot(WIDTH, (owner[:, None] * 8 + jnp.arange(8, dtype=jnp.int32)[None, :]).reshape(-1))


def gather_pack(rows):
    chunk = rows.shape[0] // 3
    parts = [rows[None, n * chunk : (n + 1) * chunk] for n in range(3)]
    for step in range(3):
        parts = [
            jnp.concatenate([part, swap(part, PACK_ORDERS[n][step])], axis=0)
            for n, part in enumerate(parts)
        ]
    return parts


def pack_spots(dp_rank, count):
    other = dp_rank ^ jnp.arange(count, dtype=jnp.int32)
    bit = {XB: other >> 2 & 1, XA: (other >> 1 ^ other >> 2) & 1, ZH: other & 1}
    return jnp.stack(
        [sum(bit[mask] << step for step, mask in enumerate(order)) for order in PACK_ORDERS]
    )


def scatter_pack(parts):
    parts = list(parts)
    for step in (2, 1, 0):
        half = 1 << step
        got = [swap(part[half:], PACK_ORDERS[n][step]) for n, part in enumerate(parts)]
        parts = [wide(part[:half]) + wide(new) for part, new in zip(parts, got)]
        if step:
            parts = [low(part) for part in parts]
    return jnp.concatenate([part[0] for part in parts], axis=0)


def scatter_chips(keep, send, order, axis):
    for step in range(6):
        got = swap(send, order[0][step], order[1][step])
        total = wide(keep) + wide(got)
        if step == 5:
            return total
        half = total.shape[axis] // 2
        keep = low(lax.slice_in_dim(total, 0, half, axis=axis))
        send = low(lax.slice_in_dim(total, half, 2 * half, axis=axis))


def on_device(
    hidden, lengths, w_query, w_key, w_value, w_out, w_gate, w_up, w_down, gains, cotangent
):
    dp_size = lax.axis_size("dp")
    dp_rank = lax.axis_index("dp")
    fsdp_rank = lax.axis_index("fsdp")
    index = dp_rank * 16 + fsdp_rank
    inputs = hidden[0]
    d_result = cotangent[0]

    local = jnp.concatenate(
        [
            hidden_units_apart(w_gate),
            hidden_units_apart(w_up),
            w_down.reshape(3, 8, WIDTH).transpose(1, 0, 2).reshape(8, -1),
            w_out.reshape(2, 8, WIDTH).transpose(1, 0, 2).reshape(8, -1),
        ],
        axis=1,
    )
    full = lax.all_gather(local, EVERY, axis=0, tiled=True)
    full_gate, full_up = full[:, :FF], full[:, FF : 2 * FF]
    full_down = [full[:, 2 * FF + k * WIDTH : 2 * FF + (k + 1) * WIDTH] for k in range(3)]
    full_out = [full[:, 3 * FF + k * WIDTH : 3 * FF + (k + 1) * WIDTH] for k in range(2)]

    heads = jnp.concatenate(
        [
            w_query.reshape(8, KV_HEADS, 256).transpose(1, 0, 2),
            w_key.reshape(8, KV_HEADS, HEAD).transpose(1, 0, 2),
            w_value.reshape(8, KV_HEADS, HEAD).transpose(1, 0, 2),
            jnp.broadcast_to(jnp.pad(gains[None, None, :], ((0, 0), (0, 7), (0, 110))), (8, 8, 128)),
        ],
        axis=2,
    )
    heads = lax.all_to_all(heads, "dp", split_axis=0, concat_axis=0, tiled=True)[None]
    for mask, bit in ((CORE, 0), (YA, 1), (YB, 2), (ZA, 3)):
        got = swap(heads, mask)
        heads = jnp.where(
            fsdp_rank >> bit & 1 == 1,
            jnp.concatenate([got, heads], axis=0),
            jnp.concatenate([heads, got], axis=0),
        )
    heads = heads.transpose(1, 0, 2, 3)
    w_heads = heads[..., :512].reshape(WIDTH, 512)
    gain_all = wide(heads[:, :, 0, 512:530].reshape(1, -1))
    gain_attn, gain_mlp = gain_all[:, :WIDTH], gain_all[:, WIDTH : 2 * WIDTH]
    gain_query = gain_all[:, 2 * WIDTH : 2 * WIDTH + HEAD]
    gain_key = gain_all[:, 2 * WIDTH + HEAD :]

    parts = gather_pack(inputs)
    spots = pack_spots(dp_rank, dp_size)
    ends = jnp.stack([lengths[0, 0], lengths[0, 0] + lengths[0, 1]]).astype(jnp.int32)
    token = jnp.arange(PACK, dtype=jnp.int32)
    position = wide(token - row_start(token, (ends[0], ends[1])))
    inverse = jnp.power(ROPE_BASE, -2.0 * jnp.arange(HEAD // 2, dtype=jnp.float32) / HEAD)
    angle = position[:, None] * inverse[None, :]
    cosine, sine = jnp.cos(angle), jnp.sin(angle)
    cosine = jnp.concatenate([cosine, cosine], axis=1)
    sine = jnp.concatenate([-sine, sine], axis=1)

    normed, pre, qkv = project(
        parts, spots, w_heads, gain_attn, gain_query, gain_key, cosine, sine
    )
    mix = feature_mix(16, 16)[0]
    attended_own, attended_mixed, inverse_total = attend(ends, qkv, mix)

    def to_tokens(values):
        moved = lax.all_to_all(
            values.reshape(dp_size, TOK, 256), "dp", split_axis=0, concat_axis=0, tiled=True
        )
        return moved.reshape(dp_size, TOK, 2, HEAD).transpose(1, 2, 0, 3).reshape(TOK, 2, WIDTH)

    def to_heads(values):
        apart = values.reshape(TOK, 2, dp_size, HEAD).transpose(2, 0, 1, 3)
        moved = lax.all_to_all(
            apart.reshape(dp_size, TOK, 256), "dp", split_axis=0, concat_axis=0, tiled=True
        )
        return moved.reshape(PACK, 256)

    attended = to_tokens(attended_mixed)
    inputs_wide = wide(inputs)
    middle = inputs_wide + dot(attended[:, 0], full_out[0]) + dot(attended[:, 1], full_out[1])
    middle_scale = norm_scale(middle)
    mixed = low(middle * middle_scale * gain_mlp)
    gate_pre = dot(mixed, full_gate)
    up_pre = dot(mixed, full_up)
    sigmoid = 1.0 / (1.0 + jnp.exp(-gate_pre))
    silu = gate_pre * sigmoid
    act = low(silu * up_pre)
    result = middle + sum(
        dot(act[:, k * WIDTH : (k + 1) * WIDTH], full_down[k]) for k in range(3)
    )
    activations = low(result)[None]

    d_act = jnp.concatenate([contract_cols(d_result, full_down[k]) for k in range(3)], axis=1)
    d_gate = low(d_act * up_pre * (sigmoid + silu * (1.0 - sigmoid)))
    d_up = low(d_act * silu)
    d_mixed = contract_cols(d_gate, full_gate) + contract_cols(d_up, full_up)
    d_middle = wide(d_result) + norm_back(middle, gain_mlp, d_mixed)
    d_gain_mlp = jnp.sum(middle * middle_scale * d_mixed, axis=0)
    d_branch = low(d_middle)
    d_attended = jnp.stack(
        [low(contract_cols(d_branch, full_out[k])) for k in range(2)], axis=1
    )
    d_heads = to_heads(d_attended)

    def of_chip(values):
        return jnp.concatenate([values, swap(values, CORE)], axis=0)

    orders = [chip_order(index, order) for order in CHIP_ORDERS]
    act_chip, d_result_chip = of_chip(act), of_chip(d_result)
    mixed_chip, d_gate_chip, d_up_chip = of_chip(mixed), of_chip(d_gate), of_chip(d_up)
    attended_chip, d_branch_chip = of_chip(attended), of_chip(d_branch)
    half = orders[0].shape[1] // 2

    def weight_grad(rows, columns, order):
        rows = low(dot(rows, orders[order]))
        keep, send = rows[..., :half], rows[..., half:]
        axis = rows.ndim - 2
        send = low(contract_rows(send, columns))
        keep = low(contract_rows(keep, columns))
        return scatter_chips(keep, send, CHIP_ORDERS[order], axis)

    sum_down = weight_grad(act_chip.reshape(-1, 3, WIDTH), d_result_chip, 2)
    sum_gate = weight_grad(mixed_chip, d_gate_chip, 0)
    sum_up = weight_grad(mixed_chip, d_up_chip, 1)
    sum_out = weight_grad(attended_chip, d_branch_chip, 2)

    d_query, d_key, d_value = attend_back(ends, qkv, d_heads, attended_own, inverse_total, mix)
    d_pre, part_a, part_b, part_c, d_gain_attn, d_gain_heads = project_back(
        spots, pre, d_query, d_key, d_value, cosine, sine, normed, w_heads, gain_query, gain_key
    )
    d_normed = scatter_pack((part_a, part_b, part_c))
    input_grad = (d_middle + norm_back(inputs_wide, gain_attn, d_normed))[None]

    d_gains = jnp.concatenate(
        [(d_gain_attn / gain_attn)[0], d_gain_mlp, d_gain_heads.reshape(-1)]
    )
    payload = jnp.concatenate(
        [
            low(contract_rows(normed, d_pre)).reshape(dp_size, 16, 8, 512),
            low(jnp.pad(d_gains.reshape(dp_size, 16, 1, 18), ((0, 0), (0, 0), (0, 7), (0, 110)))),
        ],
        axis=3,
    )
    for mask, bit in ((CORE, 0), (YB, 2), (YA, 1), (ZA, 3)):
        rest = payload.shape[1]
        bits = {CORE: 0, YB: 1, YA: 0, ZA: 0}[mask]
        high = rest >> (bits + 1)
        split = payload.reshape(dp_size, high, 2, 1 << bits, 8, 640)
        mine = fsdp_rank >> bit & 1
        keep = lax.dynamic_index_in_dim(split, mine, 2, keepdims=False)
        send = lax.dynamic_index_in_dim(split, 1 - mine, 2, keepdims=False)
        payload = low(wide(keep) + wide(swap(send, mask))).reshape(dp_size, rest // 2, 8, 640)
    heads_grad = lax.all_to_all(
        payload.reshape(dp_size, 8, 640), "dp", split_axis=0, concat_axis=0, tiled=True
    )
    heads_grad = wide(heads_grad)
    sum_query = heads_grad[..., :256].transpose(1, 0, 2).reshape(8, -1)
    sum_key = heads_grad[..., 256:384].transpose(1, 0, 2).reshape(8, -1)
    sum_value = heads_grad[..., 384:512].transpose(1, 0, 2).reshape(8, -1)
    sum_gains = jnp.sum(heads_grad[:, 0, 512:530], axis=0)
    return (
        activations,
        input_grad,
        sum_query,
        sum_key,
        sum_value,
        sum_out.reshape(16, WIDTH),
        hidden_units_back(sum_gate),
        hidden_units_back(sum_up),
        sum_down.reshape(24, WIDTH),
        sum_gains,
    )


def solution(mesh):
    rows = P(("dp", "fsdp"), None)
    tokens = P("fsdp", "dp", None)
    return jax.shard_map(
        on_device,
        mesh=mesh,
        in_specs=(tokens, P("fsdp", None), *([rows] * 7), P(("dp", "fsdp")), tokens),
        out_specs=(tokens, tokens, *([rows] * 7), P(("dp", "fsdp"))),
        check_vma=False,
    )
```

```python
import jax
import jax.numpy as jnp
import numpy as np
from jax import lax
from jax.experimental import pallas as pl
from jax.experimental.pallas import tpu as pltpu
from jax.sharding import PartitionSpec as P

HEADS = 16
KV_HEADS = 8
HEAD = 128
EPSILON = 1e-06
ROPE_BASE = 1000000.0
DEVICES = 128
WIDTH = 1024
FF = 3072
TOK = 192
PACK = 1536
BLOCK = 256
LOG2E = 1.4426950408889634
SCALE = HEAD ** (-0.5)
EVERY = ("dp", "fsdp")
VMEM_LIMIT = 48 * 1024 * 1024

XA, XB, ZH, ZA, ZB, YA, YB, CORE = 32, 96, 16, 8, 24, 2, 6, 1
HALVES = ((XA, YA, ZA), (XB, YB, ZB))


def spanned(masks, spot):
    return (spot & 1) * masks[0] ^ (spot >> 1 & 1) * masks[1] ^ (spot >> 2 & 1) * masks[2]


def cubes(stage):
    groups = []
    for core in range(2):
        inner, outer = HALVES[core ^ stage], HALVES[core ^ stage ^ 1]
        for base in range(8):
            groups.append([core ^ spanned(outer, base) ^ spanned(inner, k) for k in range(8)])
    return groups


def swap(values, mask, other_mask=None):
    masks = (mask, mask if other_mask is None else other_mask)
    return lax.ppermute(values, EVERY, [(k, k ^ masks[k & 1]) for k in range(DEVICES)])


def low(values):
    return values.astype(jnp.bfloat16)


def wide(values):
    return values.astype(jnp.float32)


def dot(left, right):
    return jnp.dot(left, right, preferred_element_type=jnp.float32)


def contract_rows(left, right):
    return lax.dot_general(
        left, right, (((0,), (0,)), ((), ())), preferred_element_type=jnp.float32
    )


def contract_cols(left, right):
    return lax.dot_general(
        left, right, (((1,), (1,)), ((), ())), preferred_element_type=jnp.float32
    )


def norm_scale(values):
    return lax.rsqrt(jnp.mean(values * values, axis=-1, keepdims=True) + EPSILON)


def norm_back(values, gain, grad):
    scale = norm_scale(values)
    normal = values * scale
    inner = grad * gain
    return scale * (inner - normal * jnp.mean(inner * normal, axis=-1, keepdims=True))


def rope(values, cosine, sine):
    return values * cosine + pltpu.roll(values, 64, 1) * sine


def rope_back(grad, cosine, sine):
    return grad * cosine + pltpu.roll(grad * sine, 64, 1)


def qkv_kernel(rank_ref, *refs):
    chunks, (w_ref, ga_ref, gq_ref, gk_ref, cos_ref, sin_ref) = refs[:8], refs[8:14]
    normed_ref, pre_ref, qkv_ref = refs[14:]
    for k, chunk in enumerate(chunks):

        @pl.when(pl.program_id(0) == k)
        def _(chunk=chunk):
            x = wide(chunk[...])
            normed_ref[...] = low(x * norm_scale(x) * ga_ref[...])

    pre = dot(normed_ref[...], w_ref[...])
    pre_ref[...] = pre[:, : 3 * HEAD]
    cosine, sine = cos_ref[...], sin_ref[...]
    for h in range(3):
        u = pre[:, h * HEAD : (h + 1) * HEAD]
        gain = gk_ref[...] if h == 2 else gq_ref[...]
        normal = u * norm_scale(u) * gain
        qkv_ref[:, h * HEAD : (h + 1) * HEAD] = low(rope(normal, cosine, sine))
    qkv_ref[:, 3 * HEAD :] = low(pre[:, 3 * HEAD :])


def project(chunks, rank, weights, gain_attn, gain_query, gain_key, cosine, sine):
    whole = lambda shape: pl.BlockSpec(shape, lambda k, rank: (0, 0))
    by_row = lambda cols: pl.BlockSpec((TOK, cols), lambda k, rank: (rank[0] ^ k, 0))
    return pl.pallas_call(
        qkv_kernel,
        grid_spec=pltpu.PrefetchScalarGridSpec(
            num_scalar_prefetch=1,
            grid=(8,),
            in_specs=[whole((TOK, WIDTH))] * 8
            + [whole((WIDTH, 512)), whole((1, WIDTH)), whole((1, HEAD)), whole((1, HEAD))]
            + [by_row(HEAD), by_row(HEAD)],
            out_specs=[by_row(WIDTH), by_row(3 * HEAD), by_row(512)],
        ),
        out_shape=[
            jax.ShapeDtypeStruct((PACK, WIDTH), jnp.bfloat16),
            jax.ShapeDtypeStruct((PACK, 3 * HEAD), jnp.float32),
            jax.ShapeDtypeStruct((PACK, 512), jnp.bfloat16),
        ],
        compiler_params=pltpu.CompilerParams(vmem_limit_bytes=VMEM_LIMIT),
        cost_estimate=pl.CostEstimate(flops=1610612736, bytes_accessed=12000000, transcendentals=0),
        name="project",
    )(rank, *chunks, weights, gain_attn, gain_query, gain_key, cosine, sine)


def row_start(rows, ends):
    first, second = ends
    return jnp.where(rows >= second, second, jnp.where(rows >= first, first, 0))


def allowed_block(q_block, k_block, ends, transposed):
    q_axis, k_axis = (1, 0) if transposed else (0, 1)
    q_rows = q_block * BLOCK + lax.broadcasted_iota(jnp.int32, (BLOCK, BLOCK), q_axis)
    k_rows = k_block * BLOCK + lax.broadcasted_iota(jnp.int32, (BLOCK, BLOCK), k_axis)
    return (k_rows <= q_rows) & (k_rows >= row_start(q_rows, ends))


def over_blocks(q_block, step, carry):
    last = PACK // BLOCK - 1
    masked_from = jnp.where(q_block == last, 1, jnp.maximum(q_block, 1))
    carry = step(0, True, carry)
    carry = lax.fori_loop(1, masked_from, lambda k, c: step(k, False, c), carry)
    return lax.fori_loop(masked_from, q_block + 1, lambda k, c: step(k, True, c), carry)


def attend_kernel(ends_ref, q_ref, k_ref, v_ref, mix_ref, out_ref, mixed_ref, inverse_ref):
    q_block = pl.program_id(0)
    ends = (ends_ref[0], ends_ref[1])
    heads = [q_ref[:, :HEAD], q_ref[:, HEAD:]]

    def step(k_block, masked, carry):
        rows = pl.ds(pl.multiple_of(k_block * BLOCK, BLOCK), BLOCK)
        keys, values = k_ref[rows, :], v_ref[rows, :]
        allowed = allowed_block(q_block, k_block, ends, False) if masked else None
        new = []
        for h in range(2):
            total, part = carry[2 * h], carry[2 * h + 1]
            shifted = jnp.exp2(contract_cols(heads[h], keys) * (SCALE * LOG2E))
            if masked:
                shifted = jnp.where(allowed, shifted, 0.0)
            new.append(total + dot(low(shifted), values))
            new.append(part + shifted[:, :HEAD] + shifted[:, HEAD:])
        return tuple(new)

    zero = jnp.zeros((BLOCK, HEAD), jnp.float32)
    carry = over_blocks(q_block, step, (zero, zero, zero, zero))
    for h in range(2):
        total, part = carry[2 * h], carry[2 * h + 1]
        row_total = jnp.sum(part, axis=1, keepdims=True)
        out_ref[:, h * HEAD : (h + 1) * HEAD] = low(total / row_total)
        across = jnp.sum(jnp.swapaxes(part, 0, 1), axis=0, keepdims=True)
        inverse_ref[h : h + 1, :] = 1.0 / across
    mixed_ref[...] = low(dot(out_ref[...], mix_ref[...]))


def attend(ends, qkv, mix):
    blocks = PACK // BLOCK
    return pl.pallas_call(
        attend_kernel,
        grid_spec=pltpu.PrefetchScalarGridSpec(
            num_scalar_prefetch=1,
            grid=(blocks,),
            in_specs=[
                pl.BlockSpec((BLOCK, 2 * HEAD), lambda q, ends: (q, 0)),
                pl.BlockSpec((PACK, HEAD), lambda q, ends: (0, 2)),
                pl.BlockSpec((PACK, HEAD), lambda q, ends: (0, 3)),
                pl.BlockSpec((2 * HEAD, 2 * HEAD), lambda q, ends: (0, 0)),
            ],
            out_specs=[
                pl.BlockSpec((BLOCK, 2 * HEAD), lambda q, ends: (q, 0)),
                pl.BlockSpec((BLOCK, 2 * HEAD), lambda q, ends: (q, 0)),
                pl.BlockSpec((2, BLOCK), lambda q, ends: (0, q)),
            ],
        ),
        out_shape=[
            jax.ShapeDtypeStruct((PACK, 2 * HEAD), jnp.bfloat16),
            jax.ShapeDtypeStruct((PACK, 2 * HEAD), jnp.bfloat16),
            jax.ShapeDtypeStruct((2, PACK), jnp.float32),
        ],
        compiler_params=pltpu.CompilerParams(vmem_limit_bytes=VMEM_LIMIT),
        cost_estimate=pl.CostEstimate(flops=3000000000, bytes_accessed=4000000, transcendentals=3000000),
        name="attend",
    )(ends, qkv, qkv, qkv, mix)


def attend_back_kernel(
    ends_ref, q_ref, k_ref, v_ref, grad_ref, out_ref, inverse_ref, mix_ref,
    dq_ref, dk_ref, dv_ref,
):
    q_block = pl.program_id(0)
    ends = (ends_ref[0], ends_ref[1])

    @pl.when(q_block == 0)
    def _():
        dk_ref[...] = jnp.zeros_like(dk_ref)
        dv_ref[...] = jnp.zeros_like(dv_ref)

    grad = low(contract_cols(grad_ref[...], mix_ref[...]))
    heads = [q_ref[:, :HEAD], q_ref[:, HEAD:]]
    grads = [grad[:, :HEAD], grad[:, HEAD:]]
    inverse = [inverse_ref[h : h + 1, :] for h in range(2)]
    delta = []
    for h in range(2):
        product = wide(grads[h]) * wide(out_ref[:, h * HEAD : (h + 1) * HEAD])
        delta.append(jnp.sum(jnp.swapaxes(product, 0, 1), axis=0, keepdims=True))

    def step(k_block, masked, carry):
        rows = pl.ds(pl.multiple_of(k_block * BLOCK, BLOCK), BLOCK)
        keys, values = k_ref[rows, :], v_ref[rows, :]
        allowed = allowed_block(q_block, k_block, ends, True) if masked else None
        new = []
        d_keys, d_values = dk_ref[rows, :], dv_ref[rows, :]
        for h in range(2):
            prob = jnp.exp2(contract_cols(keys, heads[h]) * (SCALE * LOG2E)) * inverse[h]
            if masked:
                prob = jnp.where(allowed, prob, 0.0)
            d_prob = contract_cols(values, grads[h])
            d_score = low(prob * (d_prob - delta[h]) * SCALE)
            d_keys += dot(d_score, heads[h])
            d_values += dot(low(prob), grads[h])
            new.append(carry[h] + contract_rows(d_score, keys))
        dk_ref[rows, :] = d_keys
        dv_ref[rows, :] = d_values
        return tuple(new)

    zero = jnp.zeros((BLOCK, HEAD), jnp.float32)
    carry = over_blocks(q_block, step, (zero, zero))
    dq_ref[:, :HEAD] = carry[0]
    dq_ref[:, HEAD:] = carry[1]


def attend_back(ends, qkv, grad, out, inverse, mix):
    blocks = PACK // BLOCK
    by_block = pl.BlockSpec((BLOCK, 2 * HEAD), lambda q, ends: (q, 0))
    whole = pl.BlockSpec((PACK, HEAD), lambda q, ends: (0, 0))
    return pl.pallas_call(
        attend_back_kernel,
        grid_spec=pltpu.PrefetchScalarGridSpec(
            num_scalar_prefetch=1,
            grid=(blocks,),
            in_specs=[
                by_block,
                pl.BlockSpec((PACK, HEAD), lambda q, ends: (0, 2)),
                pl.BlockSpec((PACK, HEAD), lambda q, ends: (0, 3)),
                by_block,
                by_block,
                pl.BlockSpec((2, BLOCK), lambda q, ends: (0, q)),
                pl.BlockSpec((2 * HEAD, 2 * HEAD), lambda q, ends: (0, 0)),
            ],
            out_specs=[by_block, whole, whole],
        ),
        out_shape=[
            jax.ShapeDtypeStruct((PACK, 2 * HEAD), jnp.float32),
            jax.ShapeDtypeStruct((PACK, HEAD), jnp.float32),
            jax.ShapeDtypeStruct((PACK, HEAD), jnp.float32),
        ],
        compiler_params=pltpu.CompilerParams(vmem_limit_bytes=VMEM_LIMIT),
        cost_estimate=pl.CostEstimate(flops=8000000000, bytes_accessed=8000000, transcendentals=3000000),
        name="attend_back",
    )(ends, qkv, qkv, qkv, grad, out, inverse, mix)


def qkv_back_kernel(rank_ref, *refs):
    pre_ref, dq_ref, dk_ref, dv_ref, cos_ref, sin_ref, normed_ref, w_ref, gq_ref, gk_ref = refs[:10]
    d_pre_ref, d_attn_ref, d_head_ref, chunks = refs[10], refs[11], refs[12], refs[13:]

    @pl.when(pl.program_id(0) == 0)
    def _():
        d_attn_ref[...] = jnp.zeros_like(d_attn_ref)
        d_head_ref[...] = jnp.zeros_like(d_head_ref)

    cosine, sine = cos_ref[...], sin_ref[...]
    for h in range(3):
        u = pre_ref[:, h * HEAD : (h + 1) * HEAD]
        gain = gk_ref[...] if h == 2 else gq_ref[...]
        grad = dk_ref[...] if h == 2 else dq_ref[:, h * HEAD : (h + 1) * HEAD]
        grad = rope_back(grad, cosine, sine)
        row = 1 if h == 2 else 0
        d_head_ref[row : row + 1, :] += jnp.sum(
            grad * u * norm_scale(u), axis=0, keepdims=True
        )
        d_pre_ref[:, h * HEAD : (h + 1) * HEAD] = low(norm_back(u, gain, grad))
    d_pre_ref[:, 3 * HEAD :] = low(dv_ref[...])
    d_normed = dot(d_pre_ref[...], w_ref[...])
    d_attn_ref[...] += jnp.sum(wide(normed_ref[...]) * d_normed, axis=0, keepdims=True)
    for k, chunk in enumerate(chunks):

        @pl.when(pl.program_id(0) == k)
        def _(chunk=chunk):
            chunk[...] = low(d_normed)


def project_back(rank, pre, d_query, d_key, d_value, cosine, sine, normed, weights, gain_query, gain_key):
    whole = lambda shape: pl.BlockSpec(shape, lambda k, rank: (0, 0))
    by_row = lambda cols: pl.BlockSpec((TOK, cols), lambda k, rank: (rank[0] ^ k, 0))
    return pl.pallas_call(
        qkv_back_kernel,
        grid_spec=pltpu.PrefetchScalarGridSpec(
            num_scalar_prefetch=1,
            grid=(8,),
            in_specs=[by_row(3 * HEAD), by_row(2 * HEAD), by_row(HEAD), by_row(HEAD)]
            + [by_row(HEAD), by_row(HEAD), by_row(WIDTH)]
            + [whole((512, WIDTH)), whole((1, HEAD)), whole((1, HEAD))],
            out_specs=[by_row(512), whole((1, WIDTH)), whole((2, HEAD))]
            + [whole((TOK, WIDTH))] * 8,
        ),
        out_shape=[
            jax.ShapeDtypeStruct((PACK, 512), jnp.bfloat16),
            jax.ShapeDtypeStruct((1, WIDTH), jnp.float32),
            jax.ShapeDtypeStruct((2, HEAD), jnp.float32),
        ]
        + [jax.ShapeDtypeStruct((TOK, WIDTH), jnp.bfloat16)] * 8,
        compiler_params=pltpu.CompilerParams(vmem_limit_bytes=VMEM_LIMIT),
        cost_estimate=pl.CostEstimate(flops=1610612736, bytes_accessed=15000000, transcendentals=0),
        name="project_back",
    )(rank, pre, d_query, d_key, d_value, cosine, sine, normed, weights, gain_query, gain_key)


def one_hot(rows, columns):
    hits = lax.broadcasted_iota(jnp.int32, (rows, columns.shape[0]), 0) == columns[None, :]
    return hits.astype(jnp.bfloat16)


def feature_mix(per_device, devices):
    slices = per_device // 8
    spot = np.arange(per_device * devices)
    k, dev, r = spot // (8 * devices), spot // 8 % devices, spot % 8
    return one_hot(per_device * devices, jnp.asarray(dev * per_device + 8 * k + r, jnp.int32)), slices


def hidden_units_apart(weights):
    mix, slices = feature_mix(24, 16)
    blocks = weights.reshape(-1, 384)
    moved = low(dot(blocks, mix))
    return moved.reshape(weights.shape[0], -1, slices, 128).transpose(0, 2, 1, 3).reshape(weights.shape)


def hidden_units_back(grads):
    mix, slices = feature_mix(24, 16)
    blocks = grads.reshape(grads.shape[0], slices, -1, 128).transpose(0, 2, 1, 3).reshape(-1, 384)
    moved = lax.dot_general(
        blocks, wide(mix), (((1,), (1,)), ((), ())), precision=lax.Precision.HIGHEST
    )
    return moved.reshape(grads.shape)


def cube_order(core):
    spots = []
    for c in range(2):
        first, second = HALVES[c], HALVES[c ^ 1]
        spots.append(
            [c ^ spanned(first, k // 8) ^ spanned(second, k % 8) for k in range(64)]
        )
    owner = jnp.where(core == 1, jnp.asarray(spots[1], jnp.int32), jnp.asarray(spots[0], jnp.int32))
    return one_hot(WIDTH, (owner[:, None] * 8 + jnp.arange(8, dtype=jnp.int32)[None, :]).reshape(-1))


def exchange(values, axes, groups=None):
    return lax.all_to_all(
        values, axes, split_axis=0, concat_axis=0, axis_index_groups=groups, tiled=True
    )


def of_chip(values):
    return jnp.concatenate([values, swap(values, CORE)], axis=0)


def first_cube(grad):
    got = exchange(grad.reshape(8, 64, -1), EVERY, cubes(0))
    return low(jnp.sum(wide(got), axis=0))


def second_cube(sums):
    pieces = [
        array.reshape(8, 8, -1, WIDTH)[:, :, k]
        for array in sums
        for k in range(array.shape[1] // WIDTH)
    ]
    got = exchange(jnp.concatenate(pieces, axis=1), EVERY, cubes(1))
    return jnp.sum(wide(got), axis=0).reshape(-1, 8, WIDTH)


def on_device(
    hidden, lengths, w_query, w_key, w_value, w_out, w_gate, w_up, w_down, gains, cotangent
):
    dp_rank = lax.axis_index("dp")
    rank = dp_rank.astype(jnp.int32)[None]
    core = lax.axis_index("fsdp") & 1
    inputs = hidden[0]
    d_result = cotangent[0]

    local = jnp.concatenate(
        [
            hidden_units_apart(w_gate),
            hidden_units_apart(w_up),
            w_down.reshape(3, 8, WIDTH).transpose(1, 0, 2).reshape(8, -1),
            w_out.reshape(2, 8, WIDTH).transpose(1, 0, 2).reshape(8, -1),
        ],
        axis=1,
    )
    full = lax.all_gather(local, EVERY, axis=0, tiled=True)
    full_gate, full_up = full[:, :FF], full[:, FF : 2 * FF]
    full_down = [full[:, 2 * FF + k * WIDTH : 2 * FF + (k + 1) * WIDTH] for k in range(3)]
    full_out = [full[:, 3 * FF + k * WIDTH : 3 * FF + (k + 1) * WIDTH] for k in range(2)]

    heads = jnp.concatenate(
        [
            w_query.reshape(8, KV_HEADS, 256).transpose(1, 0, 2),
            w_key.reshape(8, KV_HEADS, HEAD).transpose(1, 0, 2),
            w_value.reshape(8, KV_HEADS, HEAD).transpose(1, 0, 2),
            jnp.broadcast_to(jnp.pad(gains[None, None, :], ((0, 0), (0, 7), (0, 110))), (8, 8, 128)),
        ],
        axis=2,
    )
    heads = jnp.broadcast_to(heads[:, None], (8, 16, 8, 640)).reshape(DEVICES, 8, 640)
    heads = exchange(heads, EVERY).reshape(8, 16, 8, 640)
    w_heads = heads[..., :512].reshape(WIDTH, 512)
    gain_all = wide(heads[:, :, 0, 512:530].reshape(1, -1))
    gain_attn, gain_mlp = gain_all[:, :WIDTH], gain_all[:, WIDTH : 2 * WIDTH]
    gain_query = gain_all[:, 2 * WIDTH : 2 * WIDTH + HEAD]
    gain_key = gain_all[:, 2 * WIDTH + HEAD :]

    chunks = [inputs] + [swap(inputs, k * 16) for k in range(1, 8)]
    ends = jnp.stack([lengths[0, 0], lengths[0, 0] + lengths[0, 1]]).astype(jnp.int32)
    token = jnp.arange(PACK, dtype=jnp.int32)
    position = wide(token - row_start(token, (ends[0], ends[1])))
    inverse = jnp.power(ROPE_BASE, -2.0 * jnp.arange(HEAD // 2, dtype=jnp.float32) / HEAD)
    angle = position[:, None] * inverse[None, :]
    cosine, sine = jnp.cos(angle), jnp.sin(angle)
    cosine = jnp.concatenate([cosine, cosine], axis=1)
    sine = jnp.concatenate([-sine, sine], axis=1)

    normed, pre, qkv = project(
        chunks, rank, w_heads, gain_attn, gain_query, gain_key, cosine, sine
    )
    mix = feature_mix(16, 16)[0]
    attended_own, attended_mixed, inverse_total = attend(ends, qkv, mix)

    def to_tokens(values):
        moved = exchange(values.reshape(8, TOK, 256), "dp")
        return moved.reshape(8, TOK, 2, HEAD).transpose(1, 2, 0, 3).reshape(TOK, 2, WIDTH)

    def to_heads(values):
        apart = values.reshape(TOK, 2, 8, HEAD).transpose(2, 0, 1, 3)
        return exchange(apart.reshape(8, TOK, 256), "dp").reshape(PACK, 256)

    attended = to_tokens(attended_mixed)
    inputs_wide = wide(inputs)
    middle = inputs_wide + dot(attended[:, 0], full_out[0]) + dot(attended[:, 1], full_out[1])
    middle_scale = norm_scale(middle)
    mixed = low(middle * middle_scale * gain_mlp)
    gate_pre = dot(mixed, full_gate)
    up_pre = dot(mixed, full_up)
    sigmoid = 1.0 / (1.0 + jnp.exp(-gate_pre))
    silu = gate_pre * sigmoid
    act = low(silu * up_pre)
    result = middle + sum(
        dot(act[:, k * WIDTH : (k + 1) * WIDTH], full_down[k]) for k in range(3)
    )
    activations = low(result)[None]

    d_act = jnp.concatenate([contract_cols(d_result, full_down[k]) for k in range(3)], axis=1)
    d_gate = low(d_act * up_pre * (sigmoid + silu * (1.0 - sigmoid)))
    d_up = low(d_act * silu)
    d_mixed = contract_cols(d_gate, full_gate) + contract_cols(d_up, full_up)
    d_middle = wide(d_result) + norm_back(middle, gain_mlp, d_mixed)
    d_gain_mlp = jnp.sum(middle * middle_scale * d_mixed, axis=0)
    d_branch = low(d_middle)
    d_attended = jnp.stack(
        [low(contract_cols(d_branch, full_out[k])) for k in range(2)], axis=1
    )
    d_heads = to_heads(d_attended)

    order = cube_order(core)
    act_rows = low(dot(of_chip(act).reshape(-1, 3, WIDTH), order))
    d_result_chip = of_chip(d_result)
    grad_down = jnp.concatenate(
        [low(contract_rows(act_rows[:, k], d_result_chip)) for k in range(3)], axis=1
    )
    mixed_rows = low(dot(of_chip(mixed), order))
    grad_gate = low(contract_rows(mixed_rows, of_chip(d_gate)))
    grad_up = low(contract_rows(mixed_rows, of_chip(d_up)))
    attended_rows = low(dot(of_chip(attended), order))
    d_branch_chip = of_chip(d_branch)
    grad_out = jnp.concatenate(
        [low(contract_rows(attended_rows[:, k], d_branch_chip)) for k in range(2)], axis=1
    )
    sums = [first_cube(grad) for grad in (grad_down, grad_gate, grad_up, grad_out)]
    d_heads = lax.optimization_barrier((d_heads, grad_down, grad_gate, grad_up, grad_out))[0]

    d_query, d_key, d_value = attend_back(ends, qkv, d_heads, attended_own, inverse_total, mix)
    d_pre, d_gain_attn, d_gain_heads, *chunks = project_back(
        rank, pre, d_query, d_key, d_value, cosine, sine, normed, w_heads.T, gain_query, gain_key
    )
    d_normed = wide(chunks[0]) + sum(wide(swap(chunks[k], k * 16)) for k in range(1, 8))
    input_grad = (d_middle + norm_back(inputs_wide, gain_attn, d_normed))[None]

    d_gains = jnp.concatenate(
        [(d_gain_attn / gain_attn)[0], d_gain_mlp, d_gain_heads.reshape(-1)]
    )
    payload = jnp.concatenate(
        [
            low(contract_rows(normed, d_pre)).reshape(DEVICES, 8, 512),
            low(jnp.pad(d_gains.reshape(DEVICES, 1, 18), ((0, 0), (0, 7), (0, 110)))),
        ],
        axis=2,
    )
    heads_grad = jnp.sum(wide(exchange(payload, EVERY).reshape(8, 16, 8, 640)), axis=1)
    sum_query = heads_grad[..., :256].transpose(1, 0, 2).reshape(8, -1)
    sum_key = heads_grad[..., 256:384].transpose(1, 0, 2).reshape(8, -1)
    sum_value = heads_grad[..., 384:512].transpose(1, 0, 2).reshape(8, -1)
    sum_gains = jnp.sum(heads_grad[:, 0, 512:530], axis=0)
    own = second_cube(sums)
    by_row = lambda pieces: pieces.transpose(1, 0, 2).reshape(8, -1)
    return (
        activations,
        input_grad,
        sum_query,
        sum_key,
        sum_value,
        own[9:].reshape(16, WIDTH),
        hidden_units_back(by_row(own[3:6])),
        hidden_units_back(by_row(own[6:9])),
        own[:3].reshape(24, WIDTH),
        sum_gains,
    )


def solution(mesh):
    rows = P(("dp", "fsdp"), None)
    tokens = P("fsdp", "dp", None)
    return jax.shard_map(
        on_device,
        mesh=mesh,
        in_specs=(tokens, P("fsdp", None), *([rows] * 7), P(("dp", "fsdp")), tokens),
        out_specs=(tokens, tokens, *([rows] * 7), P(("dp", "fsdp"))),
        check_vma=False,
    )
```

```python
import jax
import jax.numpy as jnp
import numpy as np
from jax import lax
from jax.experimental import pallas as pl
from jax.experimental.pallas import tpu as pltpu
from jax.sharding import PartitionSpec as P

HEADS = 16
KV_HEADS = 8
HEAD = 128
EPSILON = 1e-06
ROPE_BASE = 1000000.0
DEVICES = 128
WIDTH = 1024
FF = 3072
TOK = 192
PACK = 1536
BLOCK = 256
LOG2E = 1.4426950408889634
SCALE = HEAD ** (-0.5)
EVERY = ("dp", "fsdp")
VMEM_LIMIT = 48 * 1024 * 1024

XA, XB, ZH, ZA, ZB, YA, YB, CORE = 32, 96, 16, 8, 24, 2, 6, 1
HALVES = ((XA, YA, ZA), (XB, YB, ZB))


def spanned(masks, spot):
    return (spot & 1) * masks[0] ^ (spot >> 1 & 1) * masks[1] ^ (spot >> 2 & 1) * masks[2]


def cubes(stage):
    groups = []
    for core in range(2):
        inner, outer = HALVES[core ^ stage], HALVES[core ^ stage ^ 1]
        for base in range(8):
            groups.append([core ^ spanned(outer, base) ^ spanned(inner, k) for k in range(8)])
    return groups


def swap(values, mask, other_mask=None):
    masks = (mask, mask if other_mask is None else other_mask)
    return lax.ppermute(values, EVERY, [(k, k ^ masks[k & 1]) for k in range(DEVICES)])


def low(values):
    return values.astype(jnp.bfloat16)


def wide(values):
    return values.astype(jnp.float32)


def dot(left, right):
    return jnp.dot(left, right, preferred_element_type=jnp.float32)


def contract_rows(left, right):
    return lax.dot_general(
        left, right, (((0,), (0,)), ((), ())), preferred_element_type=jnp.float32
    )


def contract_cols(left, right):
    return lax.dot_general(
        left, right, (((1,), (1,)), ((), ())), preferred_element_type=jnp.float32
    )


def norm_scale(values):
    return lax.rsqrt(jnp.mean(values * values, axis=-1, keepdims=True) + EPSILON)


def norm_back(values, gain, grad):
    scale = norm_scale(values)
    normal = values * scale
    inner = grad * gain
    return scale * (inner - normal * jnp.mean(inner * normal, axis=-1, keepdims=True))


def rope(values, cosine, sine):
    return values * cosine + pltpu.roll(values, 64, 1) * sine


def rope_back(grad, cosine, sine):
    return grad * cosine + pltpu.roll(grad * sine, 64, 1)


def qkv_kernel(rank_ref, *refs):
    chunks, (w_ref, ga_ref, gq_ref, gk_ref, cos_ref, sin_ref) = refs[:8], refs[8:14]
    normed_ref, pre_ref, qkv_ref = refs[14:]
    for k, chunk in enumerate(chunks):

        @pl.when(pl.program_id(0) == k)
        def _(chunk=chunk):
            x = wide(chunk[...])
            normed_ref[...] = low(x * norm_scale(x) * ga_ref[...])

    pre = dot(normed_ref[...], w_ref[...])
    pre_ref[...] = pre[:, : 3 * HEAD]
    cosine, sine = cos_ref[...], sin_ref[...]
    for h in range(3):
        u = pre[:, h * HEAD : (h + 1) * HEAD]
        gain = gk_ref[...] if h == 2 else gq_ref[...]
        normal = u * norm_scale(u) * gain
        qkv_ref[:, h * HEAD : (h + 1) * HEAD] = low(rope(normal, cosine, sine))
    qkv_ref[:, 3 * HEAD :] = low(pre[:, 3 * HEAD :])


def project(chunks, rank, weights, gain_attn, gain_query, gain_key, cosine, sine):
    whole = lambda shape: pl.BlockSpec(shape, lambda k, rank: (0, 0))
    by_row = lambda cols: pl.BlockSpec((TOK, cols), lambda k, rank: (rank[0] ^ k, 0))
    return pl.pallas_call(
        qkv_kernel,
        grid_spec=pltpu.PrefetchScalarGridSpec(
            num_scalar_prefetch=1,
            grid=(8,),
            in_specs=[whole((TOK, WIDTH))] * 8
            + [whole((WIDTH, 512)), whole((1, WIDTH)), whole((1, HEAD)), whole((1, HEAD))]
            + [by_row(HEAD), by_row(HEAD)],
            out_specs=[by_row(WIDTH), by_row(3 * HEAD), by_row(512)],
        ),
        out_shape=[
            jax.ShapeDtypeStruct((PACK, WIDTH), jnp.bfloat16),
            jax.ShapeDtypeStruct((PACK, 3 * HEAD), jnp.float32),
            jax.ShapeDtypeStruct((PACK, 512), jnp.bfloat16),
        ],
        compiler_params=pltpu.CompilerParams(vmem_limit_bytes=VMEM_LIMIT),
        cost_estimate=pl.CostEstimate(flops=1610612736, bytes_accessed=12000000, transcendentals=0),
        name="project",
    )(rank, *chunks, weights, gain_attn, gain_query, gain_key, cosine, sine)


def row_start(rows, ends):
    first, second = ends
    return jnp.where(rows >= second, second, jnp.where(rows >= first, first, 0))


def allowed_block(q_block, k_block, ends, transposed):
    q_axis, k_axis = (1, 0) if transposed else (0, 1)
    q_rows = q_block * BLOCK + lax.broadcasted_iota(jnp.int32, (BLOCK, BLOCK), q_axis)
    k_rows = k_block * BLOCK + lax.broadcasted_iota(jnp.int32, (BLOCK, BLOCK), k_axis)
    return (k_rows <= q_rows) & (k_rows >= row_start(q_rows, ends))


def over_blocks(q_block, step, carry):
    last = PACK // BLOCK - 1
    masked_from = jnp.where(q_block == last, 1, jnp.maximum(q_block, 1))
    carry = step(0, True, carry)
    carry = lax.fori_loop(1, masked_from, lambda k, c: step(k, False, c), carry)
    return lax.fori_loop(masked_from, q_block + 1, lambda k, c: step(k, True, c), carry)


def attend_kernel(ends_ref, q_ref, k_ref, v_ref, mix_ref, out_ref, mixed_ref, inverse_ref):
    q_block = pl.program_id(0)
    ends = (ends_ref[0], ends_ref[1])
    heads = [q_ref[:, :HEAD], q_ref[:, HEAD:]]

    def step(k_block, masked, carry):
        rows = pl.ds(pl.multiple_of(k_block * BLOCK, BLOCK), BLOCK)
        keys, values = k_ref[rows, :], v_ref[rows, :]
        allowed = allowed_block(q_block, k_block, ends, False) if masked else None
        new = []
        for h in range(2):
            total, part = carry[2 * h], carry[2 * h + 1]
            shifted = jnp.exp2(contract_cols(heads[h], keys) * (SCALE * LOG2E))
            if masked:
                shifted = jnp.where(allowed, shifted, 0.0)
            new.append(total + dot(low(shifted), values))
            new.append(part + shifted[:, :HEAD] + shifted[:, HEAD:])
        return tuple(new)

    zero = jnp.zeros((BLOCK, HEAD), jnp.float32)
    carry = over_blocks(q_block, step, (zero, zero, zero, zero))
    for h in range(2):
        total, part = carry[2 * h], carry[2 * h + 1]
        row_total = jnp.sum(part, axis=1, keepdims=True)
        out_ref[:, h * HEAD : (h + 1) * HEAD] = low(total / row_total)
        across = jnp.sum(jnp.swapaxes(part, 0, 1), axis=0, keepdims=True)
        inverse_ref[h : h + 1, :] = 1.0 / across
    mixed_ref[...] = low(dot(out_ref[...], mix_ref[...]))


def attend(ends, qkv, mix):
    blocks = PACK // BLOCK
    return pl.pallas_call(
        attend_kernel,
        grid_spec=pltpu.PrefetchScalarGridSpec(
            num_scalar_prefetch=1,
            grid=(blocks,),
            in_specs=[
                pl.BlockSpec((BLOCK, 2 * HEAD), lambda q, ends: (q, 0)),
                pl.BlockSpec((PACK, HEAD), lambda q, ends: (0, 2)),
                pl.BlockSpec((PACK, HEAD), lambda q, ends: (0, 3)),
                pl.BlockSpec((2 * HEAD, 2 * HEAD), lambda q, ends: (0, 0)),
            ],
            out_specs=[
                pl.BlockSpec((BLOCK, 2 * HEAD), lambda q, ends: (q, 0)),
                pl.BlockSpec((BLOCK, 2 * HEAD), lambda q, ends: (q, 0)),
                pl.BlockSpec((2, BLOCK), lambda q, ends: (0, q)),
            ],
        ),
        out_shape=[
            jax.ShapeDtypeStruct((PACK, 2 * HEAD), jnp.bfloat16),
            jax.ShapeDtypeStruct((PACK, 2 * HEAD), jnp.bfloat16),
            jax.ShapeDtypeStruct((2, PACK), jnp.float32),
        ],
        compiler_params=pltpu.CompilerParams(vmem_limit_bytes=VMEM_LIMIT),
        cost_estimate=pl.CostEstimate(flops=3000000000, bytes_accessed=4000000, transcendentals=3000000),
        name="attend",
    )(ends, qkv, qkv, qkv, mix)


def attend_back_kernel(
    ends_ref, q_ref, k_ref, v_ref, grad_ref, out_ref, inverse_ref, mix_ref,
    dq_ref, dk_ref, dv_ref,
):
    q_block = pl.program_id(0)
    ends = (ends_ref[0], ends_ref[1])

    @pl.when(q_block == 0)
    def _():
        dk_ref[...] = jnp.zeros_like(dk_ref)
        dv_ref[...] = jnp.zeros_like(dv_ref)

    grad = low(contract_cols(grad_ref[...], mix_ref[...]))
    heads = [q_ref[:, :HEAD], q_ref[:, HEAD:]]
    grads = [grad[:, :HEAD], grad[:, HEAD:]]
    inverse = [inverse_ref[h : h + 1, :] for h in range(2)]
    delta = []
    for h in range(2):
        product = wide(grads[h]) * wide(out_ref[:, h * HEAD : (h + 1) * HEAD])
        delta.append(jnp.sum(jnp.swapaxes(product, 0, 1), axis=0, keepdims=True))

    def step(k_block, masked, carry):
        rows = pl.ds(pl.multiple_of(k_block * BLOCK, BLOCK), BLOCK)
        keys, values = k_ref[rows, :], v_ref[rows, :]
        allowed = allowed_block(q_block, k_block, ends, True) if masked else None
        new = []
        d_keys, d_values = dk_ref[rows, :], dv_ref[rows, :]
        for h in range(2):
            prob = jnp.exp2(contract_cols(keys, heads[h]) * (SCALE * LOG2E)) * inverse[h]
            if masked:
                prob = jnp.where(allowed, prob, 0.0)
            d_prob = contract_cols(values, grads[h])
            d_score = low(prob * (d_prob - delta[h]) * SCALE)
            d_keys += dot(d_score, heads[h])
            d_values += dot(low(prob), grads[h])
            new.append(carry[h] + contract_rows(d_score, keys))
        dk_ref[rows, :] = d_keys
        dv_ref[rows, :] = d_values
        return tuple(new)

    zero = jnp.zeros((BLOCK, HEAD), jnp.float32)
    carry = over_blocks(q_block, step, (zero, zero))
    dq_ref[:, :HEAD] = carry[0]
    dq_ref[:, HEAD:] = carry[1]


def attend_back(ends, qkv, grad, out, inverse, mix):
    blocks = PACK // BLOCK
    by_block = pl.BlockSpec((BLOCK, 2 * HEAD), lambda q, ends: (q, 0))
    whole = pl.BlockSpec((PACK, HEAD), lambda q, ends: (0, 0))
    return pl.pallas_call(
        attend_back_kernel,
        grid_spec=pltpu.PrefetchScalarGridSpec(
            num_scalar_prefetch=1,
            grid=(blocks,),
            in_specs=[
                by_block,
                pl.BlockSpec((PACK, HEAD), lambda q, ends: (0, 2)),
                pl.BlockSpec((PACK, HEAD), lambda q, ends: (0, 3)),
                by_block,
                by_block,
                pl.BlockSpec((2, BLOCK), lambda q, ends: (0, q)),
                pl.BlockSpec((2 * HEAD, 2 * HEAD), lambda q, ends: (0, 0)),
            ],
            out_specs=[by_block, whole, whole],
        ),
        out_shape=[
            jax.ShapeDtypeStruct((PACK, 2 * HEAD), jnp.float32),
            jax.ShapeDtypeStruct((PACK, HEAD), jnp.float32),
            jax.ShapeDtypeStruct((PACK, HEAD), jnp.float32),
        ],
        compiler_params=pltpu.CompilerParams(vmem_limit_bytes=VMEM_LIMIT),
        cost_estimate=pl.CostEstimate(flops=8000000000, bytes_accessed=8000000, transcendentals=3000000),
        name="attend_back",
    )(ends, qkv, qkv, qkv, grad, out, inverse, mix)


def qkv_back_kernel(rank_ref, *refs):
    pre_ref, dq_ref, dk_ref, dv_ref, cos_ref, sin_ref, normed_ref, w_ref, gq_ref, gk_ref = refs[:10]
    d_pre_ref, d_attn_ref, d_head_ref, chunks = refs[10], refs[11], refs[12], refs[13:]

    @pl.when(pl.program_id(0) == 0)
    def _():
        d_attn_ref[...] = jnp.zeros_like(d_attn_ref)
        d_head_ref[...] = jnp.zeros_like(d_head_ref)

    cosine, sine = cos_ref[...], sin_ref[...]
    for h in range(3):
        u = pre_ref[:, h * HEAD : (h + 1) * HEAD]
        gain = gk_ref[...] if h == 2 else gq_ref[...]
        grad = dk_ref[...] if h == 2 else dq_ref[:, h * HEAD : (h + 1) * HEAD]
        grad = rope_back(grad, cosine, sine)
        row = 1 if h == 2 else 0
        d_head_ref[row : row + 1, :] += jnp.sum(
            grad * u * norm_scale(u), axis=0, keepdims=True
        )
        d_pre_ref[:, h * HEAD : (h + 1) * HEAD] = low(norm_back(u, gain, grad))
    d_pre_ref[:, 3 * HEAD :] = low(dv_ref[...])
    d_normed = dot(d_pre_ref[...], w_ref[...])
    d_attn_ref[...] += jnp.sum(wide(normed_ref[...]) * d_normed, axis=0, keepdims=True)
    for k, chunk in enumerate(chunks):

        @pl.when(pl.program_id(0) == k)
        def _(chunk=chunk):
            chunk[...] = low(d_normed)


def project_back(rank, pre, d_query, d_key, d_value, cosine, sine, normed, weights, gain_query, gain_key):
    whole = lambda shape: pl.BlockSpec(shape, lambda k, rank: (0, 0))
    by_row = lambda cols: pl.BlockSpec((TOK, cols), lambda k, rank: (rank[0] ^ k, 0))
    return pl.pallas_call(
        qkv_back_kernel,
        grid_spec=pltpu.PrefetchScalarGridSpec(
            num_scalar_prefetch=1,
            grid=(8,),
            in_specs=[by_row(3 * HEAD), by_row(2 * HEAD), by_row(HEAD), by_row(HEAD)]
            + [by_row(HEAD), by_row(HEAD), by_row(WIDTH)]
            + [whole((512, WIDTH)), whole((1, HEAD)), whole((1, HEAD))],
            out_specs=[by_row(512), whole((1, WIDTH)), whole((2, HEAD))]
            + [whole((TOK, WIDTH))] * 8,
        ),
        out_shape=[
            jax.ShapeDtypeStruct((PACK, 512), jnp.bfloat16),
            jax.ShapeDtypeStruct((1, WIDTH), jnp.float32),
            jax.ShapeDtypeStruct((2, HEAD), jnp.float32),
        ]
        + [jax.ShapeDtypeStruct((TOK, WIDTH), jnp.bfloat16)] * 8,
        compiler_params=pltpu.CompilerParams(vmem_limit_bytes=VMEM_LIMIT),
        cost_estimate=pl.CostEstimate(flops=1610612736, bytes_accessed=15000000, transcendentals=0),
        name="project_back",
    )(rank, pre, d_query, d_key, d_value, cosine, sine, normed, weights, gain_query, gain_key)


def one_hot(rows, columns):
    hits = lax.broadcasted_iota(jnp.int32, (rows, columns.shape[0]), 0) == columns[None, :]
    return hits.astype(jnp.bfloat16)


def feature_mix(per_device, devices):
    slices = per_device // 8
    spot = np.arange(per_device * devices)
    k, dev, r = spot // (8 * devices), spot // 8 % devices, spot % 8
    return one_hot(per_device * devices, jnp.asarray(dev * per_device + 8 * k + r, jnp.int32)), slices


def cube_order(core):
    spots = []
    for c in range(2):
        first, second = HALVES[c], HALVES[c ^ 1]
        spots.append(
            [c ^ spanned(first, k // 8) ^ spanned(second, k % 8) for k in range(64)]
        )
    owner = jnp.where(core == 1, jnp.asarray(spots[1], jnp.int32), jnp.asarray(spots[0], jnp.int32))
    return one_hot(WIDTH, (owner[:, None] * 8 + jnp.arange(8, dtype=jnp.int32)[None, :]).reshape(-1))


def exchange(values, axes, groups=None):
    return lax.all_to_all(
        values, axes, split_axis=0, concat_axis=0, axis_index_groups=groups, tiled=True
    )


def of_chip(values):
    return jnp.concatenate([values, swap(values, CORE)], axis=0)


def first_cube(grad):
    got = exchange(grad.reshape(8, 64, -1), EVERY, cubes(0))
    return low(jnp.sum(wide(got), axis=0))


def second_cube(sums):
    pieces = sums.reshape(8, 8, -1, WIDTH).transpose(0, 2, 1, 3).reshape(8, -1, WIDTH)
    got = exchange(pieces, EVERY, cubes(1))
    return jnp.sum(wide(got), axis=0).reshape(-1, 8, WIDTH)


def gather_ring(rows):
    for first, second in ((YA, YB), (YB, YA)):
        rows = jnp.concatenate([rows, swap(rows, first, second)], axis=0)
    return rows


def scatter_ring(own, other):
    total = wide(own) + wide(swap(low(other), CORE))
    for first, second in ((YB, YA), (YA, YB)):
        half = total.shape[0] // 2
        total = total[:half] + wide(swap(low(total[half:]), first, second))
    return total


def other_axis_first(core, blocks):
    return jnp.where(core == 1, jnp.swapaxes(blocks, 0, 1), blocks)


def bit_of(index, mask):
    return index >> {XA: 5, XB: 6, ZA: 3, ZB: 4}[mask] & 1


PLANE = ((ZA, XA), (ZB, XB), (XA, ZA), (XB, ZB))


def gather_plane(index, block):
    block = block[None]
    for first, second in PLANE:
        got = swap(block, first, second)
        later = jnp.where(index & 1 == 1, bit_of(index, second), bit_of(index, first)) == 1
        block = jnp.where(
            later, jnp.concatenate([got, block], axis=0), jnp.concatenate([block, got], axis=0)
        )
    return other_axis_first(index & 1, block.reshape((4, 4) + block.shape[1:]))


def scatter_plane(index, blocks):
    blocks = other_axis_first(index & 1, blocks)
    blocks = blocks.reshape((16,) + blocks.shape[2:])
    for first, second in PLANE[::-1]:
        later = jnp.where(index & 1 == 1, bit_of(index, second), bit_of(index, first))
        half = blocks.shape[0] // 2
        keep = lax.dynamic_slice_in_dim(blocks, later * half, half, axis=0)
        send = lax.dynamic_slice_in_dim(blocks, (1 - later) * half, half, axis=0)
        total = wide(keep) + wide(swap(send, first, second))
        blocks = low(total)
    return total[0]


def on_device(
    hidden, lengths, w_query, w_key, w_value, w_out, w_gate, w_up, w_down, gains, cotangent
):
    dp_rank = lax.axis_index("dp")
    rank = dp_rank.astype(jnp.int32)[None]
    index = dp_rank * 16 + lax.axis_index("fsdp")
    core = index & 1
    inputs = hidden[0]

    local = w_out.reshape(2, 8, WIDTH).transpose(1, 0, 2).reshape(8, -1)
    full = lax.all_gather(local, EVERY, axis=0, tiled=True)
    full_out = [full[:, k * WIDTH : (k + 1) * WIDTH] for k in range(2)]

    heads = jnp.concatenate(
        [
            w_query.reshape(8, KV_HEADS, 256).transpose(1, 0, 2),
            w_key.reshape(8, KV_HEADS, HEAD).transpose(1, 0, 2),
            w_value.reshape(8, KV_HEADS, HEAD).transpose(1, 0, 2),
            jnp.broadcast_to(jnp.pad(gains[None, None, :], ((0, 0), (0, 7), (0, 110))), (8, 8, 128)),
        ],
        axis=2,
    )
    heads = jnp.broadcast_to(heads[:, None], (8, 16, 8, 640)).reshape(DEVICES, 8, 640)
    heads = exchange(heads, EVERY).reshape(8, 16, 8, 640)
    w_heads = heads[..., :512].reshape(WIDTH, 512)
    gain_all = wide(heads[:, :, 0, 512:530].reshape(1, -1))
    gain_attn, gain_mlp = gain_all[:, :WIDTH], gain_all[:, WIDTH : 2 * WIDTH]
    gain_query = gain_all[:, 2 * WIDTH : 2 * WIDTH + HEAD]
    gain_key = gain_all[:, 2 * WIDTH + HEAD :]

    chunks = [inputs] + [swap(inputs, k * 16) for k in range(1, 8)]
    ends = jnp.stack([lengths[0, 0], lengths[0, 0] + lengths[0, 1]]).astype(jnp.int32)
    token = jnp.arange(PACK, dtype=jnp.int32)
    position = wide(token - row_start(token, (ends[0], ends[1])))
    inverse = jnp.power(ROPE_BASE, -2.0 * jnp.arange(HEAD // 2, dtype=jnp.float32) / HEAD)
    angle = position[:, None] * inverse[None, :]
    cosine, sine = jnp.cos(angle), jnp.sin(angle)
    cosine = jnp.concatenate([cosine, cosine], axis=1)
    sine = jnp.concatenate([-sine, sine], axis=1)

    normed, pre, qkv = project(
        chunks, rank, w_heads, gain_attn, gain_query, gain_key, cosine, sine
    )
    w_gate, w_up, w_down, d_result, qkv = lax.optimization_barrier(
        (w_gate, w_up, w_down, cotangent[0], qkv)
    )
    units = jnp.concatenate(
        [
            weight.reshape(8, 16, 8, 24).transpose(2, 0, 1, 3).reshape(8, 8, 384)
            for weight in (w_gate, w_up)
        ],
        axis=2,
    )
    ring = [list(range(8 * k, 8 * k + 8)) for k in range(16)]
    units = exchange(units, EVERY, ring).reshape(64, 768)
    down = w_down.reshape(3, 8, 8, HEAD).transpose(2, 1, 0, 3).reshape(64, 384)
    units = gather_plane(index, jnp.concatenate([units, down], axis=1))
    full_units = units[..., :768].reshape(WIDTH, 768)
    full_down = (
        units[..., 768:].reshape(16, 8, 8, 3, HEAD).transpose(0, 3, 2, 1, 4).reshape(384, WIDTH)
    )
    d_result_own = gather_ring(d_result)
    d_result_other = swap(d_result_own, CORE)

    mix = feature_mix(16, 16)[0]
    attended_own, attended_mixed, inverse_total = attend(ends, qkv, mix)

    def to_tokens(values):
        moved = exchange(values.reshape(8, TOK, 256), "dp")
        return moved.reshape(8, TOK, 2, HEAD).transpose(1, 2, 0, 3).reshape(TOK, 2, WIDTH)

    def to_heads(values):
        apart = values.reshape(TOK, 2, 8, HEAD).transpose(2, 0, 1, 3)
        return exchange(apart.reshape(8, TOK, 256), "dp").reshape(PACK, 256)

    attended = to_tokens(attended_mixed)
    inputs_wide = wide(inputs)
    middle = inputs_wide + dot(attended[:, 0], full_out[0]) + dot(attended[:, 1], full_out[1])
    middle_scale = norm_scale(middle)
    mixed = low(middle * middle_scale * gain_mlp)
    mixed_own = gather_ring(mixed)
    mixed_other = swap(mixed_own, CORE)

    def feed_forward(rows, d_rows):
        pre = dot(rows, full_units)
        gate_pre, up_pre = pre[:, :384], pre[:, 384:]
        sigmoid = 1.0 / (1.0 + jnp.exp(-gate_pre))
        silu = gate_pre * sigmoid
        act = low(silu * up_pre)
        d_act = contract_cols(d_rows, full_down)
        d_gate = low(d_act * up_pre * (sigmoid + silu * (1.0 - sigmoid)))
        d_up = low(d_act * silu)
        d_pre = jnp.concatenate([d_gate, d_up], axis=1)
        return act, d_pre, contract_cols(d_pre, full_units)

    act_own, d_pre_own, d_mixed_own = feed_forward(mixed_own, d_result_own)
    act_other, d_pre_other, d_mixed_other = feed_forward(mixed_other, d_result_other)
    d_mixed = scatter_ring(d_mixed_own, d_mixed_other)
    d_middle = wide(d_result) + norm_back(middle, gain_mlp, d_mixed)
    d_gain_mlp = jnp.sum(middle * middle_scale * d_mixed, axis=0)
    d_branch = low(d_middle)
    d_attended = jnp.stack(
        [low(contract_cols(d_branch, full_out[k])) for k in range(2)], axis=1
    )
    d_heads = to_heads(d_attended)

    activations = low(
        middle + scatter_ring(dot(act_own, full_down), dot(act_other, full_down))
    )[None]
    grad_units = contract_rows(mixed_own, d_pre_own) + contract_rows(mixed_other, d_pre_other)
    grad_down = contract_rows(act_own, d_result_own) + contract_rows(act_other, d_result_other)
    grad_down = low(grad_down).reshape(16, 3, 8, 8, HEAD).transpose(0, 3, 2, 1, 4)
    grads = jnp.concatenate(
        [low(grad_units).reshape(16, 64, 768), grad_down.reshape(16, 64, 384)], axis=2
    )
    sums = scatter_plane(index, grads.reshape(4, 4, 64, 1152))
    sum_down = sums[:, 768:].reshape(8, 8, 3, HEAD).transpose(2, 1, 0, 3).reshape(24, WIDTH)
    units_grad = exchange(sums[:, :768].reshape(8, 8, 768), EVERY, ring)
    by_unit = lambda grad: grad.reshape(8, 8, 16, 24).transpose(1, 2, 0, 3).reshape(8, FF)

    order = cube_order(core)
    attended_rows = low(dot(of_chip(attended), order))
    d_branch_chip = of_chip(d_branch)
    grad_out = jnp.concatenate(
        [low(contract_rows(attended_rows[:, k], d_branch_chip)) for k in range(2)], axis=1
    )
    sum_out = second_cube(first_cube(grad_out)).reshape(16, WIDTH)
    d_heads = lax.optimization_barrier((d_heads, grads, grad_out))[0]

    d_query, d_key, d_value = attend_back(ends, qkv, d_heads, attended_own, inverse_total, mix)
    d_pre, d_gain_attn, d_gain_heads, *chunks = project_back(
        rank, pre, d_query, d_key, d_value, cosine, sine, normed, w_heads.T, gain_query, gain_key
    )
    d_normed = wide(chunks[0]) + sum(wide(swap(chunks[k], k * 16)) for k in range(1, 8))
    input_grad = (d_middle + norm_back(inputs_wide, gain_attn, d_normed))[None]

    d_gains = jnp.concatenate(
        [(d_gain_attn / gain_attn)[0], d_gain_mlp, d_gain_heads.reshape(-1)]
    )
    payload = jnp.concatenate(
        [
            low(contract_rows(normed, d_pre)).reshape(DEVICES, 8, 512),
            low(jnp.pad(d_gains.reshape(DEVICES, 1, 18), ((0, 0), (0, 7), (0, 110)))),
        ],
        axis=2,
    )
    heads_grad = jnp.sum(wide(exchange(payload, EVERY).reshape(8, 16, 8, 640)), axis=1)
    sum_query = heads_grad[..., :256].transpose(1, 0, 2).reshape(8, -1)
    sum_key = heads_grad[..., 256:384].transpose(1, 0, 2).reshape(8, -1)
    sum_value = heads_grad[..., 384:512].transpose(1, 0, 2).reshape(8, -1)
    sum_gains = jnp.sum(heads_grad[:, 0, 512:530], axis=0)
    return (
        activations,
        input_grad,
        sum_query,
        sum_key,
        sum_value,
        sum_out,
        by_unit(units_grad[..., :384]),
        by_unit(units_grad[..., 384:]),
        sum_down,
        sum_gains,
    )


def solution(mesh):
    rows = P(("dp", "fsdp"), None)
    tokens = P("fsdp", "dp", None)
    return jax.shard_map(
        on_device,
        mesh=mesh,
        in_specs=(tokens, P("fsdp", None), *([rows] * 7), P(("dp", "fsdp")), tokens),
        out_specs=(tokens, tokens, *([rows] * 7), P(("dp", "fsdp"))),
        check_vma=False,
    )
```

```python
import jax
import jax.numpy as jnp
from jax import lax
from jax.experimental import pallas as pl
from jax.experimental.pallas import tpu as pltpu
from jax.sharding import PartitionSpec as P

HEADS = 16
KV_HEADS = 8
HEAD = 128
EPSILON = 1e-06
ROPE_BASE = 1000000.0
DEVICES = 128
WIDTH = 1024
FF = 3072
TOK = 192
PACK = 1536
BLOCK = 256
LOG2E = 1.4426950408889634
SCALE = HEAD ** (-0.5)
EVERY = ("dp", "fsdp")
VMEM_LIMIT = 48 * 1024 * 1024

XA, XB, ZA, ZB, YA, YB, CORE = 32, 96, 8, 24, 2, 6, 1
CHIPS = [list(range(core, DEVICES, 2)) for core in range(2)]
RINGS = [[x << 5 | zy << 1 | core for x in range(4) for core in range(2)] for zy in range(16)]


def after(value, *others):
    return lax.optimization_barrier((value, *others))[0]


def swap(values, mask, other_mask=None):
    masks = (mask, mask if other_mask is None else other_mask)
    return lax.ppermute(values, EVERY, [(k, k ^ masks[k & 1]) for k in range(DEVICES)])


def low(values):
    return values.astype(jnp.bfloat16)


def wide(values):
    return values.astype(jnp.float32)


def dot(left, right):
    return jnp.dot(left, right, preferred_element_type=jnp.float32)


def contract_rows(left, right):
    return lax.dot_general(
        left, right, (((0,), (0,)), ((), ())), preferred_element_type=jnp.float32
    )


def contract_cols(left, right):
    return lax.dot_general(
        left, right, (((1,), (1,)), ((), ())), preferred_element_type=jnp.float32
    )


def norm_scale(values):
    return lax.rsqrt(jnp.mean(values * values, axis=-1, keepdims=True) + EPSILON)


def norm_back(values, gain, grad):
    scale = norm_scale(values)
    normal = values * scale
    inner = grad * gain
    return scale * (inner - normal * jnp.mean(inner * normal, axis=-1, keepdims=True))


def rope(values, cosine, sine):
    return values * cosine + pltpu.roll(values, 64, 1) * sine


def rope_back(grad, cosine, sine):
    return grad * cosine + pltpu.roll(grad * sine, 64, 1)


def qkv_kernel(rank_ref, *refs):
    chunks, (w_ref, ga_ref, gq_ref, gk_ref, cos_ref, sin_ref) = refs[:8], refs[8:14]
    normed_ref, pre_ref, qkv_ref = refs[14:]
    for k, chunk in enumerate(chunks):

        @pl.when(pl.program_id(0) == k)
        def _(chunk=chunk):
            x = wide(chunk[...])
            normed_ref[...] = low(x * norm_scale(x) * ga_ref[...])

    pre = dot(normed_ref[...], w_ref[...])
    pre_ref[...] = pre[:, : 3 * HEAD]
    cosine, sine = cos_ref[...], sin_ref[...]
    for h in range(3):
        u = pre[:, h * HEAD : (h + 1) * HEAD]
        gain = gk_ref[...] if h == 2 else gq_ref[...]
        normal = u * norm_scale(u) * gain
        qkv_ref[:, h * HEAD : (h + 1) * HEAD] = low(rope(normal, cosine, sine))
    qkv_ref[:, 3 * HEAD :] = low(pre[:, 3 * HEAD :])


def project(chunks, rank, weights, gain_attn, gain_query, gain_key, cosine, sine):
    whole = lambda shape: pl.BlockSpec(shape, lambda k, rank: (0, 0))
    by_row = lambda cols: pl.BlockSpec((TOK, cols), lambda k, rank: (rank[0] ^ k, 0))
    return pl.pallas_call(
        qkv_kernel,
        grid_spec=pltpu.PrefetchScalarGridSpec(
            num_scalar_prefetch=1,
            grid=(8,),
            in_specs=[whole((TOK, WIDTH))] * 8
            + [whole((WIDTH, 512)), whole((1, WIDTH)), whole((1, HEAD)), whole((1, HEAD))]
            + [by_row(HEAD), by_row(HEAD)],
            out_specs=[by_row(WIDTH), by_row(3 * HEAD), by_row(512)],
        ),
        out_shape=[
            jax.ShapeDtypeStruct((PACK, WIDTH), jnp.bfloat16),
            jax.ShapeDtypeStruct((PACK, 3 * HEAD), jnp.float32),
            jax.ShapeDtypeStruct((PACK, 512), jnp.bfloat16),
        ],
        compiler_params=pltpu.CompilerParams(vmem_limit_bytes=VMEM_LIMIT),
        cost_estimate=pl.CostEstimate(flops=1610612736, bytes_accessed=12000000, transcendentals=0),
        name="project",
    )(rank, *chunks, weights, gain_attn, gain_query, gain_key, cosine, sine)


def row_start(rows, ends):
    first, second = ends
    return jnp.where(rows >= second, second, jnp.where(rows >= first, first, 0))


def allowed_block(q_block, k_block, ends, transposed):
    q_axis, k_axis = (1, 0) if transposed else (0, 1)
    q_rows = q_block * BLOCK + lax.broadcasted_iota(jnp.int32, (BLOCK, BLOCK), q_axis)
    k_rows = k_block * BLOCK + lax.broadcasted_iota(jnp.int32, (BLOCK, BLOCK), k_axis)
    return (k_rows <= q_rows) & (k_rows >= row_start(q_rows, ends))


def over_blocks(q_block, step, carry):
    last = PACK // BLOCK - 1
    masked_from = jnp.where(q_block == last, 1, jnp.maximum(q_block, 1))
    carry = step(0, True, carry)
    carry = lax.fori_loop(1, masked_from, lambda k, c: step(k, False, c), carry)
    return lax.fori_loop(masked_from, q_block + 1, lambda k, c: step(k, True, c), carry)


def attend_kernel(ends_ref, q_ref, k_ref, v_ref, out_ref, inverse_ref):
    q_block = pl.program_id(0)
    ends = (ends_ref[0], ends_ref[1])
    heads = [q_ref[:, :HEAD], q_ref[:, HEAD:]]

    def step(k_block, masked, carry):
        rows = pl.ds(pl.multiple_of(k_block * BLOCK, BLOCK), BLOCK)
        keys, values = k_ref[rows, :], v_ref[rows, :]
        allowed = allowed_block(q_block, k_block, ends, False) if masked else None
        new = []
        for h in range(2):
            total, part = carry[2 * h], carry[2 * h + 1]
            shifted = jnp.exp2(contract_cols(heads[h], keys) * (SCALE * LOG2E))
            if masked:
                shifted = jnp.where(allowed, shifted, 0.0)
            new.append(total + dot(low(shifted), values))
            new.append(part + shifted[:, :HEAD] + shifted[:, HEAD:])
        return tuple(new)

    zero = jnp.zeros((BLOCK, HEAD), jnp.float32)
    carry = over_blocks(q_block, step, (zero, zero, zero, zero))
    for h in range(2):
        total, part = carry[2 * h], carry[2 * h + 1]
        row_total = jnp.sum(part, axis=1, keepdims=True)
        out_ref[:, h * HEAD : (h + 1) * HEAD] = low(total / row_total)
        across = jnp.sum(jnp.swapaxes(part, 0, 1), axis=0, keepdims=True)
        inverse_ref[h : h + 1, :] = 1.0 / across


def attend(ends, qkv):
    blocks = PACK // BLOCK
    return pl.pallas_call(
        attend_kernel,
        grid_spec=pltpu.PrefetchScalarGridSpec(
            num_scalar_prefetch=1,
            grid=(blocks,),
            in_specs=[
                pl.BlockSpec((BLOCK, 2 * HEAD), lambda q, ends: (q, 0)),
                pl.BlockSpec((PACK, HEAD), lambda q, ends: (0, 2)),
                pl.BlockSpec((PACK, HEAD), lambda q, ends: (0, 3)),
            ],
            out_specs=[
                pl.BlockSpec((BLOCK, 2 * HEAD), lambda q, ends: (q, 0)),
                pl.BlockSpec((2, BLOCK), lambda q, ends: (0, q)),
            ],
        ),
        out_shape=[
            jax.ShapeDtypeStruct((PACK, 2 * HEAD), jnp.bfloat16),
            jax.ShapeDtypeStruct((2, PACK), jnp.float32),
        ],
        compiler_params=pltpu.CompilerParams(vmem_limit_bytes=VMEM_LIMIT),
        cost_estimate=pl.CostEstimate(flops=3000000000, bytes_accessed=4000000, transcendentals=3000000),
        name="attend",
    )(ends, qkv, qkv, qkv)


def attend_back_kernel(
    ends_ref, q_ref, k_ref, v_ref, grad_ref, out_ref, inverse_ref,
    dq_ref, dk_ref, dv_ref,
):
    q_block = pl.program_id(0)
    ends = (ends_ref[0], ends_ref[1])

    @pl.when(q_block == 0)
    def _():
        dk_ref[...] = jnp.zeros_like(dk_ref)
        dv_ref[...] = jnp.zeros_like(dv_ref)

    heads = [q_ref[:, :HEAD], q_ref[:, HEAD:]]
    grads = [grad_ref[:, :HEAD], grad_ref[:, HEAD:]]
    inverse = [inverse_ref[h : h + 1, :] for h in range(2)]
    delta = []
    for h in range(2):
        product = wide(grads[h]) * wide(out_ref[:, h * HEAD : (h + 1) * HEAD])
        delta.append(jnp.sum(jnp.swapaxes(product, 0, 1), axis=0, keepdims=True))

    def step(k_block, masked, carry):
        rows = pl.ds(pl.multiple_of(k_block * BLOCK, BLOCK), BLOCK)
        keys, values = k_ref[rows, :], v_ref[rows, :]
        allowed = allowed_block(q_block, k_block, ends, True) if masked else None
        new = []
        d_keys, d_values = dk_ref[rows, :], dv_ref[rows, :]
        for h in range(2):
            prob = jnp.exp2(contract_cols(keys, heads[h]) * (SCALE * LOG2E)) * inverse[h]
            if masked:
                prob = jnp.where(allowed, prob, 0.0)
            d_prob = contract_cols(values, grads[h])
            d_score = low(prob * (d_prob - delta[h]) * SCALE)
            d_keys += dot(d_score, heads[h])
            d_values += dot(low(prob), grads[h])
            new.append(carry[h] + contract_rows(d_score, keys))
        dk_ref[rows, :] = d_keys
        dv_ref[rows, :] = d_values
        return tuple(new)

    zero = jnp.zeros((BLOCK, HEAD), jnp.float32)
    carry = over_blocks(q_block, step, (zero, zero))
    dq_ref[:, :HEAD] = carry[0]
    dq_ref[:, HEAD:] = carry[1]


def attend_back(ends, qkv, grad, out, inverse):
    blocks = PACK // BLOCK
    by_block = pl.BlockSpec((BLOCK, 2 * HEAD), lambda q, ends: (q, 0))
    whole = pl.BlockSpec((PACK, HEAD), lambda q, ends: (0, 0))
    return pl.pallas_call(
        attend_back_kernel,
        grid_spec=pltpu.PrefetchScalarGridSpec(
            num_scalar_prefetch=1,
            grid=(blocks,),
            in_specs=[
                by_block,
                pl.BlockSpec((PACK, HEAD), lambda q, ends: (0, 2)),
                pl.BlockSpec((PACK, HEAD), lambda q, ends: (0, 3)),
                by_block,
                by_block,
                pl.BlockSpec((2, BLOCK), lambda q, ends: (0, q)),
            ],
            out_specs=[by_block, whole, whole],
        ),
        out_shape=[
            jax.ShapeDtypeStruct((PACK, 2 * HEAD), jnp.float32),
            jax.ShapeDtypeStruct((PACK, HEAD), jnp.float32),
            jax.ShapeDtypeStruct((PACK, HEAD), jnp.float32),
        ],
        compiler_params=pltpu.CompilerParams(vmem_limit_bytes=VMEM_LIMIT),
        cost_estimate=pl.CostEstimate(flops=8000000000, bytes_accessed=8000000, transcendentals=3000000),
        name="attend_back",
    )(ends, qkv, qkv, qkv, grad, out, inverse)


def qkv_back_kernel(rank_ref, *refs):
    pre_ref, dq_ref, dk_ref, dv_ref, cos_ref, sin_ref, normed_ref, w_ref, gq_ref, gk_ref = refs[:10]
    d_pre_ref, d_attn_ref, d_head_ref, chunks = refs[10], refs[11], refs[12], refs[13:]

    @pl.when(pl.program_id(0) == 0)
    def _():
        d_attn_ref[...] = jnp.zeros_like(d_attn_ref)
        d_head_ref[...] = jnp.zeros_like(d_head_ref)

    cosine, sine = cos_ref[...], sin_ref[...]
    for h in range(3):
        u = pre_ref[:, h * HEAD : (h + 1) * HEAD]
        gain = gk_ref[...] if h == 2 else gq_ref[...]
        grad = dk_ref[...] if h == 2 else dq_ref[:, h * HEAD : (h + 1) * HEAD]
        grad = rope_back(grad, cosine, sine)
        row = 1 if h == 2 else 0
        d_head_ref[row : row + 1, :] += jnp.sum(
            grad * u * norm_scale(u), axis=0, keepdims=True
        )
        d_pre_ref[:, h * HEAD : (h + 1) * HEAD] = low(norm_back(u, gain, grad))
    d_pre_ref[:, 3 * HEAD :] = low(dv_ref[...])
    d_normed = dot(d_pre_ref[...], w_ref[...])
    d_attn_ref[...] += jnp.sum(wide(normed_ref[...]) * d_normed, axis=0, keepdims=True)
    for k, chunk in enumerate(chunks):

        @pl.when(pl.program_id(0) == k)
        def _(chunk=chunk):
            chunk[...] = low(d_normed)


def project_back(rank, pre, d_query, d_key, d_value, cosine, sine, normed, weights, gain_query, gain_key):
    whole = lambda shape: pl.BlockSpec(shape, lambda k, rank: (0, 0))
    by_row = lambda cols: pl.BlockSpec((TOK, cols), lambda k, rank: (rank[0] ^ k, 0))
    return pl.pallas_call(
        qkv_back_kernel,
        grid_spec=pltpu.PrefetchScalarGridSpec(
            num_scalar_prefetch=1,
            grid=(8,),
            in_specs=[by_row(3 * HEAD), by_row(2 * HEAD), by_row(HEAD), by_row(HEAD)]
            + [by_row(HEAD), by_row(HEAD), by_row(WIDTH)]
            + [whole((512, WIDTH)), whole((1, HEAD)), whole((1, HEAD))],
            out_specs=[by_row(512), whole((1, WIDTH)), whole((2, HEAD))]
            + [whole((TOK, WIDTH))] * 8,
        ),
        out_shape=[
            jax.ShapeDtypeStruct((PACK, 512), jnp.bfloat16),
            jax.ShapeDtypeStruct((1, WIDTH), jnp.float32),
            jax.ShapeDtypeStruct((2, HEAD), jnp.float32),
        ]
        + [jax.ShapeDtypeStruct((TOK, WIDTH), jnp.bfloat16)] * 8,
        compiler_params=pltpu.CompilerParams(vmem_limit_bytes=VMEM_LIMIT),
        cost_estimate=pl.CostEstimate(flops=1610612736, bytes_accessed=15000000, transcendentals=0),
        name="project_back",
    )(rank, pre, d_query, d_key, d_value, cosine, sine, normed, weights, gain_query, gain_key)


def exchange(values, axes, groups=None):
    return lax.all_to_all(
        values, axes, split_axis=0, concat_axis=0, axis_index_groups=groups, tiled=True
    )


RING_ORDER = ((XA, XB), (XB, XA))
PLANE = ((YA, ZA), (YB, ZB), (ZA, YA), (ZB, YB))
BIT = {YA: 1, YB: 2, ZA: 3, ZB: 4}


def core_order(core, blocks):
    return jnp.where(core == 1, jnp.swapaxes(blocks, 0, 1), blocks)


def gather_plane(index, block, gates):
    block = block[None]
    for (first, second), gate in zip(PLANE, gates):
        got = swap(after(block, *gate), first, second)
        later = jnp.where(index & 1 == 1, index >> BIT[second], index >> BIT[first]) & 1
        block = jnp.where(
            later == 1,
            jnp.concatenate([got, block], axis=0),
            jnp.concatenate([block, got], axis=0),
        )
    return core_order(index & 1, block.reshape((4, 4) + block.shape[1:]))


def scatter_plane(index, blocks, gates):
    blocks = core_order(index & 1, blocks)
    blocks = blocks.reshape((16,) + blocks.shape[2:])
    for (first, second), gate in zip(PLANE[::-1], gates):
        blocks = after(blocks, *gate)
        later = jnp.where(index & 1 == 1, index >> BIT[second], index >> BIT[first]) & 1
        half = blocks.shape[0] // 2
        keep = lax.dynamic_slice_in_dim(blocks, later * half, half, axis=0)
        send = lax.dynamic_slice_in_dim(blocks, (1 - later) * half, half, axis=0)
        total = wide(keep) + wide(swap(send, first, second))
        blocks = low(total)
    return total[0]


def on_device(
    hidden, lengths, w_query, w_key, w_value, w_out, w_gate, w_up, w_down, gains, cotangent
):
    dp_rank = lax.axis_index("dp")
    rank = dp_rank.astype(jnp.int32)[None]
    index = dp_rank * 16 + lax.axis_index("fsdp")
    core = index & 1
    inputs = hidden[0]

    full_out = lax.all_gather(w_out, EVERY, axis=0, tiled=True)

    heads = jnp.concatenate(
        [
            w_query.reshape(8, KV_HEADS, 256).transpose(1, 0, 2),
            w_key.reshape(8, KV_HEADS, HEAD).transpose(1, 0, 2),
            w_value.reshape(8, KV_HEADS, HEAD).transpose(1, 0, 2),
            jnp.broadcast_to(jnp.pad(gains[None, None, :], ((0, 0), (0, 7), (0, 110))), (8, 8, 128)),
        ],
        axis=2,
    )
    heads = exchange(heads, "dp")[None]
    for mask, bit in ((ZA, 3), (YA, 1), (YB, 2), (CORE, 0)):
        got = swap(heads, mask)
        heads = jnp.where(
            index >> bit & 1 == 1,
            jnp.concatenate([got, heads], axis=0),
            jnp.concatenate([heads, got], axis=0),
        )
    heads = heads.reshape(2, 4, 2, 8, 8, 640).transpose(3, 2, 1, 0, 4, 5).reshape(8, 16, 8, 640)
    w_heads = heads[..., :512].reshape(WIDTH, 512)
    gain_all = wide(heads[:, :, 0, 512:530].reshape(1, -1))
    gain_attn, gain_mlp = gain_all[:, :WIDTH], gain_all[:, WIDTH : 2 * WIDTH]
    gain_query = gain_all[:, 2 * WIDTH : 2 * WIDTH + HEAD]
    gain_key = gain_all[:, 2 * WIDTH + HEAD :]

    chunks = [inputs] + [swap(inputs, k * 16) for k in range(1, 8)]
    ends = jnp.stack([lengths[0, 0], lengths[0, 0] + lengths[0, 1]]).astype(jnp.int32)
    token = jnp.arange(PACK, dtype=jnp.int32)
    position = wide(token - row_start(token, (ends[0], ends[1])))
    inverse = jnp.power(ROPE_BASE, -2.0 * jnp.arange(HEAD // 2, dtype=jnp.float32) / HEAD)
    angle = position[:, None] * inverse[None, :]
    cosine, sine = jnp.cos(angle), jnp.sin(angle)
    cosine = jnp.concatenate([cosine, cosine], axis=1)
    sine = jnp.concatenate([-sine, sine], axis=1)

    normed, pre, qkv = project(
        chunks, rank, w_heads, gain_attn, gain_query, gain_key, cosine, sine
    )
    attended_own, inverse_total = attend(ends, qkv)
    attended = exchange(attended_own.reshape(8, TOK, 256), "dp")
    attended_rows = attended.transpose(1, 0, 2).reshape(TOK, 2048)

    w_gate, w_up = (after(weight, chunks[1]) for weight in (w_gate, w_up))
    units = jnp.concatenate(
        [
            weight.reshape(8, 4, 16, 2, 24).transpose(1, 3, 0, 2, 4).reshape(8, 8, 384)
            for weight in (w_gate, w_up)
        ],
        axis=2,
    )
    units = exchange(units, EVERY, RINGS).reshape(64, 768)
    down = w_down.reshape(3, 8, 8, HEAD).transpose(2, 1, 0, 3).reshape(64, 384)
    units = gather_plane(
        index,
        jnp.concatenate([units, down], axis=1),
        ((), (normed,), (attended_own,), (attended_own,)),
    ).reshape(16, 64, 1152)
    full_units = (
        units[..., :768].reshape(16, 4, 2, 8, 768).transpose(1, 0, 2, 3, 4).reshape(WIDTH, 768)
    )
    full_down = (
        units[..., 768:].reshape(16, 8, 8, 3, HEAD).transpose(0, 3, 2, 1, 4).reshape(384, WIDTH)
    )

    def gather_ring(rows, gates):
        for (first, second), gate in zip(RING_ORDER, gates):
            rows = after(rows, *gate)
            rows = jnp.concatenate([rows, swap(rows, first, second)], axis=0)
        return rows

    d_result = cotangent[0]
    d_result_own = gather_ring(d_result, ((normed,), (attended_own,)))
    d_result_other = swap(after(d_result_own, attended), CORE)

    inputs_wide = wide(inputs)
    middle = inputs_wide + dot(attended_rows, full_out)
    middle_scale = norm_scale(middle)
    mixed = low(middle * middle_scale * gain_mlp)
    mixed_own = gather_ring(mixed, ((), ()))
    mixed_other = swap(mixed_own, CORE)

    def feed_forward(rows, d_rows):
        pre = dot(rows, full_units)
        gate_pre, up_pre = pre[:, :384], pre[:, 384:]
        sigmoid = 1.0 / (1.0 + jnp.exp(-gate_pre))
        silu = gate_pre * sigmoid
        act = low(silu * up_pre)
        d_act = contract_cols(d_rows, full_down)
        d_gate = low(d_act * up_pre * (sigmoid + silu * (1.0 - sigmoid)))
        d_up = low(d_act * silu)
        d_pre = jnp.concatenate([d_gate, d_up], axis=1)
        return act, d_pre, contract_cols(d_pre, full_units)

    def scatter_ring(own, other, gates):
        total = wide(own) + wide(after(swap(low(other), CORE), *gates[0]))
        for (first, second), gate in zip(RING_ORDER[::-1], gates[1:]):
            half = total.shape[0] // 2
            got = swap(low(total[half:]), first, second)
            total = total[:half] + wide(after(got, *gate))
        return total

    act_own, d_pre_own, d_mixed_own = feed_forward(mixed_own, d_result_own)
    act_other, d_pre_other, d_mixed_other = feed_forward(mixed_other, d_result_other)
    d_mixed = scatter_ring(d_mixed_own, d_mixed_other, ((), (), ()))
    d_middle = wide(d_result) + norm_back(middle, gain_mlp, d_mixed)
    d_gain_mlp = jnp.sum(middle * middle_scale * d_mixed, axis=0)
    d_branch = low(d_middle)
    d_attended = low(contract_cols(d_branch, full_out))
    d_heads = exchange(d_attended.reshape(TOK, 8, 256).transpose(1, 0, 2), "dp").reshape(PACK, 256)

    act_own, act_other, d_pre_own, d_pre_other = lax.optimization_barrier(
        (act_own, act_other, d_pre_own, d_pre_other, d_mixed_other)
    )[:4]
    grad_units = contract_rows(mixed_own, d_pre_own) + contract_rows(mixed_other, d_pre_other)
    grad_down = contract_rows(act_own, d_result_own) + contract_rows(act_other, d_result_other)
    grad_down = low(grad_down).reshape(16, 3, 8, 8, HEAD).transpose(0, 3, 2, 1, 4)
    grad_units = low(grad_units).reshape(4, 16, 2, 8, 768).transpose(1, 0, 2, 3, 4)
    grads = jnp.concatenate(
        [grad_units.reshape(16, 64, 768), grad_down.reshape(16, 64, 384)], axis=2
    )
    act_own, act_other = (after(act, d_attended) for act in (act_own, act_other))
    result_own, result_other = dot(act_own, full_down), low(dot(act_other, full_down))

    spot = jnp.arange(HEAD, dtype=jnp.int32)
    own_rows = spot // 16 * 32 + spot % 16
    take = lambda c: (
        lax.broadcasted_iota(jnp.int32, (256, HEAD), 0) == own_rows[None, :] + 16 * c
    ).astype(jnp.bfloat16)
    attended_wide = attended.transpose(1, 0, 2)
    send = low(dot(attended_wide, take(1 - core))).reshape(TOK, WIDTH)
    keep = low(dot(attended_wide, take(core))).reshape(TOK, WIDTH)
    d_branch_late = after(d_branch, d_attended)
    got_out = swap(low(contract_rows(send, d_branch_late)), CORE)
    grad_out = contract_rows(keep, d_branch_late)

    d_heads = after(d_heads, grads, grad_out, result_own, result_other)
    d_query, d_key, d_value = attend_back(ends, qkv, d_heads, attended_own, inverse_total)
    grad_out = low(grad_out + wide(after(got_out, d_query)))
    d_pre, d_gain_attn, d_gain_heads, *chunks = project_back(
        rank, pre, d_query, d_key, d_value, cosine, sine, normed, w_heads.T, gain_query, gain_key
    )
    got = [swap(chunks[k], k * 16) for k in range(1, 8)]
    d_normed = wide(chunks[0]) + sum(wide(chunk) for chunk in got)
    input_grad = (d_middle + norm_back(inputs_wide, gain_attn, d_normed))[None]

    activations = low(
        middle + scatter_ring(result_own, result_other, ((d_query,), (chunks[0],), (chunks[0],)))
    )[None]
    sum_out = jnp.sum(wide(exchange(grad_out.reshape(64, 16, WIDTH), EVERY, CHIPS)), axis=0)
    sums = scatter_plane(
        index, grads.reshape(4, 4, 64, 1152), ((), (d_query,), (chunks[0],), (chunks[0],))
    )
    sum_down = sums[:, 768:].reshape(8, 8, 3, HEAD).transpose(2, 1, 0, 3).reshape(24, WIDTH)
    units_grad = exchange(sums[:, :768].reshape(8, 8, 768), EVERY, RINGS)
    by_unit = lambda grad: (
        grad.reshape(4, 2, 8, 16, 24).transpose(2, 0, 3, 1, 4).reshape(8, FF)
    )

    d_gains = jnp.concatenate(
        [(d_gain_attn / gain_attn)[0], d_gain_mlp, d_gain_heads.reshape(-1)]
    )
    payload = jnp.concatenate(
        [
            low(contract_rows(normed, after(d_pre, got[0]))).reshape(DEVICES, 8, 512),
            low(jnp.pad(d_gains.reshape(DEVICES, 1, 18), ((0, 0), (0, 7), (0, 110)))),
        ],
        axis=2,
    )
    payload = payload.reshape(8, 16, 8, 640).transpose(1, 0, 2, 3).reshape(16, 64, 640)
    heads_grad = low(jnp.sum(wide(exchange(payload, "fsdp")), axis=0))
    heads_grad = wide(exchange(heads_grad.reshape(8, 8, 640), "dp"))
    sum_query = heads_grad[..., :256].transpose(1, 0, 2).reshape(8, -1)
    sum_key = heads_grad[..., 256:384].transpose(1, 0, 2).reshape(8, -1)
    sum_value = heads_grad[..., 384:512].transpose(1, 0, 2).reshape(8, -1)
    sum_gains = jnp.sum(heads_grad[:, 0, 512:530], axis=0)
    return (
        activations,
        input_grad,
        sum_query,
        sum_key,
        sum_value,
        sum_out,
        by_unit(units_grad[..., :384]),
        by_unit(units_grad[..., 384:]),
        sum_down,
        sum_gains,
    )


def solution(mesh):
    rows = P(("dp", "fsdp"), None)
    tokens = P("fsdp", "dp", None)
    return jax.shard_map(
        on_device,
        mesh=mesh,
        in_specs=(tokens, P("fsdp", None), *([rows] * 7), P(("dp", "fsdp")), tokens),
        out_specs=(tokens, tokens, *([rows] * 7), P(("dp", "fsdp"))),
        check_vma=False,
    )
```

```python
import jax
import jax.numpy as jnp
from jax import lax
from jax.experimental import pallas as pl
from jax.experimental.pallas import tpu as pltpu
from jax.sharding import Mesh
from jax.sharding import PartitionSpec as P

HEADS = 16
KV_HEADS = 8
HEAD = 128
EPSILON = 1e-06
ROPE_BASE = 1000000.0
DEVICES = 128
WIDTH = 1024
FF = 3072
TOK = 192
PACK = 1536
BLOCK = 256
LOG2E = 1.4426950408889634
SCALE = HEAD ** (-0.5)
VMEM_LIMIT = 48 * 1024 * 1024

AXES = ("x", "zh", "zl", "y", "core")
RING = ("x", "core")
PLANE = ("zh", "zl", "y")
XA, XB, ZA, ZB, YA, YB, CORE = 32, 96, 8, 24, 2, 6, 1
RING_STEPS = ((XA, XB), (XB, XA))
RING_SPOTS = ((0, 1, 3, 2), (0, 3, 1, 2))
PLANE_STEPS = ((YA, ZA), (YB, ZB), (ZA, YA), (ZB, YB))
BIT = {YA: 1, YB: 2, ZA: 3, ZB: 4}


def swap(values, mask, other_mask=None):
    masks = (mask, mask if other_mask is None else other_mask)
    return lax.ppermute(values, AXES, [(k, k ^ masks[k & 1]) for k in range(DEVICES)])


def cross(values):
    pairs = [(k, k ^ 17 if (k >> 4 ^ k) & 1 else k) for k in range(DEVICES)]
    return lax.ppermute(values, AXES, pairs)


def after(value, *others):
    return lax.optimization_barrier((value, *others))[0] if others else value


def low(values):
    return values.astype(jnp.bfloat16)


def wide(values):
    return values.astype(jnp.float32)


def dot(left, right):
    return jnp.dot(left, right, preferred_element_type=jnp.float32)


def contract_rows(left, right):
    return lax.dot_general(
        left, right, (((0,), (0,)), ((), ())), preferred_element_type=jnp.float32
    )


def contract_cols(left, right):
    return lax.dot_general(
        left, right, (((1,), (1,)), ((), ())), preferred_element_type=jnp.float32
    )


def norm_scale(values):
    return lax.rsqrt(jnp.mean(values * values, axis=-1, keepdims=True) + EPSILON)


def norm_back(values, gain, grad):
    scale = norm_scale(values)
    normal = values * scale
    inner = grad * gain
    return scale * (inner - normal * jnp.mean(inner * normal, axis=-1, keepdims=True))


def rope(values, cosine, sine):
    return values * cosine + pltpu.roll(values, 64, 1) * sine


def rope_back(grad, cosine, sine):
    return grad * cosine + pltpu.roll(grad * sine, 64, 1)


def ring_specs(columns):
    return [
        pl.BlockSpec((TOK, columns), lambda k, spots: (jnp.minimum(k, 3), 0)),
        pl.BlockSpec((TOK, columns), lambda k, spots: (jnp.maximum(k - 4, 0), 0)),
    ]


def pack_spec(columns, column=0):
    return pl.BlockSpec((TOK, columns), lambda k, spots: (spots[k], column))


def whole_spec(shape):
    return pl.BlockSpec(shape, lambda k, spots: (0, 0))


def ring_call(kernel, name, in_specs, out_specs, out_shape, flops, spots, *operands):
    return pl.pallas_call(
        kernel,
        grid_spec=pltpu.PrefetchScalarGridSpec(
            num_scalar_prefetch=1, grid=(8,), in_specs=in_specs, out_specs=out_specs
        ),
        out_shape=[jax.ShapeDtypeStruct(shape, dtype) for shape, dtype in out_shape],
        compiler_params=pltpu.CompilerParams(vmem_limit_bytes=VMEM_LIMIT),
        cost_estimate=pl.CostEstimate(flops=flops, bytes_accessed=12000000, transcendentals=0),
        name=name,
    )(spots, *operands)


def on_half(own, other, step):
    @pl.when(pl.program_id(0) < 4)
    def _():
        step(own)

    @pl.when(pl.program_id(0) >= 4)
    def _():
        step(other)


def qkv_kernel(
    spots, own_ref, other_ref, w_ref, ga_ref, gq_ref, gk_ref, cos_ref, sin_ref,
    normed_ref, pre_ref, qkv_ref,
):
    def norm(rows_ref):
        x = wide(rows_ref[...])
        normed_ref[...] = low(x * norm_scale(x) * ga_ref[...])

    on_half(own_ref, other_ref, norm)
    pre = dot(normed_ref[...], w_ref[...])
    pre_ref[...] = pre[:, : 3 * HEAD]
    cosine, sine = cos_ref[...], sin_ref[...]
    for h in range(3):
        u = pre[:, h * HEAD : (h + 1) * HEAD]
        gain = gk_ref[...] if h == 2 else gq_ref[...]
        normal = u * norm_scale(u) * gain
        qkv_ref[:, h * HEAD : (h + 1) * HEAD] = low(rope(normal, cosine, sine))
    qkv_ref[:, 3 * HEAD :] = low(pre[:, 3 * HEAD :])


def project(spots, own, other, weights, gain_attn, gain_query, gain_key, cosine, sine):
    return ring_call(
        qkv_kernel,
        "project",
        ring_specs(WIDTH)
        + [whole_spec((WIDTH, 512)), whole_spec((1, WIDTH)), whole_spec((1, HEAD)), whole_spec((1, HEAD))]
        + [pack_spec(HEAD), pack_spec(HEAD)],
        [pack_spec(WIDTH), pack_spec(3 * HEAD), pack_spec(512)],
        [
            ((PACK, WIDTH), jnp.bfloat16),
            ((PACK, 3 * HEAD), jnp.float32),
            ((PACK, 512), jnp.bfloat16),
        ],
        1610612736, spots, own, other, weights, gain_attn, gain_query, gain_key, cosine, sine,
    )


def to_ring_kernel(spots, rows_ref, w_ref, own_ref, other_ref):
    product = low(dot(rows_ref[...], w_ref[...]))

    def put(ref):
        ref[...] = product

    on_half(own_ref, other_ref, put)


def to_ring(spots, rows, weights):
    half = ((PACK // 2, WIDTH), jnp.bfloat16)
    return ring_call(
        to_ring_kernel, "to_ring", [pack_spec(256), whole_spec((256, WIDTH))], ring_specs(WIDTH),
        [half, half], 800000000, spots, rows, weights,
    )


def to_pack_kernel(spots, own_ref, other_ref, w_ref, rows_ref):
    def put(ref):
        rows_ref[...] = low(dot(ref[...], w_ref[...]))

    on_half(own_ref, other_ref, put)


def to_pack(spots, own, other, weights):
    return ring_call(
        to_pack_kernel, "to_pack", ring_specs(own.shape[1]) + [whole_spec(weights.shape)],
        [pack_spec(WIDTH)], [((PACK, WIDTH), jnp.bfloat16)], 1200000000, spots, own, other, weights,
    )[0]


def out_back_kernel(spots, own_ref, other_ref, attended_ref, w_ref, d_attended_ref, d_w_ref):
    @pl.when(pl.program_id(0) == 0)
    def _():
        d_w_ref[...] = jnp.zeros_like(d_w_ref)

    def step(ref):
        d_attended_ref[...] = low(contract_cols(ref[...], w_ref[...]))
        d_w_ref[...] += contract_rows(attended_ref[...], ref[...])

    on_half(own_ref, other_ref, step)


def out_back(spots, own, other, attended, weights):
    return ring_call(
        out_back_kernel, "out_back",
        ring_specs(WIDTH) + [pack_spec(256), whole_spec((256, WIDTH))],
        [pack_spec(256), whole_spec((256, WIDTH))],
        [((PACK, 256), jnp.bfloat16), ((256, WIDTH), jnp.float32)],
        1600000000, spots, own, other, attended, weights,
    )


def row_start(rows, ends):
    first, second = ends
    return jnp.where(rows >= second, second, jnp.where(rows >= first, first, 0))


def allowed_block(q_block, k_block, ends, transposed):
    q_axis, k_axis = (1, 0) if transposed else (0, 1)
    q_rows = q_block * BLOCK + lax.broadcasted_iota(jnp.int32, (BLOCK, BLOCK), q_axis)
    k_rows = k_block * BLOCK + lax.broadcasted_iota(jnp.int32, (BLOCK, BLOCK), k_axis)
    return (k_rows <= q_rows) & (k_rows >= row_start(q_rows, ends))


def over_blocks(q_block, step, carry):
    last = PACK // BLOCK - 1
    masked_from = jnp.where(q_block == last, 1, jnp.maximum(q_block, 1))
    carry = step(0, True, carry)
    carry = lax.fori_loop(1, masked_from, lambda k, c: step(k, False, c), carry)
    return lax.fori_loop(masked_from, q_block + 1, lambda k, c: step(k, True, c), carry)


def attend_kernel(ends_ref, q_ref, k_ref, v_ref, out_ref, inverse_ref):
    q_block = pl.program_id(0)
    ends = (ends_ref[0], ends_ref[1])
    heads = [q_ref[:, :HEAD], q_ref[:, HEAD:]]

    def step(k_block, masked, carry):
        rows = pl.ds(pl.multiple_of(k_block * BLOCK, BLOCK), BLOCK)
        keys, values = k_ref[rows, :], v_ref[rows, :]
        allowed = allowed_block(q_block, k_block, ends, False) if masked else None
        new = []
        for h in range(2):
            total, part = carry[2 * h], carry[2 * h + 1]
            shifted = jnp.exp2(contract_cols(heads[h], keys) * (SCALE * LOG2E))
            if masked:
                shifted = jnp.where(allowed, shifted, 0.0)
            new.append(total + dot(low(shifted), values))
            new.append(part + shifted[:, :HEAD] + shifted[:, HEAD:])
        return tuple(new)

    zero = jnp.zeros((BLOCK, HEAD), jnp.float32)
    carry = over_blocks(q_block, step, (zero, zero, zero, zero))
    for h in range(2):
        total, part = carry[2 * h], carry[2 * h + 1]
        row_total = jnp.sum(part, axis=1, keepdims=True)
        out_ref[:, h * HEAD : (h + 1) * HEAD] = low(total / row_total)
        across = jnp.sum(jnp.swapaxes(part, 0, 1), axis=0, keepdims=True)
        inverse_ref[h : h + 1, :] = 1.0 / across


def attend(ends, qkv):
    blocks = PACK // BLOCK
    return pl.pallas_call(
        attend_kernel,
        grid_spec=pltpu.PrefetchScalarGridSpec(
            num_scalar_prefetch=1,
            grid=(blocks,),
            in_specs=[
                pl.BlockSpec((BLOCK, 2 * HEAD), lambda q, ends: (q, 0)),
                pl.BlockSpec((PACK, HEAD), lambda q, ends: (0, 2)),
                pl.BlockSpec((PACK, HEAD), lambda q, ends: (0, 3)),
            ],
            out_specs=[
                pl.BlockSpec((BLOCK, 2 * HEAD), lambda q, ends: (q, 0)),
                pl.BlockSpec((2, BLOCK), lambda q, ends: (0, q)),
            ],
        ),
        out_shape=[
            jax.ShapeDtypeStruct((PACK, 2 * HEAD), jnp.bfloat16),
            jax.ShapeDtypeStruct((2, PACK), jnp.float32),
        ],
        compiler_params=pltpu.CompilerParams(vmem_limit_bytes=VMEM_LIMIT),
        cost_estimate=pl.CostEstimate(flops=3000000000, bytes_accessed=4000000, transcendentals=3000000),
        name="attend",
    )(ends, qkv, qkv, qkv)


def attend_back_kernel(
    ends_ref, q_ref, k_ref, v_ref, grad_ref, out_ref, inverse_ref,
    dq_ref, dk_ref, dv_ref,
):
    q_block = pl.program_id(0)
    ends = (ends_ref[0], ends_ref[1])

    @pl.when(q_block == 0)
    def _():
        dk_ref[...] = jnp.zeros_like(dk_ref)
        dv_ref[...] = jnp.zeros_like(dv_ref)

    heads = [q_ref[:, :HEAD], q_ref[:, HEAD:]]
    grads = [grad_ref[:, :HEAD], grad_ref[:, HEAD:]]
    inverse = [inverse_ref[h : h + 1, :] for h in range(2)]
    delta = []
    for h in range(2):
        product = wide(grads[h]) * wide(out_ref[:, h * HEAD : (h + 1) * HEAD])
        delta.append(jnp.sum(jnp.swapaxes(product, 0, 1), axis=0, keepdims=True))

    def step(k_block, masked, carry):
        rows = pl.ds(pl.multiple_of(k_block * BLOCK, BLOCK), BLOCK)
        keys, values = k_ref[rows, :], v_ref[rows, :]
        allowed = allowed_block(q_block, k_block, ends, True) if masked else None
        new = []
        d_keys, d_values = dk_ref[rows, :], dv_ref[rows, :]
        for h in range(2):
            prob = jnp.exp2(contract_cols(keys, heads[h]) * (SCALE * LOG2E)) * inverse[h]
            if masked:
                prob = jnp.where(allowed, prob, 0.0)
            d_prob = contract_cols(values, grads[h])
            d_score = low(prob * (d_prob - delta[h]) * SCALE)
            d_keys += dot(d_score, heads[h])
            d_values += dot(low(prob), grads[h])
            new.append(carry[h] + contract_rows(d_score, keys))
        dk_ref[rows, :] = d_keys
        dv_ref[rows, :] = d_values
        return tuple(new)

    zero = jnp.zeros((BLOCK, HEAD), jnp.float32)
    carry = over_blocks(q_block, step, (zero, zero))
    dq_ref[:, :HEAD] = carry[0]
    dq_ref[:, HEAD:] = carry[1]


def attend_back(ends, qkv, grad, out, inverse):
    blocks = PACK // BLOCK
    by_block = pl.BlockSpec((BLOCK, 2 * HEAD), lambda q, ends: (q, 0))
    whole = pl.BlockSpec((PACK, HEAD), lambda q, ends: (0, 0))
    return pl.pallas_call(
        attend_back_kernel,
        grid_spec=pltpu.PrefetchScalarGridSpec(
            num_scalar_prefetch=1,
            grid=(blocks,),
            in_specs=[
                by_block,
                pl.BlockSpec((PACK, HEAD), lambda q, ends: (0, 2)),
                pl.BlockSpec((PACK, HEAD), lambda q, ends: (0, 3)),
                by_block,
                by_block,
                pl.BlockSpec((2, BLOCK), lambda q, ends: (0, q)),
            ],
            out_specs=[by_block, whole, whole],
        ),
        out_shape=[
            jax.ShapeDtypeStruct((PACK, 2 * HEAD), jnp.float32),
            jax.ShapeDtypeStruct((PACK, HEAD), jnp.float32),
            jax.ShapeDtypeStruct((PACK, HEAD), jnp.float32),
        ],
        compiler_params=pltpu.CompilerParams(vmem_limit_bytes=VMEM_LIMIT),
        cost_estimate=pl.CostEstimate(flops=8000000000, bytes_accessed=8000000, transcendentals=3000000),
        name="attend_back",
    )(ends, qkv, qkv, qkv, grad, out, inverse)


def qkv_back_kernel(
    spots, pre_ref, dq_ref, dk_ref, dv_ref, cos_ref, sin_ref, normed_ref, w_ref, gq_ref, gk_ref,
    d_pre_ref, d_attn_ref, d_head_ref, own_ref, other_ref,
):
    @pl.when(pl.program_id(0) == 0)
    def _():
        d_attn_ref[...] = jnp.zeros_like(d_attn_ref)
        d_head_ref[...] = jnp.zeros_like(d_head_ref)

    cosine, sine = cos_ref[...], sin_ref[...]
    for h in range(3):
        u = pre_ref[:, h * HEAD : (h + 1) * HEAD]
        gain = gk_ref[...] if h == 2 else gq_ref[...]
        grad = dk_ref[...] if h == 2 else dq_ref[:, h * HEAD : (h + 1) * HEAD]
        grad = rope_back(grad, cosine, sine)
        row = 1 if h == 2 else 0
        d_head_ref[row : row + 1, :] += jnp.sum(
            grad * u * norm_scale(u), axis=0, keepdims=True
        )
        d_pre_ref[:, h * HEAD : (h + 1) * HEAD] = low(norm_back(u, gain, grad))
    d_pre_ref[:, 3 * HEAD :] = low(dv_ref[...])
    d_normed = dot(d_pre_ref[...], w_ref[...])
    d_attn_ref[...] += jnp.sum(wide(normed_ref[...]) * d_normed, axis=0, keepdims=True)

    def put(ref):
        ref[...] = low(d_normed)

    on_half(own_ref, other_ref, put)


def project_back(spots, pre, d_query, d_key, d_value, cosine, sine, normed, weights, gain_query, gain_key):
    half = ((PACK // 2, WIDTH), jnp.bfloat16)
    return ring_call(
        qkv_back_kernel,
        "project_back",
        [pack_spec(3 * HEAD), pack_spec(2 * HEAD), pack_spec(HEAD), pack_spec(HEAD)]
        + [pack_spec(HEAD), pack_spec(HEAD), pack_spec(WIDTH)]
        + [whole_spec((512, WIDTH)), whole_spec((1, HEAD)), whole_spec((1, HEAD))],
        [pack_spec(512), whole_spec((1, WIDTH)), whole_spec((2, HEAD))] + ring_specs(WIDTH),
        [((PACK, 512), jnp.bfloat16), ((1, WIDTH), jnp.float32), ((2, HEAD), jnp.float32), half, half],
        1610612736, spots, pre, d_query, d_key, d_value, cosine, sine, normed, weights, gain_query, gain_key,
    )


def exchange(values, axes):
    return lax.all_to_all(values, axes, split_axis=0, concat_axis=0, tiled=True)


def gather_plane(index, block):
    core = index & 1
    shape = block.shape
    block = block[None]
    for first, second in PLANE_STEPS:
        got = swap(block, first, second)
        later = jnp.where(core == 1, index >> BIT[second], index >> BIT[first]) & 1
        block = jnp.where(
            later == 1,
            jnp.concatenate([got, block], axis=0),
            jnp.concatenate([block, got], axis=0),
        )
    block = block.reshape((4, 4) + shape)
    return jnp.where(core == 1, jnp.swapaxes(block, 0, 1), block).reshape((16,) + shape)


def gather_ring(rows, gates=((), ())):
    for (first, second), gate in zip(RING_STEPS, gates):
        rows = after(rows, *gate)
        rows = jnp.concatenate([rows, swap(rows, first, second)], axis=0)
    return rows


def scatter_ring(own, other):
    total = wide(own) + wide(swap(other, CORE))
    for first, second in RING_STEPS[::-1]:
        half = total.shape[0] // 2
        total = total[:half] + wide(swap(low(total[half:]), first, second))
    return total


def tiles_tall(block):
    return block.reshape(-1, 8, 8, HEAD).transpose(2, 1, 0, 3).reshape(64, -1)


def tiles_flat(block):
    lead = block.shape[:-2]
    n = len(lead)
    block = block.reshape(lead + (8, 8, -1, HEAD))
    block = block.transpose(tuple(range(n)) + (n + 2, n + 1, n, n + 3))
    return block.reshape(lead + (-1, WIDTH))


def rows_by_device(blocks):
    n = blocks.shape[-1]
    return blocks.reshape(16, 4, 2, 8, n).transpose(1, 0, 2, 3, 4).reshape(WIDTH, n)


def rows_by_plane(rows):
    n = rows.shape[-1]
    return rows.reshape(4, 16, 2, 8, n).transpose(1, 0, 2, 3, 4).reshape(16, 64, n)


def on_device(
    hidden, lengths, w_query, w_key, w_value, w_out, w_gate, w_up, w_down, gains, cotangent
):
    index = lax.axis_index(AXES).astype(jnp.int32)
    core, x = index & 1, index >> 5
    straight = (index >> 4 & 1) == core
    order = lambda c: jnp.where(c == 1, jnp.asarray(RING_SPOTS[1]), jnp.asarray(RING_SPOTS[0]))
    spots = jnp.concatenate(
        [(x ^ order(core)) * 2 + core, (x ^ order(1 - core)) * 2 + 1 - core]
    ).astype(jnp.int32)

    heads = jnp.concatenate(
        [
            w_query.reshape(8, KV_HEADS, 256).transpose(1, 0, 2),
            w_key.reshape(8, KV_HEADS, HEAD).transpose(1, 0, 2),
            w_value.reshape(8, KV_HEADS, HEAD).transpose(1, 0, 2),
            jnp.broadcast_to(jnp.pad(gains[None, None, :], ((0, 0), (0, 7), (0, 110))), (8, 8, 128)),
        ],
        axis=2,
    )
    heads = exchange(heads, RING).reshape(64, 640)
    crossed = cross(jnp.concatenate([hidden[0], w_out], axis=0))
    inputs = crossed[:TOK]
    heads = gather_plane(index, jnp.concatenate([heads, tiles_tall(crossed[TOK:])], axis=1))
    w_heads = rows_by_device(heads[..., :512])
    gain_all = heads[..., 512:530].reshape(16, 4, 2, 8, 18)[:, :, :, 0].transpose(1, 0, 2, 3)
    gain_all = wide(gain_all.reshape(1, -1))
    gain_attn, gain_mlp = gain_all[:, :WIDTH], gain_all[:, WIDTH : 2 * WIDTH]
    gain_query = gain_all[:, 2 * WIDTH : 2 * WIDTH + HEAD]
    gain_key = gain_all[:, 2 * WIDTH + HEAD :]
    w_rows = tiles_flat(heads[..., 640:]).reshape(2, 8, 16, WIDTH).transpose(1, 0, 2, 3)
    w_rows = w_rows.reshape(256, WIDTH)

    inputs_own = gather_ring(inputs)
    inputs_other = swap(inputs_own, CORE)
    lengths = jnp.where(straight, lengths, swap(lengths, CORE))
    ends = jnp.stack([lengths[0, 0], lengths[0, 0] + lengths[0, 1]]).astype(jnp.int32)
    token = jnp.arange(PACK, dtype=jnp.int32)
    position = wide(token - row_start(token, (ends[0], ends[1])))
    inverse = jnp.power(ROPE_BASE, -2.0 * jnp.arange(HEAD // 2, dtype=jnp.float32) / HEAD)
    angle = position[:, None] * inverse[None, :]
    cosine, sine = jnp.cos(angle), jnp.sin(angle)
    cosine = jnp.concatenate([cosine, cosine], axis=1)
    sine = jnp.concatenate([-sine, sine], axis=1)

    normed, pre, qkv = project(
        spots, inputs_own, inputs_other, w_heads, gain_attn, gain_query, gain_key, cosine, sine
    )
    attended, inverse_total = attend(ends, qkv)

    w_gate, w_up = (after(weight, inputs) for weight in (w_gate, w_up))
    units = jnp.concatenate(
        [
            weight.reshape(8, 4, 16, 2, 24).transpose(1, 3, 0, 2, 4).reshape(8, 8, 384)
            for weight in (w_gate, w_up)
        ],
        axis=2,
    )
    units = jnp.concatenate([exchange(units, RING).reshape(64, 768), tiles_tall(w_down)], axis=1)
    units = lax.all_gather(units, PLANE, axis=0, tiled=True).reshape(16, 64, 1152)
    full_units = rows_by_device(units[..., :768])
    full_down = tiles_flat(units[..., 768:]).reshape(384, WIDTH)

    out_own, out_other = to_ring(spots, attended, w_rows)
    middle = wide(inputs) + scatter_ring(out_own, out_other)
    middle_scale = norm_scale(middle)
    mixed = low(middle * middle_scale * gain_mlp)
    mixed_own = gather_ring(mixed)
    mixed_other = swap(mixed_own, CORE)

    d_result = cross(after(cotangent[0], normed))
    d_result_own = gather_ring(d_result, ((attended,), (middle,)))
    d_result_other = swap(d_result_own, CORE)

    def feed_forward(rows, d_rows):
        pre = dot(rows, full_units)
        gate_pre, up_pre = pre[:, :384], pre[:, 384:]
        sigmoid = 1.0 / (1.0 + jnp.exp(-gate_pre))
        silu = gate_pre * sigmoid
        act = low(silu * up_pre)
        d_act = contract_cols(d_rows, full_down)
        d_gate = low(d_act * up_pre * (sigmoid + silu * (1.0 - sigmoid)))
        d_up = low(d_act * silu)
        d_pre = jnp.concatenate([d_gate, d_up], axis=1)
        return act, d_pre, low(contract_cols(d_pre, full_units))

    act_own, d_pre_own, d_mixed_own = feed_forward(mixed_own, d_result_own)
    act_other, d_pre_other, d_mixed_other = feed_forward(mixed_other, d_result_other)
    d_mixed = scatter_ring(d_mixed_own, d_mixed_other)
    d_middle = wide(d_result) + norm_back(middle, gain_mlp, d_mixed)
    d_gain_mlp = jnp.sum(middle * middle_scale * d_mixed, axis=0)
    d_branch_own = gather_ring(low(d_middle))
    d_branch_other = swap(d_branch_own, CORE)

    act_own, act_other, d_pre_own, d_pre_other = lax.optimization_barrier(
        (act_own, act_other, d_pre_own, d_pre_other, d_mixed_other)
    )[:4]
    grad_units = contract_rows(mixed_own, d_pre_own) + contract_rows(mixed_other, d_pre_other)
    grad_down = contract_rows(act_own, d_result_own) + contract_rows(act_other, d_result_other)
    grad_down = low(grad_down).reshape(16, 3, 8, 8, HEAD).transpose(0, 3, 2, 1, 4)
    grads = jnp.concatenate(
        [rows_by_plane(low(grad_units)), grad_down.reshape(16, 64, 384)], axis=2
    ).reshape(WIDTH, 1152)
    sums = lax.psum_scatter(grads, ("zh", "zl"), scatter_dimension=0, tiled=True)
    sums = lax.psum_scatter(sums, "y", scatter_dimension=0, tiled=True)
    result = to_pack(spots, act_own, act_other, full_down)
    result = lax.psum_scatter(result, RING, scatter_dimension=0, tiled=True)

    d_attended, grad_out = out_back(spots, d_branch_own, d_branch_other, attended, w_rows)
    d_attended = after(d_attended, grads, result)
    d_query, d_key, d_value = attend_back(ends, qkv, d_attended, attended, inverse_total)
    grad_out = low(grad_out).reshape(8, 2, 16, WIDTH).transpose(1, 0, 2, 3).reshape(16, 16, WIDTH)
    sum_out = jnp.sum(wide(exchange(grad_out, PLANE)), axis=0)
    d_pre, d_gain_attn, d_gain_heads, d_normed_own, d_normed_other = project_back(
        spots, pre, d_query, d_key, d_value, cosine, sine, normed, w_heads.T, gain_query, gain_key
    )
    d_normed = scatter_ring(d_normed_own, d_normed_other)
    input_grad = d_middle + norm_back(wide(inputs), gain_attn, d_normed)
    input_grad = jnp.where(straight, input_grad, wide(cross(low(input_grad))))
    activations = cross(low(middle + wide(result)))
    sum_out = jnp.where(straight, sum_out, wide(cross(low(sum_out))))

    sum_down = tiles_flat(sums[:, 768:])
    units_grad = exchange(sums[:, :768].reshape(8, 8, 768), RING)
    by_unit = lambda grad: (
        wide(grad).reshape(4, 2, 8, 16, 24).transpose(2, 0, 3, 1, 4).reshape(8, FF)
    )

    d_gains = jnp.concatenate(
        [(d_gain_attn / gain_attn)[0], d_gain_mlp, d_gain_heads.reshape(-1)]
    )
    payload = jnp.concatenate(
        [
            low(contract_rows(normed, d_pre)).reshape(DEVICES, 8, 512),
            low(jnp.pad(d_gains.reshape(DEVICES, 1, 18), ((0, 0), (0, 7), (0, 110)))),
        ],
        axis=2,
    )
    heads_grad = wide(exchange(payload, AXES)).reshape(4, 16, 2, 8, 640)
    heads_grad = jnp.sum(heads_grad, axis=1).reshape(8, 8, 640)
    sum_query = heads_grad[..., :256].transpose(1, 0, 2).reshape(8, -1)
    sum_key = heads_grad[..., 256:384].transpose(1, 0, 2).reshape(8, -1)
    sum_value = heads_grad[..., 384:512].transpose(1, 0, 2).reshape(8, -1)
    sum_gains = jnp.sum(heads_grad[:, 0, 512:530], axis=0)
    return (
        activations[None],
        input_grad[None],
        sum_query,
        sum_key,
        sum_value,
        sum_out,
        by_unit(units_grad[..., :384]),
        by_unit(units_grad[..., 384:]),
        wide(sum_down),
        sum_gains,
    )


def solution(mesh):
    chips = Mesh(mesh.devices.reshape(4, 2, 2, 4, 2), AXES)
    rows = P(AXES, None)
    tokens = P(("zl", "y", "core"), ("x", "zh"), None)
    lengths = P(("zl", "y", "core"), None)
    return jax.shard_map(
        on_device,
        mesh=chips,
        in_specs=(tokens, lengths, *([rows] * 7), P(AXES), tokens),
        out_specs=(tokens, tokens, *([rows] * 7), P(AXES)),
        check_vma=False,
    )
```

```python
import jax
import jax.numpy as jnp
from jax import lax
from jax.experimental import pallas as pl
from jax.experimental.pallas import tpu as pltpu
from jax.sharding import Mesh
from jax.sharding import PartitionSpec as P

HEADS = 16
KV_HEADS = 8
HEAD = 128
EPSILON = 1e-06
ROPE_BASE = 1000000.0
DEVICES = 128
WIDTH = 1024
FF = 3072
TOK = 192
PACK = 1536
BLOCK = 256
LOG2E = 1.4426950408889634
SCALE = HEAD ** (-0.5)
VMEM_LIMIT = 48 * 1024 * 1024

AXES = ("x", "zh", "zl", "y", "core")
RING = ("x", "core")
PLANE = ("zh", "zl", "y")
XA, XB, ZA, ZB, YA, YB, CORE = 32, 96, 8, 24, 2, 6, 1
RING_STEPS = ((XA, XB), (XB, XA))
RING_SPOTS = ((0, 1, 3, 2), (0, 2, 3, 1))
PLANE_STEPS = ((YA, ZA), (YB, ZB), (ZA, YA), (ZB, YB))
BIT = {YA: 1, YB: 2, ZA: 3, ZB: 4}


def swap(values, mask, other_mask=None):
    masks = (mask, mask if other_mask is None else other_mask)
    return lax.ppermute(values, AXES, [(k, k ^ masks[k & 1]) for k in range(DEVICES)])


def cross(values):
    pairs = [(k, k ^ 17 if (k >> 4 ^ k) & 1 else k) for k in range(DEVICES)]
    return lax.ppermute(values, AXES, pairs)


def after(value, *others):
    return lax.optimization_barrier((value, *others))[0] if others else value


def low(values):
    return values.astype(jnp.bfloat16)


def wide(values):
    return values.astype(jnp.float32)


def dot(left, right):
    return jnp.dot(left, right, preferred_element_type=jnp.float32)


def contract_rows(left, right):
    return lax.dot_general(
        left, right, (((0,), (0,)), ((), ())), preferred_element_type=jnp.float32
    )


def contract_cols(left, right):
    return lax.dot_general(
        left, right, (((1,), (1,)), ((), ())), preferred_element_type=jnp.float32
    )


def norm_scale(values):
    return lax.rsqrt(jnp.mean(values * values, axis=-1, keepdims=True) + EPSILON)


def norm_back(values, gain, grad):
    scale = norm_scale(values)
    normal = values * scale
    inner = grad * gain
    return scale * (inner - normal * jnp.mean(inner * normal, axis=-1, keepdims=True))


def rope(values, cosine, sine):
    return values * cosine + pltpu.roll(values, 64, 1) * sine


def rope_back(grad, cosine, sine):
    return grad * cosine + pltpu.roll(grad * sine, 64, 1)


def ring_specs(columns):
    return [
        pl.BlockSpec((TOK, columns), lambda x, spots: (spots[x], 0)),
        pl.BlockSpec((TOK, columns), lambda x, spots: (spots[4 + x], 0)),
    ]


def pack_spec(columns):
    return pl.BlockSpec((2 * TOK, columns), lambda x, spots: (x, 0))


def whole_spec(shape):
    return pl.BlockSpec(shape, lambda x, spots: (0, 0))


def own_rows(spots):
    return pl.ds(pl.multiple_of(spots[8] * TOK, TOK), TOK)


def other_rows(spots):
    return pl.ds(pl.multiple_of((1 - spots[8]) * TOK, TOK), TOK)


def ring_call(kernel, name, in_specs, out_specs, out_shape, flops, spots, *operands, scratch=()):
    return pl.pallas_call(
        kernel,
        grid_spec=pltpu.PrefetchScalarGridSpec(
            num_scalar_prefetch=1,
            grid=(4,),
            in_specs=in_specs,
            out_specs=out_specs,
            scratch_shapes=scratch,
        ),
        out_shape=[jax.ShapeDtypeStruct(shape, dtype) for shape, dtype in out_shape],
        compiler_params=pltpu.CompilerParams(vmem_limit_bytes=VMEM_LIMIT),
        cost_estimate=pl.CostEstimate(flops=flops, bytes_accessed=12000000, transcendentals=0),
        name=name,
    )(spots, *operands)


def qkv_kernel(
    spots, own_ref, other_ref, w_ref, ga_ref, gq_ref, gk_ref, cos_ref, sin_ref,
    normed_ref, pre_ref, qkv_ref,
):
    for ref, rows in ((own_ref, own_rows(spots)), (other_ref, other_rows(spots))):
        x = wide(ref[...])
        normed_ref[rows, :] = low(x * norm_scale(x) * ga_ref[...])
    pre = dot(normed_ref[...], w_ref[...])
    pre_ref[...] = pre[:, : 3 * HEAD]
    cosine, sine = cos_ref[...], sin_ref[...]
    for h in range(3):
        u = pre[:, h * HEAD : (h + 1) * HEAD]
        gain = gk_ref[...] if h == 2 else gq_ref[...]
        normal = u * norm_scale(u) * gain
        qkv_ref[:, h * HEAD : (h + 1) * HEAD] = low(rope(normal, cosine, sine))
    qkv_ref[:, 3 * HEAD :] = low(pre[:, 3 * HEAD :])


def project(spots, own, other, weights, gain_attn, gain_query, gain_key, cosine, sine):
    return ring_call(
        qkv_kernel,
        "project",
        ring_specs(WIDTH)
        + [whole_spec((WIDTH, 512)), whole_spec((1, WIDTH)), whole_spec((1, HEAD)), whole_spec((1, HEAD))]
        + [pack_spec(HEAD), pack_spec(HEAD)],
        [pack_spec(WIDTH), pack_spec(3 * HEAD), pack_spec(512)],
        [
            ((PACK, WIDTH), jnp.bfloat16),
            ((PACK, 3 * HEAD), jnp.float32),
            ((PACK, 512), jnp.bfloat16),
        ],
        1610612736, spots, own, other, weights, gain_attn, gain_query, gain_key, cosine, sine,
    )


def to_ring_kernel(spots, rows_ref, w_ref, own_ref, other_ref):
    own_ref[...] = low(dot(rows_ref[own_rows(spots), :], w_ref[...]))
    other_ref[...] = low(dot(rows_ref[other_rows(spots), :], w_ref[...]))


def to_ring(spots, rows, weights):
    half = ((PACK // 2, WIDTH), jnp.bfloat16)
    return ring_call(
        to_ring_kernel, "to_ring", [pack_spec(256), whole_spec((256, WIDTH))], ring_specs(WIDTH),
        [half, half], 800000000, spots, rows, weights,
    )


def to_pack_kernel(spots, own_ref, other_ref, w_ref, rows_ref):
    rows_ref[own_rows(spots), :] = low(dot(own_ref[...], w_ref[...]))
    rows_ref[other_rows(spots), :] = low(dot(other_ref[...], w_ref[...]))


def to_pack(spots, own, other, weights):
    return ring_call(
        to_pack_kernel, "to_pack", ring_specs(own.shape[1]) + [whole_spec(weights.shape)],
        [pack_spec(WIDTH)], [((PACK, WIDTH), jnp.bfloat16)], 1200000000, spots, own, other, weights,
    )[0]


def out_back_kernel(spots, own_ref, other_ref, attended_ref, w_ref, d_attended_ref, d_w_ref, rows_ref):
    @pl.when(pl.program_id(0) == 0)
    def _():
        d_w_ref[...] = jnp.zeros_like(d_w_ref)

    rows_ref[own_rows(spots), :] = own_ref[...]
    rows_ref[other_rows(spots), :] = other_ref[...]
    d_attended_ref[...] = low(contract_cols(rows_ref[...], w_ref[...]))
    d_w_ref[...] += contract_rows(attended_ref[...], rows_ref[...])


def out_back(spots, own, other, attended, weights):
    return ring_call(
        out_back_kernel, "out_back",
        ring_specs(WIDTH) + [pack_spec(256), whole_spec((256, WIDTH))],
        [pack_spec(256), whole_spec((256, WIDTH))],
        [((PACK, 256), jnp.bfloat16), ((256, WIDTH), jnp.float32)],
        1600000000, spots, own, other, attended, weights,
        scratch=[pltpu.VMEM((2 * TOK, WIDTH), jnp.bfloat16)],
    )


def row_start(rows, ends):
    first, second = ends
    return jnp.where(rows >= second, second, jnp.where(rows >= first, first, 0))


def block_mask(q_block, k_block, ends, transposed):
    last = PACK // BLOCK - 1
    q_axis, k_axis = (1, 0) if transposed else (0, 1)
    q_rows = q_block * BLOCK + lax.broadcasted_iota(jnp.int32, (BLOCK, BLOCK), q_axis)
    k_rows = k_block * BLOCK + lax.broadcasted_iota(jnp.int32, (BLOCK, BLOCK), k_axis)
    mask = None
    if k_block == q_block:
        mask = k_rows <= q_rows
    if k_block == 0 or q_block == last:
        begun = k_rows >= row_start(q_rows, ends)
        mask = begun if mask is None else mask & begun
    return mask


def for_each_block(step):
    for q_block in range(PACK // BLOCK):

        @pl.when(pl.program_id(0) == q_block)
        def _(q_block=q_block):
            step(q_block)


def attend_kernel(ends_ref, q_ref, k_ref, v_ref, out_ref, inverse_ref):
    ends = (ends_ref[0], ends_ref[1])

    def step(q_block):
        seen = (q_block + 1) * BLOCK
        for h in range(2):
            columns = slice(h * HEAD, (h + 1) * HEAD)
            scores = contract_cols(q_ref[:, columns], k_ref[:seen, :])
            part, shifted = 0.0, []
            for k_block in range(q_block + 1):
                block = scores[:, k_block * BLOCK : (k_block + 1) * BLOCK]
                block = jnp.exp2(block * (SCALE * LOG2E))
                mask = block_mask(q_block, k_block, ends, False)
                if mask is not None:
                    block = jnp.where(mask, block, 0.0)
                part += block[:, :HEAD] + block[:, HEAD:]
                shifted.append(low(block))
            total = dot(jnp.concatenate(shifted, axis=1), v_ref[:seen, :])
            row_total = jnp.sum(part, axis=1, keepdims=True)
            out_ref[:, columns] = low(total * (1.0 / row_total))
            across = jnp.sum(jnp.swapaxes(part, 0, 1), axis=0, keepdims=True)
            inverse_ref[h : h + 1, :] = 1.0 / across

    for_each_block(step)


def attend(ends, qkv):
    return pl.pallas_call(
        attend_kernel,
        grid_spec=pltpu.PrefetchScalarGridSpec(
            num_scalar_prefetch=1,
            grid=(PACK // BLOCK,),
            in_specs=[
                pl.BlockSpec((BLOCK, 2 * HEAD), lambda q, ends: (q, 0)),
                pl.BlockSpec((PACK, HEAD), lambda q, ends: (0, 2)),
                pl.BlockSpec((PACK, HEAD), lambda q, ends: (0, 3)),
            ],
            out_specs=[
                pl.BlockSpec((BLOCK, 2 * HEAD), lambda q, ends: (q, 0)),
                pl.BlockSpec((2, BLOCK), lambda q, ends: (0, q)),
            ],
        ),
        out_shape=[
            jax.ShapeDtypeStruct((PACK, 2 * HEAD), jnp.bfloat16),
            jax.ShapeDtypeStruct((2, PACK), jnp.float32),
        ],
        compiler_params=pltpu.CompilerParams(vmem_limit_bytes=VMEM_LIMIT),
        cost_estimate=pl.CostEstimate(flops=3000000000, bytes_accessed=4000000, transcendentals=3000000),
        name="attend",
    )(ends, qkv, qkv, qkv)


def attend_back_kernel(
    ends_ref, q_ref, k_ref, v_ref, grad_ref, out_ref, inverse_ref, dq_ref, dk_ref, dv_ref
):
    ends = (ends_ref[0], ends_ref[1])

    @pl.when(pl.program_id(0) == 0)
    def _():
        dk_ref[...] = jnp.zeros_like(dk_ref)
        dv_ref[...] = jnp.zeros_like(dv_ref)

    def both_heads(ref):
        return jnp.concatenate([ref[:, :HEAD], ref[:, HEAD:]], axis=0)

    def step(q_block):
        seen = (q_block + 1) * BLOCK
        queries, grads = both_heads(q_ref), both_heads(grad_ref)
        product = wide(grads) * wide(both_heads(out_ref))
        delta = jnp.sum(jnp.swapaxes(product, 0, 1), axis=0, keepdims=True)
        inverse = jnp.concatenate([inverse_ref[0:1, :], inverse_ref[1:2, :]], axis=1)
        scores = contract_cols(k_ref[:seen, :], queries)
        d_probs = contract_cols(v_ref[:seen, :], grads)
        probs, d_scores = [], []
        for k_block in range(q_block + 1):
            rows = slice(k_block * BLOCK, (k_block + 1) * BLOCK)
            prob = jnp.exp2(scores[rows] * (SCALE * LOG2E)) * inverse
            mask = block_mask(q_block, k_block, ends, True)
            if mask is not None:
                prob = jnp.where(jnp.concatenate([mask, mask], axis=1), prob, 0.0)
            d_scores.append(low(prob * ((d_probs[rows] - delta) * SCALE)))
            probs.append(low(prob))
        probs = jnp.concatenate(probs, axis=0)
        d_scores = jnp.concatenate(d_scores, axis=0)
        dk_ref[:seen, :] += dot(d_scores, queries)
        dv_ref[:seen, :] += dot(probs, grads)
        d_queries = contract_rows(d_scores, k_ref[:seen, :])
        dq_ref[:, :HEAD] = d_queries[:BLOCK]
        dq_ref[:, HEAD:] = d_queries[BLOCK:]

    for_each_block(step)


def attend_back(ends, qkv, grad, out, inverse):
    by_block = pl.BlockSpec((BLOCK, 2 * HEAD), lambda q, ends: (q, 0))
    whole = pl.BlockSpec((PACK, HEAD), lambda q, ends: (0, 0))
    return pl.pallas_call(
        attend_back_kernel,
        grid_spec=pltpu.PrefetchScalarGridSpec(
            num_scalar_prefetch=1,
            grid=(PACK // BLOCK,),
            in_specs=[
                by_block,
                pl.BlockSpec((PACK, HEAD), lambda q, ends: (0, 2)),
                pl.BlockSpec((PACK, HEAD), lambda q, ends: (0, 3)),
                by_block,
                by_block,
                pl.BlockSpec((2, BLOCK), lambda q, ends: (0, q)),
            ],
            out_specs=[by_block, whole, whole],
        ),
        out_shape=[
            jax.ShapeDtypeStruct((PACK, 2 * HEAD), jnp.float32),
            jax.ShapeDtypeStruct((PACK, HEAD), jnp.float32),
            jax.ShapeDtypeStruct((PACK, HEAD), jnp.float32),
        ],
        compiler_params=pltpu.CompilerParams(vmem_limit_bytes=VMEM_LIMIT),
        cost_estimate=pl.CostEstimate(flops=8000000000, bytes_accessed=8000000, transcendentals=3000000),
        name="attend_back",
    )(ends, qkv, qkv, qkv, grad, out, inverse)


def qkv_back_kernel(
    spots, pre_ref, dq_ref, dk_ref, dv_ref, cos_ref, sin_ref, normed_ref, w_ref, gq_ref, gk_ref,
    d_pre_ref, d_attn_ref, d_head_ref, own_ref, other_ref, rows_ref,
):
    @pl.when(pl.program_id(0) == 0)
    def _():
        d_attn_ref[...] = jnp.zeros_like(d_attn_ref)
        d_head_ref[...] = jnp.zeros_like(d_head_ref)

    cosine, sine = cos_ref[...], sin_ref[...]
    for h in range(3):
        u = pre_ref[:, h * HEAD : (h + 1) * HEAD]
        gain = gk_ref[...] if h == 2 else gq_ref[...]
        grad = dk_ref[...] if h == 2 else dq_ref[:, h * HEAD : (h + 1) * HEAD]
        grad = rope_back(grad, cosine, sine)
        row = 1 if h == 2 else 0
        d_head_ref[row : row + 1, :] += jnp.sum(
            grad * u * norm_scale(u), axis=0, keepdims=True
        )
        d_pre_ref[:, h * HEAD : (h + 1) * HEAD] = low(norm_back(u, gain, grad))
    d_pre_ref[:, 3 * HEAD :] = low(dv_ref[...])
    d_normed = dot(d_pre_ref[...], w_ref[...])
    d_attn_ref[...] += jnp.sum(wide(normed_ref[...]) * d_normed, axis=0, keepdims=True)
    rows_ref[...] = low(d_normed)
    own_ref[...] = rows_ref[own_rows(spots), :]
    other_ref[...] = rows_ref[other_rows(spots), :]


def project_back(spots, pre, d_query, d_key, d_value, cosine, sine, normed, weights, gain_query, gain_key):
    half = ((PACK // 2, WIDTH), jnp.bfloat16)
    return ring_call(
        qkv_back_kernel,
        "project_back",
        [pack_spec(3 * HEAD), pack_spec(2 * HEAD), pack_spec(HEAD), pack_spec(HEAD)]
        + [pack_spec(HEAD), pack_spec(HEAD), pack_spec(WIDTH)]
        + [whole_spec((512, WIDTH)), whole_spec((1, HEAD)), whole_spec((1, HEAD))],
        [pack_spec(512), whole_spec((1, WIDTH)), whole_spec((2, HEAD))] + ring_specs(WIDTH),
        [((PACK, 512), jnp.bfloat16), ((1, WIDTH), jnp.float32), ((2, HEAD), jnp.float32), half, half],
        1610612736, spots, pre, d_query, d_key, d_value, cosine, sine, normed, weights, gain_query, gain_key,
        scratch=[pltpu.VMEM((2 * TOK, WIDTH), jnp.bfloat16)],
    )


def exchange(values, axes):
    return lax.all_to_all(values, axes, split_axis=0, concat_axis=0, tiled=True)


def plane_order(core, blocks):
    return jnp.where(core == 1, jnp.swapaxes(blocks, 0, 1), blocks)


def plane_bit(index, masks):
    return jnp.where(index & 1 == 1, index >> BIT[masks[1]], index >> BIT[masks[0]]) & 1


def gather_plane_step(index, block, step):
    got = swap(block, *PLANE_STEPS[step])
    return jnp.where(
        plane_bit(index, PLANE_STEPS[step]) == 1,
        jnp.concatenate([got, block], axis=0),
        jnp.concatenate([block, got], axis=0),
    )


def gather_plane_end(index, block):
    shape = block.shape[1:]
    return plane_order(index & 1, block.reshape((4, 4) + shape)).reshape((16,) + shape)


def scatter_plane_step(index, blocks, step):
    later = plane_bit(index, PLANE_STEPS[step])
    half = blocks.shape[0] // 2
    keep = lax.dynamic_slice_in_dim(blocks, later * half, half, axis=0)
    send = lax.dynamic_slice_in_dim(blocks, (1 - later) * half, half, axis=0)
    return wide(keep) + wide(swap(send, *PLANE_STEPS[step]))


def gather_ring(rows):
    for masks in RING_STEPS:
        rows = jnp.concatenate([rows, swap(rows, *masks)], axis=0)
    return rows


def scatter_ring(own, other):
    totals = [wide(own) + wide(swap(other, CORE))]
    for masks in RING_STEPS[::-1]:
        half = totals[-1].shape[0] // 2
        totals.append(totals[-1][:half] + wide(swap(low(totals[-1][half:]), *masks)))
    return totals


def tiles_tall(block):
    return block.reshape(-1, 8, 8, HEAD).transpose(2, 1, 0, 3).reshape(64, -1)


def tiles_flat(block):
    lead = block.shape[:-2]
    n = len(lead)
    block = block.reshape(lead + (8, 8, -1, HEAD))
    block = block.transpose(tuple(range(n)) + (n + 2, n + 1, n, n + 3))
    return block.reshape(lead + (-1, WIDTH))


def rows_by_device(blocks):
    n = blocks.shape[-1]
    return blocks.reshape(16, 4, 2, 8, n).transpose(1, 0, 2, 3, 4).reshape(WIDTH, n)


def rows_by_plane(rows):
    n = rows.shape[-1]
    return rows.reshape(4, 16, 2, 8, n).transpose(1, 0, 2, 3, 4).reshape(16, 64, n)


def on_device(
    hidden, lengths, w_query, w_key, w_value, w_out, w_gate, w_up, w_down, gains, cotangent
):
    index = lax.axis_index(AXES).astype(jnp.int32)
    core, x = index & 1, index >> 5
    straight = (index >> 4 & 1) == core
    spot_of = lambda c: jnp.where(c == 1, jnp.asarray(RING_SPOTS[1]), jnp.asarray(RING_SPOTS[0]))
    chips = x ^ jnp.arange(4, dtype=jnp.int32)
    spots = jnp.concatenate(
        [spot_of(core)[chips], spot_of(1 - core)[chips], core[None]]
    ).astype(jnp.int32)

    heads = jnp.concatenate(
        [
            w_query.reshape(8, KV_HEADS, 256).transpose(1, 0, 2),
            w_key.reshape(8, KV_HEADS, HEAD).transpose(1, 0, 2),
            w_value.reshape(8, KV_HEADS, HEAD).transpose(1, 0, 2),
            jnp.broadcast_to(jnp.pad(gains[None, None, :], ((0, 0), (0, 7), (0, 110))), (8, 8, 128)),
        ],
        axis=2,
    )
    heads_local = heads
    heads = exchange(heads, RING).reshape(64, 640)
    crossed = cross(jnp.concatenate([hidden[0], w_out], axis=0))
    inputs = crossed[:TOK]
    heads = jnp.concatenate([heads, tiles_tall(crossed[TOK:])], axis=1)[None]
    for step in range(4):
        heads = gather_plane_step(index, heads, step)
    heads = gather_plane_end(index, heads)
    w_heads = rows_by_device(heads[..., :512])
    gain_all = heads[..., 512:530].reshape(16, 4, 2, 8, 18)[:, :, :, 0].transpose(1, 0, 2, 3)
    gain_all = wide(gain_all.reshape(1, -1))
    gain_attn, gain_mlp = gain_all[:, :WIDTH], gain_all[:, WIDTH : 2 * WIDTH]
    gain_query = gain_all[:, 2 * WIDTH : 2 * WIDTH + HEAD]
    gain_key = gain_all[:, 2 * WIDTH + HEAD :]
    w_rows = tiles_flat(heads[..., 640:]).reshape(2, 8, 16, WIDTH).transpose(1, 0, 2, 3)
    w_rows = w_rows.reshape(256, WIDTH)

    inputs_own = gather_ring(inputs)
    inputs_other = swap(inputs_own, CORE)
    lengths = jnp.where(straight, lengths, swap(lengths, CORE))
    ends = jnp.stack([lengths[0, 0], lengths[0, 0] + lengths[0, 1]]).astype(jnp.int32)
    token = jnp.arange(PACK, dtype=jnp.int32)
    position = wide(token - row_start(token, (ends[0], ends[1])))
    inverse = jnp.power(ROPE_BASE, -2.0 * jnp.arange(HEAD // 2, dtype=jnp.float32) / HEAD)
    angle = position[:, None] * inverse[None, :]
    cosine, sine = jnp.cos(angle), jnp.sin(angle)
    cosine = jnp.concatenate([cosine, cosine], axis=1)
    sine = jnp.concatenate([-sine, sine], axis=1)

    w_gate, w_up = (after(weight, heads_local) for weight in (w_gate, w_up))
    units = jnp.concatenate(
        [
            weight.reshape(8, 4, 16, 2, 24).transpose(1, 3, 0, 2, 4).reshape(8, 8, 384)
            for weight in (w_gate, w_up)
        ],
        axis=2,
    )
    units = jnp.concatenate([exchange(units, RING).reshape(64, 768), tiles_tall(w_down)], axis=1)
    d_result = cross(after(cotangent[0], heads_local))
    units = gather_plane_step(index, units[None], 0)

    w_heads, units, d_result = lax.optimization_barrier((w_heads, units, d_result))
    normed, pre, qkv = project(
        spots, inputs_own, inputs_other, w_heads, gain_attn, gain_query, gain_key, cosine, sine
    )
    units = gather_plane_step(index, units, 1)
    d_result_own = jnp.concatenate([d_result, swap(d_result, *RING_STEPS[0])], axis=0)
    qkv, units, d_result_own = lax.optimization_barrier((qkv, units, d_result_own))
    attended, inverse_total = attend(ends, qkv)
    units = gather_plane_step(index, units, 2)
    out_own, out_other = to_ring(spots, attended, w_rows)
    d_result_own = jnp.concatenate([d_result_own, swap(d_result_own, *RING_STEPS[1])], axis=0)
    units = after(units, out_own)
    d_result_own = after(d_result_own, out_own)
    units = gather_plane_end(index, gather_plane_step(index, units, 3))
    d_result_other = swap(d_result_own, CORE)
    full_units = rows_by_device(units[..., :768])
    full_down = tiles_flat(units[..., 768:]).reshape(384, WIDTH)

    middle = wide(inputs) + scatter_ring(out_own, out_other)[-1]
    middle_scale = norm_scale(middle)
    mixed = low(middle * middle_scale * gain_mlp)
    mixed_own = gather_ring(mixed)
    mixed_other = swap(mixed_own, CORE)

    def feed_forward(rows, d_rows):
        pre = dot(rows, full_units)
        gate_pre, up_pre = pre[:, :384], pre[:, 384:]
        sigmoid = 1.0 / (1.0 + jnp.exp(-gate_pre))
        silu = gate_pre * sigmoid
        act = low(silu * up_pre)
        d_act = contract_cols(d_rows, full_down)
        d_gate = low(d_act * up_pre * (sigmoid + silu * (1.0 - sigmoid)))
        d_up = low(d_act * silu)
        d_pre = jnp.concatenate([d_gate, d_up], axis=1)
        return act, d_pre, low(contract_cols(d_pre, full_units))

    act_own, d_pre_own, d_mixed_own = feed_forward(mixed_own, d_result_own)
    act_other, d_pre_other, d_mixed_other = feed_forward(mixed_other, d_result_other)
    d_mixed_steps = scatter_ring(d_mixed_own, d_mixed_other)
    d_mixed = d_mixed_steps[-1]
    d_middle = wide(d_result) + norm_back(middle, gain_mlp, d_mixed)
    d_gain_mlp = jnp.sum(middle * middle_scale * d_mixed, axis=0)
    d_branch_own = gather_ring(low(d_middle))
    d_branch_other = swap(d_branch_own, CORE)

    act_own, act_other, d_pre_own, d_pre_other = lax.optimization_barrier(
        (act_own, act_other, d_pre_own, d_pre_other, d_mixed_steps[0])
    )[:4]
    grad_units = contract_rows(mixed_own, d_pre_own) + contract_rows(mixed_other, d_pre_other)
    grad_down = contract_rows(act_own, d_result_own) + contract_rows(act_other, d_result_other)
    grad_down = low(grad_down).reshape(16, 3, 8, 8, HEAD).transpose(0, 3, 2, 1, 4)
    grads = jnp.concatenate(
        [rows_by_plane(low(grad_units)), grad_down.reshape(16, 64, 384)], axis=2
    )
    grads = plane_order(core, grads.reshape(4, 4, 64, 1152)).reshape(16, 64, 1152)
    act_own, act_other = (after(act, d_middle) for act in (act_own, act_other))
    result = to_pack(spots, act_own, act_other, full_down)
    result = lax.psum_scatter(after(result, d_branch_own), RING, scatter_dimension=0, tiled=True)
    sums = scatter_plane_step(index, grads, 3)

    d_attended, grad_out = out_back(spots, d_branch_own, d_branch_other, attended, w_rows)
    grad_out = low(grad_out).reshape(8, 2, 16, WIDTH).transpose(1, 0, 2, 3).reshape(16, 16, WIDTH)
    d_attended, sums, grad_out = lax.optimization_barrier((d_attended, low(sums), grad_out))
    sum_out = exchange(grad_out, PLANE)
    sums = scatter_plane_step(index, sums, 2)
    d_query, d_key, d_value = attend_back(ends, qkv, d_attended, attended, inverse_total)
    d_query, sums, sum_out = lax.optimization_barrier((d_query, low(sums), sum_out))
    sums = scatter_plane_step(index, sums, 1)
    sum_out = jnp.sum(wide(sum_out), axis=0)
    d_pre, d_gain_attn, d_gain_heads, d_normed_own, d_normed_other = project_back(
        spots, pre, d_query, d_key, d_value, cosine, sine, normed, w_heads.T, gain_query, gain_key
    )
    d_normed_steps = scatter_ring(d_normed_own, d_normed_other)
    d_normed = d_normed_steps[-1]
    input_grad = d_middle + norm_back(wide(inputs), gain_attn, d_normed)
    input_grad = jnp.where(straight, input_grad, wide(cross(low(input_grad))))

    sums = after(low(sums), d_normed_steps[0])
    sums = scatter_plane_step(index, sums, 0)[0]
    activations = cross(after(low(middle + wide(result)), d_normed_steps[0]))
    sum_out = jnp.where(straight, sum_out, wide(cross(after(low(sum_out), d_normed_steps[0]))))
    d_pre = after(d_pre, d_normed_steps[0])

    d_gains = jnp.concatenate(
        [(d_gain_attn / gain_attn)[0], d_gain_mlp, d_gain_heads.reshape(-1)]
    )
    payload = jnp.concatenate(
        [
            low(contract_rows(normed, d_pre)).reshape(DEVICES, 8, 512),
            low(jnp.pad(d_gains.reshape(DEVICES, 1, 18), ((0, 0), (0, 7), (0, 110)))),
        ],
        axis=2,
    )
    heads_grad = wide(exchange(payload, AXES)).reshape(4, 16, 2, 8, 640)
    heads_grad = jnp.sum(heads_grad, axis=1).reshape(8, 8, 640)
    sum_down = tiles_flat(sums[:, 768:])
    units_grad = exchange(after(low(sums[:, :768]), heads_grad).reshape(8, 8, 768), RING)
    by_unit = lambda grad: (
        wide(grad).reshape(4, 2, 8, 16, 24).transpose(2, 0, 3, 1, 4).reshape(8, FF)
    )
    sum_query = heads_grad[..., :256].transpose(1, 0, 2).reshape(8, -1)
    sum_key = heads_grad[..., 256:384].transpose(1, 0, 2).reshape(8, -1)
    sum_value = heads_grad[..., 384:512].transpose(1, 0, 2).reshape(8, -1)
    sum_gains = jnp.sum(heads_grad[:, 0, 512:530], axis=0)
    return (
        activations[None],
        input_grad[None],
        sum_query,
        sum_key,
        sum_value,
        sum_out,
        by_unit(units_grad[..., :384]),
        by_unit(units_grad[..., 384:]),
        sum_down,
        sum_gains,
    )


def solution(mesh):
    chips = Mesh(mesh.devices.reshape(4, 2, 2, 4, 2), AXES)
    rows = P(AXES, None)
    tokens = P(("zl", "y", "core"), ("x", "zh"), None)
    lengths = P(("zl", "y", "core"), None)
    return jax.shard_map(
        on_device,
        mesh=chips,
        in_specs=(tokens, lengths, *([rows] * 7), P(AXES), tokens),
        out_specs=(tokens, tokens, *([rows] * 7), P(AXES)),
        check_vma=False,
    )
```

```python
import jax
import jax.numpy as jnp
from jax import lax
from jax.experimental import pallas as pl
from jax.experimental.pallas import tpu as pltpu
from jax.sharding import Mesh
from jax.sharding import PartitionSpec as P

HEADS = 16
KV_HEADS = 8
HEAD = 128
EPSILON = 1e-06
ROPE_BASE = 1000000.0
DEVICES = 128
WIDTH = 1024
FF = 3072
TOK = 192
PACK = 1536
BLOCK = 256
LOG2E = 1.4426950408889634
SCALE = HEAD ** (-0.5)
VMEM_LIMIT = 58 * 1024 * 1024

AXES = ("x", "zh", "zl", "y", "core")
RING = ("x", "core")
PLANE = ("zh", "zl", "y")
XA, XB, ZA, ZB, YA, YB, CORE = 32, 96, 8, 24, 2, 6, 1
RING_STEPS = ((XA, XB), (XB, XA))
RING_SPOTS = ((0, 1, 3, 2), (0, 2, 3, 1))
PLANE_STEPS = ((YA, ZA), (YB, ZB), (ZA, YA), (ZB, YB))
BIT = {YA: 1, YB: 2, ZA: 3, ZB: 4}


def swap(values, mask, other_mask=None):
    masks = (mask, mask if other_mask is None else other_mask)
    return lax.ppermute(values, AXES, [(k, k ^ masks[k & 1]) for k in range(DEVICES)])


def crossed(k):
    return k ^ 17 if (k >> 4 ^ k) & 1 else k


def cross(values):
    return lax.ppermute(values, AXES, [(k, crossed(k)) for k in range(DEVICES)])


def cross_and_swap(values, masks):
    return lax.ppermute(
        values, AXES, [(crossed(k ^ masks[k & 1]), k) for k in range(DEVICES)]
    )


def swap_and_cross(values, masks):
    return lax.ppermute(
        values, AXES, [(k, crossed(k ^ masks[k & 1])) for k in range(DEVICES)]
    )


def after(value, *others):
    return lax.optimization_barrier((value, *others))[0] if others else value


def low(values):
    return values.astype(jnp.bfloat16)


def wide(values):
    return values.astype(jnp.float32)


def dot(left, right):
    return jnp.dot(left, right, preferred_element_type=jnp.float32)


def contract_rows(left, right):
    return lax.dot_general(
        left, right, (((0,), (0,)), ((), ())), preferred_element_type=jnp.float32
    )


def contract_cols(left, right):
    return lax.dot_general(
        left, right, (((1,), (1,)), ((), ())), preferred_element_type=jnp.float32
    )


def norm_scale(values):
    return lax.rsqrt(jnp.mean(values * values, axis=-1, keepdims=True) + EPSILON)


def norm_back(values, gain, grad):
    scale = norm_scale(values)
    normal = values * scale
    inner = grad * gain
    return scale * (inner - normal * jnp.mean(inner * normal, axis=-1, keepdims=True))


def rope(values, cosine, sine):
    return values * cosine + pltpu.roll(values, 64, 1) * sine


def rope_back(grad, cosine, sine):
    return grad * cosine + pltpu.roll(grad * sine, 64, 1)


def ring_specs(columns):
    return [
        pl.BlockSpec((TOK, columns), lambda x, spots: (spots[x], 0)),
        pl.BlockSpec((TOK, columns), lambda x, spots: (spots[4 + x], 0)),
    ]


def pack_spec(columns):
    return pl.BlockSpec((2 * TOK, columns), lambda x, spots: (x, 0))


def whole_spec(shape):
    return pl.BlockSpec(shape, lambda x, spots: (0, 0))


def own_rows(spots):
    return pl.ds(pl.multiple_of(spots[8] * TOK, TOK), TOK)


def other_rows(spots):
    return pl.ds(pl.multiple_of((1 - spots[8]) * TOK, TOK), TOK)


def ring_call(kernel, name, in_specs, out_specs, out_shape, flops, spots, *operands, scratch=()):
    return pl.pallas_call(
        kernel,
        grid_spec=pltpu.PrefetchScalarGridSpec(
            num_scalar_prefetch=1,
            grid=(4,),
            in_specs=in_specs,
            out_specs=out_specs,
            scratch_shapes=scratch,
        ),
        out_shape=[jax.ShapeDtypeStruct(shape, dtype) for shape, dtype in out_shape],
        compiler_params=pltpu.CompilerParams(vmem_limit_bytes=VMEM_LIMIT),
        cost_estimate=pl.CostEstimate(flops=flops, bytes_accessed=12000000, transcendentals=0),
        name=name,
    )(spots, *operands)


def qkv_kernel(
    spots, own_ref, other_ref, heads_ref, ga_ref, gq_ref, gk_ref, cos_ref, sin_ref,
    normed_ref, pre_ref, qkv_ref, w_ref,
):
    @pl.when(pl.program_id(0) == 0)
    def _():
        for z in range(4):
            for y in range(4):
                block = jnp.where(spots[9] == 1, y * 4 + z, z * 4 + y)
                for x in range(4):
                    row = (x * 16 + z * 4 + y) * 16
                    w_ref[row : row + 16, :] = heads_ref[block, x * 16 : x * 16 + 16, :512]

    for ref, rows in ((own_ref, own_rows(spots)), (other_ref, other_rows(spots))):
        x = wide(ref[...])
        normed_ref[rows, :] = low(x * norm_scale(x) * ga_ref[...])
    pre = dot(normed_ref[...], w_ref[...])
    pre_ref[...] = pre[:, : 3 * HEAD]
    cosine, sine = cos_ref[...], sin_ref[...]
    for h in range(3):
        u = pre[:, h * HEAD : (h + 1) * HEAD]
        gain = gk_ref[...] if h == 2 else gq_ref[...]
        normal = u * norm_scale(u) * gain
        qkv_ref[:, h * HEAD : (h + 1) * HEAD] = low(rope(normal, cosine, sine))
    qkv_ref[:, 3 * HEAD :] = low(pre[:, 3 * HEAD :])


def project(spots, own, other, heads, gain_attn, gain_query, gain_key, cosine, sine):
    return ring_call(
        qkv_kernel,
        "project",
        ring_specs(WIDTH)
        + [pl.BlockSpec(heads.shape, lambda x, spots: (0, 0, 0))]
        + [whole_spec((1, WIDTH)), whole_spec((1, HEAD)), whole_spec((1, HEAD))]
        + [pack_spec(HEAD), pack_spec(HEAD)],
        [pack_spec(WIDTH), pack_spec(3 * HEAD), pack_spec(512), whole_spec((WIDTH, 512))],
        [
            ((PACK, WIDTH), jnp.bfloat16),
            ((PACK, 3 * HEAD), jnp.float32),
            ((PACK, 512), jnp.bfloat16),
            ((WIDTH, 512), jnp.bfloat16),
        ],
        1610612736, spots, own, other, heads, gain_attn, gain_query, gain_key, cosine, sine,
    )


def to_ring_kernel(spots, rows_ref, w_ref, own_ref, other_ref):
    own_ref[...] = low(dot(rows_ref[own_rows(spots), :], w_ref[...]))
    other_ref[...] = low(dot(rows_ref[other_rows(spots), :], w_ref[...]))


def to_ring(spots, rows, weights):
    half = ((PACK // 2, WIDTH), jnp.bfloat16)
    return ring_call(
        to_ring_kernel, "to_ring", [pack_spec(256), whole_spec((256, WIDTH))], ring_specs(WIDTH),
        [half, half], 800000000, spots, rows, weights,
    )


def to_pack_kernel(spots, own_ref, other_ref, w_ref, rows_ref):
    rows_ref[own_rows(spots), :] = low(dot(own_ref[...], w_ref[...]))
    rows_ref[other_rows(spots), :] = low(dot(other_ref[...], w_ref[...]))


def to_pack(spots, own, other, weights):
    return ring_call(
        to_pack_kernel, "to_pack", ring_specs(own.shape[1]) + [whole_spec(weights.shape)],
        [pack_spec(WIDTH)], [((PACK, WIDTH), jnp.bfloat16)], 1200000000, spots, own, other, weights,
    )[0]


def out_back_kernel(spots, own_ref, other_ref, attended_ref, w_ref, d_attended_ref, d_w_ref, rows_ref):
    @pl.when(pl.program_id(0) == 0)
    def _():
        d_w_ref[...] = jnp.zeros_like(d_w_ref)

    rows_ref[own_rows(spots), :] = own_ref[...]
    rows_ref[other_rows(spots), :] = other_ref[...]
    d_attended_ref[...] = low(contract_cols(rows_ref[...], w_ref[...]))
    d_w_ref[...] += contract_rows(attended_ref[...], rows_ref[...])


def out_back(spots, own, other, attended, weights):
    return ring_call(
        out_back_kernel, "out_back",
        ring_specs(WIDTH) + [pack_spec(256), whole_spec((256, WIDTH))],
        [pack_spec(256), whole_spec((256, WIDTH))],
        [((PACK, 256), jnp.bfloat16), ((256, WIDTH), jnp.float32)],
        1600000000, spots, own, other, attended, weights,
        scratch=[pltpu.VMEM((2 * TOK, WIDTH), jnp.bfloat16)],
    )


def row_start(rows, ends):
    first, second = ends
    return jnp.where(rows >= second, second, jnp.where(rows >= first, first, 0))


def block_mask(q_block, k_block, ends, transposed):
    last = PACK // BLOCK - 1
    q_axis, k_axis = (1, 0) if transposed else (0, 1)
    q_rows = q_block * BLOCK + lax.broadcasted_iota(jnp.int32, (BLOCK, BLOCK), q_axis)
    k_rows = k_block * BLOCK + lax.broadcasted_iota(jnp.int32, (BLOCK, BLOCK), k_axis)
    mask = None
    if k_block == q_block:
        mask = k_rows <= q_rows
    if k_block == 0 or q_block == last:
        begun = k_rows >= row_start(q_rows, ends)
        mask = begun if mask is None else mask & begun
    return mask


def for_each_block(step):
    for q_block in range(PACK // BLOCK):

        @pl.when(pl.program_id(0) == q_block)
        def _(q_block=q_block):
            step(q_block)


def attend_kernel(ends_ref, q_ref, k_ref, v_ref, out_ref, inverse_ref):
    ends = (ends_ref[0], ends_ref[1])

    def step(q_block):
        seen = (q_block + 1) * BLOCK
        for h in range(2):
            columns = slice(h * HEAD, (h + 1) * HEAD)
            scores = contract_cols(q_ref[:, columns], k_ref[:seen, :])
            part, shifted = 0.0, []
            for k_block in range(q_block + 1):
                block = scores[:, k_block * BLOCK : (k_block + 1) * BLOCK]
                block = jnp.exp2(block * (SCALE * LOG2E))
                mask = block_mask(q_block, k_block, ends, False)
                if mask is not None:
                    block = jnp.where(mask, block, 0.0)
                part += block[:, :HEAD] + block[:, HEAD:]
                shifted.append(low(block))
            total = dot(jnp.concatenate(shifted, axis=1), v_ref[:seen, :])
            row_total = jnp.sum(part, axis=1, keepdims=True)
            out_ref[:, columns] = low(total * (1.0 / row_total))
            across = jnp.sum(jnp.swapaxes(part, 0, 1), axis=0, keepdims=True)
            inverse_ref[h : h + 1, :] = 1.0 / across

    for_each_block(step)


def attend(ends, qkv):
    return pl.pallas_call(
        attend_kernel,
        grid_spec=pltpu.PrefetchScalarGridSpec(
            num_scalar_prefetch=1,
            grid=(PACK // BLOCK,),
            in_specs=[
                pl.BlockSpec((BLOCK, 2 * HEAD), lambda q, ends: (q, 0)),
                pl.BlockSpec((PACK, HEAD), lambda q, ends: (0, 2)),
                pl.BlockSpec((PACK, HEAD), lambda q, ends: (0, 3)),
            ],
            out_specs=[
                pl.BlockSpec((BLOCK, 2 * HEAD), lambda q, ends: (q, 0)),
                pl.BlockSpec((2, BLOCK), lambda q, ends: (0, q)),
            ],
        ),
        out_shape=[
            jax.ShapeDtypeStruct((PACK, 2 * HEAD), jnp.bfloat16),
            jax.ShapeDtypeStruct((2, PACK), jnp.float32),
        ],
        compiler_params=pltpu.CompilerParams(vmem_limit_bytes=VMEM_LIMIT),
        cost_estimate=pl.CostEstimate(flops=3000000000, bytes_accessed=4000000, transcendentals=3000000),
        name="attend",
    )(ends, qkv, qkv, qkv)


def attend_back_kernel(
    ends_ref, q_ref, k_ref, v_ref, grad_ref, out_ref, inverse_ref, dq_ref, dk_ref, dv_ref
):
    ends = (ends_ref[0], ends_ref[1])

    @pl.when(pl.program_id(0) == 0)
    def _():
        dk_ref[...] = jnp.zeros_like(dk_ref)
        dv_ref[...] = jnp.zeros_like(dv_ref)

    def both_heads(ref):
        return jnp.concatenate([ref[:, :HEAD], ref[:, HEAD:]], axis=0)

    def step(q_block):
        seen = (q_block + 1) * BLOCK
        queries, grads = both_heads(q_ref), both_heads(grad_ref)
        product = wide(grads) * wide(both_heads(out_ref))
        delta = jnp.sum(jnp.swapaxes(product, 0, 1), axis=0, keepdims=True)
        inverse = jnp.concatenate([inverse_ref[0:1, :], inverse_ref[1:2, :]], axis=1)
        scores = contract_cols(k_ref[:seen, :], queries)
        d_probs = contract_cols(v_ref[:seen, :], grads)
        probs, d_scores = [], []
        for k_block in range(q_block + 1):
            rows = slice(k_block * BLOCK, (k_block + 1) * BLOCK)
            prob = jnp.exp2(scores[rows] * (SCALE * LOG2E)) * inverse
            mask = block_mask(q_block, k_block, ends, True)
            if mask is not None:
                prob = jnp.where(jnp.concatenate([mask, mask], axis=1), prob, 0.0)
            d_scores.append(low(prob * ((d_probs[rows] - delta) * SCALE)))
            probs.append(low(prob))
        probs = jnp.concatenate(probs, axis=0)
        d_scores = jnp.concatenate(d_scores, axis=0)
        dk_ref[:seen, :] += dot(d_scores, queries)
        dv_ref[:seen, :] += dot(probs, grads)
        d_queries = contract_rows(d_scores, k_ref[:seen, :])
        dq_ref[:, :HEAD] = d_queries[:BLOCK]
        dq_ref[:, HEAD:] = d_queries[BLOCK:]

    for_each_block(step)


def attend_back(ends, qkv, grad, out, inverse):
    by_block = pl.BlockSpec((BLOCK, 2 * HEAD), lambda q, ends: (q, 0))
    whole = pl.BlockSpec((PACK, HEAD), lambda q, ends: (0, 0))
    return pl.pallas_call(
        attend_back_kernel,
        grid_spec=pltpu.PrefetchScalarGridSpec(
            num_scalar_prefetch=1,
            grid=(PACK // BLOCK,),
            in_specs=[
                by_block,
                pl.BlockSpec((PACK, HEAD), lambda q, ends: (0, 2)),
                pl.BlockSpec((PACK, HEAD), lambda q, ends: (0, 3)),
                by_block,
                by_block,
                pl.BlockSpec((2, BLOCK), lambda q, ends: (0, q)),
            ],
            out_specs=[by_block, whole, whole],
        ),
        out_shape=[
            jax.ShapeDtypeStruct((PACK, 2 * HEAD), jnp.float32),
            jax.ShapeDtypeStruct((PACK, HEAD), jnp.float32),
            jax.ShapeDtypeStruct((PACK, HEAD), jnp.float32),
        ],
        compiler_params=pltpu.CompilerParams(vmem_limit_bytes=VMEM_LIMIT),
        cost_estimate=pl.CostEstimate(flops=8000000000, bytes_accessed=8000000, transcendentals=3000000),
        name="attend_back",
    )(ends, qkv, qkv, qkv, grad, out, inverse)


def qkv_back_kernel(
    spots, pre_ref, dq_ref, dk_ref, dv_ref, cos_ref, sin_ref, normed_ref, w_ref, gq_ref, gk_ref,
    d_pre_ref, d_attn_ref, d_head_ref, own_ref, other_ref, rows_ref,
):
    @pl.when(pl.program_id(0) == 0)
    def _():
        d_attn_ref[...] = jnp.zeros_like(d_attn_ref)
        d_head_ref[...] = jnp.zeros_like(d_head_ref)

    cosine, sine = cos_ref[...], sin_ref[...]
    for h in range(3):
        u = pre_ref[:, h * HEAD : (h + 1) * HEAD]
        gain = gk_ref[...] if h == 2 else gq_ref[...]
        grad = dk_ref[...] if h == 2 else dq_ref[:, h * HEAD : (h + 1) * HEAD]
        grad = rope_back(grad, cosine, sine)
        row = 1 if h == 2 else 0
        d_head_ref[row : row + 1, :] += jnp.sum(
            grad * u * norm_scale(u), axis=0, keepdims=True
        )
        d_pre_ref[:, h * HEAD : (h + 1) * HEAD] = low(norm_back(u, gain, grad))
    d_pre_ref[:, 3 * HEAD :] = low(dv_ref[...])
    d_normed = dot(d_pre_ref[...], w_ref[...])
    d_attn_ref[...] += jnp.sum(wide(normed_ref[...]) * d_normed, axis=0, keepdims=True)
    rows_ref[...] = low(d_normed)
    own_ref[...] = rows_ref[own_rows(spots), :]
    other_ref[...] = rows_ref[other_rows(spots), :]


def project_back(spots, pre, d_query, d_key, d_value, cosine, sine, normed, weights, gain_query, gain_key):
    half = ((PACK // 2, WIDTH), jnp.bfloat16)
    return ring_call(
        qkv_back_kernel,
        "project_back",
        [pack_spec(3 * HEAD), pack_spec(2 * HEAD), pack_spec(HEAD), pack_spec(HEAD)]
        + [pack_spec(HEAD), pack_spec(HEAD), pack_spec(WIDTH)]
        + [whole_spec((512, WIDTH)), whole_spec((1, HEAD)), whole_spec((1, HEAD))],
        [pack_spec(512), whole_spec((1, WIDTH)), whole_spec((2, HEAD))] + ring_specs(WIDTH),
        [((PACK, 512), jnp.bfloat16), ((1, WIDTH), jnp.float32), ((2, HEAD), jnp.float32), half, half],
        1610612736, spots, pre, d_query, d_key, d_value, cosine, sine, normed, weights, gain_query, gain_key,
        scratch=[pltpu.VMEM((2 * TOK, WIDTH), jnp.bfloat16)],
    )


def exchange(values, axes):
    return lax.all_to_all(values, axes, split_axis=0, concat_axis=0, tiled=True)


def plane_order(core, blocks):
    return jnp.where(core == 1, jnp.swapaxes(blocks, 0, 1), blocks)


def plane_bit(index, masks):
    return jnp.where(index & 1 == 1, index >> BIT[masks[1]], index >> BIT[masks[0]]) & 1


def gather_plane_step(index, block, step):
    got = swap(block, *PLANE_STEPS[step])
    return jnp.where(
        plane_bit(index, PLANE_STEPS[step]) == 1,
        jnp.concatenate([got, block], axis=0),
        jnp.concatenate([block, got], axis=0),
    )


def gather_plane_end(index, block):
    shape = block.shape[1:]
    return plane_order(index & 1, block.reshape((4, 4) + shape)).reshape((16,) + shape)


def gather_ring(rows):
    for masks in RING_STEPS:
        rows = jnp.concatenate([rows, swap(rows, *masks)], axis=0)
    return rows


def scatter_ring(own, other, steps=2):
    totals = [wide(own) + wide(swap(other, CORE))]
    for masks in RING_STEPS[:-steps-1:-1]:
        half = totals[-1].shape[0] // 2
        totals.append(totals[-1][:half] + wide(swap(low(totals[-1][half:]), *masks)))
    return totals


def tiles_tall(block):
    lead = block.shape[:-2]
    n = len(lead)
    block = block.reshape(lead + (-1, 8, 8, HEAD))
    block = block.transpose(tuple(range(n)) + (n + 2, n + 1, n, n + 3))
    return block.reshape(lead + (64, -1))


def tiles_flat(block):
    lead = block.shape[:-2]
    n = len(lead)
    block = block.reshape(lead + (8, 8, -1, HEAD))
    block = block.transpose(tuple(range(n)) + (n + 2, n + 1, n, n + 3))
    return block.reshape(lead + (-1, WIDTH))


def rows_by_device(blocks):
    n = blocks.shape[-1]
    return blocks.reshape(16, 4, 2, 8, n).transpose(1, 0, 2, 3, 4).reshape(WIDTH, n)


def rows_by_plane(rows):
    n = rows.shape[-1]
    return rows.reshape(4, 16, 2, 8, n).transpose(1, 0, 2, 3, 4).reshape(16, 64, n)


def on_device(
    hidden, lengths, w_query, w_key, w_value, w_out, w_gate, w_up, w_down, gains, cotangent
):
    index = lax.axis_index(AXES).astype(jnp.int32)
    core, x = index & 1, index >> 5
    straight = (index >> 4 & 1) == core
    spot_of = lambda c: jnp.where(c == 1, jnp.asarray(RING_SPOTS[1]), jnp.asarray(RING_SPOTS[0]))
    chips = x ^ jnp.arange(4, dtype=jnp.int32)
    spots = jnp.concatenate(
        [spot_of(core)[chips], spot_of(1 - core)[chips], core[None], core[None]]
    ).astype(jnp.int32)

    first = cross(jnp.concatenate([hidden[0], w_out], axis=0))
    second = cross_and_swap(hidden[0], RING_STEPS[0])
    local = jnp.concatenate(
        [
            w_query.reshape(8, KV_HEADS, 256).transpose(1, 0, 2),
            w_key.reshape(8, KV_HEADS, HEAD).transpose(1, 0, 2),
            w_value.reshape(8, KV_HEADS, HEAD).transpose(1, 0, 2),
            jnp.broadcast_to(jnp.pad(gains[None, None, :], ((0, 0), (0, 7), (0, 110))), (8, 8, 128)),
        ]
        + [
            weight.reshape(8, 4, 16, 2, 24).transpose(1, 3, 0, 2, 4).reshape(8, 8, 384)
            for weight in (w_gate, w_up)
        ],
        axis=2,
    )
    local = exchange(local, RING).reshape(64, 1408)
    inputs = first[:TOK]
    heads = jnp.concatenate([local[:, :640], tiles_tall(first[TOK:])], axis=1)[None]
    for step in range(4):
        heads = gather_plane_step(index, heads, step)
    gain_all = plane_order(core, heads[:, ::8, 512:530].reshape(4, 4, 8, 18))
    gain_all = gain_all.reshape(16, 4, 2, 18).transpose(1, 0, 2, 3)
    gain_all = wide(gain_all.reshape(1, -1))
    gain_attn, gain_mlp = gain_all[:, :WIDTH], gain_all[:, WIDTH : 2 * WIDTH]
    gain_query = gain_all[:, 2 * WIDTH : 2 * WIDTH + HEAD]
    gain_key = gain_all[:, 2 * WIDTH + HEAD :]

    inputs_own = jnp.concatenate([inputs, second], axis=0)
    inputs_own = jnp.concatenate([inputs_own, swap(inputs_own, *RING_STEPS[1])], axis=0)
    inputs_other = swap(inputs_own, CORE)
    lengths = jnp.where(straight, lengths, swap(lengths, CORE))
    ends = jnp.stack([lengths[0, 0], lengths[0, 0] + lengths[0, 1]]).astype(jnp.int32)
    token = jnp.arange(PACK, dtype=jnp.int32)
    position = wide(token - row_start(token, (ends[0], ends[1])))
    inverse = jnp.power(ROPE_BASE, -2.0 * jnp.arange(HEAD // 2, dtype=jnp.float32) / HEAD)
    angle = position[:, None] * inverse[None, :]
    cosine, sine = jnp.cos(angle), jnp.sin(angle)
    cosine = jnp.concatenate([cosine, cosine], axis=1)
    sine = jnp.concatenate([-sine, sine], axis=1)

    d_result = cross(after(cotangent[0], local))
    heads, d_result = lax.optimization_barrier((heads, d_result))
    normed, pre, qkv, w_heads = project(
        spots, inputs_own, inputs_other, heads, gain_attn, gain_query, gain_key, cosine, sine
    )
    d_result_own = jnp.concatenate([d_result, swap(d_result, *RING_STEPS[0])], axis=0)
    qkv, d_result_own, heads = lax.optimization_barrier((qkv, d_result_own, heads))
    attended, inverse_total = attend(ends, qkv)
    w_rows = plane_order(core, heads[..., 640:].reshape(4, 4, 64, 256)).reshape(16, 64, 256)
    w_rows = tiles_flat(w_rows).reshape(2, 8, 16, WIDTH).transpose(1, 0, 2, 3).reshape(256, WIDTH)
    out_own, out_other = to_ring(spots, attended, w_rows)
    d_result_own = jnp.concatenate([d_result_own, swap(d_result_own, *RING_STEPS[1])], axis=0)
    middle_steps = scatter_ring(out_own, out_other)
    d_result_other = swap(after(d_result_own, middle_steps[0]), CORE)

    units = jnp.concatenate([local[:, 640:], tiles_tall(w_down)], axis=1)[None]
    units = gather_plane_step(index, after(units, out_own), 0)
    units = gather_plane_step(index, after(units, middle_steps[0]), 1)
    units = gather_plane_step(index, after(units, middle_steps[1]), 2)
    middle = wide(inputs) + middle_steps[2]
    middle_scale = norm_scale(middle)
    mixed = low(middle * middle_scale * gain_mlp)
    mixed_own = gather_ring(mixed)
    mixed_other = swap(mixed_own, CORE)
    units = gather_plane_step(index, units, 3)
    units = plane_order(core, units.reshape(4, 4, 64, 1152)).reshape(16, 64, 1152)
    full_units = rows_by_device(units[..., :768])
    full_down = tiles_flat(units[..., 768:]).reshape(384, WIDTH)

    def feed_forward(rows, d_rows):
        pre = dot(rows, full_units)
        gate_pre, up_pre = pre[:, :384], pre[:, 384:]
        sigmoid = 1.0 / (1.0 + jnp.exp(-gate_pre))
        silu = gate_pre * sigmoid
        act = low(silu * up_pre)
        d_act = contract_cols(d_rows, full_down)
        d_gate = low(d_act * up_pre * (sigmoid + silu * (1.0 - sigmoid)))
        d_up = low(d_act * silu)
        d_pre = jnp.concatenate([d_gate, d_up], axis=1)
        return act, d_pre, low(contract_cols(d_pre, full_units))

    act_own, d_pre_own, d_mixed_own = feed_forward(mixed_own, d_result_own)
    act_other, d_pre_other, d_mixed_other = feed_forward(mixed_other, d_result_other)
    d_mixed_steps = scatter_ring(d_mixed_own, d_mixed_other)
    d_mixed = d_mixed_steps[-1]
    d_middle = wide(d_result) + norm_back(middle, gain_mlp, d_mixed)
    d_gain_mlp = jnp.sum(middle * middle_scale * d_mixed, axis=0)
    d_branch_own = gather_ring(low(d_middle))
    d_branch_other = swap(d_branch_own, CORE)

    act_own, act_other, d_pre_own, d_pre_other = lax.optimization_barrier(
        (act_own, act_other, d_pre_own, d_pre_other, d_mixed_steps[0])
    )[:4]
    grad_units = contract_rows(mixed_own, d_pre_own) + contract_rows(mixed_other, d_pre_other)
    grad_down = contract_rows(act_own, d_result_own) + contract_rows(act_other, d_result_other)
    grad_down = low(grad_down).reshape(16, 3, 8, 8, HEAD).transpose(0, 3, 2, 1, 4)
    grads = jnp.concatenate(
        [rows_by_plane(low(grad_units)), grad_down.reshape(16, 64, 384)], axis=2
    )
    grads = exchange(grads, PLANE)
    act_own, act_other = (after(act, d_middle) for act in (act_own, act_other))
    result = to_pack(spots, act_own, act_other, full_down)
    result = lax.psum_scatter(after(result, d_branch_own), RING, scatter_dimension=0, tiled=True)
    d_middle_home = jnp.where(straight, d_middle, wide(cross(low(d_middle))))

    d_attended, grad_out = out_back(spots, d_branch_own, d_branch_other, attended, w_rows)
    d_query, d_key, d_value = attend_back(ends, qkv, d_attended, attended, inverse_total)
    d_query, grads = lax.optimization_barrier((d_query, grads))
    sums = jnp.sum(wide(grads), axis=0)
    grad_out = low(grad_out).reshape(8, 2, 16, WIDTH).transpose(1, 0, 2, 3).reshape(16, 16, WIDTH)
    grad_out = tiles_tall(grad_out)
    d_query, sums, grad_out = lax.optimization_barrier((d_query, sums, grad_out))
    d_pre, d_gain_attn, d_gain_heads, d_normed_own, d_normed_other = project_back(
        spots, pre, d_query, d_key, d_value, cosine, sine, normed, w_heads.T, gain_query, gain_key
    )
    d_normed_steps = scatter_ring(d_normed_own, d_normed_other, 1)
    halves = low(d_normed_steps[1][:TOK]), low(d_normed_steps[1][TOK:])
    d_normed = wide(cross(halves[0])) + wide(swap_and_cross(halves[1], RING_STEPS[0]))
    input_grad = d_middle_home + norm_back(wide(hidden[0]), gain_attn, d_normed)

    d_pre = after(d_pre, d_normed_steps[0])
    d_gains = jnp.concatenate(
        [(d_gain_attn / gain_attn)[0], d_gain_mlp, d_gain_heads.reshape(-1)]
    )
    d_gains = d_gains.reshape(4, 16, 2, 1, 18).transpose(1, 0, 2, 3, 4)
    payload = jnp.concatenate(
        [
            rows_by_plane(low(contract_rows(normed, d_pre))),
            low(jnp.pad(d_gains, ((0, 0),) * 3 + ((0, 7), (0, 110)))).reshape(16, 64, 128),
            grad_out,
        ],
        axis=2,
    )
    heads_sums = jnp.sum(wide(exchange(payload, PLANE)), axis=0)
    ring_grads = jnp.concatenate([low(heads_sums[:, :640]), low(sums[:, :768])], axis=1)
    ring_grads = wide(exchange(ring_grads.reshape(8, 8, 1408), RING))
    heads_grad, units_grad = ring_grads[..., :640], ring_grads[..., 640:]
    sum_out = tiles_flat(heads_sums[:, 640:])
    sum_out = jnp.where(straight, sum_out, wide(cross(low(sum_out))))
    activations = cross(after(low(middle + wide(result)), d_normed_steps[0]))
    sum_down = tiles_flat(sums[:, 768:])
    by_unit = lambda grad: (
        grad.reshape(4, 2, 8, 16, 24).transpose(2, 0, 3, 1, 4).reshape(8, FF)
    )
    sum_query = heads_grad[..., :256].transpose(1, 0, 2).reshape(8, -1)
    sum_key = heads_grad[..., 256:384].transpose(1, 0, 2).reshape(8, -1)
    sum_value = heads_grad[..., 384:512].transpose(1, 0, 2).reshape(8, -1)
    sum_gains = jnp.sum(heads_grad[:, 0, 512:530], axis=0)
    return (
        activations[None],
        input_grad[None],
        sum_query,
        sum_key,
        sum_value,
        sum_out,
        by_unit(units_grad[..., :384]),
        by_unit(units_grad[..., 384:]),
        sum_down,
        sum_gains,
    )


def solution(mesh):
    chips = Mesh(mesh.devices.reshape(4, 2, 2, 4, 2), AXES)
    rows = P(AXES, None)
    tokens = P(("zl", "y", "core"), ("x", "zh"), None)
    lengths = P(("zl", "y", "core"), None)
    return jax.shard_map(
        on_device,
        mesh=chips,
        in_specs=(tokens, lengths, *([rows] * 7), P(AXES), tokens),
        out_specs=(tokens, tokens, *([rows] * 7), P(AXES)),
        check_vma=False,
    )
```

```python
import jax
import jax.numpy as jnp
from jax import lax
from jax.experimental import pallas as pl
from jax.experimental.pallas import tpu as pltpu
from jax.sharding import Mesh
from jax.sharding import PartitionSpec as P

HEADS = 16
KV_HEADS = 8
HEAD = 128
EPSILON = 1e-06
ROPE_BASE = 1000000.0
DEVICES = 128
WIDTH = 1024
FF = 3072
TOK = 192
PACK = 1536
BLOCK = 256
LOG2E = 1.4426950408889634
SCALE = HEAD ** (-0.5)
VMEM_LIMIT = 48 * 1024 * 1024
VMEM_MOST = 58 * 1024 * 1024

AXES = ("x", "zh", "zl", "y", "core")
RING = ("x", "core")
PLANE = ("zh", "zl", "y")
XA, XB, ZA, ZB, YA, YB, CORE = 32, 96, 8, 24, 2, 6, 1
RING_STEPS = ((XA, XB), (XB, XA))
RING_SPOTS = ((0, 1, 3, 2), (0, 2, 3, 1))
PLANE_STEPS = ((YA, ZA), (YB, ZB), (ZA, YA), (ZB, YB))
BIT = {YA: 1, YB: 2, ZA: 3, ZB: 4}


def swap(values, mask, other_mask=None):
    masks = (mask, mask if other_mask is None else other_mask)
    return lax.ppermute(values, AXES, [(k, k ^ masks[k & 1]) for k in range(DEVICES)])


def crossed(k):
    return k ^ 17 if (k >> 4 ^ k) & 1 else k


def cross(values):
    return lax.ppermute(values, AXES, [(k, crossed(k)) for k in range(DEVICES)])


def cross_and_swap(values, masks):
    return lax.ppermute(
        values, AXES, [(crossed(k ^ masks[k & 1]), k) for k in range(DEVICES)]
    )


def swap_and_cross(values, masks):
    return lax.ppermute(
        values, AXES, [(k, crossed(k ^ masks[k & 1])) for k in range(DEVICES)]
    )


def after(value, *others):
    return lax.optimization_barrier((value, *others))[0] if others else value


def low(values):
    return values.astype(jnp.bfloat16)


def wide(values):
    return values.astype(jnp.float32)


def dot(left, right):
    return jnp.dot(left, right, preferred_element_type=jnp.float32)


def contract_rows(left, right):
    return lax.dot_general(
        left, right, (((0,), (0,)), ((), ())), preferred_element_type=jnp.float32
    )


def contract_cols(left, right):
    return lax.dot_general(
        left, right, (((1,), (1,)), ((), ())), preferred_element_type=jnp.float32
    )


def norm_scale(values):
    return lax.rsqrt(jnp.mean(values * values, axis=-1, keepdims=True) + EPSILON)


def norm_back(values, gain, grad):
    scale = norm_scale(values)
    normal = values * scale
    inner = grad * gain
    return scale * (inner - normal * jnp.mean(inner * normal, axis=-1, keepdims=True))


def rope(values, cosine, sine):
    return values * cosine + pltpu.roll(values, 64, 1) * sine


def rope_back(grad, cosine, sine):
    return grad * cosine + pltpu.roll(grad * sine, 64, 1)


def ring_specs(columns, stride=1):
    return [
        pl.BlockSpec((TOK, columns), lambda x, spots: (spots[x] * stride, 0)),
        pl.BlockSpec((TOK, columns), lambda x, spots: (spots[4 + x] * stride, 0)),
    ]


def pack_spec(columns):
    return pl.BlockSpec((2 * TOK, columns), lambda x, spots: (x, 0))


def whole_spec(shape):
    return pl.BlockSpec(shape, lambda x, spots: (0, 0))


def own_rows(spots):
    return pl.ds(pl.multiple_of(spots[8] * TOK, TOK), TOK)


def other_rows(spots):
    return pl.ds(pl.multiple_of((1 - spots[8]) * TOK, TOK), TOK)


def ring_call(
    kernel, name, in_specs, out_specs, out_shape, flops, spots, *operands, scratch=(), limit=VMEM_LIMIT
):
    return pl.pallas_call(
        kernel,
        grid_spec=pltpu.PrefetchScalarGridSpec(
            num_scalar_prefetch=1,
            grid=(4,),
            in_specs=in_specs,
            out_specs=out_specs,
            scratch_shapes=scratch,
        ),
        out_shape=[jax.ShapeDtypeStruct(shape, dtype) for shape, dtype in out_shape],
        compiler_params=pltpu.CompilerParams(vmem_limit_bytes=limit),
        cost_estimate=pl.CostEstimate(flops=flops, bytes_accessed=12000000, transcendentals=0),
        name=name,
    )(spots, *operands)


def qkv_kernel(
    spots, own_ref, other_ref, heads_ref, ga_ref, gq_ref, gk_ref, cos_ref, sin_ref,
    normed_ref, pre_ref, qkv_ref, w_ref,
):
    @pl.when(pl.program_id(0) == 0)
    def _():
        for z in range(4):
            for y in range(4):
                block = jnp.where(spots[9] == 1, y * 4 + z, z * 4 + y)
                for x in range(4):
                    row = (x * 16 + z * 4 + y) * 16
                    w_ref[row : row + 16, :] = heads_ref[block, x * 16 : x * 16 + 16, :512]

    for ref, rows in ((own_ref, own_rows(spots)), (other_ref, other_rows(spots))):
        x = wide(ref[...])
        normed_ref[rows, :] = low(x * norm_scale(x) * ga_ref[...])
    pre = dot(normed_ref[...], w_ref[...])
    pre_ref[...] = pre[:, : 3 * HEAD]
    cosine, sine = cos_ref[...], sin_ref[...]
    for h in range(3):
        u = pre[:, h * HEAD : (h + 1) * HEAD]
        gain = gk_ref[...] if h == 2 else gq_ref[...]
        normal = u * norm_scale(u) * gain
        qkv_ref[:, h * HEAD : (h + 1) * HEAD] = low(rope(normal, cosine, sine))
    qkv_ref[:, 3 * HEAD :] = low(pre[:, 3 * HEAD :])


def project(spots, own, other, heads, gain_attn, gain_query, gain_key, cosine, sine):
    return ring_call(
        qkv_kernel,
        "project",
        ring_specs(WIDTH, 2)
        + [pl.BlockSpec(heads.shape, lambda x, spots: (0, 0, 0))]
        + [whole_spec((1, WIDTH)), whole_spec((1, HEAD)), whole_spec((1, HEAD))]
        + [pack_spec(HEAD), pack_spec(HEAD)],
        [pack_spec(WIDTH), pack_spec(3 * HEAD), pack_spec(512), whole_spec((WIDTH, 512))],
        [
            ((PACK, WIDTH), jnp.bfloat16),
            ((PACK, 3 * HEAD), jnp.float32),
            ((PACK, 512), jnp.bfloat16),
            ((WIDTH, 512), jnp.bfloat16),
        ],
        1610612736, spots, own, other, heads, gain_attn, gain_query, gain_key, cosine, sine,
    )


def to_ring_kernel(spots, rows_ref, w_ref, own_ref, other_ref):
    own_ref[...] = low(dot(rows_ref[own_rows(spots), :], w_ref[...]))
    other_ref[...] = low(dot(rows_ref[other_rows(spots), :], w_ref[...]))


def to_ring(spots, rows, weights):
    half = ((PACK // 2, WIDTH), jnp.bfloat16)
    return ring_call(
        to_ring_kernel, "to_ring", [pack_spec(256), whole_spec((256, WIDTH))], ring_specs(WIDTH),
        [half, half], 800000000, spots, rows, weights,
    )


def to_pack_kernel(spots, own_ref, other_ref, w_ref, rows_ref):
    rows_ref[own_rows(spots), :] = low(dot(own_ref[...], w_ref[...]))
    rows_ref[other_rows(spots), :] = low(dot(other_ref[...], w_ref[...]))


def to_pack(spots, own, other, weights):
    return ring_call(
        to_pack_kernel, "to_pack", ring_specs(own.shape[1]) + [whole_spec(weights.shape)],
        [pack_spec(WIDTH)], [((PACK, WIDTH), jnp.bfloat16)], 1200000000, spots, own, other, weights,
    )[0]


def out_back_kernel(spots, own_ref, other_ref, attended_ref, w_ref, d_attended_ref, d_w_ref, rows_ref):
    @pl.when(pl.program_id(0) == 0)
    def _():
        d_w_ref[...] = jnp.zeros_like(d_w_ref)

    rows_ref[own_rows(spots), :] = own_ref[...]
    rows_ref[other_rows(spots), :] = other_ref[...]
    d_attended_ref[...] = low(contract_cols(rows_ref[...], w_ref[...]))
    d_w_ref[...] += contract_rows(attended_ref[...], rows_ref[...])


def out_back(spots, own, other, attended, weights):
    return ring_call(
        out_back_kernel, "out_back",
        ring_specs(WIDTH) + [pack_spec(256), whole_spec((256, WIDTH))],
        [pack_spec(256), whole_spec((256, WIDTH))],
        [((PACK, 256), jnp.bfloat16), ((256, WIDTH), jnp.float32)],
        1600000000, spots, own, other, attended, weights,
        scratch=[pltpu.VMEM((2 * TOK, WIDTH), jnp.bfloat16)],
    )


def row_start(rows, ends):
    first, second = ends
    return jnp.where(rows >= second, second, jnp.where(rows >= first, first, 0))


def block_mask(q_block, k_block, ends, transposed):
    last = PACK // BLOCK - 1
    q_axis, k_axis = (1, 0) if transposed else (0, 1)
    q_rows = q_block * BLOCK + lax.broadcasted_iota(jnp.int32, (BLOCK, BLOCK), q_axis)
    k_rows = k_block * BLOCK + lax.broadcasted_iota(jnp.int32, (BLOCK, BLOCK), k_axis)
    mask = None
    if k_block == q_block:
        mask = k_rows <= q_rows
    if k_block == 0 or q_block == last:
        begun = k_rows >= row_start(q_rows, ends)
        mask = begun if mask is None else mask & begun
    return mask


def for_each_block(step):
    for q_block in range(PACK // BLOCK):

        @pl.when(pl.program_id(0) == q_block)
        def _(q_block=q_block):
            step(q_block)


def attend_kernel(ends_ref, q_ref, k_ref, v_ref, out_ref, inverse_ref):
    ends = (ends_ref[0], ends_ref[1])

    def step(q_block):
        seen = (q_block + 1) * BLOCK
        for h in range(2):
            columns = slice(h * HEAD, (h + 1) * HEAD)
            scores = contract_cols(q_ref[:, columns], k_ref[:seen, :])
            part, shifted = 0.0, []
            for k_block in range(q_block + 1):
                block = scores[:, k_block * BLOCK : (k_block + 1) * BLOCK]
                block = jnp.exp2(block * (SCALE * LOG2E))
                mask = block_mask(q_block, k_block, ends, False)
                if mask is not None:
                    block = jnp.where(mask, block, 0.0)
                part += block[:, :HEAD] + block[:, HEAD:]
                shifted.append(low(block))
            total = dot(jnp.concatenate(shifted, axis=1), v_ref[:seen, :])
            row_total = jnp.sum(part, axis=1, keepdims=True)
            out_ref[:, columns] = low(total * (1.0 / row_total))
            across = jnp.sum(jnp.swapaxes(part, 0, 1), axis=0, keepdims=True)
            inverse_ref[h : h + 1, :] = 1.0 / across

    for_each_block(step)


def attend(ends, qkv):
    return pl.pallas_call(
        attend_kernel,
        grid_spec=pltpu.PrefetchScalarGridSpec(
            num_scalar_prefetch=1,
            grid=(PACK // BLOCK,),
            in_specs=[
                pl.BlockSpec((BLOCK, 2 * HEAD), lambda q, ends: (q, 0)),
                pl.BlockSpec((PACK, HEAD), lambda q, ends: (0, 2)),
                pl.BlockSpec((PACK, HEAD), lambda q, ends: (0, 3)),
            ],
            out_specs=[
                pl.BlockSpec((BLOCK, 2 * HEAD), lambda q, ends: (q, 0)),
                pl.BlockSpec((2, BLOCK), lambda q, ends: (0, q)),
            ],
        ),
        out_shape=[
            jax.ShapeDtypeStruct((PACK, 2 * HEAD), jnp.bfloat16),
            jax.ShapeDtypeStruct((2, PACK), jnp.float32),
        ],
        compiler_params=pltpu.CompilerParams(vmem_limit_bytes=VMEM_LIMIT),
        cost_estimate=pl.CostEstimate(flops=3000000000, bytes_accessed=4000000, transcendentals=3000000),
        name="attend",
    )(ends, qkv, qkv, qkv)


def attend_back_kernel(
    ends_ref, q_ref, k_ref, v_ref, grad_ref, out_ref, inverse_ref, dq_ref, dk_ref, dv_ref
):
    ends = (ends_ref[0], ends_ref[1])

    @pl.when(pl.program_id(0) == 0)
    def _():
        dk_ref[...] = jnp.zeros_like(dk_ref)
        dv_ref[...] = jnp.zeros_like(dv_ref)

    def both_heads(ref):
        return jnp.concatenate([ref[:, :HEAD], ref[:, HEAD:]], axis=0)

    def step(q_block):
        seen = (q_block + 1) * BLOCK
        queries, grads = both_heads(q_ref), both_heads(grad_ref)
        product = wide(grads) * wide(both_heads(out_ref))
        delta = jnp.sum(jnp.swapaxes(product, 0, 1), axis=0, keepdims=True)
        inverse = jnp.concatenate([inverse_ref[0:1, :], inverse_ref[1:2, :]], axis=1)
        scores = contract_cols(k_ref[:seen, :], queries)
        d_probs = contract_cols(v_ref[:seen, :], grads)
        probs, d_scores = [], []
        for k_block in range(q_block + 1):
            rows = slice(k_block * BLOCK, (k_block + 1) * BLOCK)
            prob = jnp.exp2(scores[rows] * (SCALE * LOG2E)) * inverse
            mask = block_mask(q_block, k_block, ends, True)
            if mask is not None:
                prob = jnp.where(jnp.concatenate([mask, mask], axis=1), prob, 0.0)
            d_scores.append(low(prob * ((d_probs[rows] - delta) * SCALE)))
            probs.append(low(prob))
        probs = jnp.concatenate(probs, axis=0)
        d_scores = jnp.concatenate(d_scores, axis=0)
        dk_ref[:seen, :] += dot(d_scores, queries)
        dv_ref[:seen, :] += dot(probs, grads)
        d_queries = contract_rows(d_scores, k_ref[:seen, :])
        dq_ref[:, :HEAD] = d_queries[:BLOCK]
        dq_ref[:, HEAD:] = d_queries[BLOCK:]

    for_each_block(step)


def attend_back(ends, qkv, grad, out, inverse):
    by_block = pl.BlockSpec((BLOCK, 2 * HEAD), lambda q, ends: (q, 0))
    whole = pl.BlockSpec((PACK, HEAD), lambda q, ends: (0, 0))
    return pl.pallas_call(
        attend_back_kernel,
        grid_spec=pltpu.PrefetchScalarGridSpec(
            num_scalar_prefetch=1,
            grid=(PACK // BLOCK,),
            in_specs=[
                by_block,
                pl.BlockSpec((PACK, HEAD), lambda q, ends: (0, 2)),
                pl.BlockSpec((PACK, HEAD), lambda q, ends: (0, 3)),
                by_block,
                by_block,
                pl.BlockSpec((2, BLOCK), lambda q, ends: (0, q)),
            ],
            out_specs=[by_block, whole, whole],
        ),
        out_shape=[
            jax.ShapeDtypeStruct((PACK, 2 * HEAD), jnp.float32),
            jax.ShapeDtypeStruct((PACK, HEAD), jnp.float32),
            jax.ShapeDtypeStruct((PACK, HEAD), jnp.float32),
        ],
        compiler_params=pltpu.CompilerParams(vmem_limit_bytes=VMEM_LIMIT),
        cost_estimate=pl.CostEstimate(flops=8000000000, bytes_accessed=8000000, transcendentals=3000000),
        name="attend_back",
    )(ends, qkv, qkv, qkv, grad, out, inverse)


def qkv_back_kernel(
    spots, pre_ref, dq_ref, dk_ref, dv_ref, cos_ref, sin_ref, normed_ref, w_ref, gq_ref, gk_ref,
    d_pre_ref, d_attn_ref, d_head_ref, own_ref, other_ref, rows_ref,
):
    @pl.when(pl.program_id(0) == 0)
    def _():
        d_attn_ref[...] = jnp.zeros_like(d_attn_ref)
        d_head_ref[...] = jnp.zeros_like(d_head_ref)

    cosine, sine = cos_ref[...], sin_ref[...]
    for h in range(3):
        u = pre_ref[:, h * HEAD : (h + 1) * HEAD]
        gain = gk_ref[...] if h == 2 else gq_ref[...]
        grad = dk_ref[...] if h == 2 else dq_ref[:, h * HEAD : (h + 1) * HEAD]
        grad = rope_back(grad, cosine, sine)
        row = 1 if h == 2 else 0
        d_head_ref[row : row + 1, :] += jnp.sum(
            grad * u * norm_scale(u), axis=0, keepdims=True
        )
        d_pre_ref[:, h * HEAD : (h + 1) * HEAD] = low(norm_back(u, gain, grad))
    d_pre_ref[:, 3 * HEAD :] = low(dv_ref[...])
    d_normed = dot(d_pre_ref[...], w_ref[...])
    d_attn_ref[...] += jnp.sum(wide(normed_ref[...]) * d_normed, axis=0, keepdims=True)
    rows_ref[...] = low(d_normed)
    own_ref[...] = rows_ref[own_rows(spots), :]
    other_ref[...] = rows_ref[other_rows(spots), :]


def project_back(spots, pre, d_query, d_key, d_value, cosine, sine, normed, weights, gain_query, gain_key):
    half = ((PACK // 2, WIDTH), jnp.bfloat16)
    return ring_call(
        qkv_back_kernel,
        "project_back",
        [pack_spec(3 * HEAD), pack_spec(2 * HEAD), pack_spec(HEAD), pack_spec(HEAD)]
        + [pack_spec(HEAD), pack_spec(HEAD), pack_spec(WIDTH)]
        + [whole_spec((512, WIDTH)), whole_spec((1, HEAD)), whole_spec((1, HEAD))],
        [pack_spec(512), whole_spec((1, WIDTH)), whole_spec((2, HEAD))] + ring_specs(WIDTH),
        [((PACK, 512), jnp.bfloat16), ((1, WIDTH), jnp.float32), ((2, HEAD), jnp.float32), half, half],
        1610612736, spots, pre, d_query, d_key, d_value, cosine, sine, normed, weights, gain_query, gain_key,
        scratch=[pltpu.VMEM((2 * TOK, WIDTH), jnp.bfloat16)], limit=VMEM_MOST,
    )


def exchange(values, axes):
    return lax.all_to_all(values, axes, split_axis=0, concat_axis=0, tiled=True)


def plane_order(core, blocks):
    return jnp.where(core == 1, jnp.swapaxes(blocks, 0, 1), blocks)


def plane_bit(index, masks):
    return jnp.where(index & 1 == 1, index >> BIT[masks[1]], index >> BIT[masks[0]]) & 1


def gather_plane_step(index, block, step):
    got = swap(block, *PLANE_STEPS[step])
    return jnp.where(
        plane_bit(index, PLANE_STEPS[step]) == 1,
        jnp.concatenate([got, block], axis=0),
        jnp.concatenate([block, got], axis=0),
    )


def gather_plane_end(index, block):
    shape = block.shape[1:]
    return plane_order(index & 1, block.reshape((4, 4) + shape)).reshape((16,) + shape)


def gather_ring(rows, beside=((), ())):
    for masks, others in zip(RING_STEPS, beside):
        rows = jnp.concatenate([rows, after(swap(rows, *masks), *others)], axis=0)
    return rows


def scatter_ring(own, other, steps=2):
    totals = [wide(own) + wide(swap(other, CORE))]
    for masks in RING_STEPS[: -steps - 1 : -1]:
        half = totals[-1].shape[0] // 2
        totals.append(totals[-1][:half] + wide(swap(low(totals[-1][half:]), *masks)))
    return totals


def exchange_ring(index, blocks):
    core, x = index & 1, index >> 5
    shape = blocks.shape[1:]
    blocks = blocks.reshape((4, 2) + shape)
    take = lambda array, at, axis: lax.dynamic_slice_in_dim(array, at, 1, axis)
    got = swap(take(blocks, 1 - core, 1), CORE)
    keep = take(blocks, core, 1)
    blocks = jnp.concatenate(
        [jnp.where(core == 1, got, keep), jnp.where(core == 1, keep, got)], axis=1
    )
    parts = [take(blocks, x, 0)] + [
        swap(take(blocks, x ^ k, 0), k << 5) for k in range(1, 4)
    ]
    parts = jnp.concatenate(parts, axis=0)
    parts = jnp.where(x & 1 == 1, parts.reshape((2, 2, 2) + shape)[:, ::-1].reshape(parts.shape), parts)
    parts = jnp.where(x & 2 == 2, parts.reshape((2, 4) + shape)[::-1].reshape(parts.shape), parts)
    return parts.reshape((8,) + shape)


def tiles_tall(block):
    lead = block.shape[:-2]
    n = len(lead)
    block = block.reshape(lead + (-1, 8, 8, HEAD))
    block = block.transpose(tuple(range(n)) + (n + 2, n + 1, n, n + 3))
    return block.reshape(lead + (64, -1))


def tiles_flat(block):
    lead = block.shape[:-2]
    n = len(lead)
    block = block.reshape(lead + (8, 8, -1, HEAD))
    block = block.transpose(tuple(range(n)) + (n + 2, n + 1, n, n + 3))
    return block.reshape(lead + (-1, WIDTH))


def rows_by_device(blocks):
    n = blocks.shape[-1]
    return blocks.reshape(16, 4, 2, 8, n).transpose(1, 0, 2, 3, 4).reshape(WIDTH, n)


def rows_by_plane(rows):
    n = rows.shape[-1]
    return rows.reshape(4, 16, 2, 8, n).transpose(1, 0, 2, 3, 4).reshape(16, 64, n)


def on_device(
    hidden, lengths, w_query, w_key, w_value, w_out, w_gate, w_up, w_down, gains, cotangent
):
    index = lax.axis_index(AXES).astype(jnp.int32)
    core, x = index & 1, index >> 5
    straight = (index >> 4 & 1) == core
    spot_of = lambda c: jnp.where(c == 1, jnp.asarray(RING_SPOTS[1]), jnp.asarray(RING_SPOTS[0]))
    chips = x ^ jnp.arange(4, dtype=jnp.int32)
    spots = jnp.concatenate(
        [spot_of(core)[chips], spot_of(1 - core)[chips], core[None], core[None]]
    ).astype(jnp.int32)

    first = cross(jnp.concatenate([hidden[0], cotangent[0], w_out], axis=0))
    second = cross_and_swap(jnp.concatenate([hidden[0], cotangent[0]], axis=0), RING_STEPS[0])
    local = jnp.concatenate(
        [
            w_query.reshape(8, KV_HEADS, 256).transpose(1, 0, 2),
            w_key.reshape(8, KV_HEADS, HEAD).transpose(1, 0, 2),
            w_value.reshape(8, KV_HEADS, HEAD).transpose(1, 0, 2),
            jnp.broadcast_to(jnp.pad(gains[None, None, :], ((0, 0), (0, 7), (0, 110))), (8, 8, 128)),
        ]
        + [
            weight.reshape(8, 4, 16, 2, 24).transpose(1, 3, 0, 2, 4).reshape(8, 8, 384)
            for weight in (w_gate, w_up)
        ],
        axis=2,
    )
    local = exchange(local, RING).reshape(64, 1408)
    inputs, d_result = first[:TOK], first[TOK : 2 * TOK]
    heads = jnp.concatenate([local[:, :640], tiles_tall(first[2 * TOK :])], axis=1)[None]
    for step in range(4):
        heads = gather_plane_step(index, heads, step)
    gain_all = plane_order(core, heads[:, ::8, 512:530].reshape(4, 4, 8, 18))
    gain_all = gain_all.reshape(16, 4, 2, 18).transpose(1, 0, 2, 3)
    gain_all = wide(gain_all.reshape(1, -1))
    gain_attn, gain_mlp = gain_all[:, :WIDTH], gain_all[:, WIDTH : 2 * WIDTH]
    gain_query = gain_all[:, 2 * WIDTH : 2 * WIDTH + HEAD]
    gain_key = gain_all[:, 2 * WIDTH + HEAD :]

    rows_own = jnp.concatenate([first[: 2 * TOK], second], axis=0)
    rows_own = jnp.concatenate([rows_own, swap(rows_own, *RING_STEPS[1])], axis=0)
    rows_other = swap(rows_own, CORE)
    lengths = jnp.where(straight, lengths, swap(lengths, CORE))
    ends = jnp.stack([lengths[0, 0], lengths[0, 0] + lengths[0, 1]]).astype(jnp.int32)
    token = jnp.arange(PACK, dtype=jnp.int32)
    position = wide(token - row_start(token, (ends[0], ends[1])))
    inverse = jnp.power(ROPE_BASE, -2.0 * jnp.arange(HEAD // 2, dtype=jnp.float32) / HEAD)
    angle = position[:, None] * inverse[None, :]
    cosine, sine = jnp.cos(angle), jnp.sin(angle)
    cosine = jnp.concatenate([cosine, cosine], axis=1)
    sine = jnp.concatenate([-sine, sine], axis=1)

    normed, pre, qkv, w_heads = project(
        spots, rows_own, rows_other, heads, gain_attn, gain_query, gain_key, cosine, sine
    )
    heads = after(heads, qkv)
    attended, inverse_total = attend(ends, qkv)
    w_rows = plane_order(core, heads[..., 640:].reshape(4, 4, 64, 256)).reshape(16, 64, 256)
    w_rows = tiles_flat(w_rows).reshape(2, 8, 16, WIDTH).transpose(1, 0, 2, 3).reshape(256, WIDTH)
    out_own, out_other = to_ring(spots, attended, w_rows)
    middle_steps = scatter_ring(out_own, out_other)
    d_result_own, d_result_other = (
        rows.reshape(4, 2, TOK, WIDTH)[:, 1].reshape(-1, WIDTH)
        for rows in (after(rows_own, middle_steps[0]), after(rows_other, middle_steps[1]))
    )

    units = jnp.concatenate([local[:, 640:], tiles_tall(w_down)], axis=1)[None]
    units = gather_plane_step(index, after(units, out_own), 0)
    units = gather_plane_step(index, after(units, middle_steps[0]), 1)
    units = gather_plane_step(index, after(units, middle_steps[1]), 2)
    middle = wide(inputs) + middle_steps[2]
    middle_scale = norm_scale(middle)
    mixed = low(middle * middle_scale * gain_mlp)
    mixed_own = gather_ring(mixed)
    mixed_other = swap(mixed_own, CORE)
    units = gather_plane_step(index, units, 3)
    units = plane_order(core, units.reshape(4, 4, 64, 1152)).reshape(16, 64, 1152)
    full_units = rows_by_device(units[..., :768])
    full_down = tiles_flat(units[..., 768:]).reshape(384, WIDTH)

    def feed_forward(rows, d_rows):
        pre = dot(rows, full_units)
        gate_pre, up_pre = pre[:, :384], pre[:, 384:]
        sigmoid = 1.0 / (1.0 + jnp.exp(-gate_pre))
        silu = gate_pre * sigmoid
        act = low(silu * up_pre)
        d_act = contract_cols(d_rows, full_down)
        d_gate = low(d_act * up_pre * (sigmoid + silu * (1.0 - sigmoid)))
        d_up = low(d_act * silu)
        d_pre = jnp.concatenate([d_gate, d_up], axis=1)
        return act, d_pre, low(contract_cols(d_pre, full_units))

    act_own, d_pre_own, d_mixed_own = feed_forward(mixed_own, d_result_own)
    act_other, d_pre_other, d_mixed_other = feed_forward(mixed_other, d_result_other)
    d_mixed_steps = scatter_ring(d_mixed_own, d_mixed_other)
    d_mixed = d_mixed_steps[-1]
    d_middle = wide(d_result) + norm_back(middle, gain_mlp, d_mixed)
    d_gain_mlp = jnp.sum(middle * middle_scale * d_mixed, axis=0)

    late = lambda array: after(array, d_mixed_steps[0])
    grad_units = contract_rows(mixed_own, late(d_pre_own)) + contract_rows(mixed_other, late(d_pre_other))
    grad_units = low(grad_units)
    late = lambda array: after(array, d_mixed_steps[1], grad_units)
    grad_down = contract_rows(late(act_own), d_result_own) + contract_rows(late(act_other), d_result_other)
    grad_down = low(grad_down).reshape(16, 3, 8, 8, HEAD).transpose(0, 3, 2, 1, 4)
    grads = jnp.concatenate([rows_by_plane(grad_units), grad_down.reshape(16, 64, 384)], axis=2)
    act_own, act_other = (after(act, grads) for act in (act_own, act_other))
    result = to_pack(spots, act_own, act_other, full_down)
    d_branch_own = gather_ring(low(d_middle), ((grads,), (result,)))
    d_branch_other = swap(d_branch_own, CORE)
    grads = exchange(grads, PLANE)
    result = lax.psum_scatter(after(result, d_branch_own), RING, scatter_dimension=0, tiled=True)
    d_middle_home = jnp.where(straight, d_middle, wide(cross(after(low(d_middle), d_branch_own))))

    d_attended, grad_out = out_back(spots, d_branch_own, d_branch_other, attended, w_rows)
    d_query, d_key, d_value = attend_back(ends, qkv, d_attended, attended, inverse_total)
    d_query, grads, grad_out = lax.optimization_barrier((d_query, grads, grad_out))
    grad_out = low(grad_out).reshape(8, 2, 16, WIDTH).transpose(1, 0, 2, 3).reshape(16, 16, WIDTH)
    grad_out = exchange(grad_out, PLANE)
    d_pre, d_gain_attn, d_gain_heads, d_normed_own, d_normed_other = project_back(
        spots, pre, d_query, d_key, d_value, cosine, sine, normed, w_heads.T, gain_query, gain_key
    )
    d_normed_steps = scatter_ring(d_normed_own, d_normed_other, 1)
    halves = low(d_normed_steps[1][:TOK]), low(d_normed_steps[1][TOK:])
    d_normed = wide(cross(halves[0])) + wide(swap_and_cross(halves[1], RING_STEPS[0]))
    input_grad = d_middle_home + norm_back(wide(hidden[0]), gain_attn, d_normed)

    d_gains = jnp.concatenate(
        [(d_gain_attn / gain_attn)[0], d_gain_mlp, d_gain_heads.reshape(-1)]
    )
    payload = jnp.concatenate(
        [
            low(contract_rows(normed, d_pre)).reshape(DEVICES, 8, 512),
            low(jnp.pad(d_gains.reshape(DEVICES, 1, 18), ((0, 0), (0, 7), (0, 110)))),
        ],
        axis=2,
    )
    heads_grad = wide(exchange(payload, AXES)).reshape(4, 16, 2, 8, 640)
    heads_grad = jnp.sum(heads_grad, axis=1).reshape(8, 8, 640)

    grads, grad_out = (after(array, d_normed_steps[0]) for array in (grads, grad_out))
    sums = jnp.sum(wide(grads), axis=0)
    units_grad = wide(exchange_ring(index, low(sums[:, :768]).reshape(8, 8, 768)))
    sum_down = tiles_flat(sums[:, 768:])
    sum_out = jnp.sum(wide(grad_out), axis=0)
    sum_out = jnp.where(straight, sum_out, wide(cross(low(sum_out))))
    activations = cross(after(low(middle + wide(result)), d_normed_steps[0]))
    by_unit = lambda grad: (
        grad.reshape(4, 2, 8, 16, 24).transpose(2, 0, 3, 1, 4).reshape(8, FF)
    )
    sum_query = heads_grad[..., :256].transpose(1, 0, 2).reshape(8, -1)
    sum_key = heads_grad[..., 256:384].transpose(1, 0, 2).reshape(8, -1)
    sum_value = heads_grad[..., 384:512].transpose(1, 0, 2).reshape(8, -1)
    sum_gains = jnp.sum(heads_grad[:, 0, 512:530], axis=0)
    return (
        activations[None],
        input_grad[None],
        sum_query,
        sum_key,
        sum_value,
        sum_out,
        by_unit(units_grad[..., :384]),
        by_unit(units_grad[..., 384:]),
        sum_down,
        sum_gains,
    )


def solution(mesh):
    chips = Mesh(mesh.devices.reshape(4, 2, 2, 4, 2), AXES)
    rows = P(AXES, None)
    tokens = P(("zl", "y", "core"), ("x", "zh"), None)
    lengths = P(("zl", "y", "core"), None)
    return jax.shard_map(
        on_device,
        mesh=chips,
        in_specs=(tokens, lengths, *([rows] * 7), P(AXES), tokens),
        out_specs=(tokens, tokens, *([rows] * 7), P(AXES)),
        check_vma=False,
    )
```

```python
import jax
import jax.numpy as jnp
from jax import lax
from jax.experimental import pallas as pl
from jax.experimental.pallas import tpu as pltpu
from jax.sharding import Mesh
from jax.sharding import PartitionSpec as P

HEADS = 16
KV_HEADS = 8
HEAD = 128
EPSILON = 1e-06
ROPE_BASE = 1000000.0
DEVICES = 128
WIDTH = 1024
FF = 3072
TOK = 192
PACK = 1536
BLOCK = 256
LOG2E = 1.4426950408889634
SCALE = HEAD ** (-0.5)
VMEM_LIMIT = 48 * 1024 * 1024

AXES = ("x", "zh", "zl", "y", "core")
RING = ("x", "core")
PLANE = ("zh", "zl", "y")
XA, XB, ZA, ZB, YA, YB, CORE = 32, 96, 8, 24, 2, 6, 1
RING_STEPS = ((XA, XB), (XB, XA))
RING_SPOTS = ((0, 1, 3, 2), (0, 2, 3, 1))
PLANE_STEPS = ((YA, ZA), (YB, ZB), (ZA, YA), (ZB, YB))
BIT = {YA: 1, YB: 2, ZA: 3, ZB: 4}


def swap(values, mask, other_mask=None):
    masks = (mask, mask if other_mask is None else other_mask)
    return lax.ppermute(values, AXES, [(k, k ^ masks[k & 1]) for k in range(DEVICES)])


def crossed(k):
    return k ^ 17 if (k >> 4 ^ k) & 1 else k


def cross(values):
    return lax.ppermute(values, AXES, [(k, crossed(k)) for k in range(DEVICES)])


def cross_and_swap(values, masks):
    return lax.ppermute(
        values, AXES, [(crossed(k ^ masks[k & 1]), k) for k in range(DEVICES)]
    )


def swap_and_cross(values, masks):
    return lax.ppermute(
        values, AXES, [(k, crossed(k ^ masks[k & 1])) for k in range(DEVICES)]
    )


def after(value, *others):
    return lax.optimization_barrier((value, *others))[0] if others else value


def low(values):
    return values.astype(jnp.bfloat16)


def wide(values):
    return values.astype(jnp.float32)


def dot(left, right):
    return jnp.dot(left, right, preferred_element_type=jnp.float32)


def contract_rows(left, right):
    return lax.dot_general(
        left, right, (((0,), (0,)), ((), ())), preferred_element_type=jnp.float32
    )


def contract_cols(left, right):
    return lax.dot_general(
        left, right, (((1,), (1,)), ((), ())), preferred_element_type=jnp.float32
    )


def norm_scale(values):
    return lax.rsqrt(jnp.mean(values * values, axis=-1, keepdims=True) + EPSILON)


def norm_back(values, gain, grad):
    scale = norm_scale(values)
    normal = values * scale
    inner = grad * gain
    return scale * (inner - normal * jnp.mean(inner * normal, axis=-1, keepdims=True))


def rope(values, cosine, sine):
    return values * cosine + pltpu.roll(values, 64, 1) * sine


def rope_back(grad, cosine, sine):
    return grad * cosine + pltpu.roll(grad * sine, 64, 1)


def ring_specs(columns):
    return [
        pl.BlockSpec((TOK, columns), lambda x, spots: (spots[x], 0)),
        pl.BlockSpec((TOK, columns), lambda x, spots: (spots[4 + x], 0)),
    ]


def pack_spec(columns):
    return pl.BlockSpec((2 * TOK, columns), lambda x, spots: (x, 0))


def whole_spec(shape):
    return pl.BlockSpec(shape, lambda x, spots: (0, 0))


def own_rows(spots):
    return pl.ds(pl.multiple_of(spots[8] * TOK, TOK), TOK)


def other_rows(spots):
    return pl.ds(pl.multiple_of((1 - spots[8]) * TOK, TOK), TOK)


def shaped(shape, dtype, kept=False):
    return pltpu.HBM(shape, dtype) if kept else jax.ShapeDtypeStruct(shape, dtype)


def in_hbm(array):
    return pltpu.with_memory_space_constraint(array, pltpu.HBM)


def cost(microseconds):
    return pl.CostEstimate(
        flops=0, bytes_accessed=int(microseconds * 3.6e6), transcendentals=0
    )


def ring_call(kernel, name, in_specs, out_specs, out_shape, time, spots, *operands, scratch=()):
    return pl.pallas_call(
        kernel,
        grid_spec=pltpu.PrefetchScalarGridSpec(
            num_scalar_prefetch=1,
            grid=(4,),
            in_specs=in_specs,
            out_specs=out_specs,
            scratch_shapes=scratch,
        ),
        out_shape=out_shape,
        compiler_params=pltpu.CompilerParams(vmem_limit_bytes=VMEM_LIMIT),
        cost_estimate=cost(time),
        name=name,
    )(spots, *operands)


def qkv_kernel(
    spots, own_ref, other_ref, heads_ref, ga_ref, gq_ref, gk_ref, cos_ref, sin_ref,
    normed_ref, pre_ref, qkv_ref, kept_ref, across_ref, w_ref,
):
    @pl.when(pl.program_id(0) == 0)
    def _():
        for z in range(4):
            for y in range(4):
                block = jnp.where(spots[9] == 1, y * 4 + z, z * 4 + y)
                for x in range(4):
                    row = (x * 16 + z * 4 + y) * 16
                    w_ref[row : row + 16, :] = heads_ref[block, x * 16 : x * 16 + 16, :512]
        across_ref[...] = w_ref[...].T

    for ref, rows in ((own_ref, own_rows(spots)), (other_ref, other_rows(spots))):
        x = wide(ref[...])
        normed_ref[rows, :] = low(x * norm_scale(x) * ga_ref[...])
    pre = dot(normed_ref[...], w_ref[...])
    pre_ref[...] = pre[:, : 3 * HEAD]
    cosine, sine = cos_ref[...], sin_ref[...]
    for h in range(3):
        u = pre[:, h * HEAD : (h + 1) * HEAD]
        gain = gk_ref[...] if h == 2 else gq_ref[...]
        normal = u * norm_scale(u) * gain
        qkv_ref[:, h * HEAD : (h + 1) * HEAD] = low(rope(normal, cosine, sine))
    qkv_ref[:, 3 * HEAD :] = low(pre[:, 3 * HEAD :])
    kept_ref[...] = qkv_ref[...]


def project(spots, own, other, heads, gain_attn, gain_query, gain_key, cosine, sine):
    return ring_call(
        qkv_kernel,
        "project",
        ring_specs(WIDTH)
        + [pl.BlockSpec(heads.shape, lambda x, spots: (0, 0, 0))]
        + [whole_spec((1, WIDTH)), whole_spec((1, HEAD)), whole_spec((1, HEAD))]
        + [pack_spec(HEAD), pack_spec(HEAD)],
        [pack_spec(WIDTH), pack_spec(3 * HEAD), pack_spec(512), pack_spec(512)]
        + [whole_spec((512, WIDTH))],
        [
            shaped((PACK, WIDTH), jnp.bfloat16, True),
            shaped((PACK, 3 * HEAD), jnp.float32, True),
            shaped((PACK, 512), jnp.bfloat16),
            shaped((PACK, 512), jnp.bfloat16, True),
            shaped((512, WIDTH), jnp.bfloat16, True),
        ],
        8, spots, own, other, heads, gain_attn, gain_query, gain_key, cosine, sine,
        scratch=[pltpu.VMEM((WIDTH, 512), jnp.bfloat16)],
    )


def to_ring_kernel(spots, rows_ref, heads_ref, own_ref, other_ref, w_ref):
    @pl.when(pl.program_id(0) == 0)
    def _():
        for z in range(4):
            for y in range(4):
                block = jnp.where(spots[9] == 1, y * 4 + z, z * 4 + y)
                row = (z % 2 * 8 + y * 2 + z // 2) * 16
                for n in range(4):
                    piece = heads_ref[block, n * 16 : n * 16 + 16, 640:]
                    w_ref[row : row + 16, n * 256 : n * 256 + 256] = piece

    own_ref[...] = low(dot(rows_ref[own_rows(spots), :], w_ref[...]))
    other_ref[...] = low(dot(rows_ref[other_rows(spots), :], w_ref[...]))


def to_ring(spots, rows, heads):
    half = shaped((PACK // 2, WIDTH), jnp.bfloat16)
    return ring_call(
        to_ring_kernel, "to_ring",
        [pack_spec(256), pl.BlockSpec(heads.shape, lambda x, spots: (0, 0, 0))],
        ring_specs(WIDTH) + [whole_spec((256, WIDTH))],
        [half, half, shaped((256, WIDTH), jnp.bfloat16, True)], 3, spots, rows, heads,
    )


def to_pack_kernel(spots, own_ref, other_ref, w_ref, rows_ref):
    rows_ref[own_rows(spots), :] = low(dot(own_ref[...], w_ref[...]))
    rows_ref[other_rows(spots), :] = low(dot(other_ref[...], w_ref[...]))


def to_pack(spots, own, other, weights):
    return ring_call(
        to_pack_kernel, "to_pack", ring_specs(own.shape[1]) + [whole_spec(weights.shape)],
        [pack_spec(WIDTH)], [shaped((PACK, WIDTH), jnp.bfloat16)], 4, spots, own, other, weights,
    )[0]


def out_back_kernel(
    spots, own_ref, other_ref, attended_ref, w_ref, d_attended_ref, d_w_ref, rows_ref, total_ref
):
    step = pl.program_id(0)

    @pl.when(step == 0)
    def _():
        total_ref[...] = jnp.zeros_like(total_ref)

    rows_ref[own_rows(spots), :] = own_ref[...]
    rows_ref[other_rows(spots), :] = other_ref[...]
    d_attended_ref[...] = low(contract_cols(rows_ref[...], w_ref[...]))
    total_ref[...] += contract_rows(attended_ref[...], rows_ref[...])

    @pl.when(step == pl.num_programs(0) - 1)
    def _():
        d_w_ref[...] = low(total_ref[...])


def out_back(spots, own, other, attended, weights):
    return ring_call(
        out_back_kernel, "out_back",
        ring_specs(WIDTH) + [pack_spec(256), whole_spec((256, WIDTH))],
        [pack_spec(256), whole_spec((256, WIDTH))],
        [shaped((PACK, 256), jnp.bfloat16), shaped((256, WIDTH), jnp.bfloat16, True)],
        5, spots, own, other, in_hbm(attended), in_hbm(weights),
        scratch=[pltpu.VMEM((2 * TOK, WIDTH), jnp.bfloat16), pltpu.VMEM((256, WIDTH), jnp.float32)],
    )


def row_start(rows, ends):
    first, second = ends
    return jnp.where(rows >= second, second, jnp.where(rows >= first, first, 0))


def block_mask(q_block, k_block, ends, transposed):
    last = PACK // BLOCK - 1
    q_axis, k_axis = (1, 0) if transposed else (0, 1)
    q_rows = q_block * BLOCK + lax.broadcasted_iota(jnp.int32, (BLOCK, BLOCK), q_axis)
    k_rows = k_block * BLOCK + lax.broadcasted_iota(jnp.int32, (BLOCK, BLOCK), k_axis)
    mask = None
    if k_block == q_block:
        mask = k_rows <= q_rows
    if k_block == 0 or q_block == last:
        begun = k_rows >= row_start(q_rows, ends)
        mask = begun if mask is None else mask & begun
    return mask


def for_each_block(step):
    for q_block in range(PACK // BLOCK):

        @pl.when(pl.program_id(0) == q_block)
        def _(q_block=q_block):
            step(q_block)


def attend_kernel(ends_ref, q_ref, k_ref, v_ref, out_ref, kept_ref, inverse_ref):
    ends = (ends_ref[0], ends_ref[1])

    def step(q_block):
        seen = (q_block + 1) * BLOCK
        for h in range(2):
            columns = slice(h * HEAD, (h + 1) * HEAD)
            scores = contract_cols(q_ref[:, columns], k_ref[:seen, :])
            part, shifted = 0.0, []
            for k_block in range(q_block + 1):
                block = scores[:, k_block * BLOCK : (k_block + 1) * BLOCK]
                block = jnp.exp2(block * (SCALE * LOG2E))
                mask = block_mask(q_block, k_block, ends, False)
                if mask is not None:
                    block = jnp.where(mask, block, 0.0)
                part += block[:, :HEAD] + block[:, HEAD:]
                shifted.append(low(block))
            total = dot(jnp.concatenate(shifted, axis=1), v_ref[:seen, :])
            row_total = jnp.sum(part, axis=1, keepdims=True)
            out_ref[:, columns] = low(total * (1.0 / row_total))
            across = jnp.sum(jnp.swapaxes(part, 0, 1), axis=0, keepdims=True)
            inverse_ref[h : h + 1, :] = 1.0 / across
        kept_ref[...] = out_ref[...]

    for_each_block(step)


def attend(ends, qkv):
    return pl.pallas_call(
        attend_kernel,
        grid_spec=pltpu.PrefetchScalarGridSpec(
            num_scalar_prefetch=1,
            grid=(PACK // BLOCK,),
            in_specs=[
                pl.BlockSpec((BLOCK, 2 * HEAD), lambda q, ends: (q, 0)),
                pl.BlockSpec((PACK, HEAD), lambda q, ends: (0, 2)),
                pl.BlockSpec((PACK, HEAD), lambda q, ends: (0, 3)),
            ],
            out_specs=[
                pl.BlockSpec((BLOCK, 2 * HEAD), lambda q, ends: (q, 0)),
                pl.BlockSpec((BLOCK, 2 * HEAD), lambda q, ends: (q, 0)),
                pl.BlockSpec((2, BLOCK), lambda q, ends: (0, q)),
            ],
        ),
        out_shape=[
            shaped((PACK, 2 * HEAD), jnp.bfloat16),
            shaped((PACK, 2 * HEAD), jnp.bfloat16, True),
            shaped((2, PACK), jnp.float32, True),
        ],
        compiler_params=pltpu.CompilerParams(vmem_limit_bytes=VMEM_LIMIT),
        cost_estimate=cost(6),
        name="attend",
    )(ends, qkv, qkv, qkv)


def attend_back_kernel(
    ends_ref, q_ref, k_ref, v_ref, grad_ref, out_ref, inverse_ref, dq_ref, dk_ref, dv_ref
):
    ends = (ends_ref[0], ends_ref[1])

    @pl.when(pl.program_id(0) == 0)
    def _():
        dk_ref[...] = jnp.zeros_like(dk_ref)
        dv_ref[...] = jnp.zeros_like(dv_ref)

    def both_heads(ref):
        return jnp.concatenate([ref[:, :HEAD], ref[:, HEAD:]], axis=0)

    def step(q_block):
        seen = (q_block + 1) * BLOCK
        queries, grads = both_heads(q_ref), both_heads(grad_ref)
        product = wide(grads) * wide(both_heads(out_ref))
        delta = jnp.sum(jnp.swapaxes(product, 0, 1), axis=0, keepdims=True)
        inverse = jnp.concatenate([inverse_ref[0:1, :], inverse_ref[1:2, :]], axis=1)
        scores = contract_cols(k_ref[:seen, :], queries)
        d_probs = contract_cols(v_ref[:seen, :], grads)
        probs, d_scores = [], []
        for k_block in range(q_block + 1):
            rows = slice(k_block * BLOCK, (k_block + 1) * BLOCK)
            prob = jnp.exp2(scores[rows] * (SCALE * LOG2E)) * inverse
            mask = block_mask(q_block, k_block, ends, True)
            if mask is not None:
                prob = jnp.where(jnp.concatenate([mask, mask], axis=1), prob, 0.0)
            d_scores.append(low(prob * ((d_probs[rows] - delta) * SCALE)))
            probs.append(low(prob))
        probs = jnp.concatenate(probs, axis=0)
        d_scores = jnp.concatenate(d_scores, axis=0)
        dk_ref[:seen, :] += dot(d_scores, queries)
        dv_ref[:seen, :] += dot(probs, grads)
        d_queries = contract_rows(d_scores, k_ref[:seen, :])
        dq_ref[:, :HEAD] = d_queries[:BLOCK]
        dq_ref[:, HEAD:] = d_queries[BLOCK:]

    for_each_block(step)


def attend_back(ends, qkv, grad, out, inverse):
    qkv, out, inverse = in_hbm(qkv), in_hbm(out), in_hbm(inverse)
    by_block = pl.BlockSpec((BLOCK, 2 * HEAD), lambda q, ends: (q, 0))
    whole = pl.BlockSpec((PACK, HEAD), lambda q, ends: (0, 0))
    return pl.pallas_call(
        attend_back_kernel,
        grid_spec=pltpu.PrefetchScalarGridSpec(
            num_scalar_prefetch=1,
            grid=(PACK // BLOCK,),
            in_specs=[
                by_block,
                pl.BlockSpec((PACK, HEAD), lambda q, ends: (0, 2)),
                pl.BlockSpec((PACK, HEAD), lambda q, ends: (0, 3)),
                by_block,
                by_block,
                pl.BlockSpec((2, BLOCK), lambda q, ends: (0, q)),
            ],
            out_specs=[by_block, whole, whole],
        ),
        out_shape=[
            jax.ShapeDtypeStruct((PACK, 2 * HEAD), jnp.float32),
            jax.ShapeDtypeStruct((PACK, HEAD), jnp.float32),
            jax.ShapeDtypeStruct((PACK, HEAD), jnp.float32),
        ],
        compiler_params=pltpu.CompilerParams(vmem_limit_bytes=VMEM_LIMIT),
        cost_estimate=cost(11),
        name="attend_back",
    )(ends, qkv, qkv, qkv, grad, out, inverse)


def qkv_back_kernel(
    spots, pre_ref, dq_ref, dk_ref, dv_ref, cos_ref, sin_ref, normed_ref, w_ref, gq_ref, gk_ref,
    d_pre_ref, d_attn_ref, d_head_ref, own_ref, other_ref, rows_ref,
):
    @pl.when(pl.program_id(0) == 0)
    def _():
        d_attn_ref[...] = jnp.zeros_like(d_attn_ref)
        d_head_ref[...] = jnp.zeros_like(d_head_ref)

    cosine, sine = cos_ref[...], sin_ref[...]
    for h in range(3):
        u = pre_ref[:, h * HEAD : (h + 1) * HEAD]
        gain = gk_ref[...] if h == 2 else gq_ref[...]
        grad = dk_ref[...] if h == 2 else dq_ref[:, h * HEAD : (h + 1) * HEAD]
        grad = rope_back(grad, cosine, sine)
        row = 1 if h == 2 else 0
        d_head_ref[row : row + 1, :] += jnp.sum(
            grad * u * norm_scale(u), axis=0, keepdims=True
        )
        d_pre_ref[:, h * HEAD : (h + 1) * HEAD] = low(norm_back(u, gain, grad))
    d_pre_ref[:, 3 * HEAD :] = low(dv_ref[...])
    d_normed = dot(d_pre_ref[...], w_ref[...])
    d_attn_ref[...] += jnp.sum(wide(normed_ref[...]) * d_normed, axis=0, keepdims=True)
    rows_ref[...] = low(d_normed)
    own_ref[...] = rows_ref[own_rows(spots), :]
    other_ref[...] = rows_ref[other_rows(spots), :]


def project_back(spots, pre, d_query, d_key, d_value, cosine, sine, normed, weights, gain_query, gain_key):
    half = shaped((PACK // 2, WIDTH), jnp.bfloat16)
    return ring_call(
        qkv_back_kernel,
        "project_back",
        [pack_spec(3 * HEAD), pack_spec(2 * HEAD), pack_spec(HEAD), pack_spec(HEAD)]
        + [pack_spec(HEAD), pack_spec(HEAD), pack_spec(WIDTH)]
        + [whole_spec((512, WIDTH)), whole_spec((1, HEAD)), whole_spec((1, HEAD))],
        [pack_spec(512), whole_spec((1, WIDTH)), whole_spec((2, HEAD))] + ring_specs(WIDTH),
        [shaped((PACK, 512), jnp.bfloat16), shaped((1, WIDTH), jnp.float32)]
        + [shaped((2, HEAD), jnp.float32), half, half],
        11, spots, in_hbm(pre), d_query, d_key, d_value, in_hbm(cosine), in_hbm(sine), in_hbm(normed),
        in_hbm(weights), gain_query, gain_key,
        scratch=[pltpu.VMEM((2 * TOK, WIDTH), jnp.bfloat16)],
    )


def plane_order(core, blocks):
    return jnp.where(core == 1, jnp.swapaxes(blocks, 0, 1), blocks)


def plane_bit(index, masks):
    return jnp.where(index & 1 == 1, index >> BIT[masks[1]], index >> BIT[masks[0]]) & 1


def gather_plane_step(index, block, step):
    got = swap(block, *PLANE_STEPS[step])
    return jnp.where(
        plane_bit(index, PLANE_STEPS[step]) == 1,
        jnp.concatenate([got, block], axis=0),
        jnp.concatenate([block, got], axis=0),
    )


def gather_plane_end(index, block):
    shape = block.shape[1:]
    return plane_order(index & 1, block.reshape((4, 4) + shape)).reshape((16,) + shape)


def scatter_plane_step(index, blocks, step, *beside):
    later = plane_bit(index, PLANE_STEPS[step])
    half = blocks.shape[0] // 2
    keep = lax.dynamic_slice_in_dim(blocks, later * half, half, axis=0)
    send = lax.dynamic_slice_in_dim(blocks, (1 - later) * half, half, axis=0)
    return low(wide(keep) + wide(after(swap(send, *PLANE_STEPS[step]), *beside)))


def plane_blocks(core, blocks):
    shape = blocks.shape[1:]
    return plane_order(core, blocks.reshape((4, 4) + shape)).reshape((16,) + shape)


def gather_ring(rows, beside=((), ())):
    for masks, others in zip(RING_STEPS, beside):
        rows = jnp.concatenate([rows, after(swap(rows, *masks), *others)], axis=0)
    return rows


def scatter_ring(own, other, steps=2):
    totals = [wide(own) + wide(swap(other, CORE))]
    for masks in RING_STEPS[: -steps - 1 : -1]:
        half = totals[-1].shape[0] // 2
        totals.append(totals[-1][:half] + wide(swap(low(totals[-1][half:]), *masks)))
    return totals


def exchange_ring(index, blocks):
    core, x = index & 1, index >> 5
    shape = blocks.shape[1:]
    blocks = blocks.reshape((4, 2) + shape)
    take = lambda array, at, axis: lax.dynamic_slice_in_dim(array, at, 1, axis)
    got = swap(take(blocks, 1 - core, 1), CORE)
    keep = take(blocks, core, 1)
    blocks = jnp.concatenate(
        [jnp.where(core == 1, got, keep), jnp.where(core == 1, keep, got)], axis=1
    )
    parts = [take(blocks, x, 0)] + [
        swap(take(blocks, x ^ k, 0), k << 5) for k in range(1, 4)
    ]
    parts = jnp.concatenate(parts, axis=0)
    parts = jnp.where(x & 1 == 1, parts.reshape((2, 2, 2) + shape)[:, ::-1].reshape(parts.shape), parts)
    parts = jnp.where(x & 2 == 2, parts.reshape((2, 4) + shape)[::-1].reshape(parts.shape), parts)
    return parts.reshape((8,) + shape)


def tiles_tall(block):
    lead = block.shape[:-2]
    n = len(lead)
    block = block.reshape(lead + (-1, 8, 8, HEAD))
    block = block.transpose(tuple(range(n)) + (n + 2, n + 1, n, n + 3))
    return block.reshape(lead + (64, -1))


def tiles_flat(block):
    lead = block.shape[:-2]
    n = len(lead)
    block = block.reshape(lead + (8, 8, -1, HEAD))
    block = block.transpose(tuple(range(n)) + (n + 2, n + 1, n, n + 3))
    return block.reshape(lead + (-1, WIDTH))


def rows_by_device(blocks):
    n = blocks.shape[-1]
    return blocks.reshape(16, 4, 2, 8, n).transpose(1, 0, 2, 3, 4).reshape(WIDTH, n)


def rows_by_plane(rows):
    n = rows.shape[-1]
    return rows.reshape(4, 16, 2, 8, n).transpose(1, 0, 2, 3, 4).reshape(16, 64, n)


def on_device(
    hidden, lengths, w_query, w_key, w_value, w_out, w_gate, w_up, w_down, gains, cotangent
):
    index = lax.axis_index(AXES).astype(jnp.int32)
    core, x = index & 1, index >> 5
    straight = (index >> 4 & 1) == core
    spot_of = lambda c: jnp.where(c == 1, jnp.asarray(RING_SPOTS[1]), jnp.asarray(RING_SPOTS[0]))
    chips = x ^ jnp.arange(4, dtype=jnp.int32)
    spots = jnp.concatenate(
        [spot_of(core)[chips], spot_of(1 - core)[chips], core[None], core[None]]
    ).astype(jnp.int32)

    local = jnp.concatenate(
        [
            w_query.reshape(8, KV_HEADS, 256).transpose(1, 0, 2),
            w_key.reshape(8, KV_HEADS, HEAD).transpose(1, 0, 2),
            w_value.reshape(8, KV_HEADS, HEAD).transpose(1, 0, 2),
            jnp.broadcast_to(jnp.pad(gains[None, None, :], ((0, 0), (0, 7), (0, 110))), (8, 8, 128)),
        ]
        + [
            weight.reshape(8, 4, 16, 2, 24).transpose(1, 3, 0, 2, 4).reshape(8, 8, 384)
            for weight in (w_gate, w_up)
        ],
        axis=2,
    )
    digits = jnp.pad(low(jnp.stack([lengths[0] // 64, lengths[0] % 64])), ((0, 14), (0, WIDTH - 3)))
    rows = after(jnp.concatenate([hidden[0], w_out, digits], axis=0), local)
    d_rows = after(cotangent[0], local)
    local = exchange_ring(index, local).reshape(64, 1408)
    first = cross(rows)
    second = cross_and_swap(rows[:TOK], RING_STEPS[0])
    d_result = cross(d_rows)
    d_result_second = cross_and_swap(d_rows, RING_STEPS[0])
    inputs = first[:TOK]
    digits = first[TOK + 16 : TOK + 18, :3].astype(jnp.int32)
    lengths = (digits[0] * 64 + digits[1])[None]
    pieces = first[TOK : TOK + 16].reshape(16, 4, 256).transpose(1, 0, 2).reshape(64, 256)
    heads = jnp.concatenate([local[:, :640], pieces], axis=1)[None]
    heads = gather_plane_step(index, heads, 0)
    second = after(second, heads)
    for step in range(1, 4):
        heads = gather_plane_step(index, heads, step)
    gain_all = plane_order(core, heads[:, ::8, 512:530].reshape(4, 4, 8, 18))
    gain_all = gain_all.reshape(16, 4, 2, 18).transpose(1, 0, 2, 3)
    gain_all = wide(gain_all.reshape(1, -1))
    gain_attn, gain_mlp = gain_all[:, :WIDTH], gain_all[:, WIDTH : 2 * WIDTH]
    gain_query = gain_all[:, 2 * WIDTH : 2 * WIDTH + HEAD]
    gain_key = gain_all[:, 2 * WIDTH + HEAD :]

    def rest_of_ring(rows):
        rows = jnp.concatenate([rows, swap(rows, *RING_STEPS[1])], axis=0)
        return rows, swap(rows, CORE)

    inputs_own, inputs_other = rest_of_ring(jnp.concatenate([inputs, second], axis=0))
    ends = jnp.stack([lengths[0, 0], lengths[0, 0] + lengths[0, 1]]).astype(jnp.int32)
    token = jnp.arange(PACK, dtype=jnp.int32)
    position = wide(token - row_start(token, (ends[0], ends[1])))
    inverse = jnp.power(ROPE_BASE, -2.0 * jnp.arange(HEAD // 2, dtype=jnp.float32) / HEAD)
    angle = position[:, None] * inverse[None, :]
    cosine, sine = jnp.cos(angle), jnp.sin(angle)
    cosine = jnp.concatenate([cosine, cosine], axis=1)
    sine = jnp.concatenate([-sine, sine], axis=1)

    d_result_own = jnp.concatenate([d_result, d_result_second], axis=0)
    d_result_own = jnp.concatenate([d_result_own, swap(d_result_own, *RING_STEPS[1])], axis=0)
    heads, d_result, d_result_second = lax.optimization_barrier((heads, d_result, d_result_second))
    normed, pre, qkv, qkv_kept, w_heads_across = project(
        spots, inputs_own, inputs_other, heads, gain_attn, gain_query, gain_key, cosine, sine
    )
    qkv, d_result_own = lax.optimization_barrier((qkv, d_result_own))
    attended, attended_kept, inverse_total = attend(ends, qkv)
    out_own, out_other, w_rows = to_ring(spots, attended, heads)
    middle_steps = scatter_ring(out_own, out_other)
    d_result_other = swap(after(d_result_own, middle_steps[0]), CORE)
    units = jnp.concatenate([local[:, 640:], tiles_tall(w_down)], axis=1)[None]
    units = gather_plane_step(index, after(units, out_own), 0)
    units = gather_plane_step(index, after(units, middle_steps[0]), 1)
    units = gather_plane_step(index, after(units, middle_steps[1]), 2)
    middle = wide(inputs) + middle_steps[2]
    middle_scale = norm_scale(middle)
    mixed = low(middle * middle_scale * gain_mlp)
    mixed_own = gather_ring(mixed)
    mixed_other = swap(mixed_own, CORE)
    units = gather_plane_step(index, units, 3)
    units = plane_blocks(core, units)
    full_units = rows_by_device(units[..., :768])
    full_down = tiles_flat(units[..., 768:]).reshape(384, WIDTH)
    full_units, full_down = lax.optimization_barrier((full_units, full_down))

    def feed_forward(rows, d_rows):
        pre = dot(rows, full_units)
        gate_pre, up_pre = pre[:, :384], pre[:, 384:]
        sigmoid = 1.0 / (1.0 + jnp.exp(-gate_pre))
        silu = gate_pre * sigmoid
        act = low(silu * up_pre)
        d_act = contract_cols(d_rows, full_down)
        d_gate = low(d_act * up_pre * (sigmoid + silu * (1.0 - sigmoid)))
        d_up = low(d_act * silu)
        d_pre = jnp.concatenate([d_gate, d_up], axis=1)
        return act, d_pre, low(contract_cols(d_pre, full_units))

    act_own, d_pre_own, d_mixed_own = feed_forward(mixed_own, d_result_own)
    act_other, d_pre_other, d_mixed_other = feed_forward(mixed_other, d_result_other)
    d_mixed_steps = scatter_ring(d_mixed_own, d_mixed_other)
    d_mixed = d_mixed_steps[-1]
    d_middle = wide(d_result) + norm_back(middle, gain_mlp, d_mixed)
    d_gain_mlp = jnp.sum(middle * middle_scale * d_mixed, axis=0)

    late = lambda array: after(array, d_mixed_steps[0])
    grad_units = contract_rows(mixed_own, late(d_pre_own)) + contract_rows(mixed_other, late(d_pre_other))
    grad_down = contract_rows(late(act_own), d_result_own) + contract_rows(late(act_other), d_result_other)
    grad_down = low(grad_down).reshape(16, 3, 8, 8, HEAD).transpose(0, 3, 2, 1, 4)
    grads = jnp.concatenate([rows_by_plane(low(grad_units)), grad_down.reshape(16, 64, 384)], axis=2)
    grads = plane_blocks(core, grads)
    act_own, act_other = (after(act, d_middle) for act in (act_own, act_other))
    result = to_pack(spots, act_own, act_other, full_down)
    d_branch_own = gather_ring(after(low(d_middle), grads), ((), (result,)))
    sums = scatter_plane_step(index, grads, 3, d_branch_own)
    d_branch_other = swap(d_branch_own, CORE)
    result = lax.psum_scatter(after(result, d_branch_own), RING, scatter_dimension=0, tiled=True)
    d_middle_home = jnp.where(straight, d_middle, wide(cross(after(low(d_middle), d_branch_own))))

    d_attended, grad_out = out_back(spots, d_branch_own, d_branch_other, attended_kept, w_rows)
    d_query, d_key, d_value = attend_back(ends, qkv_kept, d_attended, attended_kept, inverse_total)
    sums = scatter_plane_step(index, sums, 2, d_query)
    grad_out = grad_out.reshape(8, 2, 16, 4, 256).transpose(1, 0, 3, 2, 4).reshape(16, 64, 256)
    grad_out = plane_blocks(core, grad_out)
    d_query, sums, grad_out = lax.optimization_barrier((d_query, sums, grad_out))
    d_pre, d_gain_attn, d_gain_heads, d_normed_own, d_normed_other = project_back(
        spots, pre, d_query, d_key, d_value, cosine, sine, normed, w_heads_across, gain_query, gain_key
    )
    d_normed_steps = scatter_ring(d_normed_own, d_normed_other, 1)
    halves = low(d_normed_steps[1][:TOK]), low(d_normed_steps[1][TOK:])
    d_normed = wide(cross(halves[0])) + wide(swap_and_cross(halves[1], RING_STEPS[0]))
    input_grad = d_middle_home + norm_back(wide(hidden[0]), gain_attn, d_normed)

    d_gains = jnp.concatenate(
        [(d_gain_attn / gain_attn)[0], d_gain_mlp, d_gain_heads.reshape(-1)]
    )
    d_gains = d_gains.reshape(4, 16, 2, 1, 18).transpose(1, 0, 2, 3, 4)
    payload = jnp.concatenate(
        [
            rows_by_plane(low(contract_rows(normed, d_pre))),
            low(jnp.pad(d_gains, ((0, 0),) * 3 + ((0, 7), (0, 110)))).reshape(16, 64, 128),
        ],
        axis=2,
    )
    heads_sums = jnp.concatenate([plane_blocks(core, payload), grad_out], axis=2)
    heads_sums = scatter_plane_step(index, heads_sums, 3, d_normed_steps[0])
    sums = scatter_plane_step(index, sums, 1, d_normed_steps[0])
    sums = scatter_plane_step(index, sums, 0)[0]
    for step in (2, 1, 0):
        heads_sums = scatter_plane_step(index, heads_sums, step)
    ring_grads = jnp.concatenate([heads_sums[0, :, :640], sums[:, :768]], axis=1)
    ring_grads = exchange_ring(index, ring_grads.reshape(8, 8, 1408))
    heads_grad, units_grad = wide(ring_grads[..., :640]), ring_grads[..., 640:]
    sum_down = wide(tiles_flat(sums[:, 768:]))
    sum_out = heads_sums[0, :, 640:].reshape(4, 16, 256).transpose(1, 0, 2).reshape(16, WIDTH)
    sum_out = wide(sum_out)
    sum_out = jnp.where(straight, sum_out, wide(cross(low(sum_out))))
    activations = cross(after(low(middle + wide(result)), d_normed_steps[0]))
    column = jnp.arange(768, dtype=jnp.int32)
    column = column // 24 % 2 * 384 + column // 48 * 24 + column % 24
    column = after(column, middle)
    hits = lax.broadcasted_iota(jnp.int32, (768, 768), 0) == column[None, :]
    units_grad = units_grad.reshape(4, 2, 8, 2, 384).transpose(3, 2, 0, 1, 4).reshape(64, 768)
    units_grad = dot(units_grad, hits.astype(jnp.bfloat16)).reshape(2, 8, FF)
    sum_query = heads_grad[..., :256].transpose(1, 0, 2).reshape(8, -1)
    sum_key = heads_grad[..., 256:384].transpose(1, 0, 2).reshape(8, -1)
    sum_value = heads_grad[..., 384:512].transpose(1, 0, 2).reshape(8, -1)
    sum_gains = jnp.sum(heads_grad[:, 0, 512:530], axis=0)
    return (
        activations[None],
        input_grad[None],
        sum_query,
        sum_key,
        sum_value,
        sum_out,
        units_grad[0],
        units_grad[1],
        sum_down,
        sum_gains,
    )


def solution(mesh):
    chips = Mesh(mesh.devices.reshape(4, 2, 2, 4, 2), AXES)
    rows = P(AXES, None)
    tokens = P(("zl", "y", "core"), ("x", "zh"), None)
    lengths = P(("zl", "y", "core"), None)
    return jax.shard_map(
        on_device,
        mesh=chips,
        in_specs=(tokens, lengths, *([rows] * 7), P(AXES), tokens),
        out_specs=(tokens, tokens, *([rows] * 7), P(AXES)),
        check_vma=False,
    )
```

```python
import jax
import jax.numpy as jnp
from jax import lax
from jax.experimental import pallas as pl
from jax.experimental.pallas import tpu as pltpu
from jax.sharding import Mesh
from jax.sharding import PartitionSpec as P

HEADS = 16
KV_HEADS = 8
HEAD = 128
EPSILON = 1e-06
ROPE_BASE = 1000000.0
DEVICES = 128
WIDTH = 1024
FF = 3072
TOK = 192
PACK = 1536
BLOCK = 256
LOG2E = 1.4426950408889634
SCALE = HEAD ** (-0.5)
VMEM_LIMIT = 48 * 1024 * 1024

AXES = ("x", "zh", "zl", "y", "core")
RING = ("x", "core")
PLANE = ("zh", "zl", "y")
XA, XB, ZA, ZB, YA, YB, CORE = 32, 96, 8, 24, 2, 6, 1
RING_STEPS = ((XA, XB), (XB, XA))
RING_SPOTS = ((0, 1, 3, 2), (0, 2, 3, 1))
PLANE_STEPS = ((YA, ZA), (YB, ZB), (ZA, YA), (ZB, YB))
BIT = {YA: 1, YB: 2, ZA: 3, ZB: 4}


def swap(values, mask, other_mask=None):
    masks = (mask, mask if other_mask is None else other_mask)
    return lax.ppermute(values, AXES, [(k, k ^ masks[k & 1]) for k in range(DEVICES)])


def crossed(k):
    return k ^ 17 if (k >> 4 ^ k) & 1 else k


def cross(values):
    return lax.ppermute(values, AXES, [(k, crossed(k)) for k in range(DEVICES)])


def cross_and_swap(values, masks):
    return lax.ppermute(
        values, AXES, [(crossed(k ^ masks[k & 1]), k) for k in range(DEVICES)]
    )


def after(value, *others):
    return lax.optimization_barrier((value, *others))[0] if others else value


def low(values):
    return values.astype(jnp.bfloat16)


def wide(values):
    return values.astype(jnp.float32)


def dot(left, right):
    return jnp.dot(left, right, preferred_element_type=jnp.float32)


def contract_rows(left, right):
    return lax.dot_general(
        left, right, (((0,), (0,)), ((), ())), preferred_element_type=jnp.float32
    )


def contract_cols(left, right):
    return lax.dot_general(
        left, right, (((1,), (1,)), ((), ())), preferred_element_type=jnp.float32
    )


def norm_scale(values):
    return lax.rsqrt(jnp.mean(values * values, axis=-1, keepdims=True) + EPSILON)


def norm_back(values, gain, grad):
    scale = norm_scale(values)
    normal = values * scale
    inner = grad * gain
    return scale * (inner - normal * jnp.mean(inner * normal, axis=-1, keepdims=True))


def rope(values, cosine, sine):
    return values * cosine + pltpu.roll(values, 64, 1) * sine


def rope_back(grad, cosine, sine):
    return grad * cosine + pltpu.roll(grad * sine, 64, 1)


def ring_specs(columns):
    return [
        pl.BlockSpec((TOK, columns), lambda x, spots: (spots[x], 0)),
        pl.BlockSpec((TOK, columns), lambda x, spots: (spots[4 + x], 0)),
    ]


def pack_spec(columns):
    return pl.BlockSpec((2 * TOK, columns), lambda x, spots: (x, 0))


def whole_spec(shape):
    return pl.BlockSpec(shape, lambda x, spots: (0, 0))


def own_rows(spots):
    return pl.ds(pl.multiple_of(spots[8] * TOK, TOK), TOK)


def other_rows(spots):
    return pl.ds(pl.multiple_of((1 - spots[8]) * TOK, TOK), TOK)


def shaped(shape, dtype, kept=False):
    return pltpu.HBM(shape, dtype) if kept else jax.ShapeDtypeStruct(shape, dtype)


def in_hbm(array):
    return pltpu.with_memory_space_constraint(array, pltpu.HBM)


def cost(microseconds):
    return pl.CostEstimate(
        flops=0, bytes_accessed=int(microseconds * 0.1e6), transcendentals=0
    )


def ring_call(kernel, name, in_specs, out_specs, out_shape, time, spots, *operands, scratch=()):
    return pl.pallas_call(
        kernel,
        grid_spec=pltpu.PrefetchScalarGridSpec(
            num_scalar_prefetch=1,
            grid=(4,),
            in_specs=in_specs,
            out_specs=out_specs,
            scratch_shapes=scratch,
        ),
        out_shape=out_shape,
        compiler_params=pltpu.CompilerParams(vmem_limit_bytes=VMEM_LIMIT),
        cost_estimate=cost(time),
        name=name,
    )(spots, *operands)


def qkv_kernel(
    spots, own_ref, other_ref, heads_ref, ga_ref, gq_ref, gk_ref, cos_ref, sin_ref,
    normed_ref, pre_ref, qkv_ref, kept_ref, across_ref, w_ref,
):
    @pl.when(pl.program_id(0) == 0)
    def _():
        for z in range(4):
            for y in range(4):
                block = jnp.where(spots[9] == 1, y * 4 + z, z * 4 + y)
                for x in range(4):
                    row = (x * 16 + z * 4 + y) * 16
                    w_ref[row : row + 16, :] = heads_ref[block, x * 16 : x * 16 + 16, :512]
        across_ref[...] = w_ref[...].T

    for ref, rows in ((own_ref, own_rows(spots)), (other_ref, other_rows(spots))):
        x = wide(ref[...])
        normed_ref[rows, :] = low(x * norm_scale(x) * ga_ref[...])
    pre = dot(normed_ref[...], w_ref[...])
    pre_ref[...] = pre[:, : 3 * HEAD]
    cosine, sine = cos_ref[...], sin_ref[...]
    for h in range(3):
        u = pre[:, h * HEAD : (h + 1) * HEAD]
        gain = gk_ref[...] if h == 2 else gq_ref[...]
        normal = u * norm_scale(u) * gain
        qkv_ref[:, h * HEAD : (h + 1) * HEAD] = low(rope(normal, cosine, sine))
    qkv_ref[:, 3 * HEAD :] = low(pre[:, 3 * HEAD :])
    kept_ref[...] = qkv_ref[...]


def project(spots, own, other, heads, gain_attn, gain_query, gain_key, cosine, sine):
    return ring_call(
        qkv_kernel,
        "project",
        ring_specs(WIDTH)
        + [pl.BlockSpec(heads.shape, lambda x, spots: (0, 0, 0))]
        + [whole_spec((1, WIDTH)), whole_spec((1, HEAD)), whole_spec((1, HEAD))]
        + [pack_spec(HEAD), pack_spec(HEAD)],
        [pack_spec(WIDTH), pack_spec(3 * HEAD), pack_spec(512), pack_spec(512)]
        + [whole_spec((512, WIDTH)), whole_spec((WIDTH, 512))],
        [
            shaped((PACK, WIDTH), jnp.bfloat16, True),
            shaped((PACK, 3 * HEAD), jnp.float32, True),
            shaped((PACK, 512), jnp.bfloat16),
            shaped((PACK, 512), jnp.bfloat16, True),
            shaped((512, WIDTH), jnp.bfloat16, True),
            shaped((WIDTH, 512), jnp.bfloat16, True),
        ],
        8, spots, own, other, heads, gain_attn, gain_query, gain_key, cosine, sine,
    )


def to_ring_kernel(spots, rows_ref, heads_ref, own_ref, other_ref, w_ref):
    @pl.when(pl.program_id(0) == 0)
    def _():
        for z in range(4):
            for y in range(4):
                block = jnp.where(spots[9] == 1, y * 4 + z, z * 4 + y)
                row = (z % 2 * 8 + y * 2 + z // 2) * 16
                for n in range(4):
                    piece = heads_ref[block, n * 16 : n * 16 + 16, 640:]
                    w_ref[row : row + 16, n * 256 : n * 256 + 256] = piece

    own_ref[...] = low(dot(rows_ref[own_rows(spots), :], w_ref[...]))
    other_ref[...] = low(dot(rows_ref[other_rows(spots), :], w_ref[...]))


def to_ring(spots, rows, heads):
    half = shaped((PACK // 2, WIDTH), jnp.bfloat16)
    return ring_call(
        to_ring_kernel, "to_ring",
        [pack_spec(256), pl.BlockSpec(heads.shape, lambda x, spots: (0, 0, 0))],
        ring_specs(WIDTH) + [whole_spec((256, WIDTH))],
        [half, half, shaped((256, WIDTH), jnp.bfloat16, True)], 3, spots, rows, heads,
    )


def to_pack_kernel(spots, own_ref, other_ref, w_ref, rows_ref):
    rows_ref[own_rows(spots), :] = low(dot(own_ref[...], w_ref[...]))
    rows_ref[other_rows(spots), :] = low(dot(other_ref[...], w_ref[...]))


def to_pack(spots, own, other, weights):
    return ring_call(
        to_pack_kernel, "to_pack", ring_specs(own.shape[1]) + [whole_spec(weights.shape)],
        [pack_spec(WIDTH)], [shaped((PACK, WIDTH), jnp.bfloat16)], 4, spots, own, other, weights,
    )[0]


def out_back_kernel(
    spots, own_ref, other_ref, attended_ref, w_ref, d_attended_ref, d_w_ref, rows_ref, total_ref
):
    step = pl.program_id(0)

    @pl.when(step == 0)
    def _():
        total_ref[...] = jnp.zeros_like(total_ref)

    rows_ref[own_rows(spots), :] = own_ref[...]
    rows_ref[other_rows(spots), :] = other_ref[...]
    d_attended_ref[...] = low(contract_cols(rows_ref[...], w_ref[...]))
    total_ref[...] += contract_rows(attended_ref[...], rows_ref[...])

    @pl.when(step == pl.num_programs(0) - 1)
    def _():
        for block in range(16):
            row = (block % 8 * 2 + block // 8) * 16
            for n in range(4):
                piece = total_ref[row : row + 16, n * 256 : n * 256 + 256]
                d_w_ref[block, n * 16 : n * 16 + 16, :] = low(piece)


def out_back(spots, own, other, attended, weights):
    return ring_call(
        out_back_kernel, "out_back",
        ring_specs(WIDTH) + [pack_spec(256), whole_spec((256, WIDTH))],
        [pack_spec(256), pl.BlockSpec((16, 64, 256), lambda x, spots: (0, 0, 0))],
        [shaped((PACK, 256), jnp.bfloat16), shaped((16, 64, 256), jnp.bfloat16, True)],
        5, spots, own, other, in_hbm(attended), in_hbm(weights),
        scratch=[pltpu.VMEM((2 * TOK, WIDTH), jnp.bfloat16), pltpu.VMEM((256, WIDTH), jnp.float32)],
    )


def row_start(rows, ends):
    first, second = ends
    return jnp.where(rows >= second, second, jnp.where(rows >= first, first, 0))


def block_mask(q_block, k_block, ends, transposed):
    last = PACK // BLOCK - 1
    q_axis, k_axis = (1, 0) if transposed else (0, 1)
    q_rows = q_block * BLOCK + lax.broadcasted_iota(jnp.int32, (BLOCK, BLOCK), q_axis)
    k_rows = k_block * BLOCK + lax.broadcasted_iota(jnp.int32, (BLOCK, BLOCK), k_axis)
    mask = None
    if k_block == q_block:
        mask = k_rows <= q_rows
    if k_block == 0 or q_block == last:
        begun = k_rows >= row_start(q_rows, ends)
        mask = begun if mask is None else mask & begun
    return mask


def for_each_block(step):
    for q_block in range(PACK // BLOCK):

        @pl.when(pl.program_id(0) == q_block)
        def _(q_block=q_block):
            step(q_block)


def attend_kernel(ends_ref, q_ref, k_ref, v_ref, out_ref, kept_ref, inverse_ref):
    ends = (ends_ref[0], ends_ref[1])

    def step(q_block):
        seen = (q_block + 1) * BLOCK
        for h in range(2):
            columns = slice(h * HEAD, (h + 1) * HEAD)
            scores = contract_cols(q_ref[:, columns], k_ref[:seen, :])
            part, shifted = 0.0, []
            for k_block in range(q_block + 1):
                block = scores[:, k_block * BLOCK : (k_block + 1) * BLOCK]
                block = jnp.exp2(block * (SCALE * LOG2E))
                mask = block_mask(q_block, k_block, ends, False)
                if mask is not None:
                    block = jnp.where(mask, block, 0.0)
                part += block[:, :HEAD] + block[:, HEAD:]
                shifted.append(low(block))
            total = dot(jnp.concatenate(shifted, axis=1), v_ref[:seen, :])
            row_total = jnp.sum(part, axis=1, keepdims=True)
            out_ref[:, columns] = low(total * (1.0 / row_total))
            across = jnp.sum(jnp.swapaxes(part, 0, 1), axis=0, keepdims=True)
            inverse_ref[h : h + 1, :] = 1.0 / across
        kept_ref[...] = out_ref[...]

    for_each_block(step)


def attend(ends, qkv):
    return pl.pallas_call(
        attend_kernel,
        grid_spec=pltpu.PrefetchScalarGridSpec(
            num_scalar_prefetch=1,
            grid=(PACK // BLOCK,),
            in_specs=[
                pl.BlockSpec((BLOCK, 2 * HEAD), lambda q, ends: (q, 0)),
                pl.BlockSpec((PACK, HEAD), lambda q, ends: (0, 2)),
                pl.BlockSpec((PACK, HEAD), lambda q, ends: (0, 3)),
            ],
            out_specs=[
                pl.BlockSpec((BLOCK, 2 * HEAD), lambda q, ends: (q, 0)),
                pl.BlockSpec((BLOCK, 2 * HEAD), lambda q, ends: (q, 0)),
                pl.BlockSpec((2, BLOCK), lambda q, ends: (0, q)),
            ],
        ),
        out_shape=[
            shaped((PACK, 2 * HEAD), jnp.bfloat16),
            shaped((PACK, 2 * HEAD), jnp.bfloat16, True),
            shaped((2, PACK), jnp.float32, True),
        ],
        compiler_params=pltpu.CompilerParams(vmem_limit_bytes=VMEM_LIMIT),
        cost_estimate=cost(6),
        name="attend",
    )(ends, qkv, qkv, qkv)


def attend_back_kernel(
    ends_ref, q_ref, k_ref, v_ref, grad_ref, out_ref, inverse_ref, dq_ref, dk_ref, dv_ref
):
    ends = (ends_ref[0], ends_ref[1])

    @pl.when(pl.program_id(0) == 0)
    def _():
        dk_ref[...] = jnp.zeros_like(dk_ref)
        dv_ref[...] = jnp.zeros_like(dv_ref)

    def both_heads(ref):
        return jnp.concatenate([ref[:, :HEAD], ref[:, HEAD:]], axis=0)

    def step(q_block):
        seen = (q_block + 1) * BLOCK
        queries, grads = both_heads(q_ref), both_heads(grad_ref)
        product = wide(grads) * wide(both_heads(out_ref))
        delta = jnp.sum(jnp.swapaxes(product, 0, 1), axis=0, keepdims=True)
        inverse = jnp.concatenate([inverse_ref[0:1, :], inverse_ref[1:2, :]], axis=1)
        scores = contract_cols(k_ref[:seen, :], queries)
        d_probs = contract_cols(v_ref[:seen, :], grads)
        probs, d_scores = [], []
        for k_block in range(q_block + 1):
            rows = slice(k_block * BLOCK, (k_block + 1) * BLOCK)
            prob = jnp.exp2(scores[rows] * (SCALE * LOG2E)) * inverse
            mask = block_mask(q_block, k_block, ends, True)
            if mask is not None:
                prob = jnp.where(jnp.concatenate([mask, mask], axis=1), prob, 0.0)
            d_scores.append(low(prob * ((d_probs[rows] - delta) * SCALE)))
            probs.append(low(prob))
        probs = jnp.concatenate(probs, axis=0)
        d_scores = jnp.concatenate(d_scores, axis=0)
        dk_ref[:seen, :] += dot(d_scores, queries)
        dv_ref[:seen, :] += dot(probs, grads)
        d_queries = contract_rows(d_scores, k_ref[:seen, :])
        dq_ref[:, :HEAD] = d_queries[:BLOCK]
        dq_ref[:, HEAD:] = d_queries[BLOCK:]

    for_each_block(step)


def attend_back(ends, qkv, grad, out, inverse):
    qkv, out, inverse = in_hbm(qkv), in_hbm(out), in_hbm(inverse)
    by_block = pl.BlockSpec((BLOCK, 2 * HEAD), lambda q, ends: (q, 0))
    whole = pl.BlockSpec((PACK, HEAD), lambda q, ends: (0, 0))
    return pl.pallas_call(
        attend_back_kernel,
        grid_spec=pltpu.PrefetchScalarGridSpec(
            num_scalar_prefetch=1,
            grid=(PACK // BLOCK,),
            in_specs=[
                by_block,
                pl.BlockSpec((PACK, HEAD), lambda q, ends: (0, 2)),
                pl.BlockSpec((PACK, HEAD), lambda q, ends: (0, 3)),
                by_block,
                by_block,
                pl.BlockSpec((2, BLOCK), lambda q, ends: (0, q)),
            ],
            out_specs=[by_block, whole, whole],
        ),
        out_shape=[
            jax.ShapeDtypeStruct((PACK, 2 * HEAD), jnp.float32),
            jax.ShapeDtypeStruct((PACK, HEAD), jnp.float32),
            jax.ShapeDtypeStruct((PACK, HEAD), jnp.float32),
        ],
        compiler_params=pltpu.CompilerParams(vmem_limit_bytes=VMEM_LIMIT),
        cost_estimate=cost(11),
        name="attend_back",
    )(ends, qkv, qkv, qkv, grad, out, inverse)


def qkv_back_kernel(
    spots, pre_ref, dq_ref, dk_ref, dv_ref, cos_ref, sin_ref, gq_ref, gk_ref, d_pre_ref, d_head_ref
):
    @pl.when(pl.program_id(0) == 0)
    def _():
        d_head_ref[...] = jnp.zeros_like(d_head_ref)

    cosine, sine = cos_ref[...], sin_ref[...]
    for h in range(3):
        u = pre_ref[:, h * HEAD : (h + 1) * HEAD]
        gain = gk_ref[...] if h == 2 else gq_ref[...]
        grad = dk_ref[...] if h == 2 else dq_ref[:, h * HEAD : (h + 1) * HEAD]
        grad = rope_back(grad, cosine, sine)
        row = 1 if h == 2 else 0
        scale = norm_scale(u)
        normal = u * scale
        d_head_ref[row : row + 1, :] += jnp.sum(grad * normal, axis=0, keepdims=True)
        inner = grad * gain
        inner = scale * (inner - normal * jnp.mean(inner * normal, axis=-1, keepdims=True))
        d_pre_ref[:, h * HEAD : (h + 1) * HEAD] = low(inner)
    d_pre_ref[:, 3 * HEAD :] = low(dv_ref[...])


def project_back(spots, pre, d_query, d_key, d_value, cosine, sine, gain_query, gain_key):
    return ring_call(
        qkv_back_kernel,
        "project_back",
        [pack_spec(3 * HEAD), pack_spec(2 * HEAD), pack_spec(HEAD), pack_spec(HEAD)]
        + [pack_spec(HEAD), pack_spec(HEAD), whole_spec((1, HEAD)), whole_spec((1, HEAD))],
        [pack_spec(512), whole_spec((2, HEAD))],
        [shaped((PACK, 512), jnp.bfloat16), shaped((2, HEAD), jnp.float32)],
        5, spots, in_hbm(pre), d_query, d_key, d_value, in_hbm(cosine), in_hbm(sine), gain_query, gain_key,
    )


def normed_back_kernel(spots, d_pre_ref, w_ref, own_ref, other_ref):
    own_ref[...] = low(dot(d_pre_ref[own_rows(spots), :], w_ref[...]))
    other_ref[...] = low(dot(d_pre_ref[other_rows(spots), :], w_ref[...]))


def normed_back(spots, d_pre, weights):
    half = shaped((PACK // 2, WIDTH), jnp.bfloat16)
    return ring_call(
        normed_back_kernel, "normed_back", [pack_spec(512), whole_spec((512, WIDTH))], ring_specs(WIDTH),
        [half, half], 4, spots, d_pre, in_hbm(weights),
    )


def plane_order(core, blocks):
    return jnp.where(core == 1, jnp.swapaxes(blocks, 0, 1), blocks)


def plane_bit(index, masks):
    return jnp.where(index & 1 == 1, index >> BIT[masks[1]], index >> BIT[masks[0]]) & 1


def gather_plane_step(index, block, step):
    got = swap(block, *PLANE_STEPS[step])
    return jnp.where(
        plane_bit(index, PLANE_STEPS[step]) == 1,
        jnp.concatenate([got, block], axis=0),
        jnp.concatenate([block, got], axis=0),
    )


def gather_plane_end(index, block):
    shape = block.shape[1:]
    return plane_order(index & 1, block.reshape((4, 4) + shape)).reshape((16,) + shape)


def plane_halves(index, blocks, step):
    later = plane_bit(index, PLANE_STEPS[step])
    half = blocks.shape[0] // 2
    keep = lax.dynamic_slice_in_dim(blocks, later * half, half, axis=0)
    send = lax.dynamic_slice_in_dim(blocks, (1 - later) * half, half, axis=0)
    return keep, swap(send, *PLANE_STEPS[step])


def scatter_plane_step(index, blocks, step, *beside):
    keep, got = plane_halves(index, blocks, step)
    return low(wide(keep) + wide(after(got, *beside)))


def plane_rest(index, blocks):
    place = jnp.where(index & 1 == 1, index >> 3, index >> 1) & 3
    block = lambda at: lax.dynamic_index_in_dim(blocks, at, 0, keepdims=False)
    return block(place), [swap(block(place ^ k), k << 1, k << 3) for k in range(1, 4)]


def plane_blocks(core, blocks):
    shape = blocks.shape[1:]
    return plane_order(core, blocks.reshape((4, 4) + shape)).reshape((16,) + shape)


def gather_ring(rows, beside=((), ())):
    for masks, others in zip(RING_STEPS, beside):
        rows = jnp.concatenate([rows, after(swap(rows, *masks), *others)], axis=0)
    return rows


def scatter_ring(own, other, steps=2):
    totals = [wide(own) + wide(swap(other, CORE))]
    for masks in RING_STEPS[: -steps - 1 : -1]:
        half = totals[-1].shape[0] // 2
        totals.append(totals[-1][:half] + wide(swap(low(totals[-1][half:]), *masks)))
    return totals


def exchange_ring(index, blocks):
    core, x = index & 1, index >> 5
    shape = blocks.shape[1:]
    blocks = blocks.reshape((4, 2) + shape)
    take = lambda array, at, axis: lax.dynamic_slice_in_dim(array, at, 1, axis)
    got = swap(take(blocks, 1 - core, 1), CORE)
    keep = take(blocks, core, 1)
    blocks = jnp.concatenate(
        [jnp.where(core == 1, got, keep), jnp.where(core == 1, keep, got)], axis=1
    )
    parts = [take(blocks, x, 0)] + [
        swap(take(blocks, x ^ k, 0), k << 5) for k in range(1, 4)
    ]
    parts = jnp.concatenate(parts, axis=0)
    parts = jnp.where(x & 1 == 1, parts.reshape((2, 2, 2) + shape)[:, ::-1].reshape(parts.shape), parts)
    parts = jnp.where(x & 2 == 2, parts.reshape((2, 4) + shape)[::-1].reshape(parts.shape), parts)
    return parts.reshape((8,) + shape)


def tiles_tall(block):
    lead = block.shape[:-2]
    n = len(lead)
    block = block.reshape(lead + (-1, 8, 8, HEAD))
    block = block.transpose(tuple(range(n)) + (n + 2, n + 1, n, n + 3))
    return block.reshape(lead + (64, -1))


def tiles_flat(block):
    lead = block.shape[:-2]
    n = len(lead)
    block = block.reshape(lead + (8, 8, -1, HEAD))
    block = block.transpose(tuple(range(n)) + (n + 2, n + 1, n, n + 3))
    return block.reshape(lead + (-1, WIDTH))


def rows_by_device(blocks):
    n = blocks.shape[-1]
    return blocks.reshape(16, 4, 2, 8, n).transpose(1, 0, 2, 3, 4).reshape(WIDTH, n)


def rows_by_plane(rows):
    n = rows.shape[-1]
    return rows.reshape(4, 16, 2, 8, n).transpose(1, 0, 2, 3, 4).reshape(16, 64, n)


def on_device(
    hidden, lengths, w_query, w_key, w_value, w_out, w_gate, w_up, w_down, gains, cotangent
):
    index = lax.axis_index(AXES).astype(jnp.int32)
    core, x = index & 1, index >> 5
    straight = (index >> 4 & 1) == core
    spot_of = lambda c: jnp.where(c == 1, jnp.asarray(RING_SPOTS[1]), jnp.asarray(RING_SPOTS[0]))
    chips = x ^ jnp.arange(4, dtype=jnp.int32)
    spots = jnp.concatenate(
        [spot_of(core)[chips], spot_of(1 - core)[chips], core[None], core[None]]
    ).astype(jnp.int32)

    local = jnp.concatenate(
        [
            w_query.reshape(8, KV_HEADS, 256).transpose(1, 0, 2),
            w_key.reshape(8, KV_HEADS, HEAD).transpose(1, 0, 2),
            w_value.reshape(8, KV_HEADS, HEAD).transpose(1, 0, 2),
            jnp.broadcast_to(jnp.pad(gains[None, None, :], ((0, 0), (0, 7), (0, 110))), (8, 8, 128)),
        ]
        + [
            weight.reshape(8, 4, 16, 2, 24).transpose(1, 3, 0, 2, 4).reshape(8, 8, 384)
            for weight in (w_gate, w_up)
        ],
        axis=2,
    )
    digits = jnp.pad(low(jnp.stack([lengths[0] // 64, lengths[0] % 64])), ((0, 14), (0, WIDTH - 3)))
    pieces = cross(jnp.concatenate([w_out, digits], axis=0))
    rows = after(hidden[0], local)
    inputs = cross(rows)
    second = cross_and_swap(rows, RING_STEPS[0])
    digits = pieces[16:18, :3].astype(jnp.int32)
    lengths = (digits[0] * 64 + digits[1])[None]
    pieces = pieces[:16].reshape(16, 4, 256).transpose(1, 0, 2).reshape(64, 256)
    local = exchange_ring(index, local).reshape(64, 1408)
    d_result = cross(after(cotangent[0], local))
    heads = jnp.concatenate([local[:, :640], pieces], axis=1)[None]
    heads = gather_plane_step(index, after(heads, inputs, second), 0)
    heads = gather_plane_step(index, after(heads, d_result), 1)
    d_result_own = jnp.concatenate([d_result, swap(d_result, *RING_STEPS[0])], axis=0)
    heads = gather_plane_step(index, heads, 2)
    heads = gather_plane_step(index, after(heads, d_result_own), 3)
    gain_all = plane_order(core, heads[:, ::8, 512:530].reshape(4, 4, 8, 18))
    gain_all = gain_all.reshape(16, 4, 2, 18).transpose(1, 0, 2, 3)
    gain_all = wide(gain_all.reshape(1, -1))
    gain_attn, gain_mlp = gain_all[:, :WIDTH], gain_all[:, WIDTH : 2 * WIDTH]
    gain_query = gain_all[:, 2 * WIDTH : 2 * WIDTH + HEAD]
    gain_key = gain_all[:, 2 * WIDTH + HEAD :]

    def rest_of_ring(rows):
        rows = jnp.concatenate([rows, swap(rows, *RING_STEPS[1])], axis=0)
        return rows, swap(rows, CORE)

    inputs_own, inputs_other = rest_of_ring(jnp.concatenate([inputs, second], axis=0))
    ends = jnp.stack([lengths[0, 0], lengths[0, 0] + lengths[0, 1]]).astype(jnp.int32)
    token = jnp.arange(PACK, dtype=jnp.int32)
    position = wide(token - row_start(token, (ends[0], ends[1])))
    inverse = jnp.power(ROPE_BASE, -2.0 * jnp.arange(HEAD // 2, dtype=jnp.float32) / HEAD)
    angle = position[:, None] * inverse[None, :]
    cosine, sine = jnp.cos(angle), jnp.sin(angle)
    cosine = jnp.concatenate([cosine, cosine], axis=1)
    sine = jnp.concatenate([-sine, sine], axis=1)

    d_result_own = jnp.concatenate([d_result_own, swap(d_result_own, *RING_STEPS[1])], axis=0)
    normed, pre, qkv, qkv_kept, w_heads_across, w_heads = project(
        spots, inputs_own, inputs_other, heads, gain_attn, gain_query, gain_key, cosine, sine
    )
    qkv, d_result_own = lax.optimization_barrier((qkv, d_result_own))
    attended, attended_kept, inverse_total = attend(ends, qkv)
    out_own, out_other, w_rows = to_ring(spots, attended, heads)
    middle_steps = scatter_ring(out_own, out_other)
    d_result_other = swap(after(d_result_own, middle_steps[0]), CORE)
    units = jnp.concatenate([local[:, 640:], tiles_tall(w_down)], axis=1)[None]
    units = gather_plane_step(index, after(units, out_own), 0)
    units = gather_plane_step(index, after(units, middle_steps[0]), 1)
    units = gather_plane_step(index, after(units, middle_steps[1]), 2)
    middle = wide(inputs) + middle_steps[2]
    middle_scale = norm_scale(middle)
    mixed = low(middle * middle_scale * gain_mlp)
    mixed_own = gather_ring(mixed)
    mixed_other = swap(mixed_own, CORE)
    units = gather_plane_step(index, units, 3)
    units = plane_blocks(core, units)
    full_units = rows_by_device(units[..., :768])
    full_down = tiles_flat(units[..., 768:]).reshape(384, WIDTH)
    full_units, full_down = lax.optimization_barrier((full_units, full_down))

    def feed_forward(rows, d_rows):
        pre = dot(rows, full_units)
        gate_pre, up_pre = pre[:, :384], pre[:, 384:]
        sigmoid = 1.0 / (1.0 + jnp.exp(-gate_pre))
        silu = gate_pre * sigmoid
        act = low(silu * up_pre)
        d_act = contract_cols(d_rows, full_down)
        d_gate = low(d_act * up_pre * (sigmoid + silu * (1.0 - sigmoid)))
        d_up = low(d_act * silu)
        d_pre = jnp.concatenate([d_gate, d_up], axis=1)
        return act, d_pre, low(contract_cols(d_pre, full_units))

    act_own, d_pre_own, d_mixed_own = feed_forward(mixed_own, d_result_own)
    act_other, d_pre_other, d_mixed_other = feed_forward(mixed_other, d_result_other)
    d_mixed_steps = scatter_ring(d_mixed_own, d_mixed_other)
    d_mixed = d_mixed_steps[-1]
    d_middle = wide(d_result) + norm_back(middle, gain_mlp, d_mixed)
    d_gain_mlp = jnp.sum(middle * middle_scale * d_mixed, axis=0)

    late = lambda array: after(array, d_mixed_steps[0])
    grad_units = contract_rows(mixed_own, late(d_pre_own)) + contract_rows(mixed_other, late(d_pre_other))
    grad_down = contract_rows(late(act_own), d_result_own) + contract_rows(late(act_other), d_result_other)
    grad_down = low(grad_down).reshape(16, 3, 8, 8, HEAD).transpose(0, 3, 2, 1, 4)
    grads = jnp.concatenate([rows_by_plane(low(grad_units)), grad_down.reshape(16, 64, 384)], axis=2)
    grads = plane_blocks(core, grads)
    act_own, act_other = (after(act, d_middle) for act in (act_own, act_other))
    result = to_pack(spots, act_own, act_other, full_down)
    keep, got = plane_halves(index, grads, 3)
    d_branch_own = gather_ring(after(low(d_middle), grads), ((), (result, got)))
    sums = low(wide(keep) + wide(got))
    d_branch_other = swap(d_branch_own, CORE)
    result = lax.psum_scatter(after(result, d_branch_own), RING, scatter_dimension=0, tiled=True)

    d_attended, grad_out = out_back(spots, d_branch_own, d_branch_other, attended_kept, w_rows)
    grad_out = plane_blocks(core, grad_out)
    d_attended, grad_out = lax.optimization_barrier((d_attended, grad_out))
    sums_keep, sums_got = plane_halves(index, sums, 2)
    out_keep, out_got = plane_halves(index, grad_out, 3)
    d_query, d_key, d_value = attend_back(ends, qkv_kept, d_attended, attended_kept, inverse_total)
    d_query, sums_got, out_got = lax.optimization_barrier((d_query, sums_got, out_got))
    sums_keep, sums_got = plane_rest(index, low(wide(sums_keep) + wide(sums_got)))
    sums_out = low(wide(out_keep) + wide(out_got))
    d_pre, d_gain_heads = project_back(
        spots, pre, d_query, d_key, d_value, cosine, sine, gain_query, gain_key
    )
    d_pre, sums_got = lax.optimization_barrier((d_pre, sums_got))
    sums = wide(sums_keep) + sum(wide(got) for got in sums_got)
    grad_heads = contract_rows(normed, d_pre)
    d_gain_attn = jnp.sum(grad_heads * wide(w_heads), axis=1) / gain_attn[0]
    d_gains = jnp.concatenate([d_gain_attn, d_gain_mlp, d_gain_heads.reshape(-1)])
    d_gains = d_gains.reshape(4, 16, 2, 1, 18).transpose(1, 0, 2, 3, 4)
    payload = jnp.concatenate(
        [
            rows_by_plane(low(grad_heads)),
            low(jnp.pad(d_gains, ((0, 0),) * 3 + ((0, 7), (0, 110)))).reshape(16, 64, 128),
        ],
        axis=2,
    )
    payload = plane_blocks(core, payload)
    d_pre, payload, result = lax.optimization_barrier((d_pre, payload, result))
    d_normed_own, d_normed_other = normed_back(spots, d_pre, w_heads_across)
    out_keep, out_got = plane_halves(index, sums_out, 2)
    got, out_got = lax.optimization_barrier((swap(d_normed_other, CORE), out_got))
    sums_out = low(wide(out_keep) + wide(out_got))
    total = wide(d_normed_own) + wide(got)
    keep, send = total[: 2 * TOK], low(total[2 * TOK :])
    payload, sums_out = (after(array, send) for array in (payload, sums_out))
    heads_keep, heads_got = plane_halves(index, payload, 3)
    out_keep, out_got = plane_rest(index, sums_out)
    got, heads_got, out_got = lax.optimization_barrier(
        (swap(send, *RING_STEPS[1]), heads_got, out_got)
    )
    sum_out = wide(out_keep) + sum(wide(part) for part in out_got)
    heads_sums = low(wide(heads_keep) + wide(heads_got))
    total = keep + wide(got)
    heads_keep, heads_got = plane_halves(index, heads_sums, 2)
    got, heads_got = lax.optimization_barrier(
        (swap(low(total[TOK:]), *RING_STEPS[0]), heads_got)
    )
    heads_sums = low(wide(heads_keep) + wide(heads_got))
    d_normed = total[:TOK] + wide(got)
    input_grad = d_middle + norm_back(wide(inputs), gain_attn, d_normed)
    heads_keep, heads_got = plane_rest(index, heads_sums)
    home, heads_got = lax.optimization_barrier((cross(low(input_grad)), heads_got))
    input_grad = jnp.where(straight, input_grad, wide(home))
    heads_sums = low(wide(heads_keep) + sum(wide(part) for part in heads_got))
    sum_down = tiles_flat(sums[:, 768:])
    sum_out = sum_out.reshape(4, 16, 256).transpose(1, 0, 2).reshape(16, WIDTH)
    result = jnp.concatenate([middle + wide(result), sum_out], axis=0)
    result = cross(after(low(result), heads_sums))
    ring_grads = jnp.concatenate([heads_sums, low(sums[:, :768])], axis=1)
    ring_grads = exchange_ring(index, ring_grads.reshape(8, 8, 1408))
    heads_grad, units_grad = wide(ring_grads[..., :640]), ring_grads[..., 640:]
    activations = result[:TOK]
    sum_out = jnp.where(straight, sum_out, wide(result[TOK:]))
    column = jnp.arange(768, dtype=jnp.int32)
    column = column // 24 % 2 * 384 + column // 48 * 24 + column % 24
    column = after(column, middle)
    hits = lax.broadcasted_iota(jnp.int32, (768, 768), 0) == column[None, :]
    units_grad = units_grad.reshape(4, 2, 8, 2, 384).transpose(3, 2, 0, 1, 4).reshape(64, 768)
    units_grad = dot(units_grad, hits.astype(jnp.bfloat16)).reshape(2, 8, FF)
    sum_query = heads_grad[..., :256].transpose(1, 0, 2).reshape(8, -1)
    sum_key = heads_grad[..., 256:384].transpose(1, 0, 2).reshape(8, -1)
    sum_value = heads_grad[..., 384:512].transpose(1, 0, 2).reshape(8, -1)
    sum_gains = jnp.sum(heads_grad[:, 0, 512:530], axis=0)
    return (
        activations[None],
        input_grad[None],
        sum_query,
        sum_key,
        sum_value,
        sum_out,
        units_grad[0],
        units_grad[1],
        sum_down,
        sum_gains,
    )


def solution(mesh):
    chips = Mesh(mesh.devices.reshape(4, 2, 2, 4, 2), AXES)
    rows = P(AXES, None)
    tokens = P(("zl", "y", "core"), ("x", "zh"), None)
    lengths = P(("zl", "y", "core"), None)
    return jax.shard_map(
        on_device,
        mesh=chips,
        in_specs=(tokens, lengths, *([rows] * 7), P(AXES), tokens),
        out_specs=(tokens, tokens, *([rows] * 7), P(AXES)),
        check_vma=False,
    )
```

```python
import jax
import jax.numpy as jnp
from jax import lax
from jax.experimental import pallas as pl
from jax.experimental.pallas import tpu as pltpu
from jax.sharding import Mesh
from jax.sharding import PartitionSpec as P

HEADS = 16
KV_HEADS = 8
HEAD = 128
EPSILON = 1e-06
ROPE_BASE = 1000000.0
DEVICES = 128
WIDTH = 1024
FF = 3072
TOK = 192
PACK = 1536
BLOCK = 256
LOG2E = 1.4426950408889634
SCALE = HEAD ** (-0.5)
VMEM_LIMIT = 48 * 1024 * 1024

AXES = ("x", "zh", "zl", "y", "core")
RING = ("x", "core")
PLANE = ("zh", "zl", "y")
XA, XB, ZA, ZB, YA, YB, CORE = 32, 96, 8, 24, 2, 6, 1
RING_STEPS = ((XA, XB), (XB, XA))
RING_SPOTS = ((0, 1, 3, 2), (0, 2, 3, 1))
PLANE_STEPS = ((YA, ZA), (YB, ZB), (ZA, YA), (ZB, YB))
BIT = {YA: 1, YB: 2, ZA: 3, ZB: 4}


def swap(values, mask, other_mask=None):
    masks = (mask, mask if other_mask is None else other_mask)
    return lax.ppermute(values, AXES, [(k, k ^ masks[k & 1]) for k in range(DEVICES)])


def crossed(k):
    return k ^ 17 if (k >> 4 ^ k) & 1 else k


def cross(values):
    return lax.ppermute(values, AXES, [(k, crossed(k)) for k in range(DEVICES)])


def cross_and_swap(values, masks):
    return lax.ppermute(
        values, AXES, [(crossed(k ^ masks[k & 1]), k) for k in range(DEVICES)]
    )


def after(value, *others):
    return lax.optimization_barrier((value, *others))[0] if others else value


def low(values):
    return values.astype(jnp.bfloat16)


def wide(values):
    return values.astype(jnp.float32)


def dot(left, right):
    return jnp.dot(left, right, preferred_element_type=jnp.float32)


def contract_rows(left, right):
    return lax.dot_general(
        left, right, (((0,), (0,)), ((), ())), preferred_element_type=jnp.float32
    )


def contract_cols(left, right):
    return lax.dot_general(
        left, right, (((1,), (1,)), ((), ())), preferred_element_type=jnp.float32
    )


def norm_scale(values):
    return lax.rsqrt(jnp.mean(values * values, axis=-1, keepdims=True) + EPSILON)


def norm_back(values, gain, grad):
    scale = norm_scale(values)
    normal = values * scale
    inner = grad * gain
    return scale * (inner - normal * jnp.mean(inner * normal, axis=-1, keepdims=True))


def rope(values, cosine, sine):
    return values * cosine + pltpu.roll(values, 64, 1) * sine


def rope_back(grad, cosine, sine):
    return grad * cosine + pltpu.roll(grad * sine, 64, 1)


def ring_specs(columns):
    return [
        pl.BlockSpec((TOK, columns), lambda x, spots: (spots[x], 0)),
        pl.BlockSpec((TOK, columns), lambda x, spots: (spots[4 + x], 0)),
    ]


def pack_spec(columns):
    return pl.BlockSpec((2 * TOK, columns), lambda x, spots: (x, 0))


def whole_spec(shape):
    return pl.BlockSpec(shape, lambda x, spots: (0, 0))


def own_rows(spots):
    return pl.ds(pl.multiple_of(spots[8] * TOK, TOK), TOK)


def other_rows(spots):
    return pl.ds(pl.multiple_of((1 - spots[8]) * TOK, TOK), TOK)


def shaped(shape, dtype, kept=False):
    return pltpu.HBM(shape, dtype) if kept else jax.ShapeDtypeStruct(shape, dtype)


def in_hbm(array):
    return pltpu.with_memory_space_constraint(array, pltpu.HBM)


def cost(microseconds):
    return pl.CostEstimate(
        flops=0, bytes_accessed=int(microseconds * 0.1e6), transcendentals=0
    )


def ring_call(kernel, name, in_specs, out_specs, out_shape, time, spots, *operands, scratch=()):
    return pl.pallas_call(
        kernel,
        grid_spec=pltpu.PrefetchScalarGridSpec(
            num_scalar_prefetch=1,
            grid=(4,),
            in_specs=in_specs,
            out_specs=out_specs,
            scratch_shapes=scratch,
        ),
        out_shape=out_shape,
        compiler_params=pltpu.CompilerParams(vmem_limit_bytes=VMEM_LIMIT),
        cost_estimate=cost(time),
        name=name,
    )(spots, *operands)


def qkv_kernel(
    spots, own_ref, other_ref, heads_ref, ga_ref, gq_ref, gk_ref, cos_ref, sin_ref,
    normed_ref, pre_ref, qkv_ref, kept_ref, across_ref, w_ref,
):
    @pl.when(pl.program_id(0) == 0)
    def _():
        for z in range(4):
            for y in range(4):
                block = jnp.where(spots[9] == 1, y * 4 + z, z * 4 + y)
                for x in range(4):
                    row = (x * 16 + z * 4 + y) * 16
                    w_ref[row : row + 16, :] = heads_ref[block, x * 16 : x * 16 + 16, :512]
        across_ref[...] = w_ref[...].T

    for ref, rows in ((own_ref, own_rows(spots)), (other_ref, other_rows(spots))):
        x = wide(ref[...])
        normed_ref[rows, :] = low(x * norm_scale(x) * ga_ref[...])
    pre = dot(normed_ref[...], w_ref[...])
    pre_ref[...] = pre[:, : 3 * HEAD]
    cosine, sine = cos_ref[...], sin_ref[...]
    for h in range(3):
        u = pre[:, h * HEAD : (h + 1) * HEAD]
        gain = gk_ref[...] if h == 2 else gq_ref[...]
        normal = u * norm_scale(u) * gain
        qkv_ref[:, h * HEAD : (h + 1) * HEAD] = low(rope(normal, cosine, sine))
    qkv_ref[:, 3 * HEAD :] = low(pre[:, 3 * HEAD :])
    kept_ref[...] = qkv_ref[...]


def project(spots, own, other, heads, gain_attn, gain_query, gain_key, cosine, sine):
    return ring_call(
        qkv_kernel,
        "project",
        ring_specs(WIDTH)
        + [pl.BlockSpec(heads.shape, lambda x, spots: (0, 0, 0))]
        + [whole_spec((1, WIDTH)), whole_spec((1, HEAD)), whole_spec((1, HEAD))]
        + [pack_spec(HEAD), pack_spec(HEAD)],
        [pack_spec(WIDTH), pack_spec(3 * HEAD), pack_spec(512), pack_spec(512)]
        + [whole_spec((512, WIDTH)), whole_spec((WIDTH, 512))],
        [
            shaped((PACK, WIDTH), jnp.bfloat16, True),
            shaped((PACK, 3 * HEAD), jnp.float32, True),
            shaped((PACK, 512), jnp.bfloat16),
            shaped((PACK, 512), jnp.bfloat16, True),
            shaped((512, WIDTH), jnp.bfloat16, True),
            shaped((WIDTH, 512), jnp.bfloat16, True),
        ],
        8, spots, own, other, heads, gain_attn, gain_query, gain_key, cosine, sine,
    )


def to_ring_kernel(spots, rows_ref, heads_ref, own_ref, other_ref, w_ref):
    @pl.when(pl.program_id(0) == 0)
    def _():
        for z in range(4):
            for y in range(4):
                block = jnp.where(spots[9] == 1, y * 4 + z, z * 4 + y)
                row = (z % 2 * 8 + y * 2 + z // 2) * 16
                for n in range(4):
                    piece = heads_ref[block, n * 16 : n * 16 + 16, 640:]
                    w_ref[row : row + 16, n * 256 : n * 256 + 256] = piece

    own_ref[...] = low(dot(rows_ref[own_rows(spots), :], w_ref[...]))
    other_ref[...] = low(dot(rows_ref[other_rows(spots), :], w_ref[...]))


def to_ring(spots, rows, heads):
    half = shaped((PACK // 2, WIDTH), jnp.bfloat16)
    return ring_call(
        to_ring_kernel, "to_ring",
        [pack_spec(256), pl.BlockSpec(heads.shape, lambda x, spots: (0, 0, 0))],
        ring_specs(WIDTH) + [whole_spec((256, WIDTH))],
        [half, half, shaped((256, WIDTH), jnp.bfloat16, True)], 3, spots, rows, heads,
    )


def to_pack_kernel(spots, own_ref, other_ref, w_ref, rows_ref):
    rows_ref[own_rows(spots), :] = low(dot(own_ref[...], w_ref[...]))
    rows_ref[other_rows(spots), :] = low(dot(other_ref[...], w_ref[...]))


def to_pack(spots, own, other, weights):
    return ring_call(
        to_pack_kernel, "to_pack", ring_specs(own.shape[1]) + [whole_spec(weights.shape)],
        [pack_spec(WIDTH)], [shaped((PACK, WIDTH), jnp.bfloat16)], 4, spots, own, other, weights,
    )[0]


def out_back_kernel(
    spots, own_ref, other_ref, attended_ref, w_ref, d_attended_ref, d_w_ref, rows_ref, total_ref
):
    step = pl.program_id(0)

    @pl.when(step == 0)
    def _():
        total_ref[...] = jnp.zeros_like(total_ref)

    rows_ref[own_rows(spots), :] = own_ref[...]
    rows_ref[other_rows(spots), :] = other_ref[...]
    d_attended_ref[...] = low(contract_cols(rows_ref[...], w_ref[...]))
    total_ref[...] += contract_rows(attended_ref[...], rows_ref[...])

    @pl.when(step == pl.num_programs(0) - 1)
    def _():
        for z in range(4):
            for y in range(4):
                spot = jnp.where(spots[9] == 1, y * 4 + z, z * 4 + y)
                spot = jnp.where(spots[10] == 1, (spot + 8) % 16, spot)
                row = (z % 2 * 8 + y * 2 + z // 2) * 16
                for n in range(4):
                    piece = total_ref[row : row + 16, n * 256 : n * 256 + 256]
                    d_w_ref[spot, n * 16 : n * 16 + 16, :] = low(piece)


def out_back(spots, own, other, attended, weights):
    return ring_call(
        out_back_kernel, "out_back",
        ring_specs(WIDTH) + [pack_spec(256), whole_spec((256, WIDTH))],
        [pack_spec(256), pl.BlockSpec((16, 64, 256), lambda x, spots: (0, 0, 0))],
        [shaped((PACK, 256), jnp.bfloat16), shaped((16, 64, 256), jnp.bfloat16, True)],
        5, spots, own, other, in_hbm(attended), in_hbm(weights),
        scratch=[pltpu.VMEM((2 * TOK, WIDTH), jnp.bfloat16), pltpu.VMEM((256, WIDTH), jnp.float32)],
    )


def row_start(rows, ends):
    first, second = ends
    return jnp.where(rows >= second, second, jnp.where(rows >= first, first, 0))


def block_mask(q_block, k_block, ends, transposed):
    last = PACK // BLOCK - 1
    q_axis, k_axis = (1, 0) if transposed else (0, 1)
    q_rows = q_block * BLOCK + lax.broadcasted_iota(jnp.int32, (BLOCK, BLOCK), q_axis)
    k_rows = k_block * BLOCK + lax.broadcasted_iota(jnp.int32, (BLOCK, BLOCK), k_axis)
    mask = None
    if k_block == q_block:
        mask = k_rows <= q_rows
    if k_block == 0 or q_block == last:
        begun = k_rows >= row_start(q_rows, ends)
        mask = begun if mask is None else mask & begun
    return mask


def for_each_block(step):
    for q_block in range(PACK // BLOCK):

        @pl.when(pl.program_id(0) == q_block)
        def _(q_block=q_block):
            step(q_block)


def attend_kernel(ends_ref, q_ref, k_ref, v_ref, out_ref, kept_ref, inverse_ref):
    ends = (ends_ref[0], ends_ref[1])

    def step(q_block):
        seen = (q_block + 1) * BLOCK
        for h in range(2):
            columns = slice(h * HEAD, (h + 1) * HEAD)
            scores = contract_cols(q_ref[:, columns], k_ref[:seen, :])
            part, shifted = 0.0, []
            for k_block in range(q_block + 1):
                block = scores[:, k_block * BLOCK : (k_block + 1) * BLOCK]
                block = jnp.exp2(block * (SCALE * LOG2E))
                mask = block_mask(q_block, k_block, ends, False)
                if mask is not None:
                    block = jnp.where(mask, block, 0.0)
                part += block[:, :HEAD] + block[:, HEAD:]
                shifted.append(low(block))
            total = dot(jnp.concatenate(shifted, axis=1), v_ref[:seen, :])
            row_total = jnp.sum(part, axis=1, keepdims=True)
            out_ref[:, columns] = low(total * (1.0 / row_total))
            across = jnp.sum(jnp.swapaxes(part, 0, 1), axis=0, keepdims=True)
            inverse_ref[h : h + 1, :] = 1.0 / across
        kept_ref[...] = out_ref[...]

    for_each_block(step)


def attend(ends, qkv):
    return pl.pallas_call(
        attend_kernel,
        grid_spec=pltpu.PrefetchScalarGridSpec(
            num_scalar_prefetch=1,
            grid=(PACK // BLOCK,),
            in_specs=[
                pl.BlockSpec((BLOCK, 2 * HEAD), lambda q, ends: (q, 0)),
                pl.BlockSpec((PACK, HEAD), lambda q, ends: (0, 2)),
                pl.BlockSpec((PACK, HEAD), lambda q, ends: (0, 3)),
            ],
            out_specs=[
                pl.BlockSpec((BLOCK, 2 * HEAD), lambda q, ends: (q, 0)),
                pl.BlockSpec((BLOCK, 2 * HEAD), lambda q, ends: (q, 0)),
                pl.BlockSpec((2, BLOCK), lambda q, ends: (0, q)),
            ],
        ),
        out_shape=[
            shaped((PACK, 2 * HEAD), jnp.bfloat16),
            shaped((PACK, 2 * HEAD), jnp.bfloat16, True),
            shaped((2, PACK), jnp.float32, True),
        ],
        compiler_params=pltpu.CompilerParams(vmem_limit_bytes=VMEM_LIMIT),
        cost_estimate=cost(6),
        name="attend",
    )(ends, qkv, qkv, qkv)


def attend_back_kernel(
    ends_ref, q_ref, k_ref, v_ref, grad_ref, out_ref, inverse_ref, dq_ref, dk_ref, dv_ref
):
    ends = (ends_ref[0], ends_ref[1])

    @pl.when(pl.program_id(0) == 0)
    def _():
        dk_ref[...] = jnp.zeros_like(dk_ref)
        dv_ref[...] = jnp.zeros_like(dv_ref)

    def both_heads(ref):
        return jnp.concatenate([ref[:, :HEAD], ref[:, HEAD:]], axis=0)

    def step(q_block):
        seen = (q_block + 1) * BLOCK
        queries, grads = both_heads(q_ref), both_heads(grad_ref)
        product = wide(grads) * wide(both_heads(out_ref))
        delta = jnp.sum(jnp.swapaxes(product, 0, 1), axis=0, keepdims=True)
        inverse = jnp.concatenate([inverse_ref[0:1, :], inverse_ref[1:2, :]], axis=1)
        scores = contract_cols(k_ref[:seen, :], queries)
        d_probs = contract_cols(v_ref[:seen, :], grads)
        probs, d_scores = [], []
        for k_block in range(q_block + 1):
            rows = slice(k_block * BLOCK, (k_block + 1) * BLOCK)
            prob = jnp.exp2(scores[rows] * (SCALE * LOG2E)) * inverse
            mask = block_mask(q_block, k_block, ends, True)
            if mask is not None:
                prob = jnp.where(jnp.concatenate([mask, mask], axis=1), prob, 0.0)
            d_scores.append(low(prob * ((d_probs[rows] - delta) * SCALE)))
            probs.append(low(prob))
        probs = jnp.concatenate(probs, axis=0)
        d_scores = jnp.concatenate(d_scores, axis=0)
        dk_ref[:seen, :] += dot(d_scores, queries)
        dv_ref[:seen, :] += dot(probs, grads)
        d_queries = contract_rows(d_scores, k_ref[:seen, :])
        dq_ref[:, :HEAD] = d_queries[:BLOCK]
        dq_ref[:, HEAD:] = d_queries[BLOCK:]

    for_each_block(step)


def attend_back(ends, qkv, grad, out, inverse):
    qkv, out, inverse = in_hbm(qkv), in_hbm(out), in_hbm(inverse)
    by_block = pl.BlockSpec((BLOCK, 2 * HEAD), lambda q, ends: (q, 0))
    whole = pl.BlockSpec((PACK, HEAD), lambda q, ends: (0, 0))
    return pl.pallas_call(
        attend_back_kernel,
        grid_spec=pltpu.PrefetchScalarGridSpec(
            num_scalar_prefetch=1,
            grid=(PACK // BLOCK,),
            in_specs=[
                by_block,
                pl.BlockSpec((PACK, HEAD), lambda q, ends: (0, 2)),
                pl.BlockSpec((PACK, HEAD), lambda q, ends: (0, 3)),
                by_block,
                by_block,
                pl.BlockSpec((2, BLOCK), lambda q, ends: (0, q)),
            ],
            out_specs=[by_block, whole, whole],
        ),
        out_shape=[
            jax.ShapeDtypeStruct((PACK, 2 * HEAD), jnp.float32),
            jax.ShapeDtypeStruct((PACK, HEAD), jnp.float32),
            jax.ShapeDtypeStruct((PACK, HEAD), jnp.float32),
        ],
        compiler_params=pltpu.CompilerParams(vmem_limit_bytes=VMEM_LIMIT),
        cost_estimate=cost(11),
        name="attend_back",
    )(ends, qkv, qkv, qkv, grad, out, inverse)


def qkv_back_kernel(
    spots, pre_ref, dq_ref, dk_ref, dv_ref, cos_ref, sin_ref, gq_ref, gk_ref, d_pre_ref, d_head_ref
):
    @pl.when(pl.program_id(0) == 0)
    def _():
        d_head_ref[...] = jnp.zeros_like(d_head_ref)

    cosine, sine = cos_ref[...], sin_ref[...]
    for h in range(3):
        u = pre_ref[:, h * HEAD : (h + 1) * HEAD]
        gain = gk_ref[...] if h == 2 else gq_ref[...]
        grad = dk_ref[...] if h == 2 else dq_ref[:, h * HEAD : (h + 1) * HEAD]
        grad = rope_back(grad, cosine, sine)
        row = 1 if h == 2 else 0
        scale = norm_scale(u)
        normal = u * scale
        d_head_ref[row : row + 1, :] += jnp.sum(grad * normal, axis=0, keepdims=True)
        inner = grad * gain
        inner = scale * (inner - normal * jnp.mean(inner * normal, axis=-1, keepdims=True))
        d_pre_ref[:, h * HEAD : (h + 1) * HEAD] = low(inner)
    d_pre_ref[:, 3 * HEAD :] = low(dv_ref[...])


def project_back(spots, pre, d_query, d_key, d_value, cosine, sine, gain_query, gain_key):
    return ring_call(
        qkv_back_kernel,
        "project_back",
        [pack_spec(3 * HEAD), pack_spec(2 * HEAD), pack_spec(HEAD), pack_spec(HEAD)]
        + [pack_spec(HEAD), pack_spec(HEAD), whole_spec((1, HEAD)), whole_spec((1, HEAD))],
        [pack_spec(512), whole_spec((2, HEAD))],
        [shaped((PACK, 512), jnp.bfloat16), shaped((2, HEAD), jnp.float32)],
        5, spots, in_hbm(pre), d_query, d_key, d_value, in_hbm(cosine), in_hbm(sine), gain_query, gain_key,
    )


def normed_back_kernel(spots, d_pre_ref, w_ref, own_ref, other_ref):
    own_ref[...] = low(dot(d_pre_ref[own_rows(spots), :], w_ref[...]))
    other_ref[...] = low(dot(d_pre_ref[other_rows(spots), :], w_ref[...]))


def normed_back(spots, d_pre, weights):
    half = shaped((PACK // 2, WIDTH), jnp.bfloat16)
    return ring_call(
        normed_back_kernel, "normed_back", [pack_spec(512), whole_spec((512, WIDTH))], ring_specs(WIDTH),
        [half, half], 4, spots, d_pre, in_hbm(weights),
    )


def plane_order(core, blocks):
    return jnp.where(core == 1, jnp.swapaxes(blocks, 0, 1), blocks)


def plane_bit(index, masks):
    return jnp.where(index & 1 == 1, index >> BIT[masks[1]], index >> BIT[masks[0]]) & 1


def gather_plane_step(index, block, step):
    got = swap(block, *PLANE_STEPS[step])
    return jnp.where(
        plane_bit(index, PLANE_STEPS[step]) == 1,
        jnp.concatenate([got, block], axis=0),
        jnp.concatenate([block, got], axis=0),
    )


def gather_plane_end(index, block):
    shape = block.shape[1:]
    return plane_order(index & 1, block.reshape((4, 4) + shape)).reshape((16,) + shape)


def plane_halves(index, blocks, step):
    later = plane_bit(index, PLANE_STEPS[step])
    half = blocks.shape[0] // 2
    keep = lax.dynamic_slice_in_dim(blocks, later * half, half, axis=0)
    send = lax.dynamic_slice_in_dim(blocks, (1 - later) * half, half, axis=0)
    return keep, swap(send, *PLANE_STEPS[step])


def scatter_plane_step(index, blocks, step, *beside):
    keep, got = plane_halves(index, blocks, step)
    return low(wide(keep) + wide(after(got, *beside)))


def plane_rest(index, blocks):
    place = jnp.where(index & 1 == 1, index >> 3, index >> 1) & 3
    block = lambda at: lax.dynamic_index_in_dim(blocks, at, 0, keepdims=False)
    return block(place), [swap(block(place ^ k), k << 1, k << 3) for k in range(1, 4)]


def plane_blocks(core, blocks):
    shape = blocks.shape[1:]
    return plane_order(core, blocks.reshape((4, 4) + shape)).reshape((16,) + shape)


def gather_ring(rows, beside=((), ())):
    for masks, others in zip(RING_STEPS, beside):
        rows = jnp.concatenate([rows, after(swap(rows, *masks), *others)], axis=0)
    return rows


def scatter_ring(own, other, steps=2):
    totals = [wide(own) + wide(swap(other, CORE))]
    for masks in RING_STEPS[: -steps - 1 : -1]:
        half = totals[-1].shape[0] // 2
        totals.append(totals[-1][:half] + wide(swap(low(totals[-1][half:]), *masks)))
    return totals


def exchange_ring(index, blocks):
    core, x = index & 1, index >> 5
    shape = blocks.shape[1:]
    blocks = blocks.reshape((4, 2) + shape)
    take = lambda array, at, axis: lax.dynamic_slice_in_dim(array, at, 1, axis)
    got = swap(take(blocks, 1 - core, 1), CORE)
    keep = take(blocks, core, 1)
    blocks = jnp.concatenate(
        [jnp.where(core == 1, got, keep), jnp.where(core == 1, keep, got)], axis=1
    )
    parts = [take(blocks, x, 0)] + [
        swap(take(blocks, x ^ k, 0), k << 5) for k in range(1, 4)
    ]
    parts = jnp.concatenate(parts, axis=0)
    parts = jnp.where(x & 1 == 1, parts.reshape((2, 2, 2) + shape)[:, ::-1].reshape(parts.shape), parts)
    parts = jnp.where(x & 2 == 2, parts.reshape((2, 4) + shape)[::-1].reshape(parts.shape), parts)
    return parts.reshape((8,) + shape)


def tiles_tall(block):
    lead = block.shape[:-2]
    n = len(lead)
    block = block.reshape(lead + (-1, 8, 8, HEAD))
    block = block.transpose(tuple(range(n)) + (n + 2, n + 1, n, n + 3))
    return block.reshape(lead + (64, -1))


def tiles_flat(block):
    lead = block.shape[:-2]
    n = len(lead)
    block = block.reshape(lead + (8, 8, -1, HEAD))
    block = block.transpose(tuple(range(n)) + (n + 2, n + 1, n, n + 3))
    return block.reshape(lead + (-1, WIDTH))


def rows_by_device(blocks):
    n = blocks.shape[-1]
    return blocks.reshape(16, 4, 2, 8, n).transpose(1, 0, 2, 3, 4).reshape(WIDTH, n)


def rows_by_plane(rows):
    n = rows.shape[-1]
    return rows.reshape(4, 16, 2, 8, n).transpose(1, 0, 2, 3, 4).reshape(16, 64, n)


def on_device(
    hidden, lengths, w_query, w_key, w_value, w_out, w_gate, w_up, w_down, gains, cotangent
):
    index = lax.axis_index(AXES).astype(jnp.int32)
    core, x = index & 1, index >> 5
    straight = (index >> 4 & 1) == core
    spot_of = lambda c: jnp.where(c == 1, jnp.asarray(RING_SPOTS[1]), jnp.asarray(RING_SPOTS[0]))
    chips = x ^ jnp.arange(4, dtype=jnp.int32)
    spots = jnp.concatenate(
        [spot_of(core)[chips], spot_of(1 - core)[chips], core[None], core[None]]
        + [plane_bit(index, PLANE_STEPS[3])[None]]
    ).astype(jnp.int32)

    local = jnp.concatenate(
        [
            w_query.reshape(8, KV_HEADS, 256).transpose(1, 0, 2),
            w_key.reshape(8, KV_HEADS, HEAD).transpose(1, 0, 2),
            w_value.reshape(8, KV_HEADS, HEAD).transpose(1, 0, 2),
            jnp.broadcast_to(jnp.pad(gains[None, None, :], ((0, 0), (0, 7), (0, 110))), (8, 8, 128)),
        ]
        + [
            weight.reshape(8, 4, 16, 2, 24).transpose(1, 3, 0, 2, 4).reshape(8, 8, 384)
            for weight in (w_gate, w_up)
        ],
        axis=2,
    )
    digits = jnp.pad(low(jnp.stack([lengths[0] // 64, lengths[0] % 64])), ((0, 14), (0, WIDTH - 3)))
    pieces = cross(jnp.concatenate([w_out, digits], axis=0))
    rows = after(hidden[0], local)
    inputs = cross(rows)
    second = cross_and_swap(rows, RING_STEPS[0])
    digits = pieces[16:18, :3].astype(jnp.int32)
    lengths = (digits[0] * 64 + digits[1])[None]
    pieces = pieces[:16].reshape(16, 4, 256).transpose(1, 0, 2).reshape(64, 256)
    local = exchange_ring(index, local).reshape(64, 1408)
    d_result = cross(after(cotangent[0], local))
    heads = jnp.concatenate([local[:, :640], pieces], axis=1)[None]
    heads = gather_plane_step(index, after(heads, inputs, second), 0)
    heads = gather_plane_step(index, after(heads, d_result), 1)
    d_result_own = jnp.concatenate([d_result, swap(d_result, *RING_STEPS[0])], axis=0)
    heads = gather_plane_step(index, heads, 2)
    heads = gather_plane_step(index, after(heads, d_result_own), 3)
    gain_all = plane_order(core, heads[:, ::8, 512:530].reshape(4, 4, 8, 18))
    gain_all = gain_all.reshape(16, 4, 2, 18).transpose(1, 0, 2, 3)
    gain_all = wide(gain_all.reshape(1, -1))
    gain_attn, gain_mlp = gain_all[:, :WIDTH], gain_all[:, WIDTH : 2 * WIDTH]
    gain_query = gain_all[:, 2 * WIDTH : 2 * WIDTH + HEAD]
    gain_key = gain_all[:, 2 * WIDTH + HEAD :]

    def rest_of_ring(rows):
        rows = jnp.concatenate([rows, swap(rows, *RING_STEPS[1])], axis=0)
        return rows, swap(rows, CORE)

    inputs_own, inputs_other = rest_of_ring(jnp.concatenate([inputs, second], axis=0))
    ends = jnp.stack([lengths[0, 0], lengths[0, 0] + lengths[0, 1]]).astype(jnp.int32)
    token = jnp.arange(PACK, dtype=jnp.int32)
    position = wide(token - row_start(token, (ends[0], ends[1])))
    inverse = jnp.power(ROPE_BASE, -2.0 * jnp.arange(HEAD // 2, dtype=jnp.float32) / HEAD)
    angle = position[:, None] * inverse[None, :]
    cosine, sine = jnp.cos(angle), jnp.sin(angle)
    cosine = jnp.concatenate([cosine, cosine], axis=1)
    sine = jnp.concatenate([-sine, sine], axis=1)

    d_result_own = jnp.concatenate([d_result_own, swap(d_result_own, *RING_STEPS[1])], axis=0)
    normed, pre, qkv, qkv_kept, w_heads_across, w_heads = project(
        spots, inputs_own, inputs_other, heads, gain_attn, gain_query, gain_key, cosine, sine
    )
    qkv, d_result_own = lax.optimization_barrier((qkv, d_result_own))
    attended, attended_kept, inverse_total = attend(ends, qkv)
    out_own, out_other, w_rows = to_ring(spots, attended, heads)
    middle_steps = scatter_ring(out_own, out_other)
    d_result_other = swap(after(d_result_own, middle_steps[0]), CORE)
    units = jnp.concatenate([local[:, 640:], tiles_tall(w_down)], axis=1)[None]
    units = gather_plane_step(index, after(units, out_own), 0)
    units = gather_plane_step(index, after(units, middle_steps[0]), 1)
    units = gather_plane_step(index, after(units, middle_steps[1]), 2)
    middle = wide(inputs) + middle_steps[2]
    middle_scale = norm_scale(middle)
    mixed = low(middle * middle_scale * gain_mlp)
    mixed_own = gather_ring(mixed)
    mixed_other = swap(mixed_own, CORE)
    units = gather_plane_step(index, units, 3)
    units = plane_blocks(core, units)
    full_units = rows_by_device(units[..., :768])
    full_down = tiles_flat(units[..., 768:]).reshape(384, WIDTH)
    full_units, full_down = lax.optimization_barrier((full_units, full_down))

    def feed_forward(rows, d_rows):
        pre = dot(rows, full_units)
        gate_pre, up_pre = pre[:, :384], pre[:, 384:]
        sigmoid = 1.0 / (1.0 + jnp.exp(-gate_pre))
        silu = gate_pre * sigmoid
        act = low(silu * up_pre)
        d_act = contract_cols(d_rows, full_down)
        d_gate = low(d_act * up_pre * (sigmoid + silu * (1.0 - sigmoid)))
        d_up = low(d_act * silu)
        d_pre = jnp.concatenate([d_gate, d_up], axis=1)
        return act, d_pre, low(contract_cols(d_pre, full_units))

    act_own, d_pre_own, d_mixed_own = feed_forward(mixed_own, d_result_own)
    act_other, d_pre_other, d_mixed_other = feed_forward(mixed_other, d_result_other)
    d_mixed_steps = scatter_ring(d_mixed_own, d_mixed_other)
    d_mixed = d_mixed_steps[-1]
    d_middle = wide(d_result) + norm_back(middle, gain_mlp, d_mixed)
    d_gain_mlp = jnp.sum(middle * middle_scale * d_mixed, axis=0)

    late = lambda array: after(array, d_mixed_steps[0])
    grad_units = contract_rows(mixed_own, late(d_pre_own)) + contract_rows(mixed_other, late(d_pre_other))
    grad_down = contract_rows(late(act_own), d_result_own) + contract_rows(late(act_other), d_result_other)
    grad_down = low(grad_down).reshape(16, 3, 8, 8, HEAD).transpose(0, 3, 2, 1, 4)
    grads = jnp.concatenate([rows_by_plane(low(grad_units)), grad_down.reshape(16, 64, 384)], axis=2)
    grads = plane_blocks(core, grads)
    act_own, act_other = (after(act, d_middle) for act in (act_own, act_other))
    result = to_pack(spots, act_own, act_other, full_down)
    keep, got = plane_halves(index, grads, 3)
    d_branch_own = gather_ring(after(low(d_middle), grads), ((), (result, got)))
    sums = low(wide(keep) + wide(got))
    d_branch_other = swap(d_branch_own, CORE)
    result = lax.psum_scatter(after(result, d_branch_own), RING, scatter_dimension=0, tiled=True)

    d_attended, grad_out = out_back(spots, d_branch_own, d_branch_other, attended_kept, w_rows)
    d_attended, grad_out = lax.optimization_barrier((d_attended, grad_out))
    sums_keep, sums_got = plane_halves(index, sums, 2)
    out_got = swap(grad_out[8:], *PLANE_STEPS[3])
    d_query, d_key, d_value = attend_back(ends, qkv_kept, d_attended, attended_kept, inverse_total)
    d_query, sums_got, out_got = lax.optimization_barrier((d_query, sums_got, out_got))
    d_pre, d_gain_heads = project_back(
        spots, pre, d_query, d_key, d_value, cosine, sine, gain_query, gain_key
    )
    grad_heads = contract_rows(normed, d_pre)
    d_gain_attn = jnp.sum(grad_heads * wide(w_heads), axis=1) / gain_attn[0]
    d_gains = jnp.concatenate([d_gain_attn, d_gain_mlp, d_gain_heads.reshape(-1)])
    d_gains = d_gains.reshape(4, 16, 2, 1, 18).transpose(1, 0, 2, 3, 4)
    payload = jnp.concatenate(
        [
            rows_by_plane(low(grad_heads)),
            low(jnp.pad(d_gains, ((0, 0),) * 3 + ((0, 7), (0, 110)))).reshape(16, 64, 128),
        ],
        axis=2,
    )
    payload = plane_blocks(core, payload)
    d_pre, payload = lax.optimization_barrier((d_pre, payload))
    d_normed_own, d_normed_other = normed_back(spots, d_pre, w_heads_across)
    got = swap(d_normed_other, CORE)
    total = wide(d_normed_own) + wide(got)
    keep, send = total[: 2 * TOK], low(total[2 * TOK :])
    payload, sums_got, out_got = (after(array, send) for array in (payload, sums_got, out_got))
    sums_keep, sums_got = plane_rest(index, low(wide(sums_keep) + wide(sums_got)))
    sums_out = low(wide(grad_out[:8]) + wide(out_got))
    heads_keep, heads_got = plane_halves(index, payload, 3)
    out_keep, out_got = plane_halves(index, sums_out, 2)
    got, heads_got, out_got, sums_got, result = lax.optimization_barrier(
        (swap(send, *RING_STEPS[1]), heads_got, out_got, sums_got, result)
    )
    sums = wide(sums_keep) + sum(wide(part) for part in sums_got)
    sums_out = low(wide(out_keep) + wide(out_got))
    heads_sums = low(wide(heads_keep) + wide(heads_got))
    total = keep + wide(got)
    heads_keep, heads_got = plane_halves(index, heads_sums, 2)
    out_keep, out_got = plane_rest(index, sums_out)
    got, heads_got, out_got = lax.optimization_barrier(
        (swap(low(total[TOK:]), *RING_STEPS[0]), heads_got, out_got)
    )
    sum_out = wide(out_keep) + sum(wide(part) for part in out_got)
    heads_sums = low(wide(heads_keep) + wide(heads_got))
    d_normed = total[:TOK] + wide(got)
    input_grad = d_middle + norm_back(wide(inputs), gain_attn, d_normed)
    heads_keep, heads_got = plane_rest(index, heads_sums)
    home, heads_got = lax.optimization_barrier((cross(low(input_grad)), heads_got))
    input_grad = jnp.where(straight, input_grad, wide(home))
    heads_sums = low(wide(heads_keep) + sum(wide(part) for part in heads_got))
    sum_down = tiles_flat(sums[:, 768:])
    sum_out = sum_out.reshape(4, 16, 256).transpose(1, 0, 2).reshape(16, WIDTH)
    result = jnp.concatenate([middle + wide(result), sum_out], axis=0)
    result = cross(after(low(result), heads_sums))
    ring_grads = jnp.concatenate([heads_sums, low(sums[:, :768])], axis=1)
    ring_grads = exchange_ring(index, ring_grads.reshape(8, 8, 1408))
    heads_grad, units_grad = wide(ring_grads[..., :640]), ring_grads[..., 640:]
    activations = result[:TOK]
    sum_out = jnp.where(straight, sum_out, wide(result[TOK:]))
    column = jnp.arange(768, dtype=jnp.int32)
    column = column // 24 % 2 * 384 + column // 48 * 24 + column % 24
    column = after(column, middle)
    hits = lax.broadcasted_iota(jnp.int32, (768, 768), 0) == column[None, :]
    units_grad = units_grad.reshape(4, 2, 8, 2, 384).transpose(3, 2, 0, 1, 4).reshape(64, 768)
    units_grad = dot(units_grad, hits.astype(jnp.bfloat16)).reshape(2, 8, FF)
    sum_query = heads_grad[..., :256].transpose(1, 0, 2).reshape(8, -1)
    sum_key = heads_grad[..., 256:384].transpose(1, 0, 2).reshape(8, -1)
    sum_value = heads_grad[..., 384:512].transpose(1, 0, 2).reshape(8, -1)
    sum_gains = jnp.sum(heads_grad[:, 0, 512:530], axis=0)
    return (
        activations[None],
        input_grad[None],
        sum_query,
        sum_key,
        sum_value,
        sum_out,
        units_grad[0],
        units_grad[1],
        sum_down,
        sum_gains,
    )


def solution(mesh):
    chips = Mesh(mesh.devices.reshape(4, 2, 2, 4, 2), AXES)
    rows = P(AXES, None)
    tokens = P(("zl", "y", "core"), ("x", "zh"), None)
    lengths = P(("zl", "y", "core"), None)
    return jax.shard_map(
        on_device,
        mesh=chips,
        in_specs=(tokens, lengths, *([rows] * 7), P(AXES), tokens),
        out_specs=(tokens, tokens, *([rows] * 7), P(AXES)),
        check_vma=False,
    )
```

```python
import jax
import jax.numpy as jnp
from jax import lax
from jax.experimental import pallas as pl
from jax.experimental.pallas import tpu as pltpu
from jax.sharding import Mesh
from jax.sharding import PartitionSpec as P

HEADS = 16
KV_HEADS = 8
HEAD = 128
EPSILON = 1e-06
ROPE_BASE = 1000000.0
DEVICES = 128
WIDTH = 1024
FF = 3072
TOK = 192
PACK = 1536
BLOCK = 256
LOG2E = 1.4426950408889634
SCALE = HEAD ** (-0.5)
VMEM_LIMIT = 48 * 1024 * 1024

AXES = ("x", "zh", "zl", "y", "core")
RING = ("x", "core")
PLANE = ("zh", "zl", "y")
XA, XB, ZA, ZB, YA, YB, CORE = 32, 96, 8, 24, 2, 6, 1
RING_STEPS = ((XA, XB), (XB, XA))
RING_SPOTS = ((0, 1, 3, 2), (0, 2, 3, 1))
PLANE_STEPS = ((YA, ZA), (YB, ZB), (ZA, YA), (ZB, YB))
BIT = {YA: 1, YB: 2, ZA: 3, ZB: 4}


def swap(values, mask, other_mask=None):
    masks = (mask, mask if other_mask is None else other_mask)
    return lax.ppermute(values, AXES, [(k, k ^ masks[k & 1]) for k in range(DEVICES)])


def crossed(k):
    return k ^ 17 if (k >> 4 ^ k) & 1 else k


def cross(values):
    return lax.ppermute(values, AXES, [(k, crossed(k)) for k in range(DEVICES)])


def cross_and_swap(values, masks):
    return lax.ppermute(
        values, AXES, [(crossed(k ^ masks[k & 1]), k) for k in range(DEVICES)]
    )


def after(value, *others):
    return lax.optimization_barrier((value, *others))[0] if others else value


def low(values):
    return values.astype(jnp.bfloat16)


def wide(values):
    return values.astype(jnp.float32)


def dot(left, right):
    return jnp.dot(left, right, preferred_element_type=jnp.float32)


def contract_rows(left, right):
    return lax.dot_general(
        left, right, (((0,), (0,)), ((), ())), preferred_element_type=jnp.float32
    )


def contract_cols(left, right):
    return lax.dot_general(
        left, right, (((1,), (1,)), ((), ())), preferred_element_type=jnp.float32
    )


def norm_scale(values):
    return lax.rsqrt(jnp.mean(values * values, axis=-1, keepdims=True) + EPSILON)


def norm_back(values, gain, grad):
    scale = norm_scale(values)
    normal = values * scale
    inner = grad * gain
    return scale * (inner - normal * jnp.mean(inner * normal, axis=-1, keepdims=True))


def rope(values, cosine, sine):
    return values * cosine + pltpu.roll(values, 64, 1) * sine


def rope_back(grad, cosine, sine):
    return grad * cosine + pltpu.roll(grad * sine, 64, 1)


def ring_specs(columns):
    return [
        pl.BlockSpec((TOK, columns), lambda x, spots: (spots[x], 0)),
        pl.BlockSpec((TOK, columns), lambda x, spots: (spots[4 + x], 0)),
    ]


def pack_spec(columns):
    return pl.BlockSpec((2 * TOK, columns), lambda x, spots: (x, 0))


def whole_spec(shape):
    return pl.BlockSpec(shape, lambda x, spots: (0, 0))


def own_rows(spots):
    return pl.ds(pl.multiple_of(spots[8] * TOK, TOK), TOK)


def other_rows(spots):
    return pl.ds(pl.multiple_of((1 - spots[8]) * TOK, TOK), TOK)


def shaped(shape, dtype, kept=False):
    return pltpu.HBM(shape, dtype) if kept else jax.ShapeDtypeStruct(shape, dtype)


def in_hbm(array):
    return pltpu.with_memory_space_constraint(array, pltpu.HBM)


def cost(microseconds):
    return pl.CostEstimate(
        flops=0, bytes_accessed=int(microseconds * 0.1e6), transcendentals=0
    )


def ring_call(kernel, name, in_specs, out_specs, out_shape, time, spots, *operands, scratch=()):
    return pl.pallas_call(
        kernel,
        grid_spec=pltpu.PrefetchScalarGridSpec(
            num_scalar_prefetch=1,
            grid=(4,),
            in_specs=in_specs,
            out_specs=out_specs,
            scratch_shapes=scratch,
        ),
        out_shape=out_shape,
        compiler_params=pltpu.CompilerParams(vmem_limit_bytes=VMEM_LIMIT),
        cost_estimate=cost(time),
        name=name,
    )(spots, *operands)


def qkv_kernel(
    spots, own_ref, other_ref, heads_ref, ga_ref, gq_ref, gk_ref, cos_ref, sin_ref,
    normed_ref, pre_ref, qkv_ref, kept_ref, across_ref, w_ref,
):
    @pl.when(pl.program_id(0) == 0)
    def _():
        for z in range(4):
            for y in range(4):
                block = jnp.where(spots[9] == 1, y * 4 + z, z * 4 + y)
                for x in range(4):
                    row = (x * 16 + z * 4 + y) * 16
                    w_ref[row : row + 16, :] = heads_ref[block, x * 16 : x * 16 + 16, :512]
        across_ref[...] = w_ref[...].T

    for ref, rows in ((own_ref, own_rows(spots)), (other_ref, other_rows(spots))):
        x = wide(ref[...])
        normed_ref[rows, :] = low(x * norm_scale(x) * ga_ref[...])
    pre = dot(normed_ref[...], w_ref[...])
    pre_ref[...] = pre[:, : 3 * HEAD]
    cosine, sine = cos_ref[...], sin_ref[...]
    for h in range(3):
        u = pre[:, h * HEAD : (h + 1) * HEAD]
        gain = gk_ref[...] if h == 2 else gq_ref[...]
        normal = u * norm_scale(u) * gain
        qkv_ref[:, h * HEAD : (h + 1) * HEAD] = low(rope(normal, cosine, sine))
    qkv_ref[:, 3 * HEAD :] = low(pre[:, 3 * HEAD :])
    kept_ref[...] = qkv_ref[...]


def project(spots, own, other, heads, gain_attn, gain_query, gain_key, cosine, sine):
    return ring_call(
        qkv_kernel,
        "project",
        ring_specs(WIDTH)
        + [pl.BlockSpec(heads.shape, lambda x, spots: (0, 0, 0))]
        + [whole_spec((1, WIDTH)), whole_spec((1, HEAD)), whole_spec((1, HEAD))]
        + [pack_spec(HEAD), pack_spec(HEAD)],
        [pack_spec(WIDTH), pack_spec(3 * HEAD), pack_spec(512), pack_spec(512)]
        + [whole_spec((512, WIDTH)), whole_spec((WIDTH, 512))],
        [
            shaped((PACK, WIDTH), jnp.bfloat16, True),
            shaped((PACK, 3 * HEAD), jnp.float32, True),
            shaped((PACK, 512), jnp.bfloat16),
            shaped((PACK, 512), jnp.bfloat16, True),
            shaped((512, WIDTH), jnp.bfloat16, True),
            shaped((WIDTH, 512), jnp.bfloat16, True),
        ],
        8, spots, own, other, heads, gain_attn, gain_query, gain_key, cosine, sine,
    )


def to_ring_kernel(spots, rows_ref, heads_ref, own_ref, other_ref, w_ref):
    @pl.when(pl.program_id(0) == 0)
    def _():
        for z in range(4):
            for y in range(4):
                block = jnp.where(spots[9] == 1, y * 4 + z, z * 4 + y)
                row = (z % 2 * 8 + y * 2 + z // 2) * 16
                for n in range(4):
                    piece = heads_ref[block, n * 16 : n * 16 + 16, 640:]
                    w_ref[row : row + 16, n * 256 : n * 256 + 256] = piece

    own_ref[...] = low(dot(rows_ref[own_rows(spots), :], w_ref[...]))
    other_ref[...] = low(dot(rows_ref[other_rows(spots), :], w_ref[...]))


def to_ring(spots, rows, heads):
    half = shaped((PACK // 2, WIDTH), jnp.bfloat16)
    return ring_call(
        to_ring_kernel, "to_ring",
        [pack_spec(256), pl.BlockSpec(heads.shape, lambda x, spots: (0, 0, 0))],
        ring_specs(WIDTH) + [whole_spec((256, WIDTH))],
        [half, half, shaped((256, WIDTH), jnp.bfloat16, True)], 3, spots, rows, heads,
    )


def to_pack_kernel(spots, own_ref, other_ref, w_ref, rows_ref):
    rows_ref[own_rows(spots), :] = low(dot(own_ref[...], w_ref[...]))
    rows_ref[other_rows(spots), :] = low(dot(other_ref[...], w_ref[...]))


def to_pack(spots, own, other, weights):
    return ring_call(
        to_pack_kernel, "to_pack", ring_specs(own.shape[1]) + [whole_spec(weights.shape)],
        [pack_spec(WIDTH)], [shaped((PACK, WIDTH), jnp.bfloat16)], 4, spots, own, other, weights,
    )[0]


def out_back_kernel(
    spots, own_ref, other_ref, attended_ref, w_ref, d_attended_ref, d_w_ref, rows_ref, total_ref
):
    step = pl.program_id(0)

    @pl.when(step == 0)
    def _():
        total_ref[...] = jnp.zeros_like(total_ref)

    rows_ref[own_rows(spots), :] = own_ref[...]
    rows_ref[other_rows(spots), :] = other_ref[...]
    d_attended_ref[...] = low(contract_cols(rows_ref[...], w_ref[...]))
    total_ref[...] += contract_rows(attended_ref[...], rows_ref[...])

    @pl.when(step == pl.num_programs(0) - 1)
    def _():
        for z in range(4):
            for y in range(4):
                spot = jnp.where(spots[9] == 1, y * 4 + z, z * 4 + y)
                spot = jnp.where(spots[10] == 1, (spot + 8) % 16, spot)
                row = (z % 2 * 8 + y * 2 + z // 2) * 16
                for n in range(4):
                    piece = total_ref[row : row + 16, n * 256 : n * 256 + 256]
                    d_w_ref[spot, n * 16 : n * 16 + 16, :] = low(piece)


def out_back(spots, own, other, attended, weights):
    return ring_call(
        out_back_kernel, "out_back",
        ring_specs(WIDTH) + [pack_spec(256), whole_spec((256, WIDTH))],
        [pack_spec(256), pl.BlockSpec((16, 64, 256), lambda x, spots: (0, 0, 0))],
        [shaped((PACK, 256), jnp.bfloat16), shaped((16, 64, 256), jnp.bfloat16, True)],
        5, spots, own, other, in_hbm(attended), in_hbm(weights),
        scratch=[pltpu.VMEM((2 * TOK, WIDTH), jnp.bfloat16), pltpu.VMEM((256, WIDTH), jnp.float32)],
    )


def row_start(rows, ends):
    first, second = ends
    return jnp.where(rows >= second, second, jnp.where(rows >= first, first, 0))


def block_mask(q_block, k_block, ends, transposed):
    last = PACK // BLOCK - 1
    q_axis, k_axis = (1, 0) if transposed else (0, 1)
    q_rows = q_block * BLOCK + lax.broadcasted_iota(jnp.int32, (BLOCK, BLOCK), q_axis)
    k_rows = k_block * BLOCK + lax.broadcasted_iota(jnp.int32, (BLOCK, BLOCK), k_axis)
    mask = None
    if k_block == q_block:
        mask = k_rows <= q_rows
    if k_block == 0 or q_block == last:
        begun = k_rows >= row_start(q_rows, ends)
        mask = begun if mask is None else mask & begun
    return mask


def for_each_block(step):
    for q_block in range(PACK // BLOCK):

        @pl.when(pl.program_id(0) == q_block)
        def _(q_block=q_block):
            step(q_block)


def attend_kernel(ends_ref, q_ref, k_ref, v_ref, out_ref, kept_ref, inverse_ref):
    ends = (ends_ref[0], ends_ref[1])

    def step(q_block):
        seen = (q_block + 1) * BLOCK
        for h in range(2):
            columns = slice(h * HEAD, (h + 1) * HEAD)
            scores = contract_cols(q_ref[:, columns], k_ref[:seen, :])
            part, shifted = 0.0, []
            for k_block in range(q_block + 1):
                block = scores[:, k_block * BLOCK : (k_block + 1) * BLOCK]
                block = jnp.exp2(block * (SCALE * LOG2E))
                mask = block_mask(q_block, k_block, ends, False)
                if mask is not None:
                    block = jnp.where(mask, block, 0.0)
                part += block[:, :HEAD] + block[:, HEAD:]
                shifted.append(low(block))
            total = dot(jnp.concatenate(shifted, axis=1), v_ref[:seen, :])
            row_total = jnp.sum(part, axis=1, keepdims=True)
            out_ref[:, columns] = low(total * (1.0 / row_total))
            across = jnp.sum(jnp.swapaxes(part, 0, 1), axis=0, keepdims=True)
            inverse_ref[h : h + 1, :] = 1.0 / across
        kept_ref[...] = out_ref[...]

    for_each_block(step)


def attend(ends, qkv):
    return pl.pallas_call(
        attend_kernel,
        grid_spec=pltpu.PrefetchScalarGridSpec(
            num_scalar_prefetch=1,
            grid=(PACK // BLOCK,),
            in_specs=[
                pl.BlockSpec((BLOCK, 2 * HEAD), lambda q, ends: (q, 0)),
                pl.BlockSpec((PACK, HEAD), lambda q, ends: (0, 2)),
                pl.BlockSpec((PACK, HEAD), lambda q, ends: (0, 3)),
            ],
            out_specs=[
                pl.BlockSpec((BLOCK, 2 * HEAD), lambda q, ends: (q, 0)),
                pl.BlockSpec((BLOCK, 2 * HEAD), lambda q, ends: (q, 0)),
                pl.BlockSpec((2, BLOCK), lambda q, ends: (0, q)),
            ],
        ),
        out_shape=[
            shaped((PACK, 2 * HEAD), jnp.bfloat16),
            shaped((PACK, 2 * HEAD), jnp.bfloat16, True),
            shaped((2, PACK), jnp.float32, True),
        ],
        compiler_params=pltpu.CompilerParams(vmem_limit_bytes=VMEM_LIMIT),
        cost_estimate=cost(6),
        name="attend",
    )(ends, qkv, qkv, qkv)


def attend_back_kernel(
    ends_ref, q_ref, k_ref, v_ref, grad_ref, out_ref, inverse_ref, dq_ref, dk_ref, dv_ref
):
    ends = (ends_ref[0], ends_ref[1])

    @pl.when(pl.program_id(0) == 0)
    def _():
        dk_ref[...] = jnp.zeros_like(dk_ref)
        dv_ref[...] = jnp.zeros_like(dv_ref)

    def both_heads(ref):
        return jnp.concatenate([ref[:, :HEAD], ref[:, HEAD:]], axis=0)

    def step(q_block):
        seen = (q_block + 1) * BLOCK
        queries, grads = both_heads(q_ref), both_heads(grad_ref)
        product = wide(grads) * wide(both_heads(out_ref))
        delta = jnp.sum(jnp.swapaxes(product, 0, 1), axis=0, keepdims=True)
        inverse = jnp.concatenate([inverse_ref[0:1, :], inverse_ref[1:2, :]], axis=1)
        scores = contract_cols(k_ref[:seen, :], queries)
        d_probs = contract_cols(v_ref[:seen, :], grads)
        probs, d_scores = [], []
        for k_block in range(q_block + 1):
            rows = slice(k_block * BLOCK, (k_block + 1) * BLOCK)
            prob = jnp.exp2(scores[rows] * (SCALE * LOG2E)) * inverse
            mask = block_mask(q_block, k_block, ends, True)
            if mask is not None:
                prob = jnp.where(jnp.concatenate([mask, mask], axis=1), prob, 0.0)
            d_scores.append(low(prob * ((d_probs[rows] - delta) * SCALE)))
            probs.append(low(prob))
        probs = jnp.concatenate(probs, axis=0)
        d_scores = jnp.concatenate(d_scores, axis=0)
        dk_ref[:seen, :] += dot(d_scores, queries)
        dv_ref[:seen, :] += dot(probs, grads)
        d_queries = contract_rows(d_scores, k_ref[:seen, :])
        dq_ref[:, :HEAD] = d_queries[:BLOCK]
        dq_ref[:, HEAD:] = d_queries[BLOCK:]

    for_each_block(step)


def attend_back(ends, qkv, grad, out, inverse):
    qkv, out, inverse = in_hbm(qkv), in_hbm(out), in_hbm(inverse)
    by_block = pl.BlockSpec((BLOCK, 2 * HEAD), lambda q, ends: (q, 0))
    whole = pl.BlockSpec((PACK, HEAD), lambda q, ends: (0, 0))
    return pl.pallas_call(
        attend_back_kernel,
        grid_spec=pltpu.PrefetchScalarGridSpec(
            num_scalar_prefetch=1,
            grid=(PACK // BLOCK,),
            in_specs=[
                by_block,
                pl.BlockSpec((PACK, HEAD), lambda q, ends: (0, 2)),
                pl.BlockSpec((PACK, HEAD), lambda q, ends: (0, 3)),
                by_block,
                by_block,
                pl.BlockSpec((2, BLOCK), lambda q, ends: (0, q)),
            ],
            out_specs=[by_block, whole, whole],
        ),
        out_shape=[
            jax.ShapeDtypeStruct((PACK, 2 * HEAD), jnp.float32),
            jax.ShapeDtypeStruct((PACK, HEAD), jnp.float32),
            jax.ShapeDtypeStruct((PACK, HEAD), jnp.float32),
        ],
        compiler_params=pltpu.CompilerParams(vmem_limit_bytes=VMEM_LIMIT),
        cost_estimate=cost(11),
        name="attend_back",
    )(ends, qkv, qkv, qkv, grad, out, inverse)


def qkv_back_kernel(
    spots, pre_ref, dq_ref, dk_ref, dv_ref, cos_ref, sin_ref, gq_ref, gk_ref, d_pre_ref, d_head_ref
):
    @pl.when(pl.program_id(0) == 0)
    def _():
        d_head_ref[...] = jnp.zeros_like(d_head_ref)

    cosine, sine = cos_ref[...], sin_ref[...]
    for h in range(3):
        u = pre_ref[:, h * HEAD : (h + 1) * HEAD]
        gain = gk_ref[...] if h == 2 else gq_ref[...]
        grad = dk_ref[...] if h == 2 else dq_ref[:, h * HEAD : (h + 1) * HEAD]
        grad = rope_back(grad, cosine, sine)
        row = 1 if h == 2 else 0
        scale = norm_scale(u)
        normal = u * scale
        d_head_ref[row : row + 1, :] += jnp.sum(grad * normal, axis=0, keepdims=True)
        inner = grad * gain
        inner = scale * (inner - normal * jnp.mean(inner * normal, axis=-1, keepdims=True))
        d_pre_ref[:, h * HEAD : (h + 1) * HEAD] = low(inner)
    d_pre_ref[:, 3 * HEAD :] = low(dv_ref[...])


def project_back(spots, pre, d_query, d_key, d_value, cosine, sine, gain_query, gain_key):
    return ring_call(
        qkv_back_kernel,
        "project_back",
        [pack_spec(3 * HEAD), pack_spec(2 * HEAD), pack_spec(HEAD), pack_spec(HEAD)]
        + [pack_spec(HEAD), pack_spec(HEAD), whole_spec((1, HEAD)), whole_spec((1, HEAD))],
        [pack_spec(512), whole_spec((2, HEAD))],
        [shaped((PACK, 512), jnp.bfloat16), shaped((2, HEAD), jnp.float32)],
        5, spots, in_hbm(pre), d_query, d_key, d_value, in_hbm(cosine), in_hbm(sine), gain_query, gain_key,
    )


def normed_back_kernel(spots, d_pre_ref, w_ref, own_ref, other_ref):
    own_ref[...] = low(dot(d_pre_ref[own_rows(spots), :], w_ref[...]))
    other_ref[...] = low(dot(d_pre_ref[other_rows(spots), :], w_ref[...]))


def normed_back(spots, d_pre, weights):
    half = shaped((PACK // 2, WIDTH), jnp.bfloat16)
    return ring_call(
        normed_back_kernel, "normed_back", [pack_spec(512), whole_spec((512, WIDTH))], ring_specs(WIDTH),
        [half, half], 4, spots, d_pre, in_hbm(weights),
    )


def plane_order(core, blocks):
    return jnp.where(core == 1, jnp.swapaxes(blocks, 0, 1), blocks)


def plane_bit(index, masks):
    return jnp.where(index & 1 == 1, index >> BIT[masks[1]], index >> BIT[masks[0]]) & 1


def gather_plane_step(index, block, step):
    got = swap(block, *PLANE_STEPS[step])
    return jnp.where(
        plane_bit(index, PLANE_STEPS[step]) == 1,
        jnp.concatenate([got, block], axis=0),
        jnp.concatenate([block, got], axis=0),
    )


def gather_plane_end(index, block):
    shape = block.shape[1:]
    return plane_order(index & 1, block.reshape((4, 4) + shape)).reshape((16,) + shape)


def plane_halves(index, blocks, step):
    later = plane_bit(index, PLANE_STEPS[step])
    half = blocks.shape[0] // 2
    keep = lax.dynamic_slice_in_dim(blocks, later * half, half, axis=0)
    send = lax.dynamic_slice_in_dim(blocks, (1 - later) * half, half, axis=0)
    return keep, swap(send, *PLANE_STEPS[step])


def scatter_plane_step(index, blocks, step, *beside):
    keep, got = plane_halves(index, blocks, step)
    return low(wide(keep) + wide(after(got, *beside)))


def plane_rest(index, blocks):
    place = jnp.where(index & 1 == 1, index >> 3, index >> 1) & 3
    block = lambda at: lax.dynamic_index_in_dim(blocks, at, 0, keepdims=False)
    return block(place), [swap(block(place ^ k), k << 1, k << 3) for k in range(1, 4)]


def plane_blocks(core, blocks):
    shape = blocks.shape[1:]
    return plane_order(core, blocks.reshape((4, 4) + shape)).reshape((16,) + shape)


def gather_ring(rows, beside=((), ())):
    for masks, others in zip(RING_STEPS, beside):
        rows = jnp.concatenate([rows, after(swap(rows, *masks), *others)], axis=0)
    return rows


def scatter_ring(own, other, steps=2):
    totals = [wide(own) + wide(swap(other, CORE))]
    for masks in RING_STEPS[: -steps - 1 : -1]:
        half = totals[-1].shape[0] // 2
        totals.append(totals[-1][:half] + wide(swap(low(totals[-1][half:]), *masks)))
    return totals


def exchange_ring(index, blocks):
    core, x = index & 1, index >> 5
    shape = blocks.shape[1:]
    blocks = blocks.reshape((4, 2) + shape)
    take = lambda array, at, axis: lax.dynamic_slice_in_dim(array, at, 1, axis)
    got = swap(take(blocks, 1 - core, 1), CORE)
    keep = take(blocks, core, 1)
    blocks = jnp.concatenate(
        [jnp.where(core == 1, got, keep), jnp.where(core == 1, keep, got)], axis=1
    )
    parts = [take(blocks, x, 0)] + [
        swap(take(blocks, x ^ k, 0), k << 5) for k in range(1, 4)
    ]
    parts = jnp.concatenate(parts, axis=0)
    parts = jnp.where(x & 1 == 1, parts.reshape((2, 2, 2) + shape)[:, ::-1].reshape(parts.shape), parts)
    parts = jnp.where(x & 2 == 2, parts.reshape((2, 4) + shape)[::-1].reshape(parts.shape), parts)
    return parts.reshape((8,) + shape)


def tiles_tall(block):
    lead = block.shape[:-2]
    n = len(lead)
    block = block.reshape(lead + (-1, 8, 8, HEAD))
    block = block.transpose(tuple(range(n)) + (n + 2, n + 1, n, n + 3))
    return block.reshape(lead + (64, -1))


def tiles_flat(block):
    lead = block.shape[:-2]
    n = len(lead)
    block = block.reshape(lead + (8, 8, -1, HEAD))
    block = block.transpose(tuple(range(n)) + (n + 2, n + 1, n, n + 3))
    return block.reshape(lead + (-1, WIDTH))


def rows_by_device(blocks):
    n = blocks.shape[-1]
    return blocks.reshape(16, 4, 2, 8, n).transpose(1, 0, 2, 3, 4).reshape(WIDTH, n)


def rows_by_plane(rows):
    n = rows.shape[-1]
    return rows.reshape(4, 16, 2, 8, n).transpose(1, 0, 2, 3, 4).reshape(16, 64, n)


def on_device(
    hidden, lengths, w_query, w_key, w_value, w_out, w_gate, w_up, w_down, gains, cotangent
):
    index = lax.axis_index(AXES).astype(jnp.int32)
    core, x = index & 1, index >> 5
    straight = (index >> 4 & 1) == core
    spot_of = lambda c: jnp.where(c == 1, jnp.asarray(RING_SPOTS[1]), jnp.asarray(RING_SPOTS[0]))
    chips = x ^ jnp.arange(4, dtype=jnp.int32)
    spots = jnp.concatenate(
        [spot_of(core)[chips], spot_of(1 - core)[chips], core[None], core[None]]
        + [plane_bit(index, PLANE_STEPS[3])[None]]
    ).astype(jnp.int32)

    local = jnp.concatenate(
        [
            w_query.reshape(8, KV_HEADS, 256).transpose(1, 0, 2),
            w_key.reshape(8, KV_HEADS, HEAD).transpose(1, 0, 2),
            w_value.reshape(8, KV_HEADS, HEAD).transpose(1, 0, 2),
            jnp.broadcast_to(jnp.pad(gains[None, None, :], ((0, 0), (0, 7), (0, 110))), (8, 8, 128)),
        ]
        + [
            weight.reshape(8, 4, 16, 2, 24).transpose(1, 3, 0, 2, 4).reshape(8, 8, 384)
            for weight in (w_gate, w_up)
        ],
        axis=2,
    )
    digits = jnp.pad(low(jnp.stack([lengths[0] // 64, lengths[0] % 64])), ((0, 14), (0, WIDTH - 3)))
    pieces = cross(jnp.concatenate([w_out, digits], axis=0))
    rows = after(hidden[0], local)
    inputs = cross(rows)
    second = cross_and_swap(rows, RING_STEPS[0])
    digits = pieces[16:18, :3].astype(jnp.int32)
    lengths = (digits[0] * 64 + digits[1])[None]
    pieces = pieces[:16].reshape(16, 4, 256).transpose(1, 0, 2).reshape(64, 256)
    local = exchange_ring(index, local).reshape(64, 1408)
    d_result = cross(after(cotangent[0], local))
    heads = jnp.concatenate([local[:, :640], pieces], axis=1)[None]
    heads = gather_plane_step(index, after(heads, inputs, second), 0)
    heads = gather_plane_step(index, after(heads, d_result), 1)
    d_result_own = jnp.concatenate([d_result, swap(d_result, *RING_STEPS[0])], axis=0)
    heads = gather_plane_step(index, heads, 2)
    heads = gather_plane_step(index, after(heads, d_result_own), 3)
    gain_all = plane_order(core, heads[:, ::8, 512:530].reshape(4, 4, 8, 18))
    gain_all = gain_all.reshape(16, 4, 2, 18).transpose(1, 0, 2, 3)
    gain_all = wide(gain_all.reshape(1, -1))
    gain_attn, gain_mlp = gain_all[:, :WIDTH], gain_all[:, WIDTH : 2 * WIDTH]
    gain_query = gain_all[:, 2 * WIDTH : 2 * WIDTH + HEAD]
    gain_key = gain_all[:, 2 * WIDTH + HEAD :]

    def rest_of_ring(rows):
        rows = jnp.concatenate([rows, swap(rows, *RING_STEPS[1])], axis=0)
        return rows, swap(rows, CORE)

    inputs_own, inputs_other = rest_of_ring(jnp.concatenate([inputs, second], axis=0))
    ends = jnp.stack([lengths[0, 0], lengths[0, 0] + lengths[0, 1]]).astype(jnp.int32)
    token = jnp.arange(PACK, dtype=jnp.int32)
    position = wide(token - row_start(token, (ends[0], ends[1])))
    inverse = jnp.power(ROPE_BASE, -2.0 * jnp.arange(HEAD // 2, dtype=jnp.float32) / HEAD)
    angle = position[:, None] * inverse[None, :]
    cosine, sine = jnp.cos(angle), jnp.sin(angle)
    cosine = jnp.concatenate([cosine, cosine], axis=1)
    sine = jnp.concatenate([-sine, sine], axis=1)

    d_result_own = jnp.concatenate([d_result_own, swap(d_result_own, *RING_STEPS[1])], axis=0)
    normed, pre, qkv, qkv_kept, w_heads_across, w_heads = project(
        spots, inputs_own, inputs_other, heads, gain_attn, gain_query, gain_key, cosine, sine
    )
    qkv, d_result_own = lax.optimization_barrier((qkv, d_result_own))
    attended, attended_kept, inverse_total = attend(ends, qkv)
    out_own, out_other, w_rows = to_ring(spots, attended, heads)
    middle_steps = scatter_ring(out_own, out_other)
    d_result_other = swap(after(d_result_own, middle_steps[0]), CORE)
    units = jnp.concatenate([local[:, 640:], tiles_tall(w_down)], axis=1)[None]
    units = gather_plane_step(index, after(units, out_own), 0)
    units = gather_plane_step(index, after(units, middle_steps[0]), 1)
    units = gather_plane_step(index, after(units, middle_steps[1]), 2)
    middle = wide(inputs) + middle_steps[2]
    middle_scale = norm_scale(middle)
    mixed = low(middle * middle_scale * gain_mlp)
    mixed_own = gather_ring(mixed)
    mixed_other = swap(mixed_own, CORE)
    units = gather_plane_step(index, units, 3)
    units = plane_blocks(core, units)
    full_units = rows_by_device(units[..., :768])
    full_down = tiles_flat(units[..., 768:]).reshape(384, WIDTH)
    full_units, full_down = lax.optimization_barrier((full_units, full_down))

    def feed_forward(rows, d_rows):
        pre = dot(rows, full_units)
        gate_pre, up_pre = pre[:, :384], pre[:, 384:]
        sigmoid = 1.0 / (1.0 + jnp.exp(-gate_pre))
        silu = gate_pre * sigmoid
        act = low(silu * up_pre)
        d_act = contract_cols(d_rows, full_down)
        d_gate = low(d_act * up_pre * (sigmoid + silu * (1.0 - sigmoid)))
        d_up = low(d_act * silu)
        d_pre = jnp.concatenate([d_gate, d_up], axis=1)
        return act, d_pre, low(contract_cols(d_pre, full_units))

    act_own, d_pre_own, d_mixed_own = feed_forward(mixed_own, d_result_own)
    act_other, d_pre_other, d_mixed_other = feed_forward(mixed_other, d_result_other)
    d_mixed_steps = scatter_ring(d_mixed_own, d_mixed_other)
    d_mixed = d_mixed_steps[-1]
    d_middle = wide(d_result) + norm_back(middle, gain_mlp, d_mixed)
    d_gain_mlp = jnp.sum(middle * middle_scale * d_mixed, axis=0)

    late = lambda array: after(array, d_mixed_steps[0])
    grad_units = contract_rows(mixed_own, late(d_pre_own)) + contract_rows(mixed_other, late(d_pre_other))
    grad_down = contract_rows(late(act_own), d_result_own) + contract_rows(late(act_other), d_result_other)
    grad_down = low(grad_down).reshape(16, 3, 8, 8, HEAD).transpose(0, 3, 2, 1, 4)
    grads = jnp.concatenate([rows_by_plane(low(grad_units)), grad_down.reshape(16, 64, 384)], axis=2)
    grads = plane_blocks(core, grads)
    act_own, act_other = (after(act, d_middle) for act in (act_own, act_other))
    result = to_pack(spots, act_own, act_other, full_down)
    keep, got = plane_halves(index, grads, 3)
    d_branch_own = gather_ring(after(low(d_middle), grads), ((), (result, got)))
    sums = low(wide(keep) + wide(got))
    d_branch_other = swap(d_branch_own, CORE)
    result = lax.psum_scatter(after(result, d_branch_own), RING, scatter_dimension=0, tiled=True)

    d_attended, grad_out = out_back(spots, d_branch_own, d_branch_other, attended_kept, w_rows)
    d_attended, grad_out = lax.optimization_barrier((d_attended, grad_out))
    sums_keep, sums_got = plane_halves(index, sums, 2)
    out_got = swap(grad_out[8:], *PLANE_STEPS[3])
    d_query, d_key, d_value = attend_back(ends, qkv_kept, d_attended, attended_kept, inverse_total)
    d_query, sums_got, out_got = lax.optimization_barrier((d_query, sums_got, out_got))
    d_pre, d_gain_heads = project_back(
        spots, pre, d_query, d_key, d_value, cosine, sine, gain_query, gain_key
    )
    grad_heads = contract_rows(normed, d_pre)
    d_gain_attn = jnp.sum(grad_heads * wide(w_heads), axis=1) / gain_attn[0]
    d_gains = jnp.concatenate([d_gain_attn, d_gain_mlp, d_gain_heads.reshape(-1)])
    d_gains = d_gains.reshape(4, 16, 2, 1, 18).transpose(1, 0, 2, 3, 4)
    payload = jnp.concatenate(
        [
            rows_by_plane(low(grad_heads)),
            low(jnp.pad(d_gains, ((0, 0),) * 3 + ((0, 7), (0, 110)))).reshape(16, 64, 128),
        ],
        axis=2,
    )
    payload = plane_blocks(core, payload)
    d_pre, payload = lax.optimization_barrier((d_pre, payload))
    d_normed_own, d_normed_other = normed_back(spots, d_pre, w_heads_across)
    got = swap(d_normed_other, CORE)
    total = wide(d_normed_own) + wide(got)
    keep, send = total[: 2 * TOK], low(total[2 * TOK :])
    payload, out_got = (after(array, send) for array in (payload, out_got))
    sums_out = low(wide(grad_out[:8]) + wide(out_got))
    heads_keep, heads_got = plane_halves(index, payload, 3)
    out_keep, out_got = plane_halves(index, sums_out, 2)
    got, heads_got, out_got, result = lax.optimization_barrier(
        (swap(send, *RING_STEPS[1]), heads_got, out_got, result)
    )
    sums_out = low(wide(out_keep) + wide(out_got))
    heads_sums = low(wide(heads_keep) + wide(heads_got))
    total = keep + wide(got)
    heads_keep, heads_got = plane_halves(index, heads_sums, 2)
    sums_keep, sums_got = plane_rest(index, low(wide(sums_keep) + wide(sums_got)))
    got, heads_got, sums_got = lax.optimization_barrier(
        (swap(low(total[TOK:]), *RING_STEPS[0]), heads_got, sums_got)
    )
    sums = wide(sums_keep) + sum(wide(part) for part in sums_got)
    heads_sums = low(wide(heads_keep) + wide(heads_got))
    d_normed = total[:TOK] + wide(got)
    input_grad = d_middle + norm_back(wide(inputs), gain_attn, d_normed)
    heads_keep, heads_got = plane_rest(index, heads_sums)
    out_keep, out_got = plane_rest(index, sums_out)
    home, heads_got, out_got = lax.optimization_barrier(
        (cross(low(input_grad)), heads_got, out_got)
    )
    sum_out = wide(out_keep) + sum(wide(part) for part in out_got)
    input_grad = jnp.where(straight, input_grad, wide(home))
    heads_sums = low(wide(heads_keep) + sum(wide(part) for part in heads_got))
    sum_down = tiles_flat(sums[:, 768:])
    sum_out = sum_out.reshape(4, 16, 256).transpose(1, 0, 2).reshape(16, WIDTH)
    result = jnp.concatenate([middle + wide(result), sum_out], axis=0)
    result = cross(after(low(result), heads_sums))
    ring_grads = jnp.concatenate([heads_sums, low(sums[:, :768])], axis=1)
    ring_grads = exchange_ring(index, ring_grads.reshape(8, 8, 1408))
    heads_grad, units_grad = wide(ring_grads[..., :640]), ring_grads[..., 640:]
    activations = result[:TOK]
    sum_out = jnp.where(straight, sum_out, wide(result[TOK:]))
    column = jnp.arange(768, dtype=jnp.int32)
    column = column // 24 % 2 * 384 + column // 48 * 24 + column % 24
    column = after(column, middle)
    hits = lax.broadcasted_iota(jnp.int32, (768, 768), 0) == column[None, :]
    units_grad = units_grad.reshape(4, 2, 8, 2, 384).transpose(3, 2, 0, 1, 4).reshape(64, 768)
    units_grad = dot(units_grad, hits.astype(jnp.bfloat16)).reshape(2, 8, FF)
    sum_query = heads_grad[..., :256].transpose(1, 0, 2).reshape(8, -1)
    sum_key = heads_grad[..., 256:384].transpose(1, 0, 2).reshape(8, -1)
    sum_value = heads_grad[..., 384:512].transpose(1, 0, 2).reshape(8, -1)
    sum_gains = jnp.sum(heads_grad[:, 0, 512:530], axis=0)
    return (
        activations[None],
        input_grad[None],
        sum_query,
        sum_key,
        sum_value,
        sum_out,
        units_grad[0],
        units_grad[1],
        sum_down,
        sum_gains,
    )


def solution(mesh):
    chips = Mesh(mesh.devices.reshape(4, 2, 2, 4, 2), AXES)
    rows = P(AXES, None)
    tokens = P(("zl", "y", "core"), ("x", "zh"), None)
    lengths = P(("zl", "y", "core"), None)
    return jax.shard_map(
        on_device,
        mesh=chips,
        in_specs=(tokens, lengths, *([rows] * 7), P(AXES), tokens),
        out_specs=(tokens, tokens, *([rows] * 7), P(AXES)),
        check_vma=False,
    )
```

```python
import jax
import jax.numpy as jnp
from jax import lax
from jax.experimental import pallas as pl
from jax.experimental.pallas import tpu as pltpu
from jax.sharding import Mesh
from jax.sharding import PartitionSpec as P

HEADS = 16
KV_HEADS = 8
HEAD = 128
EPSILON = 1e-06
ROPE_BASE = 1000000.0
DEVICES = 128
WIDTH = 1024
FF = 3072
TOK = 192
PACK = 1536
BLOCK = 256
LOG2E = 1.4426950408889634
SCALE = HEAD ** (-0.5)
VMEM_LIMIT = 48 * 1024 * 1024

AXES = ("x", "zh", "zl", "y", "core")
RING = ("x", "core")
PLANE = ("zh", "zl", "y")
XA, XB, ZA, ZB, YA, YB, CORE = 32, 96, 8, 24, 2, 6, 1
RING_STEPS = ((XA, XB), (XB, XA))
RING_SPOTS = ((0, 1, 3, 2), (0, 2, 3, 1))
PLANE_STEPS = ((YA, ZA), (YB, ZB), (ZA, YA), (ZB, YB))
BIT = {YA: 1, YB: 2, ZA: 3, ZB: 4}


def swap(values, mask, other_mask=None):
    masks = (mask, mask if other_mask is None else other_mask)
    return lax.ppermute(values, AXES, [(k, k ^ masks[k & 1]) for k in range(DEVICES)])


def crossed(k):
    return k ^ 17 if (k >> 4 ^ k) & 1 else k


def cross(values):
    return lax.ppermute(values, AXES, [(k, crossed(k)) for k in range(DEVICES)])


def after(value, *others):
    return lax.optimization_barrier((value, *others))[0] if others else value


def low(values):
    return values.astype(jnp.bfloat16)


def wide(values):
    return values.astype(jnp.float32)


def dot(left, right):
    return jnp.dot(left, right, preferred_element_type=jnp.float32)


def contract_rows(left, right):
    return lax.dot_general(
        left, right, (((0,), (0,)), ((), ())), preferred_element_type=jnp.float32
    )


def contract_cols(left, right):
    return lax.dot_general(
        left, right, (((1,), (1,)), ((), ())), preferred_element_type=jnp.float32
    )


def norm_scale(values):
    return lax.rsqrt(jnp.mean(values * values, axis=-1, keepdims=True) + EPSILON)


def norm_back(values, gain, grad):
    scale = norm_scale(values)
    normal = values * scale
    inner = grad * gain
    return scale * (inner - normal * jnp.mean(inner * normal, axis=-1, keepdims=True))


def rope(values, cosine, sine):
    return values * cosine + pltpu.roll(values, 64, 1) * sine


def rope_back(grad, cosine, sine):
    return grad * cosine + pltpu.roll(grad * sine, 64, 1)


def ring_specs(columns):
    return [
        pl.BlockSpec((TOK, columns), lambda x, spots: (spots[x], 0)),
        pl.BlockSpec((TOK, columns), lambda x, spots: (spots[4 + x], 0)),
    ]


def pack_spec(columns):
    return pl.BlockSpec((2 * TOK, columns), lambda x, spots: (x, 0))


def whole_spec(shape):
    return pl.BlockSpec(shape, lambda x, spots: (0, 0))


def own_rows(spots):
    return pl.ds(pl.multiple_of(spots[8] * TOK, TOK), TOK)


def other_rows(spots):
    return pl.ds(pl.multiple_of((1 - spots[8]) * TOK, TOK), TOK)


def shaped(shape, dtype, kept=False):
    return pltpu.HBM(shape, dtype) if kept else jax.ShapeDtypeStruct(shape, dtype)


def in_hbm(array):
    return pltpu.with_memory_space_constraint(array, pltpu.HBM)


def cost(microseconds):
    return pl.CostEstimate(
        flops=0, bytes_accessed=int(microseconds * 0.1e6), transcendentals=0
    )


def ring_call(kernel, name, in_specs, out_specs, out_shape, time, spots, *operands, scratch=()):
    return pl.pallas_call(
        kernel,
        grid_spec=pltpu.PrefetchScalarGridSpec(
            num_scalar_prefetch=1,
            grid=(4,),
            in_specs=in_specs,
            out_specs=out_specs,
            scratch_shapes=scratch,
        ),
        out_shape=out_shape,
        compiler_params=pltpu.CompilerParams(vmem_limit_bytes=VMEM_LIMIT),
        cost_estimate=cost(time),
        name=name,
    )(spots, *operands)


def qkv_kernel(
    spots, own_ref, other_ref, heads_ref, ga_ref, gq_ref, gk_ref, cos_ref, sin_ref,
    normed_ref, pre_ref, qkv_ref, kept_ref, across_ref, w_ref,
):
    @pl.when(pl.program_id(0) == 0)
    def _():
        for z in range(4):
            for y in range(4):
                block = jnp.where(spots[9] == 1, y * 4 + z, z * 4 + y)
                for x in range(4):
                    row = (x * 16 + z * 4 + y) * 16
                    w_ref[row : row + 16, :] = heads_ref[block, x * 16 : x * 16 + 16, :512]
        across_ref[...] = w_ref[...].T

    for ref, rows in ((own_ref, own_rows(spots)), (other_ref, other_rows(spots))):
        x = wide(ref[...])
        normed_ref[rows, :] = low(x * norm_scale(x) * ga_ref[...])
    pre = dot(normed_ref[...], w_ref[...])
    pre_ref[...] = pre[:, : 3 * HEAD]
    cosine, sine = cos_ref[...], sin_ref[...]
    for h in range(3):
        u = pre[:, h * HEAD : (h + 1) * HEAD]
        gain = gk_ref[...] if h == 2 else gq_ref[...]
        normal = u * norm_scale(u) * gain
        qkv_ref[:, h * HEAD : (h + 1) * HEAD] = low(rope(normal, cosine, sine))
    qkv_ref[:, 3 * HEAD :] = low(pre[:, 3 * HEAD :])
    kept_ref[...] = qkv_ref[...]


def project(spots, own, other, heads, gain_attn, gain_query, gain_key, cosine, sine):
    return ring_call(
        qkv_kernel,
        "project",
        ring_specs(WIDTH)
        + [pl.BlockSpec(heads.shape, lambda x, spots: (0, 0, 0))]
        + [whole_spec((1, WIDTH)), whole_spec((1, HEAD)), whole_spec((1, HEAD))]
        + [pack_spec(HEAD), pack_spec(HEAD)],
        [pack_spec(WIDTH), pack_spec(3 * HEAD), pack_spec(512), pack_spec(512)]
        + [whole_spec((512, WIDTH)), whole_spec((WIDTH, 512))],
        [
            shaped((PACK, WIDTH), jnp.bfloat16, True),
            shaped((PACK, 3 * HEAD), jnp.float32, True),
            shaped((PACK, 512), jnp.bfloat16),
            shaped((PACK, 512), jnp.bfloat16, True),
            shaped((512, WIDTH), jnp.bfloat16, True),
            shaped((WIDTH, 512), jnp.bfloat16, True),
        ],
        8, spots, own, other, heads, gain_attn, gain_query, gain_key, cosine, sine,
    )


def to_ring_kernel(spots, rows_ref, heads_ref, own_ref, other_ref, w_ref):
    @pl.when(pl.program_id(0) == 0)
    def _():
        for z in range(4):
            for y in range(4):
                block = jnp.where(spots[9] == 1, y * 4 + z, z * 4 + y)
                row = (z % 2 * 8 + y * 2 + z // 2) * 16
                for n in range(4):
                    piece = heads_ref[block, n * 16 : n * 16 + 16, 640:]
                    w_ref[row : row + 16, n * 256 : n * 256 + 256] = piece

    own_ref[...] = low(dot(rows_ref[own_rows(spots), :], w_ref[...]))
    other_ref[...] = low(dot(rows_ref[other_rows(spots), :], w_ref[...]))


def to_ring(spots, rows, heads):
    half = shaped((PACK // 2, WIDTH), jnp.bfloat16)
    return ring_call(
        to_ring_kernel, "to_ring",
        [pack_spec(256), pl.BlockSpec(heads.shape, lambda x, spots: (0, 0, 0))],
        ring_specs(WIDTH) + [whole_spec((256, WIDTH))],
        [half, half, shaped((256, WIDTH), jnp.bfloat16, True)], 3, spots, rows, heads,
    )


def to_pack_kernel(spots, own_ref, other_ref, w_ref, rows_ref):
    rows_ref[own_rows(spots), :] = low(dot(own_ref[...], w_ref[...]))
    rows_ref[other_rows(spots), :] = low(dot(other_ref[...], w_ref[...]))


def to_pack(spots, own, other, weights):
    return ring_call(
        to_pack_kernel, "to_pack", ring_specs(own.shape[1]) + [whole_spec(weights.shape)],
        [pack_spec(WIDTH)], [shaped((PACK, WIDTH), jnp.bfloat16)], 4, spots, own, other, weights,
    )[0]


def out_back_kernel(
    spots, own_ref, other_ref, attended_ref, w_ref, d_attended_ref, d_w_ref, rows_ref, total_ref
):
    step = pl.program_id(0)

    @pl.when(step == 0)
    def _():
        total_ref[...] = jnp.zeros_like(total_ref)

    rows_ref[own_rows(spots), :] = own_ref[...]
    rows_ref[other_rows(spots), :] = other_ref[...]
    d_attended_ref[...] = low(contract_cols(rows_ref[...], w_ref[...]))
    total_ref[...] += contract_rows(attended_ref[...], rows_ref[...])

    @pl.when(step == pl.num_programs(0) - 1)
    def _():
        for z in range(4):
            for y in range(4):
                spot = jnp.where(spots[9] == 1, y * 4 + z, z * 4 + y)
                spot = jnp.where(spots[10] == 1, (spot + 8) % 16, spot)
                row = (z % 2 * 8 + y * 2 + z // 2) * 16
                for n in range(4):
                    piece = total_ref[row : row + 16, n * 256 : n * 256 + 256]
                    d_w_ref[spot, n * 16 : n * 16 + 16, :] = low(piece)


def out_back(spots, own, other, attended, weights):
    return ring_call(
        out_back_kernel, "out_back",
        ring_specs(WIDTH) + [pack_spec(256), whole_spec((256, WIDTH))],
        [pack_spec(256), pl.BlockSpec((16, 64, 256), lambda x, spots: (0, 0, 0))],
        [shaped((PACK, 256), jnp.bfloat16), shaped((16, 64, 256), jnp.bfloat16, True)],
        5, spots, own, other, in_hbm(attended), in_hbm(weights),
        scratch=[pltpu.VMEM((2 * TOK, WIDTH), jnp.bfloat16), pltpu.VMEM((256, WIDTH), jnp.float32)],
    )


def row_start(rows, ends):
    first, second = ends
    return jnp.where(rows >= second, second, jnp.where(rows >= first, first, 0))


def block_mask(q_block, k_block, ends, transposed):
    last = PACK // BLOCK - 1
    q_axis, k_axis = (1, 0) if transposed else (0, 1)
    q_rows = q_block * BLOCK + lax.broadcasted_iota(jnp.int32, (BLOCK, BLOCK), q_axis)
    k_rows = k_block * BLOCK + lax.broadcasted_iota(jnp.int32, (BLOCK, BLOCK), k_axis)
    mask = None
    if k_block == q_block:
        mask = k_rows <= q_rows
    if k_block == 0 or q_block == last:
        begun = k_rows >= row_start(q_rows, ends)
        mask = begun if mask is None else mask & begun
    return mask


def for_each_block(step):
    for q_block in range(PACK // BLOCK):

        @pl.when(pl.program_id(0) == q_block)
        def _(q_block=q_block):
            step(q_block)


def attend_kernel(ends_ref, q_ref, k_ref, v_ref, out_ref, kept_ref, inverse_ref):
    ends = (ends_ref[0], ends_ref[1])

    def step(q_block):
        seen = (q_block + 1) * BLOCK
        for h in range(2):
            columns = slice(h * HEAD, (h + 1) * HEAD)
            scores = contract_cols(q_ref[:, columns], k_ref[:seen, :])
            part, shifted = 0.0, []
            for k_block in range(q_block + 1):
                block = scores[:, k_block * BLOCK : (k_block + 1) * BLOCK]
                block = jnp.exp2(block * (SCALE * LOG2E))
                mask = block_mask(q_block, k_block, ends, False)
                if mask is not None:
                    block = jnp.where(mask, block, 0.0)
                part += block[:, :HEAD] + block[:, HEAD:]
                shifted.append(low(block))
            total = dot(jnp.concatenate(shifted, axis=1), v_ref[:seen, :])
            row_total = jnp.sum(part, axis=1, keepdims=True)
            out_ref[:, columns] = low(total * (1.0 / row_total))
            across = jnp.sum(jnp.swapaxes(part, 0, 1), axis=0, keepdims=True)
            inverse_ref[h : h + 1, :] = 1.0 / across
        kept_ref[...] = out_ref[...]

    for_each_block(step)


def attend(ends, qkv):
    return pl.pallas_call(
        attend_kernel,
        grid_spec=pltpu.PrefetchScalarGridSpec(
            num_scalar_prefetch=1,
            grid=(PACK // BLOCK,),
            in_specs=[
                pl.BlockSpec((BLOCK, 2 * HEAD), lambda q, ends: (q, 0)),
                pl.BlockSpec((PACK, HEAD), lambda q, ends: (0, 2)),
                pl.BlockSpec((PACK, HEAD), lambda q, ends: (0, 3)),
            ],
            out_specs=[
                pl.BlockSpec((BLOCK, 2 * HEAD), lambda q, ends: (q, 0)),
                pl.BlockSpec((BLOCK, 2 * HEAD), lambda q, ends: (q, 0)),
                pl.BlockSpec((2, BLOCK), lambda q, ends: (0, q)),
            ],
        ),
        out_shape=[
            shaped((PACK, 2 * HEAD), jnp.bfloat16),
            shaped((PACK, 2 * HEAD), jnp.bfloat16, True),
            shaped((2, PACK), jnp.float32, True),
        ],
        compiler_params=pltpu.CompilerParams(vmem_limit_bytes=VMEM_LIMIT),
        cost_estimate=cost(6),
        name="attend",
    )(ends, qkv, qkv, qkv)


def attend_back_kernel(
    ends_ref, q_ref, k_ref, v_ref, grad_ref, out_ref, inverse_ref, dq_ref, dk_ref, dv_ref
):
    ends = (ends_ref[0], ends_ref[1])

    @pl.when(pl.program_id(0) == 0)
    def _():
        dk_ref[...] = jnp.zeros_like(dk_ref)
        dv_ref[...] = jnp.zeros_like(dv_ref)

    def both_heads(ref):
        return jnp.concatenate([ref[:, :HEAD], ref[:, HEAD:]], axis=0)

    def step(q_block):
        seen = (q_block + 1) * BLOCK
        queries, grads = both_heads(q_ref), both_heads(grad_ref)
        product = wide(grads) * wide(both_heads(out_ref))
        delta = jnp.sum(jnp.swapaxes(product, 0, 1), axis=0, keepdims=True)
        inverse = jnp.concatenate([inverse_ref[0:1, :], inverse_ref[1:2, :]], axis=1)
        scores = contract_cols(k_ref[:seen, :], queries)
        d_probs = contract_cols(v_ref[:seen, :], grads)
        probs, d_scores = [], []
        for k_block in range(q_block + 1):
            rows = slice(k_block * BLOCK, (k_block + 1) * BLOCK)
            prob = jnp.exp2(scores[rows] * (SCALE * LOG2E)) * inverse
            mask = block_mask(q_block, k_block, ends, True)
            if mask is not None:
                prob = jnp.where(jnp.concatenate([mask, mask], axis=1), prob, 0.0)
            d_scores.append(low(prob * ((d_probs[rows] - delta) * SCALE)))
            probs.append(low(prob))
        probs = jnp.concatenate(probs, axis=0)
        d_scores = jnp.concatenate(d_scores, axis=0)
        dk_ref[:seen, :] += dot(d_scores, queries)
        dv_ref[:seen, :] += dot(probs, grads)
        d_queries = contract_rows(d_scores, k_ref[:seen, :])
        dq_ref[:, :HEAD] = d_queries[:BLOCK]
        dq_ref[:, HEAD:] = d_queries[BLOCK:]

    for_each_block(step)


def attend_back(ends, qkv, grad, out, inverse):
    qkv, out, inverse = in_hbm(qkv), in_hbm(out), in_hbm(inverse)
    by_block = pl.BlockSpec((BLOCK, 2 * HEAD), lambda q, ends: (q, 0))
    whole = pl.BlockSpec((PACK, HEAD), lambda q, ends: (0, 0))
    return pl.pallas_call(
        attend_back_kernel,
        grid_spec=pltpu.PrefetchScalarGridSpec(
            num_scalar_prefetch=1,
            grid=(PACK // BLOCK,),
            in_specs=[
                by_block,
                pl.BlockSpec((PACK, HEAD), lambda q, ends: (0, 2)),
                pl.BlockSpec((PACK, HEAD), lambda q, ends: (0, 3)),
                by_block,
                by_block,
                pl.BlockSpec((2, BLOCK), lambda q, ends: (0, q)),
            ],
            out_specs=[by_block, whole, whole],
        ),
        out_shape=[
            jax.ShapeDtypeStruct((PACK, 2 * HEAD), jnp.float32),
            jax.ShapeDtypeStruct((PACK, HEAD), jnp.float32),
            jax.ShapeDtypeStruct((PACK, HEAD), jnp.float32),
        ],
        compiler_params=pltpu.CompilerParams(vmem_limit_bytes=VMEM_LIMIT),
        cost_estimate=cost(11),
        name="attend_back",
    )(ends, qkv, qkv, qkv, grad, out, inverse)


def qkv_back_kernel(
    spots, pre_ref, dq_ref, dk_ref, dv_ref, cos_ref, sin_ref, gq_ref, gk_ref, d_pre_ref, d_head_ref
):
    @pl.when(pl.program_id(0) == 0)
    def _():
        d_head_ref[...] = jnp.zeros_like(d_head_ref)

    cosine, sine = cos_ref[...], sin_ref[...]
    for h in range(3):
        u = pre_ref[:, h * HEAD : (h + 1) * HEAD]
        gain = gk_ref[...] if h == 2 else gq_ref[...]
        grad = dk_ref[...] if h == 2 else dq_ref[:, h * HEAD : (h + 1) * HEAD]
        grad = rope_back(grad, cosine, sine)
        row = 1 if h == 2 else 0
        scale = norm_scale(u)
        normal = u * scale
        d_head_ref[row : row + 1, :] += jnp.sum(grad * normal, axis=0, keepdims=True)
        inner = grad * gain
        inner = scale * (inner - normal * jnp.mean(inner * normal, axis=-1, keepdims=True))
        d_pre_ref[:, h * HEAD : (h + 1) * HEAD] = low(inner)
    d_pre_ref[:, 3 * HEAD :] = low(dv_ref[...])


def project_back(spots, pre, d_query, d_key, d_value, cosine, sine, gain_query, gain_key):
    return ring_call(
        qkv_back_kernel,
        "project_back",
        [pack_spec(3 * HEAD), pack_spec(2 * HEAD), pack_spec(HEAD), pack_spec(HEAD)]
        + [pack_spec(HEAD), pack_spec(HEAD), whole_spec((1, HEAD)), whole_spec((1, HEAD))],
        [pack_spec(512), whole_spec((2, HEAD))],
        [shaped((PACK, 512), jnp.bfloat16), shaped((2, HEAD), jnp.float32)],
        5, spots, in_hbm(pre), d_query, d_key, d_value, in_hbm(cosine), in_hbm(sine), gain_query, gain_key,
    )


def normed_back_kernel(spots, d_pre_ref, w_ref, own_ref, other_ref):
    own_ref[...] = low(dot(d_pre_ref[own_rows(spots), :], w_ref[...]))
    other_ref[...] = low(dot(d_pre_ref[other_rows(spots), :], w_ref[...]))


def normed_back(spots, d_pre, weights):
    half = shaped((PACK // 2, WIDTH), jnp.bfloat16)
    return ring_call(
        normed_back_kernel, "normed_back", [pack_spec(512), whole_spec((512, WIDTH))], ring_specs(WIDTH),
        [half, half], 4, spots, d_pre, in_hbm(weights),
    )


def plane_order(core, blocks):
    return jnp.where(core == 1, jnp.swapaxes(blocks, 0, 1), blocks)


def plane_bit(index, masks):
    return jnp.where(index & 1 == 1, index >> BIT[masks[1]], index >> BIT[masks[0]]) & 1


def gather_plane_step(index, block, step):
    got = swap(block, *PLANE_STEPS[step])
    return jnp.where(
        plane_bit(index, PLANE_STEPS[step]) == 1,
        jnp.concatenate([got, block], axis=0),
        jnp.concatenate([block, got], axis=0),
    )


def gather_plane_end(index, block):
    shape = block.shape[1:]
    return plane_order(index & 1, block.reshape((4, 4) + shape)).reshape((16,) + shape)


def plane_halves(index, blocks, step):
    later = plane_bit(index, PLANE_STEPS[step])
    half = blocks.shape[0] // 2
    keep = lax.dynamic_slice_in_dim(blocks, later * half, half, axis=0)
    send = lax.dynamic_slice_in_dim(blocks, (1 - later) * half, half, axis=0)
    return keep, swap(send, *PLANE_STEPS[step])


def scatter_plane_step(index, blocks, step, *beside):
    keep, got = plane_halves(index, blocks, step)
    return low(wide(keep) + wide(after(got, *beside)))


def plane_rest(index, blocks):
    place = jnp.where(index & 1 == 1, index >> 3, index >> 1) & 3
    block = lambda at: lax.dynamic_index_in_dim(blocks, at, 0, keepdims=False)
    return block(place), [swap(block(place ^ k), k << 1, k << 3) for k in range(1, 4)]


def plane_blocks(core, blocks):
    shape = blocks.shape[1:]
    return plane_order(core, blocks.reshape((4, 4) + shape)).reshape((16,) + shape)


def gather_ring(rows, beside=((), ())):
    for masks, others in zip(RING_STEPS, beside):
        rows = jnp.concatenate([rows, after(swap(rows, *masks), *others)], axis=0)
    return rows


def scatter_ring(own, other, steps=2):
    totals = [wide(own) + wide(swap(other, CORE))]
    for masks in RING_STEPS[: -steps - 1 : -1]:
        half = totals[-1].shape[0] // 2
        totals.append(totals[-1][:half] + wide(swap(low(totals[-1][half:]), *masks)))
    return totals


def exchange_ring(index, blocks):
    core, x = index & 1, index >> 5
    shape = blocks.shape[1:]
    blocks = blocks.reshape((4, 2) + shape)
    take = lambda array, at, axis: lax.dynamic_slice_in_dim(array, at, 1, axis)
    got = swap(take(blocks, 1 - core, 1), CORE)
    keep = take(blocks, core, 1)
    blocks = jnp.concatenate(
        [jnp.where(core == 1, got, keep), jnp.where(core == 1, keep, got)], axis=1
    )
    parts = [take(blocks, x, 0)] + [
        swap(take(blocks, x ^ k, 0), k << 5) for k in range(1, 4)
    ]
    parts = jnp.concatenate(parts, axis=0)
    parts = jnp.where(x & 1 == 1, parts.reshape((2, 2, 2) + shape)[:, ::-1].reshape(parts.shape), parts)
    parts = jnp.where(x & 2 == 2, parts.reshape((2, 4) + shape)[::-1].reshape(parts.shape), parts)
    return parts.reshape((8,) + shape)


def tiles_tall(block):
    lead = block.shape[:-2]
    n = len(lead)
    block = block.reshape(lead + (-1, 8, 8, HEAD))
    block = block.transpose(tuple(range(n)) + (n + 2, n + 1, n, n + 3))
    return block.reshape(lead + (64, -1))


def tiles_flat(block):
    lead = block.shape[:-2]
    n = len(lead)
    block = block.reshape(lead + (8, 8, -1, HEAD))
    block = block.transpose(tuple(range(n)) + (n + 2, n + 1, n, n + 3))
    return block.reshape(lead + (-1, WIDTH))


def rows_by_device(blocks):
    n = blocks.shape[-1]
    return blocks.reshape(16, 4, 2, 8, n).transpose(1, 0, 2, 3, 4).reshape(WIDTH, n)


def rows_by_plane(rows):
    n = rows.shape[-1]
    return rows.reshape(4, 16, 2, 8, n).transpose(1, 0, 2, 3, 4).reshape(16, 64, n)


def on_device(
    hidden, lengths, w_query, w_key, w_value, w_out, w_gate, w_up, w_down, gains, cotangent
):
    index = lax.axis_index(AXES).astype(jnp.int32)
    core, x = index & 1, index >> 5
    straight = (index >> 4 & 1) == core
    spot_of = lambda c: jnp.where(c == 1, jnp.asarray(RING_SPOTS[1]), jnp.asarray(RING_SPOTS[0]))
    chips = x ^ jnp.arange(4, dtype=jnp.int32)
    spots = jnp.concatenate(
        [spot_of(core)[chips], spot_of(1 - core)[chips], core[None], core[None]]
        + [plane_bit(index, PLANE_STEPS[3])[None]]
    ).astype(jnp.int32)

    local = jnp.concatenate(
        [
            w_query.reshape(8, KV_HEADS, 256).transpose(1, 0, 2),
            w_key.reshape(8, KV_HEADS, HEAD).transpose(1, 0, 2),
            w_value.reshape(8, KV_HEADS, HEAD).transpose(1, 0, 2),
            jnp.broadcast_to(jnp.pad(gains[None, None, :], ((0, 0), (0, 7), (0, 110))), (8, 8, 128)),
        ]
        + [
            weight.reshape(8, 4, 16, 2, 24).transpose(1, 3, 0, 2, 4).reshape(8, 8, 384)
            for weight in (w_gate, w_up)
        ],
        axis=2,
    )
    digits = jnp.pad(low(jnp.stack([lengths[0] // 64, lengths[0] % 64])), ((0, 14), (0, WIDTH - 3)))
    pieces = cross(jnp.concatenate([w_out, digits], axis=0))
    rows = after(hidden[0], local)
    inputs = cross(rows)
    second = swap(inputs, *RING_STEPS[0])
    digits = pieces[16:18, :3].astype(jnp.int32)
    lengths = (digits[0] * 64 + digits[1])[None]
    pieces = pieces[:16].reshape(16, 4, 256).transpose(1, 0, 2).reshape(64, 256)
    local = exchange_ring(index, local).reshape(64, 1408)
    d_result = cross(after(cotangent[0], local))
    heads = jnp.concatenate([local[:, :640], pieces], axis=1)[None]
    heads = gather_plane_step(index, after(heads, inputs, second), 0)
    heads = gather_plane_step(index, after(heads, d_result), 1)
    d_result_own = jnp.concatenate([d_result, swap(d_result, *RING_STEPS[0])], axis=0)
    heads = gather_plane_step(index, heads, 2)
    heads = gather_plane_step(index, after(heads, d_result_own), 3)
    gain_all = plane_order(core, heads[:, ::8, 512:530].reshape(4, 4, 8, 18))
    gain_all = gain_all.reshape(16, 4, 2, 18).transpose(1, 0, 2, 3)
    gain_all = wide(gain_all.reshape(1, -1))
    gain_attn, gain_mlp = gain_all[:, :WIDTH], gain_all[:, WIDTH : 2 * WIDTH]
    gain_query = gain_all[:, 2 * WIDTH : 2 * WIDTH + HEAD]
    gain_key = gain_all[:, 2 * WIDTH + HEAD :]

    def rest_of_ring(rows):
        rows = jnp.concatenate([rows, swap(rows, *RING_STEPS[1])], axis=0)
        return rows, swap(rows, CORE)

    inputs_own, inputs_other = rest_of_ring(jnp.concatenate([inputs, second], axis=0))
    ends = jnp.stack([lengths[0, 0], lengths[0, 0] + lengths[0, 1]]).astype(jnp.int32)
    token = jnp.arange(PACK, dtype=jnp.int32)
    position = wide(token - row_start(token, (ends[0], ends[1])))
    inverse = jnp.power(ROPE_BASE, -2.0 * jnp.arange(HEAD // 2, dtype=jnp.float32) / HEAD)
    angle = position[:, None] * inverse[None, :]
    cosine, sine = jnp.cos(angle), jnp.sin(angle)
    cosine = jnp.concatenate([cosine, cosine], axis=1)
    sine = jnp.concatenate([-sine, sine], axis=1)

    d_result_own = jnp.concatenate([d_result_own, swap(d_result_own, *RING_STEPS[1])], axis=0)
    normed, pre, qkv, qkv_kept, w_heads_across, w_heads = project(
        spots, inputs_own, inputs_other, heads, gain_attn, gain_query, gain_key, cosine, sine
    )
    qkv, d_result_own = lax.optimization_barrier((qkv, d_result_own))
    attended, attended_kept, inverse_total = attend(ends, qkv)
    out_own, out_other, w_rows = to_ring(spots, attended, heads)
    middle_steps = scatter_ring(out_own, out_other)
    d_result_other = swap(after(d_result_own, middle_steps[0]), CORE)
    units = jnp.concatenate([local[:, 640:], tiles_tall(w_down)], axis=1)[None]
    units = gather_plane_step(index, after(units, out_own), 0)
    units = gather_plane_step(index, after(units, middle_steps[0]), 1)
    units = gather_plane_step(index, after(units, middle_steps[1]), 2)
    middle = wide(inputs) + middle_steps[2]
    middle_scale = norm_scale(middle)
    mixed = low(middle * middle_scale * gain_mlp)
    mixed_own = gather_ring(mixed)
    mixed_other = swap(mixed_own, CORE)
    units = gather_plane_step(index, units, 3)
    units = plane_blocks(core, units)
    full_units = rows_by_device(units[..., :768])
    full_down = tiles_flat(units[..., 768:]).reshape(384, WIDTH)
    full_units, full_down = lax.optimization_barrier((full_units, full_down))

    def feed_forward(rows, d_rows):
        pre = dot(rows, full_units)
        gate_pre, up_pre = pre[:, :384], pre[:, 384:]
        sigmoid = 1.0 / (1.0 + jnp.exp(-gate_pre))
        silu = gate_pre * sigmoid
        act = low(silu * up_pre)
        d_act = contract_cols(d_rows, full_down)
        d_gate = low(d_act * up_pre * (sigmoid + silu * (1.0 - sigmoid)))
        d_up = low(d_act * silu)
        d_pre = jnp.concatenate([d_gate, d_up], axis=1)
        return act, d_pre, low(contract_cols(d_pre, full_units))

    act_own, d_pre_own, d_mixed_own = feed_forward(mixed_own, d_result_own)
    act_other, d_pre_other, d_mixed_other = feed_forward(mixed_other, d_result_other)
    d_mixed_steps = scatter_ring(d_mixed_own, d_mixed_other)
    d_mixed = d_mixed_steps[-1]
    d_middle = wide(d_result) + norm_back(middle, gain_mlp, d_mixed)
    d_gain_mlp = jnp.sum(middle * middle_scale * d_mixed, axis=0)

    late = lambda array: after(array, d_mixed_steps[0])
    grad_units = contract_rows(mixed_own, late(d_pre_own)) + contract_rows(mixed_other, late(d_pre_other))
    grad_down = contract_rows(late(act_own), d_result_own) + contract_rows(late(act_other), d_result_other)
    grad_down = low(grad_down).reshape(16, 3, 8, 8, HEAD).transpose(0, 3, 2, 1, 4)
    grads = jnp.concatenate([rows_by_plane(low(grad_units)), grad_down.reshape(16, 64, 384)], axis=2)
    grads = plane_blocks(core, grads)
    act_own, act_other = (after(act, d_middle) for act in (act_own, act_other))
    result = to_pack(spots, act_own, act_other, full_down)
    keep, got = plane_halves(index, grads, 3)
    d_branch_own = gather_ring(after(low(d_middle), grads), ((), (result, got)))
    sums = low(wide(keep) + wide(got))
    d_branch_other = swap(d_branch_own, CORE)
    result = lax.psum_scatter(after(result, d_branch_own), RING, scatter_dimension=0, tiled=True)

    d_attended, grad_out = out_back(spots, d_branch_own, d_branch_other, attended_kept, w_rows)
    d_attended, grad_out = lax.optimization_barrier((d_attended, grad_out))
    sums_keep, sums_got = plane_halves(index, sums, 2)
    out_got = swap(grad_out[8:], *PLANE_STEPS[3])
    d_query, d_key, d_value = attend_back(ends, qkv_kept, d_attended, attended_kept, inverse_total)
    d_query, sums_got, out_got = lax.optimization_barrier((d_query, sums_got, out_got))
    d_pre, d_gain_heads = project_back(
        spots, pre, d_query, d_key, d_value, cosine, sine, gain_query, gain_key
    )
    grad_heads = contract_rows(normed, d_pre)
    d_gain_attn = jnp.sum(grad_heads * wide(w_heads), axis=1) / gain_attn[0]
    d_gains = jnp.concatenate([d_gain_attn, d_gain_mlp, d_gain_heads.reshape(-1)])
    d_gains = d_gains.reshape(4, 16, 2, 1, 18).transpose(1, 0, 2, 3, 4)
    payload = jnp.concatenate(
        [
            rows_by_plane(low(grad_heads)),
            low(jnp.pad(d_gains, ((0, 0),) * 3 + ((0, 7), (0, 110)))).reshape(16, 64, 128),
        ],
        axis=2,
    )
    payload = plane_blocks(core, payload)
    d_pre, payload = lax.optimization_barrier((d_pre, payload))
    d_normed_own, d_normed_other = normed_back(spots, d_pre, w_heads_across)
    got = swap(d_normed_other, CORE)
    total = wide(d_normed_own) + wide(got)
    keep, send = total[: 2 * TOK], low(total[2 * TOK :])
    payload, out_got = (after(array, send) for array in (payload, out_got))
    sums_out = low(wide(grad_out[:8]) + wide(out_got))
    heads_keep, heads_got = plane_halves(index, payload, 3)
    out_keep, out_got = plane_halves(index, sums_out, 2)
    got, heads_got, out_got, result = lax.optimization_barrier(
        (swap(send, *RING_STEPS[1]), heads_got, out_got, result)
    )
    sums_out = low(wide(out_keep) + wide(out_got))
    heads_sums = low(wide(heads_keep) + wide(heads_got))
    total = keep + wide(got)
    heads_keep, heads_got = plane_halves(index, heads_sums, 2)
    sums_keep, sums_got = plane_rest(index, low(wide(sums_keep) + wide(sums_got)))
    got, heads_got, sums_got = lax.optimization_barrier(
        (swap(low(total[TOK:]), *RING_STEPS[0]), heads_got, sums_got)
    )
    sums = wide(sums_keep) + sum(wide(part) for part in sums_got)
    heads_sums = low(wide(heads_keep) + wide(heads_got))
    d_normed = total[:TOK] + wide(got)
    input_grad = d_middle + norm_back(wide(inputs), gain_attn, d_normed)
    heads_keep, heads_got = plane_rest(index, heads_sums)
    out_keep, out_got = plane_rest(index, sums_out)
    home, heads_got, out_got = lax.optimization_barrier(
        (cross(low(input_grad)), heads_got, out_got)
    )
    sum_out = wide(out_keep) + sum(wide(part) for part in out_got)
    input_grad = jnp.where(straight, input_grad, wide(home))
    heads_sums = low(wide(heads_keep) + sum(wide(part) for part in heads_got))
    sum_down = tiles_flat(sums[:, 768:])
    sum_out = sum_out.reshape(4, 16, 256).transpose(1, 0, 2).reshape(16, WIDTH)
    result = jnp.concatenate([middle + wide(result), sum_out], axis=0)
    result = cross(after(low(result), heads_sums))
    ring_grads = jnp.concatenate([heads_sums, low(sums[:, :768])], axis=1)
    ring_grads = exchange_ring(index, ring_grads.reshape(8, 8, 1408))
    heads_grad, units_grad = wide(ring_grads[..., :640]), ring_grads[..., 640:]
    activations = result[:TOK]
    sum_out = jnp.where(straight, sum_out, wide(result[TOK:]))
    column = jnp.arange(768, dtype=jnp.int32)
    column = column // 24 % 2 * 384 + column // 48 * 24 + column % 24
    column = after(column, middle)
    hits = lax.broadcasted_iota(jnp.int32, (768, 768), 0) == column[None, :]
    units_grad = units_grad.reshape(4, 2, 8, 2, 384).transpose(3, 2, 0, 1, 4).reshape(64, 768)
    units_grad = dot(units_grad, hits.astype(jnp.bfloat16)).reshape(2, 8, FF)
    sum_query = heads_grad[..., :256].transpose(1, 0, 2).reshape(8, -1)
    sum_key = heads_grad[..., 256:384].transpose(1, 0, 2).reshape(8, -1)
    sum_value = heads_grad[..., 384:512].transpose(1, 0, 2).reshape(8, -1)
    sum_gains = jnp.sum(heads_grad[:, 0, 512:530], axis=0)
    return (
        activations[None],
        input_grad[None],
        sum_query,
        sum_key,
        sum_value,
        sum_out,
        units_grad[0],
        units_grad[1],
        sum_down,
        sum_gains,
    )


def solution(mesh):
    chips = Mesh(mesh.devices.reshape(4, 2, 2, 4, 2), AXES)
    rows = P(AXES, None)
    tokens = P(("zl", "y", "core"), ("x", "zh"), None)
    lengths = P(("zl", "y", "core"), None)
    return jax.shard_map(
        on_device,
        mesh=chips,
        in_specs=(tokens, lengths, *([rows] * 7), P(AXES), tokens),
        out_specs=(tokens, tokens, *([rows] * 7), P(AXES)),
        check_vma=False,
    )
```
